32 devices in a mesh: frames: 2 (over y), row: 4 (over x, core), col: 4 (over z).
Axes of the slice: x: 2, y: 2, z: 4, core: 2. Of those that a mesh axis runs over, the one named last changes fastest.
Arguments:
- mask_pixels: int32 [2048, 2048], P(('frames', 'row'), 'col'), parts along dimension 0, may hold values 0 or 1
- across_taps: bfloat16 [12, 2, 33], replicated, may hold values from -1 to 1
- down_taps: bfloat16 [12, 2, 33], replicated, may hold values from -1 to 1
- kernel_weights: float32 [12], replicated, may hold values from 0.05 to 0.5
- library: bfloat16 [32, 64, 128], P('col'), may hold values from 0 to 4
- cell_ids: int32 [8, 4, 8], P(('frames', 'row'), 'col'), parts along dimension 0, may hold values from 0 to 31, as said below
- cell_slots: int32 [8, 4, 8], P(('frames', 'row'), 'col'), parts along dimension 0, may hold values from 0 to 15, as said below
- cell_count: int32 [8, 4], P(('frames', 'row'), 'col'), parts along dimension 0, may hold values from 2 to 8
Outputs:
- resist: float32 [2048, 2048], P(('frames', 'row'), 'col'), parts along dimension 0
The draws below stay inside these ranges and needn't reach their ends.
There are 2 independent parts, one for each index of `frames`. The reference program is written for one: setup_inputs(seed, part) draws one part's arguments, and reference() takes and returns one part's arrays. A program takes and returns all parts, laid end to end along the dimension named above; an argument that names none is the same for every part. Nothing has to cross between parts.
Inputs may be any that keep to these rules, and one draw needn't show every extreme that they name: `cell_ids`: among the 8 entries of a tile's list, at most 2 name cells of one block of 8 consecutive ids (k * 8 to k * 8 + 7), and the first two entries name cells of one such block. `cell_slots`: the slots of a tile's list are distinct.
All inputs are finite; a program needn't handle non-finite values. No bound on the sum of `mask_pixels` on one device may be relied on, other than what follows from the above.
Results may differ from the reference program's by a relative error of at most 0.00045.
Values may be sent and summed in bfloat16 or wider, within the bound.
No kernel may reach another device: no remote copies, remote signals or barrier semaphores. Data moves between devices by JAX's collectives and lax.ppermute only.
A program may use at most 64 MiB of HBM per device.

```python
import math
import jax
import jax.numpy as jnp
from jax import lax

KERNELS = 12
XHALF = 16
BLUR_HALF = 8
CELL_R = 64
CELL_C = 128
CELL_DEV = 8
ROWS = 1024
COLS = 2048
NCELL = 32
SLOTS = 16
MAXI = 8
N_ROW = 4
N_COL = 4


def draw_library(key, part):
    key_list = jax.random.split(jax.random.fold_in(key, 5003), 2)
    block_shape = (NCELL, CELL_R // 4, CELL_C // 4)
    theta = jax.random.uniform(key_list[0], block_shape, jnp.float32, 0.0, 6.283185307)
    level = 2.0 + 1.96 * jnp.tanh(4.0 * jnp.sin(theta))
    factor = jax.random.uniform(key_list[1], (NCELL, CELL_R, CELL_C), jnp.float32, 0.8, 1.0)
    level = jnp.repeat(jnp.repeat(level, 4, axis=1), 4, axis=2)
    return (level * factor).astype(jnp.bfloat16)


def instance_tables(key):
    key_list = jax.random.split(jax.random.fold_in(key, 7001), 12)
    tile_grid = (N_ROW, N_COL)
    band_owner = jax.random.randint(key_list[0], (N_ROW, 1), 0, N_COL)
    tile_owner = jax.random.randint(key_list[1], tile_grid, 0, N_COL)
    band_flag = jax.random.randint(key_list[2], (N_ROW, 1), 0, 2)
    forced_band = jax.random.randint(key_list[3], (), 0, N_ROW)
    band_flag = jnp.where(jnp.arange(N_ROW, dtype=jnp.int32)[:, None] == forced_band, 1, band_flag)
    first_owner = jnp.where(band_flag == 1, band_owner, tile_owner)
    owner_iota = jnp.arange(N_COL, dtype=jnp.int32)
    owner_score = jax.random.randint(key_list[4], tile_grid + (N_COL,), 0, 1 << 20) * N_COL + owner_iota
    owner_score = jnp.where(owner_iota == first_owner[..., None], -1, owner_score)
    ranked = jnp.argsort(owner_score, axis=-1).astype(jnp.int32)
    others = jnp.concatenate([ranked[..., 1:], ranked[..., 1:]], axis=-1)
    spare = 2 * N_COL - 2
    shuffle_score = jax.random.randint(key_list[5], tile_grid + (spare,), 0, 1 << 20) * (2 * N_COL) + jnp.arange(spare, dtype=jnp.int32)
    shuffle_order = jnp.argsort(shuffle_score, axis=-1)
    others = jnp.take_along_axis(others, shuffle_order, axis=-1)
    owners = jnp.concatenate([ranked[..., :1], ranked[..., :1], others], axis=-1)[..., :MAXI]
    local_index = jax.random.randint(key_list[6], tile_grid + (MAXI,), 0, CELL_DEV)
    cell_ids = owners * CELL_DEV + local_index
    slot_score = jax.random.randint(key_list[7], tile_grid + (SLOTS,), 0, 1 << 20) * SLOTS + jnp.arange(SLOTS, dtype=jnp.int32)
    cell_slots = jnp.argsort(slot_score, axis=-1)[..., :MAXI]
    first_draw = jax.random.randint(key_list[8], tile_grid, 0, MAXI)
    second_draw = jax.random.randint(key_list[9], tile_grid, 0, MAXI)
    cell_count = MAXI - first_draw * second_draw // MAXI
    tile_iota = jnp.arange(N_ROW * N_COL, dtype=jnp.int32).reshape(tile_grid)
    full_tile = jax.random.randint(key_list[10], (), 0, N_ROW * N_COL)
    short_tile = (full_tile + 1 + jax.random.randint(key_list[11], (), 0, N_ROW * N_COL - 1)) % (N_ROW * N_COL)
    cell_count = jnp.where(tile_iota == full_tile, MAXI, cell_count)
    cell_count = jnp.where(tile_iota == short_tile, 2, cell_count)
    return (cell_ids.astype(jnp.int32), cell_slots.astype(jnp.int32), cell_count.astype(jnp.int32))


def draw_cell_ids(key, part):
    return instance_tables(key)[0]


def draw_cell_slots(key, part):
    return instance_tables(key)[1]


def draw_cell_count(key, part):
    return instance_tables(key)[2]


def set_ends(values, key, least, largest):
    shape = values.shape
    place = [jax.random.randint(jax.random.fold_in(key, axis), (), 0, shape[axis]) for axis in range(len(shape))]
    values = values.at[tuple(place)].set(least)
    longest = shape.index(max(shape))
    place[longest] = (place[longest] + 1) % shape[longest]
    return values.at[tuple(place)].set(largest)


def scatter_about(stream_key, extent, width, reach, kind=jnp.bfloat16):
    return jnp.clip(width * jax.random.normal(stream_key, extent, jnp.float32), -reach, reach).astype(kind)


def setup_inputs(seed: int = 0, part: int = 0) -> dict:
    streams_of = jax.random.split(jax.random.key(seed), 9)
    part_keys = jax.random.split(jax.random.fold_in(streams_of[8], part), 9)
    return {
        "mask_pixels": set_ends((jax.random.randint(part_keys[0], (ROWS, COLS), 0, 2) < 1).astype(jnp.int32), jax.random.fold_in(part_keys[0], 1), 0, 1),
        "across_taps": scatter_about(streams_of[1], (KERNELS, 2, 2 * XHALF + 1), (2 * XHALF + 1) ** -0.5, 1.0),
        "down_taps": scatter_about(streams_of[2], (KERNELS, 2, 2 * XHALF + 1), (2 * XHALF + 1) ** -0.5, 1.0),
        "kernel_weights": jnp.clip(jnp.exp(jax.random.uniform(streams_of[3], (KERNELS,), jnp.float32, math.log(0.05), math.log(0.5))), 0.05, 0.5),
        "library": draw_library(jax.random.fold_in(streams_of[8], 71), part),
        "cell_ids": draw_cell_ids(jax.random.fold_in(jax.random.fold_in(streams_of[8], part), 71), part),
        "cell_slots": draw_cell_slots(jax.random.fold_in(jax.random.fold_in(streams_of[8], part), 71), part),
        "cell_count": draw_cell_count(jax.random.fold_in(jax.random.fold_in(streams_of[8], part), 71), part),
    }


BLUR_SIGMA = 4.0


def band_matrix(tap_values, half_width):
    window = 128 + 2 * half_width
    grid_shape = (window, 128, 2 * half_width + 1)
    in_index = lax.broadcasted_iota(jnp.int32, grid_shape, 0)
    out_index = lax.broadcasted_iota(jnp.int32, grid_shape, 1)
    lag_index = lax.broadcasted_iota(jnp.int32, grid_shape, 2)
    picker = (in_index - out_index == lag_index).astype(jnp.float32)
    return jnp.einsum("...t,ijt->...ij", tap_values.astype(jnp.float32), picker, precision=lax.Precision.HIGHEST)


def blur_taps(half_width):
    offsets = lax.broadcasted_iota(jnp.int32, (2 * half_width + 1,), 0).astype(jnp.float32) - half_width
    weights = jnp.exp(-offsets * offsets / (2.0 * BLUR_SIGMA * BLUR_SIGMA))
    return weights / jnp.sum(weights)


def windows_last(padded, half_width):
    length = padded.shape[-1] - 2 * half_width
    blocks = length // 128
    pad_spec = [(0, 0)] * (padded.ndim - 1) + [(0, 128 - 2 * half_width)]
    spread = jnp.pad(padded, pad_spec).reshape(padded.shape[:-1] + (blocks + 1, 128))
    return jnp.concatenate([spread[..., :blocks, :], spread[..., 1:, :2 * half_width]], axis=-1)


def windows_rows(padded, half_width):
    length = padded.shape[-2] - 2 * half_width
    blocks = length // 128
    pad_spec = [(0, 0)] * (padded.ndim - 2) + [(0, 128 - 2 * half_width), (0, 0)]
    spread = jnp.pad(padded, pad_spec).reshape(padded.shape[:-2] + (blocks + 1, 128, padded.shape[-1]))
    return jnp.concatenate([spread[..., :blocks, :, :], spread[..., 1:, :2 * half_width, :]], axis=-2)


def blur_straight(extended, blur_mat, half_width):
    sideways = jnp.einsum("rbi,ij->rbj", windows_last(extended, half_width), blur_mat, precision=lax.Precision.HIGHEST)
    sideways = sideways.reshape(extended.shape[0], -1)
    downward = jnp.einsum("biw,ij->bjw", windows_rows(sideways, half_width), blur_mat, precision=lax.Precision.HIGHEST)
    return downward.reshape(-1, sideways.shape[1])


def reference(mask_pixels, across_taps, down_taps, kernel_weights, library, cell_ids, cell_slots, cell_count):
    half_width = (across_taps.shape[-1] - 1) // 2
    frame_rows, frame_cols = mask_pixels.shape
    pixels = mask_pixels.astype(jnp.float32)
    padded_mask = jnp.pad(pixels, ((0, 0), (half_width, half_width)))
    mask_windows = windows_last(padded_mask, half_width)
    first_mats = band_matrix(across_taps, half_width)
    second_mats = band_matrix(down_taps, half_width)
    flat_image = jnp.zeros((frame_rows, frame_cols), jnp.float32)
    for kernel in range(across_taps.shape[0]):
        pass_one = jnp.einsum("rbi,pij->prbj", mask_windows, first_mats[kernel], precision=lax.Precision.HIGHEST)
        pass_one = pass_one.reshape(2, frame_rows, frame_cols)
        pass_one = lax.optimization_barrier(pass_one.astype(jnp.bfloat16)).astype(jnp.float32)
        extended = jnp.pad(pass_one, ((0, 0), (half_width, half_width), (0, 0)))
        pass_two = jnp.einsum("pbiw,pij->pbjw", windows_rows(extended, half_width), second_mats[kernel], precision=lax.Precision.HIGHEST)
        pass_two = pass_two.reshape(2, frame_rows, frame_cols)
        flat_image = flat_image + kernel_weights[kernel] * jnp.sum(pass_two * pass_two, axis=0)
    tiles_r, tiles_c, entries = cell_ids.shape
    tile_rows = frame_rows // tiles_r
    tile_cols = frame_cols // tiles_c
    cell_rows, cell_cols = library.shape[1], library.shape[2]
    slot_rows = tile_rows // cell_rows
    slot_cols = tile_cols // cell_cols
    is_live = lax.broadcasted_iota(jnp.int32, (tiles_r, tiles_c, entries), 2) < cell_count[:, :, None]
    slot_hit = (cell_slots[..., None] == lax.broadcasted_iota(jnp.int32, (1, 1, 1, slot_rows * slot_cols), 3)) & is_live[..., None]
    slot_hit = slot_hit.astype(jnp.float32).reshape(tiles_r, tiles_c, entries, slot_rows, slot_cols)
    images = jnp.take(library, cell_ids, axis=0).astype(jnp.float32)
    placed = jnp.einsum("rcmab,rcmpq->rapcbq", slot_hit, images, precision=lax.Precision.HIGHEST)
    placed = placed.reshape(frame_rows, frame_cols)
    intensity = flat_image + placed
    blur_mat = band_matrix(blur_taps(BLUR_HALF), BLUR_HALF)
    extended = jnp.pad(intensity, ((BLUR_HALF, BLUR_HALF), (BLUR_HALF, BLUR_HALF)))
    return blur_straight(extended, blur_mat, BLUR_HALF)
```

```python
import functools
import math

import jax
import jax.numpy as jnp
from jax import lax
from jax.experimental import pallas as pl
from jax.experimental.pallas import tpu as pltpu
from jax.sharding import PartitionSpec as P

BLUR_HALF = 8
BLUR_SIGMA = 4.0
HALF = 16
RIM = HALF + BLUR_HALF
STRIP = 32
CB = 176
NB = 3
MAIN = 224
EDGE_IN = 80
EDGE_OUT = 48
EDGE_AT = (0, 48, 128)
WIDE = 640
F32 = jnp.float32
BF16 = jnp.bfloat16
VMEM = pl.BlockSpec(memory_space=pltpu.VMEM)
SMEM = pl.BlockSpec(memory_space=pltpu.SMEM)
PARAMS = pltpu.CompilerParams(vmem_limit_bytes=40 * 1024 * 1024)


def dot_nt(a, b):
    return lax.dot_general(a, b, (((1,), (1,)), ((), ())), preferred_element_type=F32)


def dot_nn(a, b):
    return lax.dot_general(a, b, (((1,), (0,)), ((), ())), preferred_element_type=F32)


def prep_kernel(mask, table, first, last, pixels):
    full = mask[...].astype(F32)
    pixels[...] = full
    cols = full.shape[1]
    first[0:STRIP, :] = full[:, 0:128].T[0:STRIP].astype(BF16)
    last[0:STRIP, :] = full[:, cols - 128 : cols].T[128 - STRIP :].astype(BF16)
    first[STRIP:, :] = table[...]
    last[STRIP:, :] = table[...]


def mid_kernel(pixels, left, right, table, top, bottom, wide):
    rows = pixels.shape[0]
    lhs = left[0:STRIP, :].astype(F32)
    rhs = right[0:STRIP, :].astype(F32)
    fill = jnp.zeros((128 - STRIP, rows), F32)
    lhs = jnp.concatenate([lhs, fill], axis=0).T
    rhs = jnp.concatenate([rhs, fill], axis=0).T
    full = jnp.concatenate(
        [lhs[:, STRIP - RIM : STRIP], pixels[...], rhs[:, 0 : WIDE - RIM - pixels.shape[1]]], axis=1
    )
    wide[...] = full
    top[0:STRIP, :] = full[0:STRIP].astype(BF16)
    bottom[0:STRIP, :] = full[rows - STRIP :].astype(BF16)
    tables = jnp.concatenate(
        [left[STRIP:, 0:128], table[:, 0:128], right[STRIP:, 0:128], jnp.zeros((16, 256), BF16)], axis=1
    )
    top[STRIP:, :] = tables
    bottom[STRIP:, :] = tables


def bands_kernel(across, down, b1, d_main, d_edge, g_hi, g_lo, g2_hi, g2_lo):
    row = lax.broadcasted_iota(jnp.int32, (128, 128), 0)
    lane = lax.broadcasted_iota(jnp.int32, (128, 128), 1)
    zero = jnp.zeros((128, 128), F32)

    def blur_matrix(width, shift):
        at = lax.broadcasted_iota(jnp.int32, (128, width), 1)
        lag = at - lax.broadcasted_iota(jnp.int32, (128, width), 0) - shift
        total = sum(math.exp(-(t * t) / (2 * BLUR_SIGMA**2)) for t in range(-BLUR_HALF, BLUR_HALF + 1))
        off = (lag - BLUR_HALF).astype(F32)
        g = jnp.exp(-off * off / (2.0 * BLUR_SIGMA * BLUR_SIGMA)) * (1.0 / total)
        g = jnp.where((lag >= 0) & (lag <= 2 * BLUR_HALF), g, 0.0)
        hi = g.astype(BF16)
        return hi, (g - hi.astype(F32)).astype(BF16)

    g_hi[...], g_lo[...] = blur_matrix(256, 0)
    g2_hi[...], g2_lo[...] = blur_matrix(384, 128 - BLUR_HALF)

    def step(kp, carry):
        taps = jnp.broadcast_to(across[pl.ds(kp, 1), :], (128, 128))
        cyc = pltpu.roll(taps, 0, 1, stride=1, stride_axis=0)
        upper = jnp.where(lane >= row, cyc, 0.0).astype(BF16)
        over = jnp.where(lane < row, cyc, 0.0).astype(BF16)
        b1[kp, 0:128, 0:128] = upper
        b1[kp, 0:128, 128:256] = over
        b1[kp, 128:CB, 0:128] = jnp.zeros((CB - 128, 128), BF16)
        b1[kp, 128:CB, 128:256] = upper[0 : CB - 128]
        taps = jnp.broadcast_to(down[pl.ds(kp, 1), :], (128, 128))
        cyc = pltpu.roll(taps, 0, 1, stride=1, stride_axis=0).T
        same = jnp.where(row >= lane, cyc, 0.0)
        over = jnp.where(row < lane, cyc, 0.0)
        d_main[kp, 0:128, 0:128] = same.astype(BF16)
        d_main[kp, 0:128, 128:256] = zero.astype(BF16)
        d_main[kp, 128:256, 0:128] = over.astype(BF16)
        d_main[kp, 128:256, 128:256] = same.astype(BF16)
        edge = jnp.where(lane < EDGE_OUT, same, 0.0)
        moved = pltpu.roll(edge, EDGE_AT[1], 1)[0:EDGE_IN].astype(BF16)
        edge = edge[0:EDGE_IN].astype(BF16)
        none = jnp.zeros((EDGE_IN, 128), BF16)
        d_edge[kp, 0:EDGE_IN, 0:128] = edge
        d_edge[kp, 0:EDGE_IN, 128:256] = none
        d_edge[kp, EDGE_IN : 2 * EDGE_IN, 0:128] = moved
        d_edge[kp, EDGE_IN : 2 * EDGE_IN, 128:256] = none
        d_edge[kp, 2 * EDGE_IN : 3 * EDGE_IN, 0:128] = none
        d_edge[kp, 2 * EDGE_IN : 3 * EDGE_IN, 128:256] = edge
        d_edge[kp, 3 * EDGE_IN :, :] = jnp.zeros((256 - 3 * EDGE_IN, 256), BF16)
        return carry

    lax.fori_loop(0, across.shape[0], step, 0)


def socs_kernel(weights, wide, above, below, b1, d_main, d_edge, acc, x_win, first):
    rows = wide.shape[0]
    full = jnp.concatenate(
        [
            above[0:STRIP, :].astype(F32)[STRIP - RIM :],
            wide[...],
            below[0:STRIP, :].astype(F32)[0:RIM],
        ],
        axis=0,
    )
    edge_rows = []
    for b in range(NB):
        part = full[:, CB * b : CB * b + 256]
        x_win[b] = part[0:256].astype(BF16)
        edge_rows.append(part[MAIN : MAIN + EDGE_IN])
    edge_rows.append(jnp.zeros((256 - NB * EDGE_IN, 256), F32))
    x_win[NB] = jnp.concatenate(edge_rows, axis=0).astype(BF16)
    acc[...] = jnp.zeros(acc.shape, F32)

    def step(k, carry):
        taps = b1[pl.ds(2 * k, 2)].reshape(2 * CB, 256)
        for j in range(NB + 1):
            part = dot_nt(taps, x_win[j]).astype(BF16)
            first[0, j] = part[0:CB]
            first[1, j] = part[CB:]
        weight = weights[k]
        total = None
        for p in range(2):
            second = dot_nn(first[p, 0:NB].reshape(NB * CB, 256), d_main[2 * k + p])
            total = second * second if total is None else total + second * second
        acc[0:NB] += (weight * total).reshape(NB, CB, 256)
        total = None
        for p in range(2):
            second = dot_nn(first[p, NB], d_edge[2 * k + p])
            total = second * second if total is None else total + second * second
        acc[NB] += weight * total
        return carry

    lax.fori_loop(0, b1.shape[0] // 2, step, 0)


def final_kernel(entries, per, tables, place, acc, g_hi, g_lo, g2_hi, g2_lo, *rest):
    shards = rest[:-6]
    out, cells, slots, placed, flat, blurred = rest[-6:]
    count = len(shards)
    rows, cols = out.shape
    for i, shard in enumerate(shards):
        cells[pl.ds(i * per, per)] = shard[...]
    empty = count * per
    cells[empty] = jnp.zeros(cells.shape[1:], BF16)
    col = place[4]

    for t in range(9):
        for s in range(16):
            slots[t * 17 + s] = empty
        live = tables[t, 2 * entries]
        for n in range(entries):
            cell = tables[t, n]
            owner = cell // per
            behind = jnp.where(owner <= col, col - owner, col - owner + count)
            at = jnp.where(n < live, tables[t, entries + n], 16)
            slots[t * 17 + at] = behind * per + cell - owner * per

    slot_rows, slot_cols = rows // 64, cols // 128
    for i in range(-1, slot_rows + 1):
        for j in range(-1, slot_cols + 1):
            ti = 0 if i < 0 else (2 if i == slot_rows else 1)
            tj = 0 if j < 0 else (2 if j == slot_cols else 1)
            image = slots[(3 * ti + tj) * 17 + (i % slot_rows) * slot_cols + j % slot_cols]
            lanes = slice(128 + 128 * j, 256 + 128 * j)
            if i < 0:
                placed[0:8, lanes] = cells[image, 48:64, :].astype(F32)[8:16]
            elif i == slot_rows:
                placed[8 + rows : 16 + rows, lanes] = cells[image, 0:16, :].astype(F32)[0:8]
            else:
                placed[8 + 64 * i : 72 + 64 * i, lanes] = cells[image].astype(F32)
    placed[16 + rows :, :] = jnp.zeros((placed.shape[0] - 16 - rows, placed.shape[1]), F32)

    at_row = lax.broadcasted_iota(jnp.int32, (CB, 384), 1) - BLUR_HALF
    row_ok = (at_row >= place[0]) & (at_row < place[1])
    at_col = lax.broadcasted_iota(jnp.int32, (CB, 384), 0) - BLUR_HALF
    for b in range(NB):
        edge = acc[NB, :, EDGE_AT[b] : EDGE_AT[b] + EDGE_OUT]
        part = jnp.concatenate(
            [acc[b, :, 0:MAIN], edge, jnp.zeros((CB, 384 - MAIN - EDGE_OUT), F32)], axis=1
        )
        here = at_col + b * CB
        keep = row_ok & (here >= place[2]) & (here < place[3])
        flat[b * CB : (b + 1) * CB, :] = jnp.where(keep, part, 0.0).astype(BF16)
    flat[NB * CB :, :] = jnp.zeros((flat.shape[0] - NB * CB, 384), BF16)

    for j in range(cols // 128):
        image = flat[128 * j : 128 * j + 256, :]
        cell = placed[:, 128 * j : 128 * j + 384].astype(BF16)
        part = dot_nn(g_hi[...], image) + dot_nn(g_lo[...], image)
        part += dot_nt(g2_hi[...], cell) + dot_nt(g2_lo[...], cell)
        high = part.astype(BF16)
        blurred[0, 128 * j : 128 * j + 128, :] = high
        blurred[1, 128 * j : 128 * j + 128, :] = (part - high.astype(F32)).astype(BF16)
    for i in range(rows // 128):
        lanes = slice(128 * i, 128 * i + 256)
        high, low = blurred[0, :, lanes], blurred[1, :, lanes]
        out[128 * i : 128 * i + 128, :] = (
            dot_nt(g_hi[...], high) + dot_nt(g_lo[...], high) + dot_nt(g_hi[...], low)
        )


def shape(dims, dtype):
    return jax.ShapeDtypeStruct(dims, dtype)


def on_device(
    mask_pixels, across_taps, down_taps, kernel_weights, library, cell_ids, cell_slots, cell_count
):
    rows, cols = mask_pixels.shape
    pairs = across_taps.shape[0] * 2
    taps = across_taps.shape[-1]
    entries = cell_ids.shape[-1]
    per = library.shape[0]
    n_row, n_col = lax.axis_size("row"), lax.axis_size("col")
    row, col = lax.axis_index("row"), lax.axis_index("col")
    table = jnp.concatenate([cell_ids.reshape(-1), cell_slots.reshape(-1), cell_count.reshape(-1)])
    table = jnp.pad(table.astype(BF16)[None, :], ((0, 15), (0, 256 - 2 * entries - 1)))

    first, last, pixels = pl.pallas_call(
        prep_kernel,
        out_shape=(
            shape((STRIP + 16, rows), BF16),
            shape((STRIP + 16, rows), BF16),
            shape((rows, cols), F32),
        ),
        in_specs=[VMEM] * 2,
        out_specs=(VMEM,) * 3,
        compiler_params=PARAMS,
        name="prep",
    )(mask_pixels, table)

    up = lambda n: [(i, i + 1) for i in range(n - 1)]
    down = lambda n: [(i + 1, i) for i in range(n - 1)]
    left = lax.ppermute(last, "col", up(n_col))
    right = lax.ppermute(first, "col", down(n_col))

    shards = [library]
    for shift in range(1, n_col):
        shards.append(lax.ppermute(library, "col", [(i, (i + shift) % n_col) for i in range(n_col)]))

    top, bottom, wide = pl.pallas_call(
        mid_kernel,
        out_shape=(
            shape((STRIP + 16, WIDE), BF16),
            shape((STRIP + 16, WIDE), BF16),
            shape((rows, WIDE), F32),
        ),
        in_specs=[VMEM] * 4,
        out_specs=(VMEM,) * 3,
        compiler_params=PARAMS,
        name="mid",
    )(pixels, left, right, table)
    above = lax.ppermute(bottom, "row", up(n_row))
    below = lax.ppermute(top, "row", down(n_row))

    pad_taps = lambda x: jnp.pad(x.reshape(pairs, taps).astype(F32), ((0, 0), (0, 128 - taps)))
    b1, d_main, d_edge, g_hi, g_lo, g2_hi, g2_lo = pl.pallas_call(
        bands_kernel,
        out_shape=(
            shape((pairs, CB, 256), BF16),
            shape((pairs, 256, 256), BF16),
            shape((pairs, 256, 256), BF16),
            shape((128, 256), BF16),
            shape((128, 256), BF16),
            shape((128, 384), BF16),
            shape((128, 384), BF16),
        ),
        in_specs=[VMEM] * 2,
        out_specs=(VMEM,) * 7,
        compiler_params=PARAMS,
        cost_estimate=pl.CostEstimate(flops=2 * 10**9, bytes_accessed=8 * 10**6, transcendentals=0),
        name="bands",
    )(pad_taps(across_taps), pad_taps(down_taps))

    acc = pl.pallas_call(
        socs_kernel,
        out_shape=shape((NB + 1, CB, 256), F32),
        in_specs=[SMEM] + [VMEM] * 6,
        out_specs=VMEM,
        scratch_shapes=[
            pltpu.VMEM((NB + 1, 256, 256), BF16),
            pltpu.VMEM((2, NB + 1, CB, 256), BF16),
        ],
        compiler_params=PARAMS,
        cost_estimate=pl.CostEstimate(flops=5 * 10**9, bytes_accessed=8 * 10**6, transcendentals=0),
        name="socs",
    )(kernel_weights, wide, above, below, b1, d_main, d_edge)

    def three(x):
        line = x[STRIP, 0:384].reshape(3, 128)
        return line

    here = jnp.stack([left[STRIP, 0:128], table[0, 0:128], right[STRIP, 0:128]])
    tables = jnp.concatenate([three(above), here, three(below)]).astype(jnp.int32)
    far = 1 << 20
    place = jnp.stack(
        [
            jnp.where(row == 0, 0, -far),
            jnp.where(row == n_row - 1, rows, far),
            jnp.where(col == 0, 0, -far),
            jnp.where(col == n_col - 1, cols, far),
            col,
        ]
    ).astype(jnp.int32)

    return pl.pallas_call(
        functools.partial(final_kernel, entries, per),
        out_shape=shape((rows, cols), F32),
        in_specs=[SMEM] * 2 + [VMEM] * (5 + len(shards)),
        out_specs=VMEM,
        scratch_shapes=[
            pltpu.VMEM((per * len(shards) + 1, 64, 128), BF16),
            pltpu.SMEM((9 * 17,), jnp.int32),
            pltpu.VMEM((384, cols + 256), F32),
            pltpu.VMEM((cols + 128, 384), BF16),
            pltpu.VMEM((2, cols, 384), BF16),
        ],
        compiler_params=PARAMS,
        name="final",
    )(tables, place, acc, g_hi, g_lo, g2_hi, g2_lo, *shards)


def solution(mesh):
    placed = (
        P(("frames", "row"), "col"),
        P(),
        P(),
        P(),
        P("col", None, None),
        P(("frames", "row"), "col", None),
        P(("frames", "row"), "col", None),
        P(("frames", "row"), "col"),
    )
    return jax.shard_map(
        on_device,
        mesh=mesh,
        in_specs=placed,
        out_specs=P(("frames", "row"), "col"),
        check_vma=False,
    )
```

```python
import functools
import math

import jax
import jax.numpy as jnp
from jax import lax
from jax.experimental import pallas as pl
from jax.experimental.pallas import tpu as pltpu
from jax.sharding import PartitionSpec as P

BLUR_HALF = 8
BLUR_SIGMA = 4.0
HALF = 16
RIM = HALF + BLUR_HALF
STRIP = 32
CB = 176
NB = 3
MAIN = 224
EDGE_IN = 80
EDGE_OUT = 48
EDGE_AT = (0, 48, 128)
WIDE = 640
F32 = jnp.float32
BF16 = jnp.bfloat16
VMEM = pl.BlockSpec(memory_space=pltpu.VMEM)
SMEM = pl.BlockSpec(memory_space=pltpu.SMEM)
HBM = pl.BlockSpec(memory_space=pltpu.HBM)
PARAMS = pltpu.CompilerParams(vmem_limit_bytes=16 * 1024 * 1024)


def dot_nt(a, b):
    return lax.dot_general(a, b, (((1,), (1,)), ((), ())), preferred_element_type=F32)


def dot_nn(a, b):
    return lax.dot_general(a, b, (((1,), (0,)), ((), ())), preferred_element_type=F32)


def prep_kernel(
    mask, ids, slots, count, across, down, first, last, ahead, back, ends, a_ids, a_slots, a_count, tap, sems
):
    rows, cols = mask.shape
    copies = [
        pltpu.make_async_copy(mask.at[:, 0:128], ends.at[0], sems.at[0]),
        pltpu.make_async_copy(mask.at[:, cols - 128 : cols], ends.at[1], sems.at[1]),
        pltpu.make_async_copy(ids, a_ids, sems.at[2]),
        pltpu.make_async_copy(slots, a_slots, sems.at[3]),
        pltpu.make_async_copy(count, a_count, sems.at[4]),
        pltpu.make_async_copy(across, tap.at[0], sems.at[5]),
        pltpu.make_async_copy(down, tap.at[1], sems.at[6]),
    ]
    for copy in copies:
        copy.start()
    for copy in copies[2:5]:
        copy.wait()
    line = lax.broadcasted_iota(jnp.int32, (16, 128), 0)
    lane = lax.broadcasted_iota(jnp.int32, (16, 128), 1)

    def spread(x):
        x = x.astype(F32)
        x = jnp.concatenate([x, jnp.zeros((1, 128 - x.shape[1]), F32)], axis=1)
        return jnp.broadcast_to(x, (16, 128))

    table = jnp.where(line == 1, spread(a_slots[0]), spread(a_count[...]))
    table = jnp.where(line == 0, spread(a_ids[0]), table)
    width = jnp.where(line == 2, 1, ids.shape[2])
    table = jnp.where((lane < width) & (line < 3), table, 0.0).astype(BF16)
    for strip in (first, last):
        strip[STRIP:, 0:128] = table
        strip[STRIP:, 128:] = jnp.zeros((16, rows - 128), BF16)
    copies[0].wait()
    first[0:STRIP, :] = ends[0].astype(F32).T[0:STRIP].astype(BF16)
    copies[1].wait()
    last[0:STRIP, :] = ends[1].astype(F32).T[128 - STRIP :].astype(BF16)
    copies[5].wait()
    copies[6].wait()
    taps = across.shape[2]
    flip = lax.broadcasted_iota(jnp.int32, (128, 128), 0) + lax.broadcasted_iota(jnp.int32, (128, 128), 1)
    flip = jnp.where(flip % 128 == 0, 1.0, 0.0).astype(BF16)
    pad = jnp.zeros((8, 128 - taps), F32)
    more = jnp.zeros((6, taps), F32)
    for k in range(across.shape[0]):
        line = jnp.concatenate([tap[0, k].astype(F32), more], axis=0)
        ahead[k] = jnp.concatenate([line, pad], axis=1)
        line = jnp.concatenate([tap[1, k].astype(F32), more], axis=0)
        back[k] = dot_nn(jnp.concatenate([line, pad], axis=1).astype(BF16), flip)


def mid_kernel(mask, left, right, own, top, bottom, ends, sems):
    rows, cols = mask.shape
    copies = [
        pltpu.make_async_copy(mask.at[0:STRIP], ends.at[0], sems.at[0]),
        pltpu.make_async_copy(mask.at[rows - STRIP : rows], ends.at[1], sems.at[1]),
    ]
    for copy in copies:
        copy.start()
    fill = jnp.zeros((128 - STRIP, 128), F32)

    def turned(strip, at):
        return jnp.concatenate([strip[0:STRIP, at : at + 128].astype(F32), fill], axis=0).T

    tables = jnp.concatenate(
        [left[STRIP:, 0:128], own[STRIP:, 0:128], right[STRIP:, 0:128], jnp.zeros((16, 256), BF16)],
        axis=1,
    )
    for i, out in enumerate((top, bottom)):
        at = 0 if i == 0 else rows - 128
        cut = slice(0, STRIP) if i == 0 else slice(128 - STRIP, 128)
        lhs = turned(left, at)[cut, STRIP - RIM : STRIP]
        rhs = turned(right, at)[cut, 0 : WIDE - RIM - cols]
        copies[i].wait()
        out[0:STRIP, :] = jnp.concatenate([lhs, ends[i].astype(F32), rhs], axis=1).astype(BF16)
        out[STRIP:, :] = tables


def window_kernel(mask, left, right, windows):
    rows, cols = mask.shape
    fill = jnp.zeros((128 - STRIP, rows), F32)
    lhs = jnp.concatenate([left[0:STRIP, :].astype(F32), fill], axis=0).T
    rhs = jnp.concatenate([right[0:STRIP, :].astype(F32), fill], axis=0).T
    full = jnp.concatenate(
        [lhs[:, STRIP - RIM : STRIP], mask[...].astype(F32), rhs[:, 0 : WIDE - RIM - cols]], axis=1
    )
    for b in range(NB):
        windows[b] = full[:, CB * b : CB * b + 256]


def socs_kernel(weights, windows, above, below, ahead, back, acc, x_win, *scratch):
    across = scratch[0:2]
    d_main = scratch[2:4]
    d_edge = scratch[4:6]
    first = scratch[6:8]
    kernels = ahead.shape[0]
    upper_rows = above[0:STRIP, :].astype(F32)[STRIP - RIM :]
    lower_rows = below[0:STRIP, :].astype(F32)[0:RIM]
    edge_rows = []
    for b in range(NB):
        lanes = slice(CB * b, CB * b + 256)
        own = windows[b]
        x_win[b] = jnp.concatenate([upper_rows[:, lanes], own[0 : 256 - RIM]], axis=0).astype(BF16)
        edge_rows += [own[MAIN - RIM :], lower_rows[:, lanes]]
    edge_rows.append(jnp.zeros((256 - NB * EDGE_IN, 256), F32))
    x_win[NB] = jnp.concatenate(edge_rows, axis=0).astype(BF16)
    acc[...] = jnp.zeros(acc.shape, F32)
    for ref in across + d_main + d_edge:
        ref[...] = jnp.zeros(ref.shape, BF16)

    row = lax.broadcasted_iota(jnp.int32, (32, 128), 0)
    lane = lax.broadcasted_iota(jnp.int32, (32, 128), 1)
    low = lane >= row + 96
    narrow = lax.broadcasted_iota(jnp.int32, (EDGE_IN, 128), 1) < EDGE_OUT

    def cycled(x):
        return pltpu.roll(jnp.broadcast_to(x, (128, 128)), 0, 1, stride=1, stride_axis=0)

    def build_across(k, s):
        for p in range(2):
            cyc = cycled(ahead[k, p : p + 1, :])
            head = cyc[0:96].astype(BF16)
            tail = cyc[96:128]
            over = jnp.where(low, 0.0, tail)
            across[s][p, 0:96, 0:128] = head
            across[s][p, 128:CB, 128:256] = head[0 : CB - 128]
            across[s][p, 96:128, 0:128] = jnp.where(low, tail, 0.0).astype(BF16)
            across[s][p, 96:128, 128:256] = over.astype(BF16)

    def build_down(k, s):
        for p in range(2):
            cyc = cycled(back[k, p : p + 1, :])
            head = cyc[0:32]
            over = jnp.where(low, head, 0.0).astype(BF16)
            head = jnp.where(low, 0.0, head)
            same = jnp.concatenate([head, cyc[32:128]], axis=0)
            edge = jnp.where(narrow, same[0:EDGE_IN], 0.0)
            same = same.astype(BF16)
            d_main[s][p, 0:128, 0:128] = same
            d_main[s][p, 128:256, 128:256] = same
            d_main[s][p, 128:160, 0:128] = over
            moved = pltpu.roll(edge, EDGE_AT[1], 1).astype(BF16)
            edge = edge.astype(BF16)
            d_edge[s][p, 0:EDGE_IN, 0:128] = edge
            d_edge[s][p, EDGE_IN : 2 * EDGE_IN, 0:128] = moved
            d_edge[s][p, 2 * EDGE_IN : 3 * EDGE_IN, 128:256] = edge

    def pass_one(s):
        taps = across[s][...].reshape(2 * CB, 256)
        for j in range(NB + 1):
            part = dot_nt(taps, x_win[j]).astype(BF16)
            first[s][0, j] = part[0:CB]
            first[s][1, j] = part[CB:]

    def pass_two(k, s):
        weight = weights[k]
        total = None
        for p in range(2):
            second = dot_nn(first[s][p, 0:NB].reshape(NB * CB, 256), d_main[s][p])
            total = second * second if total is None else total + second * second
        acc[0:NB] += (weight * total).reshape(NB, CB, 256)
        total = None
        for p in range(2):
            second = dot_nn(first[s][p, NB], d_edge[s][p])
            total = second * second if total is None else total + second * second
        acc[NB] += weight * total

    def stage(k, s):
        pass_one(s)
        build_down(k, s)
        build_across(jnp.minimum(k + 1, kernels - 1), 1 - s)
        pass_two(k - 1, 1 - s)

    build_across(0, 0)
    pass_one(0)
    build_down(0, 0)
    build_across(1, 1)

    def step(m, carry):
        stage(2 * m + 1, 1)
        stage(2 * m + 2, 0)
        return carry

    lax.fori_loop(0, kernels // 2 - 1, step, 0)
    stage(kernels - 1, 1)
    pass_two(kernels - 1, 1)


def blur_matrix(shape, axis):
    lag = lax.broadcasted_iota(jnp.int32, shape, axis) - lax.broadcasted_iota(jnp.int32, shape, 1 - axis)
    total = sum(math.exp(-(t * t) / (2 * BLUR_SIGMA**2)) for t in range(-BLUR_HALF, BLUR_HALF + 1))
    off = (lag - BLUR_HALF).astype(F32)
    g = jnp.exp(-off * off / (2.0 * BLUR_SIGMA * BLUR_SIGMA)) * (1.0 / total)
    g = jnp.where((lag >= 0) & (lag <= 2 * BLUR_HALF), g, 0.0)
    high = g.astype(BF16)
    return high, (g - high.astype(F32)).astype(BF16)


def final_kernel(entries, per, n_row, n_col, acc, above, left, own, right, below, *rest):
    shards = rest[:-9]
    out, cells, tab, tables, slots, placed, flat, blurred, sem = rest[-9:]
    count = len(shards)
    rows, cols = out.shape
    row, col = lax.axis_index("row"), lax.axis_index("col")

    for i, strip in enumerate((above, below)):
        tab[:, 768 * i : 768 * i + 384] = strip[STRIP:, 0:384].astype(F32).astype(jnp.int32)[0:8]
    for i, strip in enumerate((left, own, right)):
        tab[:, 384 + 128 * i : 512 + 128 * i] = strip[STRIP:, 0:128].astype(F32).astype(jnp.int32)[0:8]
    fetch = pltpu.make_async_copy(tab, tables, sem)
    fetch.start()
    for i, shard in enumerate(shards):
        cells[pl.ds(i * per, per)] = shard[...]
    empty = count * per
    cells[empty] = jnp.zeros(cells.shape[1:], BF16)

    far = 1 << 20
    at_row = lax.broadcasted_iota(jnp.int32, (CB, 384), 1) - BLUR_HALF
    row_ok = (at_row >= jnp.where(row == 0, 0, -far)) & (at_row < jnp.where(row == n_row - 1, rows, far))
    at_col = lax.broadcasted_iota(jnp.int32, (CB, 384), 0) - BLUR_HALF
    for b in range(NB):
        edge = acc[NB, :, EDGE_AT[b] : EDGE_AT[b] + EDGE_OUT]
        part = jnp.concatenate(
            [acc[b, :, 0:MAIN], edge, jnp.zeros((CB, 384 - MAIN - EDGE_OUT), F32)], axis=1
        )
        here = at_col + b * CB
        keep = row_ok & (here >= jnp.where(col == 0, 0, -far))
        keep = keep & (here < jnp.where(col == n_col - 1, cols, far))
        flat[b * CB : (b + 1) * CB, :] = jnp.where(keep, part, 0.0).astype(BF16)
    flat[NB * CB :, :] = jnp.zeros((flat.shape[0] - NB * CB, 384), BF16)

    fetch.wait()
    for t in range(9):
        for s in range(16):
            slots[t * 17 + s] = empty
        live = tables[2, 128 * t]
        for n in range(entries):
            cell = tables[0, 128 * t + n]
            owner = cell // per
            behind = jnp.where(owner <= col, col - owner, col - owner + count)
            at = jnp.where(n < live, tables[1, 128 * t + n], 16)
            slots[t * 17 + at] = behind * per + cell - owner * per

    slot_rows, slot_cols = rows // 64, cols // 128
    for i in range(-1, slot_rows + 1):
        for j in range(-1, slot_cols + 1):
            ti = 0 if i < 0 else (2 if i == slot_rows else 1)
            tj = 0 if j < 0 else (2 if j == slot_cols else 1)
            image = slots[(3 * ti + tj) * 17 + (i % slot_rows) * slot_cols + j % slot_cols]
            lanes = slice(128 + 128 * j, 256 + 128 * j)
            if i < 0:
                placed[0:8, lanes] = cells[image, 48:64, :].astype(F32)[8:16]
            elif i == slot_rows:
                placed[8 + rows : 16 + rows, lanes] = cells[image, 0:16, :].astype(F32)[0:8]
            else:
                placed[8 + 64 * i : 72 + 64 * i, lanes] = cells[image].astype(F32)
    placed[16 + rows :, :] = jnp.zeros((placed.shape[0] - 16 - rows, placed.shape[1]), F32)

    g_high, g_low = blur_matrix((128, 256), 1)
    g_both = jnp.concatenate([g_high, g_low], axis=0)
    for i in range(rows // 128):
        part = dot_nt(g_both, flat[:, 128 * i : 128 * i + 256])
        cell = dot_nn(g_both, placed[128 * i : 128 * i + 256, :].astype(BF16))
        part = part[0:128] + part[128:]
        cell = cell[0:128] + cell[128:]
        part += cell[:, 128 - BLUR_HALF : 128 - BLUR_HALF + part.shape[1]]
        high = part.astype(BF16)
        blurred[0, 128 * i : 128 * i + 128, :] = high
        blurred[1, 128 * i : 128 * i + 128, :] = (part - high.astype(F32)).astype(BF16)
    g_high, g_low = blur_matrix((256, 128), 0)
    g_both = jnp.concatenate([g_high, g_low], axis=1)
    for j in range(cols // 128):
        lanes = slice(128 * j, 128 * j + 256)
        part = dot_nn(blurred[0, :, lanes], g_both)
        out[:, 128 * j : 128 * j + 128] = (
            part[:, 0:128] + part[:, 128:] + dot_nn(blurred[1, :, lanes], g_high)
        )


def shape(dims, dtype):
    return jax.ShapeDtypeStruct(dims, dtype)


def on_device(
    mask_pixels, across_taps, down_taps, kernel_weights, library, cell_ids, cell_slots, cell_count
):
    rows, cols = mask_pixels.shape
    kernels = across_taps.shape[0]
    entries = cell_ids.shape[-1]
    per = library.shape[0]
    n_row, n_col = lax.axis_size("row"), lax.axis_size("col")

    first, last, ahead, back = pl.pallas_call(
        prep_kernel,
        out_shape=(shape((STRIP + 16, rows), BF16),) * 2 + (shape((kernels, 8, 128), F32),) * 2,
        in_specs=[HBM] * 6,
        out_specs=(VMEM,) * 4,
        scratch_shapes=[
            pltpu.VMEM((2, rows, 128), jnp.int32),
            pltpu.VMEM(cell_ids.shape, jnp.int32),
            pltpu.VMEM(cell_slots.shape, jnp.int32),
            pltpu.VMEM(cell_count.shape, jnp.int32),
            pltpu.VMEM((2,) + across_taps.shape, BF16),
            pltpu.SemaphoreType.DMA((7,)),
        ],
        compiler_params=PARAMS,
        name="prep",
    )(mask_pixels, cell_ids, cell_slots, cell_count, across_taps, down_taps)
    library, first, last = lax.optimization_barrier((library, first, last))

    up = lambda n: [(i, i + 1) for i in range(n - 1)]
    down = lambda n: [(i + 1, i) for i in range(n - 1)]
    left = lax.ppermute(last, "col", up(n_col))
    right = lax.ppermute(first, "col", down(n_col))

    shards = [library]
    for shift in range(1, n_col):
        shards.append(lax.ppermute(library, "col", [(i, (i + shift) % n_col) for i in range(n_col)]))

    top, bottom = pl.pallas_call(
        mid_kernel,
        out_shape=(shape((STRIP + 16, WIDE), BF16),) * 2,
        in_specs=[HBM] + [VMEM] * 3,
        out_specs=(VMEM,) * 2,
        scratch_shapes=[pltpu.VMEM((2, STRIP, cols), jnp.int32), pltpu.SemaphoreType.DMA((2,))],
        compiler_params=PARAMS,
        name="mid",
    )(mask_pixels, left, right, first)
    above = lax.ppermute(bottom, "row", up(n_row))
    below = lax.ppermute(top, "row", down(n_row))

    windows = pl.pallas_call(
        window_kernel,
        out_shape=shape((NB, rows, 256), F32),
        in_specs=[VMEM] * 3,
        out_specs=VMEM,
        compiler_params=PARAMS,
        cost_estimate=pl.CostEstimate(flops=10**6, bytes_accessed=10**6, transcendentals=0),
        name="window",
    )(mask_pixels, left, right)

    acc = pl.pallas_call(
        socs_kernel,
        out_shape=shape((NB + 1, CB, 256), F32),
        in_specs=[SMEM] + [VMEM] * 5,
        out_specs=VMEM,
        scratch_shapes=[pltpu.VMEM((NB + 1, 256, 256), BF16)]
        + [pltpu.VMEM((2, CB, 256), BF16)] * 2
        + [pltpu.VMEM((2, 256, 256), BF16)] * 4
        + [pltpu.VMEM((2, NB + 1, CB, 256), BF16)] * 2,
        compiler_params=PARAMS,
        cost_estimate=pl.CostEstimate(flops=5 * 10**9, bytes_accessed=8 * 10**6, transcendentals=0),
        name="socs",
    )(kernel_weights, windows, above, below, ahead, back)

    return pl.pallas_call(
        functools.partial(final_kernel, entries, per, n_row, n_col),
        out_shape=shape((rows, cols), F32),
        in_specs=[VMEM] * (6 + len(shards)),
        out_specs=VMEM,
        scratch_shapes=[
            pltpu.VMEM((per * len(shards) + 1, 64, 128), BF16),
            pltpu.VMEM((8, 9 * 128), jnp.int32),
            pltpu.SMEM((8, 9 * 128), jnp.int32),
            pltpu.SMEM((9 * 17,), jnp.int32),
            pltpu.VMEM((384, cols + 256), F32),
            pltpu.VMEM((WIDE, 384), BF16),
            pltpu.VMEM((2, rows, WIDE), BF16),
            pltpu.SemaphoreType.DMA,
        ],
        compiler_params=PARAMS,
        name="final",
    )(acc, above, left, first, right, below, *shards)


def solution(mesh):
    placed = (
        P(("frames", "row"), "col"),
        P(),
        P(),
        P(),
        P("col", None, None),
        P(("frames", "row"), "col", None),
        P(("frames", "row"), "col", None),
        P(("frames", "row"), "col"),
    )
    return jax.shard_map(
        on_device,
        mesh=mesh,
        in_specs=placed,
        out_specs=P(("frames", "row"), "col"),
        check_vma=False,
    )
```

```python
import functools
import math

import jax
import jax.numpy as jnp
from jax import lax
from jax.experimental import pallas as pl
from jax.experimental.pallas import tpu as pltpu
from jax.sharding import PartitionSpec as P

BLUR_HALF = 8
BLUR_SIGMA = 4.0
HALF = 16
RIM = HALF + BLUR_HALF
STRIP = 32
CB = 176
NB = 3
MAIN = 224
EDGE_IN = 80
EDGE_OUT = 48
EDGE_AT = (0, 48, 128)
WIDE = 640
SLOTS = 16
F32 = jnp.float32
BF16 = jnp.bfloat16
VMEM = pl.BlockSpec(memory_space=pltpu.VMEM)
SMEM = pl.BlockSpec(memory_space=pltpu.SMEM)
HBM = pl.BlockSpec(memory_space=pltpu.HBM)
PARAMS = pltpu.CompilerParams(vmem_limit_bytes=16 * 1024 * 1024)


def dot_nt(a, b):
    return lax.dot_general(a, b, (((1,), (1,)), ((), ())), preferred_element_type=F32)


def dot_nn(a, b):
    return lax.dot_general(a, b, (((1,), (0,)), ((), ())), preferred_element_type=F32)


def prep_kernel(
    mask, ids, slots, count, first, last, ends, a_ids, a_slots, sems
):
    rows, cols = mask.shape
    copies = [
        pltpu.make_async_copy(mask.at[:, 0:128], ends.at[0], sems.at[0]),
        pltpu.make_async_copy(mask.at[:, cols - 128 : cols], ends.at[1], sems.at[1]),
        pltpu.make_async_copy(ids, a_ids, sems.at[2]),
        pltpu.make_async_copy(slots, a_slots, sems.at[3]),
    ]
    for copy in copies:
        copy.start()
    for copy in copies[2:4]:
        copy.wait()
    line = lax.broadcasted_iota(jnp.int32, (16, 128), 0)
    lane = lax.broadcasted_iota(jnp.int32, (16, 128), 1)

    def spread(x):
        x = x.astype(F32)
        x = jnp.concatenate([x, jnp.zeros((1, 128 - x.shape[1]), F32)], axis=1)
        return jnp.broadcast_to(x, (16, 128))

    table = jnp.where(line == 1, spread(a_slots[0]), count[0, 0].astype(F32))
    table = jnp.where(line == 0, spread(a_ids[0]), table)
    width = jnp.where(line == 2, 1, ids.shape[2])
    table = jnp.where((lane < width) & (line < 3), table, 0.0).astype(BF16)
    for strip in (first, last):
        strip[STRIP:, 0:128] = table
        strip[STRIP:, 128:] = jnp.zeros((16, rows - 128), BF16)
    copies[0].wait()
    first[0:STRIP, :] = ends[0].astype(F32).T[0:STRIP].astype(BF16)
    copies[1].wait()
    last[0:STRIP, :] = ends[1].astype(F32).T[128 - STRIP :].astype(BF16)


def mid_kernel(mask, left, right, own, top, bottom, ends, sems):
    rows, cols = mask.shape
    copies = [
        pltpu.make_async_copy(mask.at[0:STRIP], ends.at[0], sems.at[0]),
        pltpu.make_async_copy(mask.at[rows - STRIP : rows], ends.at[1], sems.at[1]),
    ]
    for copy in copies:
        copy.start()
    fill = jnp.zeros((128 - STRIP, 128), F32)

    def turned(strip, at):
        return jnp.concatenate([strip[0:STRIP, at : at + 128].astype(F32), fill], axis=0).T

    tables = jnp.concatenate(
        [left[STRIP:, 0:128], own[STRIP:, 0:128], right[STRIP:, 0:128], jnp.zeros((16, 256), BF16)],
        axis=1,
    )
    for i, out in enumerate((top, bottom)):
        at = 0 if i == 0 else rows - 128
        cut = slice(0, STRIP) if i == 0 else slice(128 - STRIP, 128)
        lhs = turned(left, at)[cut, STRIP - RIM : STRIP]
        rhs = turned(right, at)[cut, 0 : WIDE - RIM - cols]
        copies[i].wait()
        out[0:STRIP, :] = jnp.concatenate([lhs, ends[i].astype(F32), rhs], axis=1).astype(BF16)
        out[STRIP:, :] = tables


def window_kernel(
    mask, left, right, across, down, weights, windows, ahead, back, scale, own, tap, line, sems
):
    rows, cols = mask.shape
    copies = [
        pltpu.make_async_copy(mask, own, sems.at[0]),
        pltpu.make_async_copy(across, tap.at[0], sems.at[1]),
        pltpu.make_async_copy(down, tap.at[1], sems.at[2]),
        pltpu.make_async_copy(weights, line, sems.at[3]),
    ]
    for copy in copies:
        copy.start()
    fill = jnp.zeros((128 - STRIP, rows), F32)
    copies[0].wait()
    lhs = jnp.concatenate([left[0:STRIP, :].astype(F32), fill], axis=0).T
    rhs = jnp.concatenate([right[0:STRIP, :].astype(F32), fill], axis=0).T
    full = jnp.concatenate(
        [lhs[:, STRIP - RIM : STRIP], own[...].astype(F32), rhs[:, 0 : WIDE - RIM - cols]], axis=1
    )
    for b in range(NB):
        windows[b] = full[:, CB * b : CB * b + 256]
    for copy in copies[1:]:
        copy.wait()
    taps = across.shape[2]
    flip = lax.broadcasted_iota(jnp.int32, (128, 128), 0) + lax.broadcasted_iota(jnp.int32, (128, 128), 1)
    flip = jnp.where(flip % 128 == 0, 1.0, 0.0).astype(BF16)
    pad = jnp.zeros((8, 128 - taps), F32)
    more = jnp.zeros((6, taps), F32)
    at = lax.broadcasted_iota(jnp.int32, (8, 128), 1)
    every = jnp.broadcast_to(line[...].reshape(1, -1), (8, line.shape[0]))
    every = jnp.concatenate([every, jnp.zeros((8, 128 - line.shape[0]), F32)], axis=1)
    for k in range(across.shape[0]):
        part = jnp.concatenate([tap[0, k].astype(F32), more], axis=0)
        ahead[k] = jnp.concatenate([part, pad], axis=1)
        part = jnp.concatenate([tap[1, k].astype(F32), more], axis=0)
        back[k] = dot_nn(jnp.concatenate([part, pad], axis=1).astype(BF16), flip)
        weight = jnp.sum(jnp.where(at == k, every, 0.0), axis=1, keepdims=True)
        scale[k] = jnp.broadcast_to(weight, (8, 256))


def socs_kernel(
    entries, windows, above, left, own, right, below, ahead, back, scale, acc, images, x_win, *scratch
):
    across = scratch[0:2]
    d_main = scratch[2:4]
    d_edge = scratch[4:6]
    first = scratch[6:8]
    kernels = ahead.shape[0]
    upper_rows = above[0:STRIP, :].astype(F32)[STRIP - RIM :]
    lower_rows = below[0:STRIP, :].astype(F32)[0:RIM]
    edge_rows = []
    for b in range(NB):
        lanes = slice(CB * b, CB * b + 256)
        part = windows[b]
        x_win[b] = jnp.concatenate([upper_rows[:, lanes], part[0 : 256 - RIM]], axis=0).astype(BF16)
        edge_rows += [part[MAIN - RIM :], lower_rows[:, lanes]]
    edge_rows.append(jnp.zeros((256 - NB * EDGE_IN, 256), F32))
    x_win[NB] = jnp.concatenate(edge_rows, axis=0).astype(BF16)
    acc[...] = jnp.zeros(acc.shape, F32)
    for ref in across + d_main + d_edge:
        ref[...] = jnp.zeros(ref.shape, BF16)

    slot = lax.broadcasted_iota(jnp.int32, (SLOTS, 128), 0).astype(F32)
    lane = lax.broadcasted_iota(jnp.int32, (SLOTS, 128), 1)
    found = jnp.zeros((SLOTS, 128), F32)
    strips = [above] * 3 + [left, own, right] + [below] * 3
    for t, strip in enumerate(strips):
        at = 0 if t in (3, 4, 5) else 128 * (t % 3)
        table = strip[STRIP:, at : at + 128].astype(F32)
        live = lane.astype(F32) < table[2:3, 0:1]
        hit = live & (table[1:2] == slot) & (lane < entries)
        image = jnp.sum(jnp.where(hit, table[0:1] + 1.0, 0.0), axis=1, keepdims=True)
        found = jnp.where(lane == t, image, found)
    images[...] = found.astype(jnp.int32)

    row = lax.broadcasted_iota(jnp.int32, (32, 128), 0)
    lane = lax.broadcasted_iota(jnp.int32, (32, 128), 1)
    low = lane >= row + 96
    narrow = lax.broadcasted_iota(jnp.int32, (EDGE_IN, 128), 1) < EDGE_OUT

    def cycled(x):
        return pltpu.roll(jnp.broadcast_to(x, (128, 128)), 0, 1, stride=1, stride_axis=0)

    def build_across(k, s):
        for p in range(2):
            cyc = cycled(ahead[k, p : p + 1, :])
            head = cyc[0:96].astype(BF16)
            tail = cyc[96:128]
            over = jnp.where(low, 0.0, tail)
            across[s][p, 0:96, 0:128] = head
            across[s][p, 128:CB, 128:256] = head[0 : CB - 128]
            across[s][p, 96:128, 0:128] = jnp.where(low, tail, 0.0).astype(BF16)
            across[s][p, 96:128, 128:256] = over.astype(BF16)

    def build_down(k, s):
        for p in range(2):
            cyc = cycled(back[k, p : p + 1, :])
            head = cyc[0:32]
            over = jnp.where(low, head, 0.0).astype(BF16)
            head = jnp.where(low, 0.0, head)
            same = jnp.concatenate([head, cyc[32:128]], axis=0)
            edge = jnp.where(narrow, same[0:EDGE_IN], 0.0)
            same = same.astype(BF16)
            d_main[s][p, 0:128, 0:128] = same
            d_main[s][p, 128:256, 128:256] = same
            d_main[s][p, 128:160, 0:128] = over
            moved = pltpu.roll(edge, EDGE_AT[1], 1).astype(BF16)
            edge = edge.astype(BF16)
            d_edge[s][p, 0:EDGE_IN, 0:128] = edge
            d_edge[s][p, EDGE_IN : 2 * EDGE_IN, 0:128] = moved
            d_edge[s][p, 2 * EDGE_IN : 3 * EDGE_IN, 128:256] = edge

    def pass_one(s):
        taps = across[s][...].reshape(2 * CB, 256)
        for j in range(NB + 1):
            part = dot_nt(taps, x_win[j]).astype(BF16)
            first[s][0, j] = part[0:CB]
            first[s][1, j] = part[CB:]

    def pass_two(k, s):
        weight = scale[k, 0:1, :]
        total = None
        for p in range(2):
            second = dot_nn(first[s][p, 0:NB].reshape(NB * CB, 256), d_main[s][p])
            total = second * second if total is None else total + second * second
        acc[0:NB] += (weight * total).reshape(NB, CB, 256)
        total = None
        for p in range(2):
            second = dot_nn(first[s][p, NB], d_edge[s][p])
            total = second * second if total is None else total + second * second
        acc[NB] += weight * total

    def stage(k, s):
        pass_one(s)
        build_down(k, s)
        build_across(jnp.minimum(k + 1, kernels - 1), 1 - s)
        pass_two(k - 1, 1 - s)

    build_across(0, 0)
    pass_one(0)
    build_down(0, 0)
    build_across(1, 1)

    def step(m, carry):
        stage(2 * m + 1, 1)
        stage(2 * m + 2, 0)
        return carry

    lax.fori_loop(0, kernels // 2 - 1, step, 0)
    stage(kernels - 1, 1)
    pass_two(kernels - 1, 1)


def blur_matrix(shape, axis):
    lag = lax.broadcasted_iota(jnp.int32, shape, axis) - lax.broadcasted_iota(jnp.int32, shape, 1 - axis)
    total = sum(math.exp(-(t * t) / (2 * BLUR_SIGMA**2)) for t in range(-BLUR_HALF, BLUR_HALF + 1))
    off = (lag - BLUR_HALF).astype(F32)
    g = jnp.exp(-off * off / (2.0 * BLUR_SIGMA * BLUR_SIGMA)) * (1.0 / total)
    g = jnp.where((lag >= 0) & (lag <= 2 * BLUR_HALF), g, 0.0)
    high = g.astype(BF16)
    return high, (g - high.astype(F32)).astype(BF16)


def final_kernel(n_row, n_col, acc, images, cells, out, table, placed, flat, blurred, sem):
    rows, cols = out.shape
    row, col = lax.axis_index("row"), lax.axis_index("col")
    fetch = pltpu.make_async_copy(images, table, sem)
    fetch.start()

    at_row = lax.broadcasted_iota(jnp.int32, (8, 384), 1) - BLUR_HALF
    row_ok = ((row > 0) | (at_row >= 0)) & ((row < n_row - 1) | (at_row < rows))
    row_ok = jnp.where(row_ok, 1.0, 0.0)
    for b in range(NB):
        edge = acc[NB, :, EDGE_AT[b] : EDGE_AT[b] + EDGE_OUT]
        part = jnp.concatenate(
            [acc[b, :, 0:MAIN], edge, jnp.zeros((CB, 384 - MAIN - EDGE_OUT), F32)], axis=1
        )
        part = part * row_ok[0:1]
        if b == 0:
            part = jnp.concatenate([jnp.where(col > 0, part[0:8], 0.0), part[8:]], axis=0)
        if b == NB - 1:
            part = jnp.concatenate([part[0 : CB - 8], jnp.where(col < n_col - 1, part[CB - 8 :], 0.0)], axis=0)
        flat[b * CB : (b + 1) * CB, :] = part.astype(BF16)
    flat[NB * CB :, :] = jnp.zeros((flat.shape[0] - NB * CB, 384), BF16)

    fetch.wait()
    slot_rows, slot_cols = rows // 64, cols // 128
    for i in range(-1, slot_rows + 1):
        for j in range(-1, slot_cols + 1):
            ti = 0 if i < 0 else (2 if i == slot_rows else 1)
            tj = 0 if j < 0 else (2 if j == slot_cols else 1)
            found = table[(i % slot_rows) * slot_cols + j % slot_cols, 3 * ti + tj]
            image = jnp.maximum(found - 1, 0)
            lanes = slice(128 + 128 * j, 256 + 128 * j)
            show = lambda x: jnp.where(found > 0, x.astype(F32), 0.0)
            if i < 0:
                placed[0:8, lanes] = show(cells[image, 48:64, :])[8:16]
            elif i == slot_rows:
                placed[8 + rows : 16 + rows, lanes] = show(cells[image, 0:16, :])[0:8]
            else:
                placed[8 + 64 * i : 72 + 64 * i, lanes] = show(cells[image])
    placed[16 + rows :, :] = jnp.zeros((placed.shape[0] - 16 - rows, placed.shape[1]), F32)

    g_high, g_low = blur_matrix((128, 256), 1)
    g_both = jnp.concatenate([g_high, g_low], axis=0)
    for i in range(rows // 128):
        part = dot_nt(g_both, flat[:, 128 * i : 128 * i + 256])
        cell = dot_nn(g_both, placed[128 * i : 128 * i + 256, :].astype(BF16))
        part = part[0:128] + part[128:]
        cell = cell[0:128] + cell[128:]
        part += cell[:, 128 - BLUR_HALF : 128 - BLUR_HALF + part.shape[1]]
        high = part.astype(BF16)
        blurred[0, 128 * i : 128 * i + 128, :] = high
        blurred[1, 128 * i : 128 * i + 128, :] = (part - high.astype(F32)).astype(BF16)
    g_high, g_low = blur_matrix((256, 128), 0)
    g_both = jnp.concatenate([g_high, g_low], axis=1)
    for j in range(cols // 128):
        lanes = slice(128 * j, 128 * j + 256)
        part = dot_nn(blurred[0, :, lanes], g_both)
        out[:, 128 * j : 128 * j + 128] = (
            part[:, 0:128] + part[:, 128:] + dot_nn(blurred[1, :, lanes], g_high)
        )


def shape(dims, dtype):
    return jax.ShapeDtypeStruct(dims, dtype)


def on_device(
    mask_pixels, across_taps, down_taps, kernel_weights, library, cell_ids, cell_slots, cell_count
):
    rows, cols = mask_pixels.shape
    kernels = across_taps.shape[0]
    entries = cell_ids.shape[-1]
    per = library.shape[0]
    n_row, n_col = lax.axis_size("row"), lax.axis_size("col")
    in_hbm = lambda x: pltpu.with_memory_space_constraint(x, pltpu.HBM)
    mask_hbm = in_hbm(mask_pixels)

    first, last = pl.pallas_call(
        prep_kernel,
        out_shape=(shape((STRIP + 16, rows), BF16),) * 2,
        in_specs=[HBM] * 3 + [SMEM],
        out_specs=(VMEM,) * 2,
        scratch_shapes=[
            pltpu.VMEM((2, rows, 128), jnp.int32),
            pltpu.VMEM(cell_ids.shape, jnp.int32),
            pltpu.VMEM(cell_slots.shape, jnp.int32),
            pltpu.SemaphoreType.DMA((4,)),
        ],
        compiler_params=PARAMS,
        name="prep",
    )(mask_hbm, in_hbm(cell_ids), in_hbm(cell_slots), cell_count)
    library, first, last = lax.optimization_barrier((library, first, last))

    up = lambda n: [(i, i + 1) for i in range(n - 1)]
    down = lambda n: [(i + 1, i) for i in range(n - 1)]
    left = lax.ppermute(last, "col", up(n_col))
    right = lax.ppermute(first, "col", down(n_col))

    cells = lax.all_to_all(jnp.broadcast_to(library[None], (n_col,) + library.shape), "col", 0, 0)
    cells = cells.reshape((n_col * per,) + library.shape[1:])

    top, bottom = pl.pallas_call(
        mid_kernel,
        out_shape=(shape((STRIP + 16, WIDE), BF16),) * 2,
        in_specs=[HBM] + [VMEM] * 3,
        out_specs=(VMEM,) * 2,
        scratch_shapes=[pltpu.VMEM((2, STRIP, cols), jnp.int32), pltpu.SemaphoreType.DMA((2,))],
        compiler_params=PARAMS,
        name="mid",
    )(mask_hbm, left, right, first)
    above = lax.ppermute(bottom, "row", up(n_row))
    below = lax.ppermute(top, "row", down(n_row))

    windows, ahead, back, scale = pl.pallas_call(
        window_kernel,
        out_shape=(
            shape((NB, rows, 256), F32),
            shape((kernels, 8, 128), F32),
            shape((kernels, 8, 128), F32),
            shape((kernels, 8, 256), F32),
        ),
        in_specs=[HBM] + [VMEM] * 2 + [HBM] * 3,
        out_specs=(VMEM,) * 4,
        scratch_shapes=[
            pltpu.VMEM(mask_pixels.shape, jnp.int32),
            pltpu.VMEM((2,) + across_taps.shape, BF16),
            pltpu.VMEM(kernel_weights.shape, F32),
            pltpu.SemaphoreType.DMA((4,)),
        ],
        compiler_params=PARAMS,
        cost_estimate=pl.CostEstimate(flops=10**6, bytes_accessed=10**6, transcendentals=0),
        name="window",
    )(mask_hbm, left, right, in_hbm(across_taps), in_hbm(down_taps), in_hbm(kernel_weights))

    acc, images = pl.pallas_call(
        functools.partial(socs_kernel, entries),
        out_shape=(shape((NB + 1, CB, 256), F32), shape((SLOTS, 128), jnp.int32)),
        in_specs=[VMEM] * 9,
        out_specs=(VMEM,) * 2,
        scratch_shapes=[pltpu.VMEM((NB + 1, 256, 256), BF16)]
        + [pltpu.VMEM((2, CB, 256), BF16)] * 2
        + [pltpu.VMEM((2, 256, 256), BF16)] * 4
        + [pltpu.VMEM((2, NB + 1, CB, 256), BF16)] * 2,
        compiler_params=PARAMS,
        cost_estimate=pl.CostEstimate(flops=5 * 10**9, bytes_accessed=8 * 10**6, transcendentals=0),
        name="socs",
    )(windows, above, left, first, right, below, ahead, back, scale)

    return pl.pallas_call(
        functools.partial(final_kernel, n_row, n_col),
        out_shape=shape((rows, cols), F32),
        in_specs=[VMEM] * 3,
        out_specs=VMEM,
        scratch_shapes=[
            pltpu.SMEM((SLOTS, 128), jnp.int32),
            pltpu.VMEM((384, cols + 256), F32),
            pltpu.VMEM((WIDE, 384), BF16),
            pltpu.VMEM((2, rows, WIDE), BF16),
            pltpu.SemaphoreType.DMA,
        ],
        compiler_params=PARAMS,
        name="final",
    )(acc, images, cells)


def solution(mesh):
    placed = (
        P(("frames", "row"), "col"),
        P(),
        P(),
        P(),
        P("col", None, None),
        P(("frames", "row"), "col", None),
        P(("frames", "row"), "col", None),
        P(("frames", "row"), "col"),
    )
    return jax.shard_map(
        on_device,
        mesh=mesh,
        in_specs=placed,
        out_specs=P(("frames", "row"), "col"),
        check_vma=False,
    )
```

```python
import functools
import math

import jax
import jax.numpy as jnp
from jax import lax
from jax.experimental import pallas as pl
from jax.experimental.pallas import tpu as pltpu
from jax.sharding import PartitionSpec as P

BLUR_HALF = 8
BLUR_SIGMA = 4.0
HALF = 16
RIM = HALF + BLUR_HALF
STRIP = 32
CB = 176
NB = 3
MAIN = 224
EDGE_IN = 80
EDGE_OUT = 48
GROUP = 2
WIDE = 640
SLOTS = 16
F32 = jnp.float32
BF16 = jnp.bfloat16
VMEM = pl.BlockSpec(memory_space=pltpu.VMEM)
SMEM = pl.BlockSpec(memory_space=pltpu.SMEM)
HBM = pl.BlockSpec(memory_space=pltpu.HBM)
PARAMS = pltpu.CompilerParams(vmem_limit_bytes=16 * 1024 * 1024)


def dot_nt(a, b):
    return lax.dot_general(a, b, (((1,), (1,)), ((), ())), preferred_element_type=F32)


def dot_nn(a, b):
    return lax.dot_general(a, b, (((1,), (0,)), ((), ())), preferred_element_type=F32)


def eye(rows, cols, shift):
    at = lax.broadcasted_iota(jnp.int32, (rows, cols), 1) - lax.broadcasted_iota(jnp.int32, (rows, cols), 0)
    return jnp.where(at == shift, 1.0, 0.0).astype(BF16)


def sides(axis, first_swap, second_swap):
    even = lax.rem(lax.axis_index(axis), 2) == 0
    return jnp.where(even, second_swap, first_swap), jnp.where(even, first_swap, second_swap)


def prep_kernel(
    mask, ids, slots, count, across, down, to_first, to_second, edges, taps, ends, a_ids, a_slots, sems
):
    rows, cols = mask.shape
    copies = [
        pltpu.make_async_copy(mask.at[:, 0:128], ends.at[0], sems.at[0]),
        pltpu.make_async_copy(mask.at[:, cols - 128 : cols], ends.at[1], sems.at[1]),
        pltpu.make_async_copy(ids, a_ids, sems.at[2]),
        pltpu.make_async_copy(slots, a_slots, sems.at[3]),
        pltpu.make_async_copy(mask.at[0:STRIP], edges.at[0], sems.at[4]),
        pltpu.make_async_copy(mask.at[rows - STRIP : rows], edges.at[1], sems.at[5]),
        pltpu.make_async_copy(across, taps.at[0], sems.at[6]),
        pltpu.make_async_copy(down, taps.at[1], sems.at[7]),
    ]
    for copy in copies:
        copy.start()
    for copy in copies[2:4]:
        copy.wait()
    line = lax.broadcasted_iota(jnp.int32, (16, 128), 0)
    lane = lax.broadcasted_iota(jnp.int32, (16, 128), 1)

    def spread(x):
        x = x.astype(F32)
        x = jnp.concatenate([x, jnp.zeros((1, 128 - x.shape[1]), F32)], axis=1)
        return jnp.broadcast_to(x, (16, 128))

    table = jnp.where(line == 1, spread(a_slots[0]), count[0, 0].astype(F32))
    table = jnp.where(line == 0, spread(a_ids[0]), table)
    width = jnp.where(line == 2, 1, ids.shape[2])
    table = jnp.where((lane < width) & (line < 3), table, 0.0).astype(BF16)
    for strip in (to_first, to_second):
        strip[STRIP:, 0:128] = table
        strip[STRIP:, 128:] = jnp.zeros((16, rows - 128), BF16)
    even = lax.rem(lax.axis_index("col"), 2) == 0
    copies[0].wait()
    first = dot_nt(eye(STRIP, 128, 0), ends[0].astype(F32).astype(BF16))
    copies[1].wait()
    last = dot_nt(eye(STRIP, 128, 128 - STRIP), ends[1].astype(F32).astype(BF16))
    to_first[0:STRIP, :] = jnp.where(even, last, first).astype(BF16)
    to_second[0:STRIP, :] = jnp.where(even, first, last).astype(BF16)
    for copy in copies[4:]:
        copy.wait()


def mid_kernel(edges, from_first, from_second, own, to_first, to_second):
    cols = edges.shape[2]
    rows = from_first.shape[1]
    left, right = sides("col", from_first[...].astype(F32), from_second[...].astype(F32))
    tables = jnp.concatenate(
        [left[STRIP:, 0:128], own[STRIP:, 0:128].astype(F32), right[STRIP:, 0:128], jnp.zeros((16, 256), F32)],
        axis=1,
    ).astype(BF16)
    fill = jnp.zeros((128 - STRIP, 128), F32)
    strips = []
    for i in range(2):
        at = 0 if i == 0 else rows - 128
        pick = eye(STRIP, 128, 0 if i == 0 else 128 - STRIP)

        def turned(strip):
            return dot_nt(pick, jnp.concatenate([strip[0:STRIP, at : at + 128], fill], axis=0).astype(BF16))

        parts = [turned(left)[:, STRIP - RIM : STRIP], edges[i].astype(F32), turned(right)[:, 0 : WIDE - RIM - cols]]
        strips.append(jnp.concatenate(parts, axis=1))
    even = lax.rem(lax.axis_index("row"), 2) == 0
    to_first[0:STRIP, :] = jnp.where(even, strips[1], strips[0]).astype(BF16)
    to_second[0:STRIP, :] = jnp.where(even, strips[0], strips[1]).astype(BF16)
    to_first[STRIP:, :] = tables
    to_second[STRIP:, :] = tables


def window_kernel(mask, from_first, from_second, taps, windows, ahead, back):
    rows, cols = mask.shape
    fill = jnp.zeros((128 - STRIP, rows), F32)
    left, right = sides("col", from_first[0:STRIP, :].astype(F32), from_second[0:STRIP, :].astype(F32))
    lhs = jnp.concatenate([left, fill], axis=0).T
    rhs = jnp.concatenate([right, fill], axis=0).T
    full = jnp.concatenate(
        [lhs[:, STRIP - RIM : STRIP], mask[...].astype(F32), rhs[:, 0 : WIDE - RIM - cols]], axis=1
    )
    for b in range(NB):
        windows[b] = full[:, CB * b : CB * b + 256]
    kernels, _, count = taps.shape[1:]
    flip = lax.broadcasted_iota(jnp.int32, (128, 128), 0) + lax.broadcasted_iota(jnp.int32, (128, 128), 1)
    flip = jnp.where(flip % 128 == 0, 1.0, 0.0).astype(BF16)
    ahead[...] = jnp.zeros(ahead.shape, F32)
    back[...] = jnp.zeros(back.shape, F32)
    for k in range(kernels):
        ahead[k, 0:2, 0:count] = taps[0, k].astype(F32)
        back[k, 0:2, 0:count] = taps[1, k].astype(F32)
    back[...] = dot_nn(back[...].reshape(kernels * 8, 128).astype(BF16), flip).reshape(kernels, 8, 128)


def socs_kernel(
    entries,
    per,
    weights,
    windows,
    row_first,
    row_second,
    col_first,
    col_second,
    own,
    ahead,
    back,
    acc,
    images,
    x_win,
    scale,
    sem,
    *scratch,
):
    across = scratch[0:2]
    down = scratch[2:4]
    first = scratch[4:6]
    groups = ahead.shape[0] // GROUP
    fetch = pltpu.make_async_copy(weights, scale, sem)
    fetch.start()
    above, below = sides("row", row_first[...].astype(F32), row_second[...].astype(F32))
    left, right = sides("col", col_first[STRIP:, 0:128].astype(F32), col_second[STRIP:, 0:128].astype(F32))
    upper_rows = above[STRIP - RIM : STRIP]
    lower_rows = below[0:RIM]
    edge_rows = []
    for b in range(NB):
        lanes = slice(CB * b, CB * b + 256)
        part = windows[b]
        x_win[b] = jnp.concatenate([upper_rows[:, lanes], part[0 : 256 - RIM]], axis=0).astype(BF16)
        edge_rows += [part[MAIN - RIM :], lower_rows[:, lanes]]
    edge_rows.append(jnp.zeros((256 - NB * EDGE_IN, 256), F32))
    x_win[NB] = jnp.concatenate(edge_rows, axis=0).astype(BF16)
    acc[...] = jnp.zeros(acc.shape, F32)
    for ref in across + down:
        ref[...] = jnp.zeros(ref.shape, BF16)

    slot = lax.broadcasted_iota(jnp.int32, (SLOTS, 128), 0).astype(F32)
    lane = lax.broadcasted_iota(jnp.int32, (SLOTS, 128), 1)
    found = jnp.zeros((SLOTS, 128), F32)
    col = lax.axis_index("col")
    tables = [above[STRIP:, 128 * t : 128 * t + 128] for t in range(3)]
    tables += [left, own[STRIP:, 0:128].astype(F32), right]
    tables += [below[STRIP:, 128 * t : 128 * t + 128] for t in range(3)]
    for t, table in enumerate(tables):
        live = lane.astype(F32) < table[2:3, 0:1]
        hit = live & (table[1:2] == slot) & (lane < entries)
        image = jnp.sum(jnp.where(hit, table[0:1] + 1.0, 0.0), axis=1, keepdims=True)
        found = jnp.where(lane == t, image, found)
    cell = found.astype(jnp.int32) - 1
    images[...] = jnp.where(cell >= 0, ((cell // per) ^ col) * per + cell % per + 1, 0)

    row = lax.broadcasted_iota(jnp.int32, (32, 128), 0)
    lane = lax.broadcasted_iota(jnp.int32, (32, 128), 1)
    low = lane >= row + 96

    def cycled(x):
        return pltpu.roll(jnp.broadcast_to(x, (128, 128)), 0, 1, stride=1, stride_axis=0)

    def build_across(m, s):
        for q in range(2 * GROUP):
            cyc = cycled(ahead[GROUP * m + q // 2, q % 2 : q % 2 + 1, :])
            head = cyc[0:96].astype(BF16)
            tail = cyc[96:128]
            over = jnp.where(low, 0.0, tail)
            across[s][q, 0:96, 0:128] = head
            across[s][q, 128:CB, 128:256] = head[0 : CB - 128]
            across[s][q, 96:128, 0:128] = jnp.where(low, tail, 0.0).astype(BF16)
            across[s][q, 96:128, 128:256] = over.astype(BF16)

    def build_down(m, s):
        for q in range(2 * GROUP):
            cyc = cycled(back[GROUP * m + q // 2, q % 2 : q % 2 + 1, :])
            head = cyc[0:32]
            over = jnp.where(low, head, 0.0).astype(BF16)
            head = jnp.where(low, 0.0, head)
            same = jnp.concatenate([head, cyc[32:128]], axis=0).astype(BF16)
            down[s][q, 0:128, 0:128] = same
            down[s][q, 128:256, 128:256] = same
            down[s][q, 128:160, 0:128] = over

    def pass_one(s):
        taps = across[s][...].reshape(2 * GROUP * CB, 256)
        for j in range(NB + 1):
            part = dot_nt(taps, x_win[j]).astype(BF16)
            for q in range(2 * GROUP):
                first[s][q, j] = part[q * CB : (q + 1) * CB]

    def pass_two(m, s):
        for g in range(GROUP):
            total = None
            for q in (2 * g, 2 * g + 1):
                second = dot_nn(first[s][q].reshape((NB + 1) * CB, 256), down[s][q])
                total = second * second if total is None else total + second * second
            acc[...] += (scale[GROUP * m + g] * total).reshape(acc.shape)

    def stage(m, s):
        pass_one(s)
        build_down(m, s)
        build_across(jnp.minimum(m + 1, groups - 1), 1 - s)
        pass_two(m - 1, 1 - s)

    build_across(0, 0)
    pass_one(0)
    build_down(0, 0)
    build_across(1, 1)
    fetch.wait()

    def step(i, carry):
        stage(2 * i + 1, 1)
        stage(2 * i + 2, 0)
        return carry

    lax.fori_loop(0, groups // 2 - 1, step, 0)
    stage(groups - 1, 1)
    pass_two(groups - 1, 1)


def blur_matrix(shape, axis):
    lag = lax.broadcasted_iota(jnp.int32, shape, axis) - lax.broadcasted_iota(jnp.int32, shape, 1 - axis)
    total = sum(math.exp(-(t * t) / (2 * BLUR_SIGMA**2)) for t in range(-BLUR_HALF, BLUR_HALF + 1))
    off = (lag - BLUR_HALF).astype(F32)
    g = jnp.exp(-off * off / (2.0 * BLUR_SIGMA * BLUR_SIGMA)) * (1.0 / total)
    g = jnp.where((lag >= 0) & (lag <= 2 * BLUR_HALF), g, 0.0)
    high = g.astype(BF16)
    return high, (g - high.astype(F32)).astype(BF16)


def final_kernel(n_row, n_col, acc, images, *rest):
    shards = rest[:-7]
    out, cells, table, placed, flat, blurred, sem = rest[-7:]
    per = shards[0].shape[0]
    rows, cols = out.shape
    row, col = lax.axis_index("row"), lax.axis_index("col")
    fetch = pltpu.make_async_copy(images, table, sem)
    fetch.start()
    for i, shard in enumerate(shards):
        cells[pl.ds(i * per, per)] = shard[...]

    at_row = lax.broadcasted_iota(jnp.int32, (8, 384), 1) - BLUR_HALF
    row_ok = ((row > 0) | (at_row >= 0)) & ((row < n_row - 1) | (at_row < rows))
    row_ok = jnp.where(row_ok, 1.0, 0.0)
    for b in range(NB):
        edge = acc[NB, :, EDGE_IN * b : EDGE_IN * b + EDGE_OUT]
        part = jnp.concatenate(
            [acc[b, :, 0:MAIN], edge, jnp.zeros((CB, 384 - MAIN - EDGE_OUT), F32)], axis=1
        )
        part = part * row_ok[0:1]
        if b == 0:
            part = jnp.concatenate([jnp.where(col > 0, part[0:8], 0.0), part[8:]], axis=0)
        if b == NB - 1:
            part = jnp.concatenate([part[0 : CB - 8], jnp.where(col < n_col - 1, part[CB - 8 :], 0.0)], axis=0)
        flat[b * CB : (b + 1) * CB, :] = part.astype(BF16)
    flat[NB * CB :, :] = jnp.zeros((flat.shape[0] - NB * CB, 384), BF16)

    fetch.wait()
    slot_rows, slot_cols = rows // 64, cols // 128
    for i in range(-1, slot_rows + 1):
        for j in range(-1, slot_cols + 1):
            ti = 0 if i < 0 else (2 if i == slot_rows else 1)
            tj = 0 if j < 0 else (2 if j == slot_cols else 1)
            found = table[(i % slot_rows) * slot_cols + j % slot_cols, 3 * ti + tj]
            image = jnp.maximum(found - 1, 0)
            lanes = slice(128 + 128 * j, 256 + 128 * j)
            show = lambda x: jnp.where(found > 0, x.astype(F32), 0.0)
            if i < 0:
                placed[0:8, lanes] = show(cells[image, 48:64, :])[8:16]
            elif i == slot_rows:
                placed[8 + rows : 16 + rows, lanes] = show(cells[image, 0:16, :])[0:8]
            else:
                placed[8 + 64 * i : 72 + 64 * i, lanes] = show(cells[image])
    placed[16 + rows :, :] = jnp.zeros((placed.shape[0] - 16 - rows, placed.shape[1]), F32)

    g_high, g_low = blur_matrix((128, 256), 1)
    g_both = jnp.concatenate([g_high, g_low], axis=0)
    for i in range(rows // 128):
        part = dot_nt(g_both, flat[:, 128 * i : 128 * i + 256])
        cell = dot_nn(g_both, placed[128 * i : 128 * i + 256, :].astype(BF16))
        part = part[0:128] + part[128:]
        cell = cell[0:128] + cell[128:]
        part += cell[:, 128 - BLUR_HALF : 128 - BLUR_HALF + part.shape[1]]
        high = part.astype(BF16)
        blurred[0, 128 * i : 128 * i + 128, :] = high
        blurred[1, 128 * i : 128 * i + 128, :] = (part - high.astype(F32)).astype(BF16)
    g_high, g_low = blur_matrix((256, 128), 0)
    g_both = jnp.concatenate([g_high, g_low], axis=1)
    for j in range(cols // 128):
        lanes = slice(128 * j, 128 * j + 256)
        part = dot_nn(blurred[0, :, lanes], g_both)
        out[:, 128 * j : 128 * j + 128] = (
            part[:, 0:128] + part[:, 128:] + dot_nn(blurred[1, :, lanes], g_high)
        )


def shape(dims, dtype):
    return jax.ShapeDtypeStruct(dims, dtype)


def on_device(
    mask_pixels, across_taps, down_taps, kernel_weights, library, cell_ids, cell_slots, cell_count
):
    rows, cols = mask_pixels.shape
    kernels = across_taps.shape[0]
    entries = cell_ids.shape[-1]
    per = library.shape[0]
    n_row, n_col = lax.axis_size("row"), lax.axis_size("col")
    in_hbm = lambda x: pltpu.with_memory_space_constraint(x, pltpu.HBM)
    mask_hbm = in_hbm(mask_pixels)

    to_first, to_second, edges, taps = pl.pallas_call(
        prep_kernel,
        out_shape=(
            shape((STRIP + 16, rows), BF16),
            shape((STRIP + 16, rows), BF16),
            shape((2, STRIP, cols), jnp.int32),
            shape((2,) + across_taps.shape, BF16),
        ),
        in_specs=[HBM] * 3 + [SMEM] + [HBM] * 2,
        out_specs=(VMEM,) * 4,
        scratch_shapes=[
            pltpu.VMEM((2, rows, 128), jnp.int32),
            pltpu.VMEM(cell_ids.shape, jnp.int32),
            pltpu.VMEM(cell_slots.shape, jnp.int32),
            pltpu.SemaphoreType.DMA((8,)),
        ],
        compiler_params=PARAMS,
        name="prep",
    )(mask_hbm, in_hbm(cell_ids), in_hbm(cell_slots), cell_count, in_hbm(across_taps), in_hbm(down_taps))
    library, to_first, to_second = lax.optimization_barrier((library, to_first, to_second))

    def swaps(n):
        rounds = []
        for start in (0, 1):
            pairs = [(i, i + 1) for i in range(start, n - 1, 2)]
            rounds.append(pairs + [(b, a) for a, b in pairs])
        return rounds

    col_first, col_second = (
        lax.ppermute(x, "col", pairs) for x, pairs in zip((to_first, to_second), swaps(n_col))
    )
    shards = [library]
    for d in range(1, n_col):
        shards.append(lax.ppermute(library, "col", [(i, i ^ d) for i in range(n_col)]))

    to_above, to_below = pl.pallas_call(
        mid_kernel,
        out_shape=(shape((STRIP + 16, WIDE), BF16),) * 2,
        in_specs=[VMEM] * 4,
        out_specs=(VMEM,) * 2,
        compiler_params=PARAMS,
        name="mid",
    )(edges, col_first, col_second, to_first)
    row_first, row_second = (
        lax.ppermute(x, "row", pairs) for x, pairs in zip((to_above, to_below), swaps(n_row))
    )

    windows, ahead, back = pl.pallas_call(
        window_kernel,
        out_shape=(
            shape((NB, rows, 256), F32),
            shape((kernels, 8, 128), F32),
            shape((kernels, 8, 128), F32),
        ),
        in_specs=[VMEM] * 4,
        out_specs=(VMEM,) * 3,
        compiler_params=PARAMS,
        cost_estimate=pl.CostEstimate(flops=10**6, bytes_accessed=10**6, transcendentals=0),
        name="window",
    )(mask_pixels, col_first, col_second, taps)

    acc, images = pl.pallas_call(
        functools.partial(socs_kernel, entries, per),
        out_shape=(shape((NB + 1, CB, 256), F32), shape((SLOTS, 128), jnp.int32)),
        in_specs=[HBM] + [VMEM] * 8,
        out_specs=(VMEM,) * 2,
        scratch_shapes=[
            pltpu.VMEM((NB + 1, 256, 256), BF16),
            pltpu.SMEM(kernel_weights.shape, F32),
            pltpu.SemaphoreType.DMA,
        ]
        + [pltpu.VMEM((2 * GROUP, CB, 256), BF16)] * 2
        + [pltpu.VMEM((2 * GROUP, 256, 256), BF16)] * 2
        + [pltpu.VMEM((2 * GROUP, NB + 1, CB, 256), BF16)] * 2,
        compiler_params=PARAMS,
        cost_estimate=pl.CostEstimate(flops=5 * 10**9, bytes_accessed=8 * 10**6, transcendentals=0),
        name="socs",
    )(in_hbm(kernel_weights), windows, row_first, row_second, col_first, col_second, to_first, ahead, back)

    return pl.pallas_call(
        functools.partial(final_kernel, n_row, n_col),
        out_shape=shape((rows, cols), F32),
        in_specs=[VMEM] * (2 + n_col),
        out_specs=VMEM,
        scratch_shapes=[
            pltpu.VMEM((n_col * per,) + library.shape[1:], BF16),
            pltpu.SMEM((SLOTS, 128), jnp.int32),
            pltpu.VMEM((384, cols + 256), F32),
            pltpu.VMEM((WIDE, 384), BF16),
            pltpu.VMEM((2, rows, WIDE), BF16),
            pltpu.SemaphoreType.DMA,
        ],
        compiler_params=PARAMS,
        name="final",
    )(acc, images, *shards)


def solution(mesh):
    placed = (
        P(("frames", "row"), "col"),
        P(),
        P(),
        P(),
        P("col", None, None),
        P(("frames", "row"), "col", None),
        P(("frames", "row"), "col", None),
        P(("frames", "row"), "col"),
    )
    return jax.shard_map(
        on_device,
        mesh=mesh,
        in_specs=placed,
        out_specs=P(("frames", "row"), "col"),
        check_vma=False,
    )
```

```python
import functools
import math

import jax
import jax.numpy as jnp
from jax import lax
from jax.experimental import pallas as pl
from jax.experimental.pallas import tpu as pltpu
from jax.sharding import PartitionSpec as P

BLUR_HALF = 8
BLUR_SIGMA = 4.0
HALF = 16
RIM = HALF + BLUR_HALF
STRIP = 32
CB = 176
NB = 3
MAIN = 224
EDGE_IN = 80
EDGE_OUT = 48
RIGHT_AT = 56
GROUP = 2
WIDE = 640
SLOTS = 16
F32 = jnp.float32
BF16 = jnp.bfloat16
VMEM = pl.BlockSpec(memory_space=pltpu.VMEM)
SMEM = pl.BlockSpec(memory_space=pltpu.SMEM)
HBM = pl.BlockSpec(memory_space=pltpu.HBM)
PARAMS = pltpu.CompilerParams(vmem_limit_bytes=16 * 1024 * 1024)


def dot_nt(a, b):
    return lax.dot_general(a, b, (((1,), (1,)), ((), ())), preferred_element_type=F32)


def dot_nn(a, b):
    return lax.dot_general(a, b, (((1,), (0,)), ((), ())), preferred_element_type=F32)


def eye(rows, cols, shift):
    at = lax.broadcasted_iota(jnp.int32, (rows, cols), 1) - lax.broadcasted_iota(jnp.int32, (rows, cols), 0)
    return jnp.where(at == shift, 1.0, 0.0).astype(BF16)


def sides(axis, first_swap, second_swap):
    even = lax.rem(lax.axis_index(axis), 2) == 0
    return jnp.where(even, second_swap, first_swap), jnp.where(even, first_swap, second_swap)


def prep_kernel(
    mask, ids, slots, count, across, down, to_first, to_second, edges, taps, ends, a_ids, a_slots, sems
):
    rows, cols = mask.shape
    copies = [
        pltpu.make_async_copy(mask.at[:, 0:128], ends.at[0], sems.at[0]),
        pltpu.make_async_copy(mask.at[:, cols - 128 : cols], ends.at[1], sems.at[1]),
        pltpu.make_async_copy(ids, a_ids, sems.at[2]),
        pltpu.make_async_copy(slots, a_slots, sems.at[3]),
        pltpu.make_async_copy(mask.at[0:STRIP], edges.at[0], sems.at[4]),
        pltpu.make_async_copy(mask.at[rows - STRIP : rows], edges.at[1], sems.at[5]),
        pltpu.make_async_copy(across, taps.at[0], sems.at[6]),
        pltpu.make_async_copy(down, taps.at[1], sems.at[7]),
    ]
    for copy in copies:
        copy.start()
    for copy in copies[2:4]:
        copy.wait()
    line = lax.broadcasted_iota(jnp.int32, (16, 128), 0)
    lane = lax.broadcasted_iota(jnp.int32, (16, 128), 1)

    def spread(x):
        x = x.astype(F32)
        x = jnp.concatenate([x, jnp.zeros((1, 128 - x.shape[1]), F32)], axis=1)
        return jnp.broadcast_to(x, (16, 128))

    table = jnp.where(line == 1, spread(a_slots[0]), count[0, 0].astype(F32))
    table = jnp.where(line == 0, spread(a_ids[0]), table)
    width = jnp.where(line == 2, 1, ids.shape[2])
    table = jnp.where((lane < width) & (line < 3), table, 0.0).astype(BF16)
    for strip in (to_first, to_second):
        strip[STRIP:, 0:128] = table
        strip[STRIP:, 128:] = jnp.zeros((16, rows - 128), BF16)
    even = lax.rem(lax.axis_index("col"), 2) == 0
    copies[0].wait()
    first = dot_nt(eye(STRIP, 128, 0), ends[0].astype(F32).astype(BF16))
    copies[1].wait()
    last = dot_nt(eye(STRIP, 128, 128 - STRIP), ends[1].astype(F32).astype(BF16))
    to_first[0:STRIP, :] = jnp.where(even, last, first).astype(BF16)
    to_second[0:STRIP, :] = jnp.where(even, first, last).astype(BF16)
    for copy in copies[4:]:
        copy.wait()


def mid_kernel(edges, from_first, from_second, own, to_first, to_second):
    cols = edges.shape[2]
    rows = from_first.shape[1]
    left, right = sides("col", from_first[...].astype(F32), from_second[...].astype(F32))
    tables = jnp.concatenate(
        [left[STRIP:, 0:128], own[STRIP:, 0:128].astype(F32), right[STRIP:, 0:128], jnp.zeros((16, 256), F32)],
        axis=1,
    ).astype(BF16)
    fill = jnp.zeros((128 - STRIP, 128), F32)
    strips = []
    for i in range(2):
        at = 0 if i == 0 else rows - 128
        pick = eye(STRIP, 128, 0 if i == 0 else 128 - STRIP)

        def turned(strip):
            return dot_nt(pick, jnp.concatenate([strip[0:STRIP, at : at + 128], fill], axis=0).astype(BF16))

        parts = [turned(left)[:, STRIP - RIM : STRIP], edges[i].astype(F32), turned(right)[:, 0 : WIDE - RIM - cols]]
        strips.append(jnp.concatenate(parts, axis=1))
    even = lax.rem(lax.axis_index("row"), 2) == 0
    to_first[0:STRIP, :] = jnp.where(even, strips[1], strips[0]).astype(BF16)
    to_second[0:STRIP, :] = jnp.where(even, strips[0], strips[1]).astype(BF16)
    to_first[STRIP:, :] = tables
    to_second[STRIP:, :] = tables


def blur_matrix(shape, axis):
    lag = lax.broadcasted_iota(jnp.int32, shape, axis) - lax.broadcasted_iota(jnp.int32, shape, 1 - axis)
    total = sum(math.exp(-(t * t) / (2 * BLUR_SIGMA**2)) for t in range(-BLUR_HALF, BLUR_HALF + 1))
    off = (lag - BLUR_HALF).astype(F32)
    g = jnp.exp(-off * off / (2.0 * BLUR_SIGMA * BLUR_SIGMA)) * (1.0 / total)
    g = jnp.where((lag >= 0) & (lag <= 2 * BLUR_HALF), g, 0.0)
    high = g.astype(BF16)
    return high, (g - high.astype(F32)).astype(BF16)


def own_kernel(mask, taps, windows, ahead, back, g_row, g_col):
    rows, cols = mask.shape
    full = jnp.concatenate(
        [jnp.zeros((rows, RIM), F32), mask[...].astype(F32), jnp.zeros((rows, WIDE - RIM - cols), F32)], axis=1
    )
    for b in range(NB):
        windows[b] = full[:, CB * b : CB * b + 256]
    kernels, _, count = taps.shape[1:]
    flip = lax.broadcasted_iota(jnp.int32, (128, 128), 0) + lax.broadcasted_iota(jnp.int32, (128, 128), 1)
    flip = jnp.where(flip % 128 == 0, 1.0, 0.0).astype(BF16)
    ahead[...] = jnp.zeros(ahead.shape, F32)
    back[...] = jnp.zeros(back.shape, F32)
    for k in range(kernels):
        ahead[k, 0:2, 0:count] = taps[0, k].astype(F32)
        back[k, 0:2, 0:count] = taps[1, k].astype(F32)
    back[...] = dot_nn(back[...].reshape(kernels * 8, 128).astype(BF16), flip).reshape(kernels, 8, 128)
    g_row[0:128], g_row[128:256] = blur_matrix((128, 256), 1)
    g_col[:, 0:128], g_col[:, 128:256] = blur_matrix((256, 128), 0)


def socs_kernel(
    entries,
    per,
    weights,
    windows,
    row_first,
    row_second,
    col_first,
    col_second,
    own,
    ahead,
    back,
    acc,
    images,
    x_win,
    scale,
    sem,
    *scratch,
):
    across = scratch[0:2]
    down = scratch[2:4]
    first = scratch[4:6]
    groups = ahead.shape[0] // GROUP
    fetch = pltpu.make_async_copy(weights, scale, sem)
    fetch.start()
    above, below = sides("row", row_first[...].astype(F32), row_second[...].astype(F32))
    left, right = sides("col", col_first[...].astype(F32), col_second[...].astype(F32))
    rows = windows.shape[1]
    turned = jnp.concatenate(
        [
            left[STRIP - RIM : STRIP],
            jnp.zeros((128 - RIM + RIGHT_AT, rows), F32),
            right[0:RIM],
            jnp.zeros((128 - RIM - RIGHT_AT, rows), F32),
        ],
        axis=0,
    )
    turned = dot_nt(eye(rows, rows, 0), turned.astype(BF16))
    left, right = left[STRIP:, 0:128], right[STRIP:, 0:128]
    upper_rows = above[STRIP - RIM : STRIP]
    lower_rows = below[0:RIM]
    edge_rows = []
    for b in range(NB):
        lanes = slice(CB * b, CB * b + 256)
        part = windows[b]
        if b == 0:
            part = jnp.concatenate([part[:, 0:128] + turned[:, 0:128], part[:, 128:256]], axis=1)
        if b == NB - 1:
            part = jnp.concatenate([part[:, 0:128], part[:, 128:256] + turned[:, 128:256]], axis=1)
        x_win[b] = jnp.concatenate([upper_rows[:, lanes], part[0 : 256 - RIM]], axis=0).astype(BF16)
        edge_rows += [part[MAIN - RIM :], lower_rows[:, lanes]]
    edge_rows.append(jnp.zeros((256 - NB * EDGE_IN, 256), F32))
    x_win[NB] = jnp.concatenate(edge_rows, axis=0).astype(BF16)
    acc[...] = jnp.zeros(acc.shape, F32)
    for ref in across + down:
        ref[...] = jnp.zeros(ref.shape, BF16)

    slot = lax.broadcasted_iota(jnp.int32, (SLOTS, 128), 0).astype(F32)
    lane = lax.broadcasted_iota(jnp.int32, (SLOTS, 128), 1)
    found = jnp.zeros((SLOTS, 128), F32)
    col = lax.axis_index("col")
    tables = [above[STRIP:, 128 * t : 128 * t + 128] for t in range(3)]
    tables += [left, own[STRIP:, 0:128].astype(F32), right]
    tables += [below[STRIP:, 128 * t : 128 * t + 128] for t in range(3)]
    for t, table in enumerate(tables):
        live = lane.astype(F32) < table[2:3, 0:1]
        hit = live & (table[1:2] == slot) & (lane < entries)
        image = jnp.sum(jnp.where(hit, table[0:1] + 1.0, 0.0), axis=1, keepdims=True)
        found = jnp.where(lane == t, image, found)
    cell = found.astype(jnp.int32) - 1
    images[...] = jnp.where(cell >= 0, ((cell // per) ^ col) * per + cell % per + 1, 0)

    row = lax.broadcasted_iota(jnp.int32, (32, 128), 0)
    lane = lax.broadcasted_iota(jnp.int32, (32, 128), 1)
    low = lane >= row + 96

    def cycled(x):
        return pltpu.roll(jnp.broadcast_to(x, (128, 128)), 0, 1, stride=1, stride_axis=0)

    def build_across(m, s):
        for q in range(2 * GROUP):
            cyc = cycled(ahead[GROUP * m + q // 2, q % 2 : q % 2 + 1, :])
            head = cyc[0:96].astype(BF16)
            tail = cyc[96:128]
            over = jnp.where(low, 0.0, tail)
            across[s][q, 0:96, 0:128] = head
            across[s][q, 128:CB, 128:256] = head[0 : CB - 128]
            across[s][q, 96:128, 0:128] = jnp.where(low, tail, 0.0).astype(BF16)
            across[s][q, 96:128, 128:256] = over.astype(BF16)

    def build_down(m, s):
        for q in range(2 * GROUP):
            cyc = cycled(back[GROUP * m + q // 2, q % 2 : q % 2 + 1, :])
            head = cyc[0:32]
            over = jnp.where(low, head, 0.0).astype(BF16)
            head = jnp.where(low, 0.0, head)
            same = jnp.concatenate([head, cyc[32:128]], axis=0).astype(BF16)
            down[s][q, 0:128, 0:128] = same
            down[s][q, 128:256, 128:256] = same
            down[s][q, 128:160, 0:128] = over

    def pass_one(s):
        taps = across[s][...].reshape(2 * GROUP * CB, 256)
        for j in range(NB + 1):
            part = dot_nt(taps, x_win[j]).astype(BF16)
            for q in range(2 * GROUP):
                first[s][q, j] = part[q * CB : (q + 1) * CB]

    def pass_two(m, s):
        for q in range(2 * GROUP):
            second = dot_nn(first[s][q].reshape((NB + 1) * CB, 256), down[s][q])
            acc[...] += (scale[GROUP * m + q // 2] * (second * second)).reshape(acc.shape)

    def stage(m, s):
        pass_one(s)
        build_down(m, s)
        build_across(jnp.minimum(m + 1, groups - 1), 1 - s)
        pass_two(m - 1, 1 - s)

    build_across(0, 0)
    pass_one(0)
    build_down(0, 0)
    build_across(1, 1)
    fetch.wait()

    def step(i, carry):
        stage(2 * i + 1, 1)
        stage(2 * i + 2, 0)
        return carry

    lax.fori_loop(0, groups // 2 - 1, step, 0)
    stage(groups - 1, 1)
    pass_two(groups - 1, 1)


def final_kernel(n_row, n_col, acc, images, g_row, g_col, *rest):
    shards = rest[:-7]
    out, cells, table, placed, flat, blurred, sem = rest[-7:]
    g_high = g_col[:, 0:128]
    per = shards[0].shape[0]
    rows, cols = out.shape
    row, col = lax.axis_index("row"), lax.axis_index("col")
    fetch = pltpu.make_async_copy(images, table, sem)
    fetch.start()
    for i, shard in enumerate(shards):
        cells[pl.ds(i * per, per)] = shard[...]

    at_row = lax.broadcasted_iota(jnp.int32, (8, 384), 1) - BLUR_HALF
    row_ok = ((row > 0) | (at_row >= 0)) & ((row < n_row - 1) | (at_row < rows))
    row_ok = jnp.where(row_ok, 1.0, 0.0)
    for b in range(NB):
        edge = acc[NB, :, EDGE_IN * b : EDGE_IN * b + EDGE_OUT]
        part = jnp.concatenate(
            [acc[b, :, 0:MAIN], edge, jnp.zeros((CB, 384 - MAIN - EDGE_OUT), F32)], axis=1
        )
        part = part * row_ok[0:1]
        if b == 0:
            part = jnp.concatenate([jnp.where(col > 0, part[0:8], 0.0), part[8:]], axis=0)
        if b == NB - 1:
            part = jnp.concatenate([part[0 : CB - 8], jnp.where(col < n_col - 1, part[CB - 8 :], 0.0)], axis=0)
        flat[b * CB : (b + 1) * CB, :] = part.astype(BF16)
    flat[NB * CB :, :] = jnp.zeros((flat.shape[0] - NB * CB, 384), BF16)

    halves = []
    for i in range(rows // 128):
        part = dot_nt(g_row[...], flat[:, 128 * i : 128 * i + 256])
        halves.append(part[0:128] + part[128:])

    fetch.wait()
    slot_rows, slot_cols = rows // 64, cols // 128
    for i in range(-1, slot_rows + 1):
        for j in range(-1, slot_cols + 1):
            ti = 0 if i < 0 else (2 if i == slot_rows else 1)
            tj = 0 if j < 0 else (2 if j == slot_cols else 1)
            found = table[(i % slot_rows) * slot_cols + j % slot_cols, 3 * ti + tj]
            image = jnp.maximum(found - 1, 0)
            lanes = slice(128 + 128 * j, 256 + 128 * j)
            show = lambda x: jnp.where(found > 0, x.astype(F32), 0.0)
            if i < 0:
                placed[0:8, lanes] = show(cells[image, 48:64, :])[8:16]
            elif i == slot_rows:
                placed[8 + rows : 16 + rows, lanes] = show(cells[image, 0:16, :])[0:8]
            else:
                placed[8 + 64 * i : 72 + 64 * i, lanes] = show(cells[image])
    placed[16 + rows :, :] = jnp.zeros((placed.shape[0] - 16 - rows, placed.shape[1]), F32)

    for i, part in enumerate(halves):
        cell = dot_nn(g_row[...], placed[128 * i : 128 * i + 256, :].astype(BF16))
        cell = cell[0:128] + cell[128:]
        part += cell[:, 128 - BLUR_HALF : 128 - BLUR_HALF + part.shape[1]]
        high = part.astype(BF16)
        blurred[0, 128 * i : 128 * i + 128, :] = high
        blurred[1, 128 * i : 128 * i + 128, :] = (part - high.astype(F32)).astype(BF16)
    for j in range(cols // 128):
        lanes = slice(128 * j, 128 * j + 256)
        part = dot_nn(blurred[0, :, lanes], g_col[...])
        out[:, 128 * j : 128 * j + 128] = (
            part[:, 0:128] + part[:, 128:] + dot_nn(blurred[1, :, lanes], g_high)
        )


def shape(dims, dtype):
    return jax.ShapeDtypeStruct(dims, dtype)


def on_device(
    mask_pixels, across_taps, down_taps, kernel_weights, library, cell_ids, cell_slots, cell_count
):
    rows, cols = mask_pixels.shape
    kernels = across_taps.shape[0]
    entries = cell_ids.shape[-1]
    per = library.shape[0]
    n_row, n_col = lax.axis_size("row"), lax.axis_size("col")
    in_hbm = lambda x: pltpu.with_memory_space_constraint(x, pltpu.HBM)
    mask_hbm = in_hbm(mask_pixels)

    to_first, to_second, edges, taps = pl.pallas_call(
        prep_kernel,
        out_shape=(
            shape((STRIP + 16, rows), BF16),
            shape((STRIP + 16, rows), BF16),
            shape((2, STRIP, cols), jnp.int32),
            shape((2,) + across_taps.shape, BF16),
        ),
        in_specs=[HBM] * 3 + [SMEM] + [HBM] * 2,
        out_specs=(VMEM,) * 4,
        scratch_shapes=[
            pltpu.VMEM((2, rows, 128), jnp.int32),
            pltpu.VMEM(cell_ids.shape, jnp.int32),
            pltpu.VMEM(cell_slots.shape, jnp.int32),
            pltpu.SemaphoreType.DMA((8,)),
        ],
        compiler_params=PARAMS,
        name="prep",
    )(mask_hbm, in_hbm(cell_ids), in_hbm(cell_slots), cell_count, in_hbm(across_taps), in_hbm(down_taps))

    def swaps(n):
        rounds = []
        for start in (0, 1):
            pairs = [(i, i + 1) for i in range(start, n - 1, 2)]
            rounds.append(pairs + [(b, a) for a, b in pairs])
        return rounds

    col_first, col_second = (
        lax.ppermute(x, "col", pairs) for x, pairs in zip((to_first, to_second), swaps(n_col))
    )
    to_above, to_below = pl.pallas_call(
        mid_kernel,
        out_shape=(shape((STRIP + 16, WIDE), BF16),) * 2,
        in_specs=[VMEM] * 4,
        out_specs=(VMEM,) * 2,
        compiler_params=PARAMS,
        name="mid",
    )(edges, col_first, col_second, to_first)
    library, to_above, to_below = lax.optimization_barrier((library, to_above, to_below))
    shards = [library]
    for d in range(1, n_col):
        shards.append(lax.ppermute(library, "col", [(i, i ^ d) for i in range(n_col)]))
    row_first, row_second = (
        lax.ppermute(x, "row", pairs) for x, pairs in zip((to_above, to_below), swaps(n_row))
    )

    windows, ahead, back, g_row, g_col = pl.pallas_call(
        own_kernel,
        out_shape=(
            shape((NB, rows, 256), F32),
            shape((kernels, 8, 128), F32),
            shape((kernels, 8, 128), F32),
            shape((256, 256), BF16),
            shape((256, 256), BF16),
        ),
        in_specs=[VMEM] * 2,
        out_specs=(VMEM,) * 5,
        compiler_params=PARAMS,
        cost_estimate=pl.CostEstimate(flops=10**6, bytes_accessed=10**6, transcendentals=0),
        name="own",
    )(mask_pixels, taps)

    acc, images = pl.pallas_call(
        functools.partial(socs_kernel, entries, per),
        out_shape=(shape((NB + 1, CB, 256), F32), shape((SLOTS, 128), jnp.int32)),
        in_specs=[HBM] + [VMEM] * 8,
        out_specs=(VMEM,) * 2,
        scratch_shapes=[
            pltpu.VMEM((NB + 1, 256, 256), BF16),
            pltpu.SMEM(kernel_weights.shape, F32),
            pltpu.SemaphoreType.DMA,
        ]
        + [pltpu.VMEM((2 * GROUP, CB, 256), BF16)] * 2
        + [pltpu.VMEM((2 * GROUP, 256, 256), BF16)] * 2
        + [pltpu.VMEM((2 * GROUP, NB + 1, CB, 256), BF16)] * 2,
        compiler_params=PARAMS,
        cost_estimate=pl.CostEstimate(flops=10**6, bytes_accessed=10**5, transcendentals=0),
        name="socs",
    )(in_hbm(kernel_weights), windows, row_first, row_second, col_first, col_second, to_first, ahead, back)

    return pl.pallas_call(
        functools.partial(final_kernel, n_row, n_col),
        out_shape=shape((rows, cols), F32),
        in_specs=[VMEM] * (4 + n_col),
        out_specs=VMEM,
        scratch_shapes=[
            pltpu.VMEM((n_col * per,) + library.shape[1:], BF16),
            pltpu.SMEM((SLOTS, 128), jnp.int32),
            pltpu.VMEM((384, cols + 256), F32),
            pltpu.VMEM((WIDE, 384), BF16),
            pltpu.VMEM((2, rows, WIDE), BF16),
            pltpu.SemaphoreType.DMA,
        ],
        compiler_params=PARAMS,
        name="final",
    )(acc, images, g_row, g_col, *shards)


def solution(mesh):
    placed = (
        P(("frames", "row"), "col"),
        P(),
        P(),
        P(),
        P("col", None, None),
        P(("frames", "row"), "col", None),
        P(("frames", "row"), "col", None),
        P(("frames", "row"), "col"),
    )
    return jax.shard_map(
        on_device,
        mesh=mesh,
        in_specs=placed,
        out_specs=P(("frames", "row"), "col"),
        check_vma=False,
    )
```

```python
import functools
import math

import jax
import jax.numpy as jnp
from jax import lax
from jax.experimental import pallas as pl
from jax.experimental.pallas import tpu as pltpu
from jax.sharding import PartitionSpec as P

BLUR_HALF = 8
BLUR_SIGMA = 4.0
HALF = 16
RIM = HALF + BLUR_HALF
STRIP = 32
CB = 176
NB = 3
MAIN = 224
EDGE_IN = 80
EDGE_OUT = 48
RIGHT_AT = 56
HALF_STRIP = STRIP + 16
GROUP = 2
WIDE = 640
SLOTS = 16
F32 = jnp.float32
BF16 = jnp.bfloat16
VMEM = pl.BlockSpec(memory_space=pltpu.VMEM)
SMEM = pl.BlockSpec(memory_space=pltpu.SMEM)
HBM = pl.BlockSpec(memory_space=pltpu.HBM)
PARAMS = pltpu.CompilerParams(vmem_limit_bytes=16 * 1024 * 1024)


def dot_nt(a, b):
    return lax.dot_general(a, b, (((1,), (1,)), ((), ())), preferred_element_type=F32)


def dot_nn(a, b):
    return lax.dot_general(a, b, (((1,), (0,)), ((), ())), preferred_element_type=F32)


def join(strip):
    halves = [strip[0:HALF_STRIP, :], strip[HALF_STRIP : 2 * HALF_STRIP, :]]
    return jnp.concatenate(halves, axis=1).astype(F32)


def eye(rows, cols, shift):
    at = lax.broadcasted_iota(jnp.int32, (rows, cols), 1) - lax.broadcasted_iota(jnp.int32, (rows, cols), 0)
    return jnp.where(at == shift, 1.0, 0.0).astype(BF16)


def sides(axis, first_swap, second_swap):
    even = lax.rem(lax.axis_index(axis), 2) == 0
    return jnp.where(even, second_swap, first_swap), jnp.where(even, first_swap, second_swap)


def prep_kernel(
    mask, ids, slots, count, across, down, library, to_first, to_second, edges, taps, ends, a_ids, a_slots, sems
):
    rows, cols = mask.shape
    copies = [
        pltpu.make_async_copy(mask.at[:, 0:128], ends.at[0], sems.at[0]),
        pltpu.make_async_copy(mask.at[:, cols - 128 : cols], ends.at[1], sems.at[1]),
        pltpu.make_async_copy(ids, a_ids, sems.at[2]),
        pltpu.make_async_copy(slots, a_slots, sems.at[3]),
        pltpu.make_async_copy(mask.at[0:STRIP], edges.at[0], sems.at[4]),
        pltpu.make_async_copy(mask.at[rows - STRIP : rows], edges.at[1], sems.at[5]),
        pltpu.make_async_copy(across, taps.at[0], sems.at[6]),
        pltpu.make_async_copy(down, taps.at[1], sems.at[7]),
        pltpu.make_async_copy(library, to_first.at[2 * HALF_STRIP :], sems.at[8]),
    ]
    for copy in copies:
        copy.start()
    for copy in copies[2:4]:
        copy.wait()
    line = lax.broadcasted_iota(jnp.int32, (16, 128), 0)
    lane = lax.broadcasted_iota(jnp.int32, (16, 128), 1)

    def spread(x):
        x = x.astype(F32)
        x = jnp.concatenate([x, jnp.zeros((1, 128 - x.shape[1]), F32)], axis=1)
        return jnp.broadcast_to(x, (16, 128))

    table = jnp.where(line == 1, spread(a_slots[0]), count[0, 0].astype(F32))
    table = jnp.where(line == 0, spread(a_ids[0]), table)
    width = jnp.where(line == 2, 1, ids.shape[2])
    table = jnp.where((lane < width) & (line < 3), table, 0.0).astype(BF16)
    for strip in (to_first, to_second):
        strip[STRIP:HALF_STRIP, :] = table
        strip[HALF_STRIP + STRIP : 2 * HALF_STRIP, :] = jnp.zeros((16, 128), BF16)
    even = lax.rem(lax.axis_index("col"), 2) == 0
    copies[0].wait()
    first = dot_nt(eye(STRIP, 128, 0), ends[0].astype(F32).astype(BF16))
    copies[1].wait()
    last = dot_nt(eye(STRIP, 128, 128 - STRIP), ends[1].astype(F32).astype(BF16))
    for strip, part in ((to_first, jnp.where(even, last, first)), (to_second, jnp.where(even, first, last))):
        strip[0:STRIP, :] = part[:, 0:128].astype(BF16)
        strip[HALF_STRIP : HALF_STRIP + STRIP, :] = part[:, 128:256].astype(BF16)
    for copy in copies[4:]:
        copy.wait()


def mid_kernel(edges, from_first, from_second, own, to_first, to_second):
    cols = edges.shape[2]
    rows = 256
    left, right = sides("col", join(from_first), join(from_second))
    tables = jnp.concatenate(
        [left[STRIP:, 0:128], own[STRIP:HALF_STRIP, :].astype(F32), right[STRIP:, 0:128], jnp.zeros((16, 256), F32)],
        axis=1,
    ).astype(BF16)
    fill = jnp.zeros((128 - STRIP, 128), F32)
    strips = []
    for i in range(2):
        at = 0 if i == 0 else rows - 128
        pick = eye(STRIP, 128, 0 if i == 0 else 128 - STRIP)

        def turned(strip):
            return dot_nt(pick, jnp.concatenate([strip[0:STRIP, at : at + 128], fill], axis=0).astype(BF16))

        parts = [turned(left)[:, STRIP - RIM : STRIP], edges[i].astype(F32), turned(right)[:, 0 : WIDE - RIM - cols]]
        strips.append(jnp.concatenate(parts, axis=1))
    even = lax.rem(lax.axis_index("row"), 2) == 0
    to_first[0:STRIP, :] = jnp.where(even, strips[1], strips[0]).astype(BF16)
    to_second[0:STRIP, :] = jnp.where(even, strips[0], strips[1]).astype(BF16)
    to_first[STRIP:, :] = tables
    to_second[STRIP:, :] = tables


def blur_matrix(shape, axis):
    lag = lax.broadcasted_iota(jnp.int32, shape, axis) - lax.broadcasted_iota(jnp.int32, shape, 1 - axis)
    total = sum(math.exp(-(t * t) / (2 * BLUR_SIGMA**2)) for t in range(-BLUR_HALF, BLUR_HALF + 1))
    off = (lag - BLUR_HALF).astype(F32)
    g = jnp.exp(-off * off / (2.0 * BLUR_SIGMA * BLUR_SIGMA)) * (1.0 / total)
    g = jnp.where((lag >= 0) & (lag <= 2 * BLUR_HALF), g, 0.0)
    high = g.astype(BF16)
    return high, (g - high.astype(F32)).astype(BF16)


def own_kernel(mask, taps, windows, ahead, back, g_row, g_col):
    rows, cols = mask.shape
    full = jnp.concatenate(
        [jnp.zeros((rows, RIM), F32), mask[...].astype(F32), jnp.zeros((rows, WIDE - RIM - cols), F32)], axis=1
    )
    for b in range(NB):
        windows[b] = full[:, CB * b : CB * b + 256]
    kernels, _, count = taps.shape[1:]
    flip = lax.broadcasted_iota(jnp.int32, (128, 128), 0) + lax.broadcasted_iota(jnp.int32, (128, 128), 1)
    flip = jnp.where(flip % 128 == 0, 1.0, 0.0).astype(BF16)
    ahead[...] = jnp.zeros(ahead.shape, F32)
    back[...] = jnp.zeros(back.shape, F32)
    for k in range(kernels):
        ahead[k, 0:2, 0:count] = taps[0, k].astype(F32)
        back[k, 0:2, 0:count] = taps[1, k].astype(F32)
    back[...] = dot_nn(back[...].reshape(kernels * 8, 128).astype(BF16), flip).reshape(kernels, 8, 128)
    g_row[0:128], g_row[128:256] = blur_matrix((128, 256), 1)
    g_col[:, 0:128], g_col[:, 128:256] = blur_matrix((256, 128), 0)


def socs_kernel(
    entries,
    per,
    weights,
    windows,
    row_first,
    row_second,
    col_first,
    col_second,
    own,
    ahead,
    back,
    acc,
    images,
    x_win,
    scale,
    sem,
    *scratch,
):
    across = scratch[0:2]
    down = scratch[2:4]
    first = scratch[4:6]
    groups = ahead.shape[0] // GROUP
    fetch = pltpu.make_async_copy(weights, scale, sem)
    fetch.start()
    above, below = sides("row", row_first[...].astype(F32), row_second[...].astype(F32))
    left, right = sides("col", join(col_first), join(col_second))
    rows = windows.shape[1]
    turned = jnp.concatenate(
        [
            left[STRIP - RIM : STRIP],
            jnp.zeros((128 - RIM + RIGHT_AT, rows), F32),
            right[0:RIM],
            jnp.zeros((128 - RIM - RIGHT_AT, rows), F32),
        ],
        axis=0,
    )
    turned = dot_nt(eye(rows, rows, 0), turned.astype(BF16))
    left, right = left[STRIP:, 0:128], right[STRIP:, 0:128]
    upper_rows = above[STRIP - RIM : STRIP]
    lower_rows = below[0:RIM]
    edge_rows = []
    for b in range(NB):
        lanes = slice(CB * b, CB * b + 256)
        part = windows[b]
        if b == 0:
            part = jnp.concatenate([part[:, 0:128] + turned[:, 0:128], part[:, 128:256]], axis=1)
        if b == NB - 1:
            part = jnp.concatenate([part[:, 0:128], part[:, 128:256] + turned[:, 128:256]], axis=1)
        x_win[b] = jnp.concatenate([upper_rows[:, lanes], part[0 : 256 - RIM]], axis=0).astype(BF16)
        edge_rows += [part[MAIN - RIM :], lower_rows[:, lanes]]
    edge_rows.append(jnp.zeros((256 - NB * EDGE_IN, 256), F32))
    x_win[NB] = jnp.concatenate(edge_rows, axis=0).astype(BF16)
    acc[...] = jnp.zeros(acc.shape, F32)
    for ref in across + down:
        ref[...] = jnp.zeros(ref.shape, BF16)

    slot = lax.broadcasted_iota(jnp.int32, (SLOTS, 128), 0).astype(F32)
    lane = lax.broadcasted_iota(jnp.int32, (SLOTS, 128), 1)
    found = jnp.zeros((SLOTS, 128), F32)
    col = lax.axis_index("col")
    tables = [above[STRIP:, 128 * t : 128 * t + 128] for t in range(3)]
    tables += [left, own[STRIP:HALF_STRIP, :].astype(F32), right]
    tables += [below[STRIP:, 128 * t : 128 * t + 128] for t in range(3)]
    for t, table in enumerate(tables):
        live = lane.astype(F32) < table[2:3, 0:1]
        hit = live & (table[1:2] == slot) & (lane < entries)
        image = jnp.sum(jnp.where(hit, table[0:1] + 1.0, 0.0), axis=1, keepdims=True)
        found = jnp.where(lane == t, image, found)
    cell = found.astype(jnp.int32) - 1
    images[...] = jnp.where(cell >= 0, ((cell // per) ^ col) * per + cell % per + 1, 0)

    row = lax.broadcasted_iota(jnp.int32, (32, 128), 0)
    lane = lax.broadcasted_iota(jnp.int32, (32, 128), 1)
    low = lane >= row + 96

    def cycled(x):
        return pltpu.roll(jnp.broadcast_to(x, (128, 128)), 0, 1, stride=1, stride_axis=0)

    def build_across(m, s):
        for q in range(2 * GROUP):
            cyc = cycled(ahead[GROUP * m + q // 2, q % 2 : q % 2 + 1, :])
            head = cyc[0:96].astype(BF16)
            tail = cyc[96:128]
            over = jnp.where(low, 0.0, tail)
            across[s][q, 0:96, 0:128] = head
            across[s][q, 128:CB, 128:256] = head[0 : CB - 128]
            across[s][q, 96:128, 0:128] = jnp.where(low, tail, 0.0).astype(BF16)
            across[s][q, 96:128, 128:256] = over.astype(BF16)

    def build_down(m, s):
        for q in range(2 * GROUP):
            cyc = cycled(back[GROUP * m + q // 2, q % 2 : q % 2 + 1, :])
            head = cyc[0:32]
            over = jnp.where(low, head, 0.0).astype(BF16)
            head = jnp.where(low, 0.0, head)
            same = jnp.concatenate([head, cyc[32:128]], axis=0).astype(BF16)
            down[s][q, 0:128, 0:128] = same
            down[s][q, 128:256, 128:256] = same
            down[s][q, 128:160, 0:128] = over

    def pass_one(s):
        taps = across[s][...].reshape(2 * GROUP * CB, 256)
        for j in range(NB + 1):
            part = dot_nt(taps, x_win[j]).astype(BF16)
            for q in range(2 * GROUP):
                first[s][q, j] = part[q * CB : (q + 1) * CB]

    def pass_two(m, s):
        for q in range(2 * GROUP):
            second = dot_nn(first[s][q].reshape((NB + 1) * CB, 256), down[s][q])
            acc[...] += (scale[GROUP * m + q // 2] * (second * second)).reshape(acc.shape)

    def stage(m, s):
        pass_one(s)
        build_down(m, s)
        build_across(jnp.minimum(m + 1, groups - 1), 1 - s)
        pass_two(m - 1, 1 - s)

    build_across(0, 0)
    pass_one(0)
    build_down(0, 0)
    build_across(1, 1)
    fetch.wait()

    def step(i, carry):
        stage(2 * i + 1, 1)
        stage(2 * i + 2, 0)
        return carry

    lax.fori_loop(0, groups // 2 - 1, step, 0)
    stage(groups - 1, 1)
    pass_two(groups - 1, 1)


def final_kernel(n_row, n_col, acc, images, g_row, g_col, *rest):
    shards = rest[:-7]
    out, cells, table, placed, flat, blurred, sem = rest[-7:]
    g_high = g_col[:, 0:128]
    per = cells.shape[0] // len(shards)
    rows, cols = out.shape
    row, col = lax.axis_index("row"), lax.axis_index("col")
    fetch = pltpu.make_async_copy(images, table, sem)
    fetch.start()
    for i, shard in enumerate(shards):
        rows_of = shard.shape[0] - per * 64
        cells[pl.ds(i * per, per)] = shard[rows_of:, :].reshape(per, 64, 128)

    at_row = lax.broadcasted_iota(jnp.int32, (8, 384), 1) - BLUR_HALF
    row_ok = ((row > 0) | (at_row >= 0)) & ((row < n_row - 1) | (at_row < rows))
    row_ok = jnp.where(row_ok, 1.0, 0.0)
    for b in range(NB):
        edge = acc[NB, :, EDGE_IN * b : EDGE_IN * b + EDGE_OUT]
        part = jnp.concatenate(
            [acc[b, :, 0:MAIN], edge, jnp.zeros((CB, 384 - MAIN - EDGE_OUT), F32)], axis=1
        )
        part = part * row_ok[0:1]
        if b == 0:
            part = jnp.concatenate([jnp.where(col > 0, part[0:8], 0.0), part[8:]], axis=0)
        if b == NB - 1:
            part = jnp.concatenate([part[0 : CB - 8], jnp.where(col < n_col - 1, part[CB - 8 :], 0.0)], axis=0)
        flat[b * CB : (b + 1) * CB, :] = part.astype(BF16)
    flat[NB * CB :, :] = jnp.zeros((flat.shape[0] - NB * CB, 384), BF16)

    halves = []
    for i in range(rows // 128):
        part = dot_nt(g_row[...], flat[:, 128 * i : 128 * i + 256])
        halves.append(part[0:128] + part[128:])

    fetch.wait()
    slot_rows, slot_cols = rows // 64, cols // 128
    for i in range(-1, slot_rows + 1):
        for j in range(-1, slot_cols + 1):
            ti = 0 if i < 0 else (2 if i == slot_rows else 1)
            tj = 0 if j < 0 else (2 if j == slot_cols else 1)
            found = table[(i % slot_rows) * slot_cols + j % slot_cols, 3 * ti + tj]
            image = jnp.maximum(found - 1, 0)
            lanes = slice(128 + 128 * j, 256 + 128 * j)
            show = lambda x: jnp.where(found > 0, x.astype(F32), 0.0)
            if i < 0:
                placed[0:8, lanes] = show(cells[image, 48:64, :])[8:16]
            elif i == slot_rows:
                placed[8 + rows : 16 + rows, lanes] = show(cells[image, 0:16, :])[0:8]
            else:
                placed[8 + 64 * i : 72 + 64 * i, lanes] = show(cells[image])
    placed[16 + rows :, :] = jnp.zeros((placed.shape[0] - 16 - rows, placed.shape[1]), F32)

    for i, part in enumerate(halves):
        cell = dot_nn(g_row[...], placed[128 * i : 128 * i + 256, :].astype(BF16))
        cell = cell[0:128] + cell[128:]
        part += cell[:, 128 - BLUR_HALF : 128 - BLUR_HALF + part.shape[1]]
        high = part.astype(BF16)
        blurred[0, 128 * i : 128 * i + 128, :] = high
        blurred[1, 128 * i : 128 * i + 128, :] = (part - high.astype(F32)).astype(BF16)
    for j in range(cols // 128):
        lanes = slice(128 * j, 128 * j + 256)
        part = dot_nn(blurred[0, :, lanes], g_col[...])
        out[:, 128 * j : 128 * j + 128] = (
            part[:, 0:128] + part[:, 128:] + dot_nn(blurred[1, :, lanes], g_high)
        )


def shape(dims, dtype):
    return jax.ShapeDtypeStruct(dims, dtype)


def on_device(
    mask_pixels, across_taps, down_taps, kernel_weights, library, cell_ids, cell_slots, cell_count
):
    rows, cols = mask_pixels.shape
    kernels = across_taps.shape[0]
    entries = cell_ids.shape[-1]
    per = library.shape[0]
    n_row, n_col = lax.axis_size("row"), lax.axis_size("col")
    library = library.reshape(per * 64, 128)
    in_hbm = lambda x: pltpu.with_memory_space_constraint(x, pltpu.HBM)
    mask_hbm = in_hbm(mask_pixels)

    to_first, to_second, edges, taps = pl.pallas_call(
        prep_kernel,
        out_shape=(
            shape((2 * HALF_STRIP + per * 64, 128), BF16),
            shape((2 * HALF_STRIP, 128), BF16),
            shape((2, STRIP, cols), jnp.int32),
            shape((2,) + across_taps.shape, BF16),
        ),
        in_specs=[HBM] * 3 + [SMEM] + [HBM] * 3,
        out_specs=(VMEM,) * 4,
        scratch_shapes=[
            pltpu.VMEM((2, rows, 128), jnp.int32),
            pltpu.VMEM(cell_ids.shape, jnp.int32),
            pltpu.VMEM(cell_slots.shape, jnp.int32),
            pltpu.SemaphoreType.DMA((9,)),
        ],
        compiler_params=PARAMS,
        name="prep",
    )(mask_hbm, in_hbm(cell_ids), in_hbm(cell_slots), cell_count, in_hbm(across_taps), in_hbm(down_taps), in_hbm(library))

    def swaps(n):
        rounds = []
        for start in (0, 1):
            pairs = [(i, i + 1) for i in range(start, n - 1, 2)]
            rounds.append(pairs + [(b, a) for a, b in pairs])
        return rounds

    pairs = swaps(n_col)
    col_second = lax.ppermute(to_second, "col", pairs[1])
    col_first = lax.ppermute(to_first, "col", pairs[0])
    shards = [library, col_first]
    to_above, to_below = pl.pallas_call(
        mid_kernel,
        out_shape=(shape((STRIP + 16, WIDE), BF16),) * 2,
        in_specs=[VMEM] * 4,
        out_specs=(VMEM,) * 2,
        compiler_params=PARAMS,
        name="mid",
    )(edges, col_first, col_second, to_first)
    for d in range(2, n_col):
        if d == 2:
            block, col_second = lax.optimization_barrier((library, col_second))
        if d == 3:
            block, to_above, to_below = lax.optimization_barrier((library, to_above, to_below))
        shards.append(lax.ppermute(block, "col", [(i, i ^ d) for i in range(n_col)]))
    row_first, row_second = (
        lax.ppermute(x, "row", pairs) for x, pairs in zip((to_above, to_below), swaps(n_row))
    )

    windows, ahead, back, g_row, g_col = pl.pallas_call(
        own_kernel,
        out_shape=(
            shape((NB, rows, 256), F32),
            shape((kernels, 8, 128), F32),
            shape((kernels, 8, 128), F32),
            shape((256, 256), BF16),
            shape((256, 256), BF16),
        ),
        in_specs=[VMEM] * 2,
        out_specs=(VMEM,) * 5,
        compiler_params=PARAMS,
        cost_estimate=pl.CostEstimate(flops=10**6, bytes_accessed=10**6, transcendentals=0),
        name="own",
    )(mask_pixels, taps)

    acc, images = pl.pallas_call(
        functools.partial(socs_kernel, entries, per),
        out_shape=(shape((NB + 1, CB, 256), F32), shape((SLOTS, 128), jnp.int32)),
        in_specs=[HBM] + [VMEM] * 8,
        out_specs=(VMEM,) * 2,
        scratch_shapes=[
            pltpu.VMEM((NB + 1, 256, 256), BF16),
            pltpu.SMEM(kernel_weights.shape, F32),
            pltpu.SemaphoreType.DMA,
        ]
        + [pltpu.VMEM((2 * GROUP, CB, 256), BF16)] * 2
        + [pltpu.VMEM((2 * GROUP, 256, 256), BF16)] * 2
        + [pltpu.VMEM((2 * GROUP, NB + 1, CB, 256), BF16)] * 2,
        compiler_params=PARAMS,
        cost_estimate=pl.CostEstimate(flops=10**6, bytes_accessed=10**5, transcendentals=0),
        name="socs",
    )(in_hbm(kernel_weights), windows, row_first, row_second, col_first, col_second, to_first, ahead, back)

    return pl.pallas_call(
        functools.partial(final_kernel, n_row, n_col),
        out_shape=shape((rows, cols), F32),
        in_specs=[VMEM] * (4 + n_col),
        out_specs=VMEM,
        scratch_shapes=[
            pltpu.VMEM((n_col * per, 64, 128), BF16),
            pltpu.SMEM((SLOTS, 128), jnp.int32),
            pltpu.VMEM((384, cols + 256), F32),
            pltpu.VMEM((WIDE, 384), BF16),
            pltpu.VMEM((2, rows, WIDE), BF16),
            pltpu.SemaphoreType.DMA,
        ],
        compiler_params=PARAMS,
        name="final",
    )(acc, images, g_row, g_col, *shards)


def solution(mesh):
    placed = (
        P(("frames", "row"), "col"),
        P(),
        P(),
        P(),
        P("col", None, None),
        P(("frames", "row"), "col", None),
        P(("frames", "row"), "col", None),
        P(("frames", "row"), "col"),
    )
    return jax.shard_map(
        on_device,
        mesh=mesh,
        in_specs=placed,
        out_specs=P(("frames", "row"), "col"),
        check_vma=False,
    )
```

```python
import functools
import math

import jax
import jax.numpy as jnp
from jax import lax
from jax.experimental import pallas as pl
from jax.experimental.pallas import tpu as pltpu
from jax.sharding import PartitionSpec as P

BLUR_HALF = 8
BLUR_SIGMA = 4.0
HALF = 16
RIM = HALF + BLUR_HALF
STRIP = 32
CB = 176
NB = 3
MAIN = 224
EDGE_IN = 80
EDGE_OUT = 48
RIGHT_AT = 56
HALF_STRIP = STRIP + 16
GROUP = 2
WIDE = 640
SLOTS = 16
F32 = jnp.float32
BF16 = jnp.bfloat16
VMEM = pl.BlockSpec(memory_space=pltpu.VMEM)
SMEM = pl.BlockSpec(memory_space=pltpu.SMEM)
HBM = pl.BlockSpec(memory_space=pltpu.HBM)
PARAMS = pltpu.CompilerParams(vmem_limit_bytes=16 * 1024 * 1024)


def dot_nt(a, b):
    return lax.dot_general(a, b, (((1,), (1,)), ((), ())), preferred_element_type=F32)


def dot_nn(a, b):
    return lax.dot_general(a, b, (((1,), (0,)), ((), ())), preferred_element_type=F32)


def join(strip):
    halves = [strip[0:HALF_STRIP, :], strip[HALF_STRIP : 2 * HALF_STRIP, :]]
    return jnp.concatenate(halves, axis=1).astype(F32)


def eye(rows, cols, shift):
    at = lax.broadcasted_iota(jnp.int32, (rows, cols), 1) - lax.broadcasted_iota(jnp.int32, (rows, cols), 0)
    return jnp.where(at == shift, 1.0, 0.0).astype(BF16)


def sides(axis, first_swap, second_swap):
    index, count = lax.axis_index(axis), lax.axis_size(axis)
    even = lax.rem(index, 2) == 0
    lower = jnp.where(even, second_swap, first_swap)
    upper = jnp.where(even, first_swap, second_swap)
    return jnp.where(index > 0, lower, 0.0), jnp.where(index < count - 1, upper, 0.0)


def prep_kernel(
    mask, ids, slots, count, across, down, library, to_first, to_second, edges, taps, ends, a_ids, a_slots, sems
):
    rows, cols = mask.shape
    copies = [
        pltpu.make_async_copy(mask.at[:, 0:128], ends.at[0], sems.at[0]),
        pltpu.make_async_copy(mask.at[:, cols - 128 : cols], ends.at[1], sems.at[1]),
        pltpu.make_async_copy(ids, a_ids, sems.at[2]),
        pltpu.make_async_copy(slots, a_slots, sems.at[3]),
        pltpu.make_async_copy(mask.at[0:STRIP], edges.at[0], sems.at[4]),
        pltpu.make_async_copy(mask.at[rows - STRIP : rows], edges.at[1], sems.at[5]),
        pltpu.make_async_copy(across, taps.at[0], sems.at[6]),
        pltpu.make_async_copy(down, taps.at[1], sems.at[7]),
        pltpu.make_async_copy(library, to_first.at[2 * HALF_STRIP :], sems.at[8]),
    ]
    for copy in copies:
        copy.start()
    for copy in copies[2:4]:
        copy.wait()
    line = lax.broadcasted_iota(jnp.int32, (16, 128), 0)
    lane = lax.broadcasted_iota(jnp.int32, (16, 128), 1)

    def spread(x):
        x = x.astype(F32)
        x = jnp.concatenate([x, jnp.zeros((1, 128 - x.shape[1]), F32)], axis=1)
        return jnp.broadcast_to(x, (16, 128))

    table = jnp.where(line == 1, spread(a_slots[0]), count[0, 0].astype(F32))
    table = jnp.where(line == 0, spread(a_ids[0]), table)
    width = jnp.where(line == 2, 1, ids.shape[2])
    table = jnp.where((lane < width) & (line < 3), table, 0.0).astype(BF16)
    for strip in (to_first, to_second):
        strip[STRIP:HALF_STRIP, :] = table
        strip[HALF_STRIP + STRIP : 2 * HALF_STRIP, :] = jnp.zeros((16, 128), BF16)
    even = lax.rem(lax.axis_index("col"), 2) == 0
    copies[0].wait()
    first = dot_nt(eye(STRIP, 128, 0), ends[0].astype(F32).astype(BF16))
    copies[1].wait()
    last = dot_nt(eye(STRIP, 128, 128 - STRIP), ends[1].astype(F32).astype(BF16))
    for strip, part in ((to_first, jnp.where(even, last, first)), (to_second, jnp.where(even, first, last))):
        strip[0:STRIP, :] = part[:, 0:128].astype(BF16)
        strip[HALF_STRIP : HALF_STRIP + STRIP, :] = part[:, 128:256].astype(BF16)
    for copy in copies[4:]:
        copy.wait()


def mid_kernel(edges, from_first, from_second, own, to_first, to_second):
    cols = edges.shape[2]
    rows = 256
    left, right = sides("col", join(from_first), join(from_second))
    tables = jnp.concatenate(
        [left[STRIP:, 0:128], own[STRIP:HALF_STRIP, :].astype(F32), right[STRIP:, 0:128], jnp.zeros((16, 256), F32)],
        axis=1,
    ).astype(BF16)
    fill = jnp.zeros((128 - STRIP, 128), F32)
    strips = []
    for i in range(2):
        at = 0 if i == 0 else rows - 128
        pick = eye(STRIP, 128, 0 if i == 0 else 128 - STRIP)

        def turned(strip):
            return dot_nt(pick, jnp.concatenate([strip[0:STRIP, at : at + 128], fill], axis=0).astype(BF16))

        parts = [turned(left)[:, STRIP - RIM : STRIP], edges[i].astype(F32), turned(right)[:, 0 : WIDE - RIM - cols]]
        strips.append(jnp.concatenate(parts, axis=1))
    even = lax.rem(lax.axis_index("row"), 2) == 0
    to_first[0:STRIP, :] = jnp.where(even, strips[1], strips[0]).astype(BF16)
    to_second[0:STRIP, :] = jnp.where(even, strips[0], strips[1]).astype(BF16)
    to_first[STRIP:, :] = tables
    to_second[STRIP:, :] = tables


def blur_matrix(shape, axis):
    lag = lax.broadcasted_iota(jnp.int32, shape, axis) - lax.broadcasted_iota(jnp.int32, shape, 1 - axis)
    total = sum(math.exp(-(t * t) / (2 * BLUR_SIGMA**2)) for t in range(-BLUR_HALF, BLUR_HALF + 1))
    off = (lag - BLUR_HALF).astype(F32)
    g = jnp.exp(-off * off / (2.0 * BLUR_SIGMA * BLUR_SIGMA)) * (1.0 / total)
    g = jnp.where((lag >= 0) & (lag <= 2 * BLUR_HALF), g, 0.0)
    high = g.astype(BF16)
    return high, (g - high.astype(F32)).astype(BF16)


def own_kernel(mask, taps, windows, ahead, back, g_row, g_col):
    rows, cols = mask.shape
    full = jnp.concatenate(
        [jnp.zeros((rows, RIM), F32), mask[...].astype(F32), jnp.zeros((rows, WIDE - RIM - cols), F32)], axis=1
    )
    for b in range(NB):
        windows[b] = full[:, CB * b : CB * b + 256]
    kernels, _, count = taps.shape[1:]
    flip = lax.broadcasted_iota(jnp.int32, (128, 128), 0) + lax.broadcasted_iota(jnp.int32, (128, 128), 1)
    flip = jnp.where(flip % 128 == 0, 1.0, 0.0).astype(BF16)
    ahead[...] = jnp.zeros(ahead.shape, F32)
    back[...] = jnp.zeros(back.shape, F32)
    for k in range(kernels):
        ahead[k, 0:2, 0:count] = taps[0, k].astype(F32)
        back[k, 0:2, 0:count] = taps[1, k].astype(F32)
    back[...] = dot_nn(back[...].reshape(kernels * 8, 128).astype(BF16), flip).reshape(kernels, 8, 128)
    g_row[0:128], g_row[128:256] = blur_matrix((128, 256), 1)
    g_col[:, 0:128], g_col[:, 128:256] = blur_matrix((256, 128), 0)


def socs_kernel(
    entries,
    per,
    weights,
    windows,
    row_first,
    row_second,
    col_first,
    col_second,
    own,
    ahead,
    back,
    acc,
    images,
    x_win,
    scale,
    sem,
    *scratch,
):
    across = scratch[0:2]
    down = scratch[2:4]
    first = scratch[4:6]
    groups = ahead.shape[0] // GROUP
    fetch = pltpu.make_async_copy(weights, scale, sem)
    fetch.start()
    above, below = sides("row", row_first[...].astype(F32), row_second[...].astype(F32))
    left, right = sides("col", join(col_first), join(col_second))
    rows = windows.shape[1]
    turned = jnp.concatenate(
        [
            left[STRIP - RIM : STRIP],
            jnp.zeros((128 - RIM + RIGHT_AT, rows), F32),
            right[0:RIM],
            jnp.zeros((128 - RIM - RIGHT_AT, rows), F32),
        ],
        axis=0,
    )
    turned = dot_nt(eye(rows, rows, 0), turned.astype(BF16))
    left, right = left[STRIP:, 0:128], right[STRIP:, 0:128]
    upper_rows = above[STRIP - RIM : STRIP]
    lower_rows = below[0:RIM]
    edge_rows = []
    for b in range(NB):
        lanes = slice(CB * b, CB * b + 256)
        part = windows[b]
        if b == 0:
            part = jnp.concatenate([part[:, 0:128] + turned[:, 0:128], part[:, 128:256]], axis=1)
        if b == NB - 1:
            part = jnp.concatenate([part[:, 0:128], part[:, 128:256] + turned[:, 128:256]], axis=1)
        x_win[b] = jnp.concatenate([upper_rows[:, lanes], part[0 : 256 - RIM]], axis=0).astype(BF16)
        edge_rows += [part[MAIN - RIM :], lower_rows[:, lanes]]
    edge_rows.append(jnp.zeros((256 - NB * EDGE_IN, 256), F32))
    x_win[NB] = jnp.concatenate(edge_rows, axis=0).astype(BF16)
    acc[...] = jnp.zeros(acc.shape, F32)
    for ref in across + down:
        ref[...] = jnp.zeros(ref.shape, BF16)

    slot = lax.broadcasted_iota(jnp.int32, (SLOTS, 128), 0).astype(F32)
    lane = lax.broadcasted_iota(jnp.int32, (SLOTS, 128), 1)
    found = jnp.zeros((SLOTS, 128), F32)
    col = lax.axis_index("col")
    tables = [above[STRIP:, 128 * t : 128 * t + 128] for t in range(3)]
    tables += [left, own[STRIP:HALF_STRIP, :].astype(F32), right]
    tables += [below[STRIP:, 128 * t : 128 * t + 128] for t in range(3)]
    for t, table in enumerate(tables):
        live = lane.astype(F32) < table[2:3, 0:1]
        hit = live & (table[1:2] == slot) & (lane < entries)
        image = jnp.sum(jnp.where(hit, table[0:1] + 1.0, 0.0), axis=1, keepdims=True)
        found = jnp.where(lane == t, image, found)
    cell = found.astype(jnp.int32) - 1
    images[...] = jnp.where(cell >= 0, ((cell // per) ^ col) * per + cell % per + 1, 0)

    row = lax.broadcasted_iota(jnp.int32, (32, 128), 0)
    lane = lax.broadcasted_iota(jnp.int32, (32, 128), 1)
    low = lane >= row + 96

    def cycled(x):
        return pltpu.roll(jnp.broadcast_to(x, (128, 128)), 0, 1, stride=1, stride_axis=0)

    def build_across(m, s):
        for q in range(2 * GROUP):
            cyc = cycled(ahead[GROUP * m + q // 2, q % 2 : q % 2 + 1, :])
            head = cyc[0:96].astype(BF16)
            tail = cyc[96:128]
            over = jnp.where(low, 0.0, tail)
            across[s][q, 0:96, 0:128] = head
            across[s][q, 128:CB, 128:256] = head[0 : CB - 128]
            across[s][q, 96:128, 0:128] = jnp.where(low, tail, 0.0).astype(BF16)
            across[s][q, 96:128, 128:256] = over.astype(BF16)

    def build_down(m, s):
        for q in range(2 * GROUP):
            cyc = cycled(back[GROUP * m + q // 2, q % 2 : q % 2 + 1, :])
            head = cyc[0:32]
            over = jnp.where(low, head, 0.0).astype(BF16)
            head = jnp.where(low, 0.0, head)
            same = jnp.concatenate([head, cyc[32:128]], axis=0).astype(BF16)
            down[s][q, 0:128, 0:128] = same
            down[s][q, 128:256, 128:256] = same
            down[s][q, 128:160, 0:128] = over

    def pass_one(s):
        taps = across[s][...].reshape(2 * GROUP * CB, 256)
        for j in range(NB + 1):
            part = dot_nt(taps, x_win[j]).astype(BF16)
            for q in range(2 * GROUP):
                first[s][q, j] = part[q * CB : (q + 1) * CB]

    def pass_two(m, s):
        for q in range(2 * GROUP):
            second = dot_nn(first[s][q].reshape((NB + 1) * CB, 256), down[s][q])
            acc[...] += (scale[GROUP * m + q // 2] * (second * second)).reshape(acc.shape)

    def stage(m, s):
        pass_one(s)
        build_down(m, s)
        if m + 1 < groups:
            build_across(m + 1, 1 - s)
        pass_two(m - 1, 1 - s)

    build_across(0, 0)
    pass_one(0)
    build_down(0, 0)
    build_across(1, 1)
    fetch.wait()

    for m in range(1, groups):
        stage(m, m % 2)
    pass_two(groups - 1, (groups - 1) % 2)


def final_kernel(n_row, n_col, acc, images, g_row, g_col, *rest):
    shards = rest[:-7]
    out, cells, table, placed, flat, blurred, sem = rest[-7:]
    g_high = g_col[:, 0:128]
    per = cells.shape[0] // len(shards)
    rows, cols = out.shape
    row, col = lax.axis_index("row"), lax.axis_index("col")
    fetch = pltpu.make_async_copy(images, table, sem)
    fetch.start()
    for i, shard in enumerate(shards):
        rows_of = shard.shape[0] - per * 64
        cells[pl.ds(i * per, per)] = shard[rows_of:, :].reshape(per, 64, 128)

    at_row = lax.broadcasted_iota(jnp.int32, (8, 384), 1) - BLUR_HALF
    row_ok = ((row > 0) | (at_row >= 0)) & ((row < n_row - 1) | (at_row < rows))
    row_ok = jnp.where(row_ok, 1.0, 0.0)
    for b in range(NB):
        edge = acc[NB, :, EDGE_IN * b : EDGE_IN * b + EDGE_OUT]
        part = jnp.concatenate(
            [acc[b, :, 0:MAIN], edge, jnp.zeros((CB, 384 - MAIN - EDGE_OUT), F32)], axis=1
        )
        part = part * row_ok[0:1]
        if b == 0:
            part = jnp.concatenate([jnp.where(col > 0, part[0:8], 0.0), part[8:]], axis=0)
        if b == NB - 1:
            part = jnp.concatenate([part[0 : CB - 8], jnp.where(col < n_col - 1, part[CB - 8 :], 0.0)], axis=0)
        flat[b * CB : (b + 1) * CB, :] = part.astype(BF16)
    flat[NB * CB :, :] = jnp.zeros((flat.shape[0] - NB * CB, 384), BF16)

    halves = []
    for i in range(rows // 128):
        part = dot_nt(g_row[...], flat[:, 128 * i : 128 * i + 256])
        halves.append(part[0:128] + part[128:])

    fetch.wait()
    slot_rows, slot_cols = rows // 64, cols // 128
    for i in range(-1, slot_rows + 1):
        for j in range(-1, slot_cols + 1):
            ti = 0 if i < 0 else (2 if i == slot_rows else 1)
            tj = 0 if j < 0 else (2 if j == slot_cols else 1)
            found = table[(i % slot_rows) * slot_cols + j % slot_cols, 3 * ti + tj]
            image = jnp.maximum(found - 1, 0)
            lanes = slice(128 + 128 * j, 256 + 128 * j)
            show = lambda x: jnp.where(found > 0, x.astype(F32), 0.0)
            if i < 0:
                placed[0:8, lanes] = show(cells[image, 48:64, :])[8:16]
            elif i == slot_rows:
                placed[8 + rows : 16 + rows, lanes] = show(cells[image, 0:16, :])[0:8]
            else:
                placed[8 + 64 * i : 72 + 64 * i, lanes] = show(cells[image])
    placed[16 + rows :, :] = jnp.zeros((placed.shape[0] - 16 - rows, placed.shape[1]), F32)

    for i, part in enumerate(halves):
        cell = dot_nn(g_row[...], placed[128 * i : 128 * i + 256, :].astype(BF16))
        cell = cell[0:128] + cell[128:]
        part += cell[:, 128 - BLUR_HALF : 128 - BLUR_HALF + part.shape[1]]
        high = part.astype(BF16)
        blurred[0, 128 * i : 128 * i + 128, :] = high
        blurred[1, 128 * i : 128 * i + 128, :] = (part - high.astype(F32)).astype(BF16)
    for j in range(cols // 128):
        lanes = slice(128 * j, 128 * j + 256)
        part = dot_nn(blurred[0, :, lanes], g_col[...])
        out[:, 128 * j : 128 * j + 128] = (
            part[:, 0:128] + part[:, 128:] + dot_nn(blurred[1, :, lanes], g_high)
        )


def shape(dims, dtype):
    return jax.ShapeDtypeStruct(dims, dtype)


def on_device(
    mask_pixels, across_taps, down_taps, kernel_weights, library, cell_ids, cell_slots, cell_count
):
    rows, cols = mask_pixels.shape
    kernels = across_taps.shape[0]
    entries = cell_ids.shape[-1]
    per = library.shape[0]
    n_row, n_col = lax.axis_size("row"), lax.axis_size("col")
    library = library.reshape(per * 64, 128)
    in_hbm = lambda x: pltpu.with_memory_space_constraint(x, pltpu.HBM)
    mask_hbm = in_hbm(mask_pixels)

    to_first, to_second, edges, taps = pl.pallas_call(
        prep_kernel,
        out_shape=(
            shape((2 * HALF_STRIP + per * 64, 128), BF16),
            shape((2 * HALF_STRIP, 128), BF16),
            shape((2, STRIP, cols), jnp.int32),
            shape((2,) + across_taps.shape, BF16),
        ),
        in_specs=[HBM] * 3 + [SMEM] + [HBM] * 3,
        out_specs=(VMEM,) * 4,
        scratch_shapes=[
            pltpu.VMEM((2, rows, 128), jnp.int32),
            pltpu.VMEM(cell_ids.shape, jnp.int32),
            pltpu.VMEM(cell_slots.shape, jnp.int32),
            pltpu.SemaphoreType.DMA((9,)),
        ],
        compiler_params=PARAMS,
        name="prep",
    )(mask_hbm, in_hbm(cell_ids), in_hbm(cell_slots), cell_count, in_hbm(across_taps), in_hbm(down_taps), in_hbm(library))

    def swaps(n):
        rounds = []
        for start in (0, 1):
            pairs = [(i, (i + 1) % n) for i in range(start, n, 2)]
            rounds.append(pairs + [(b, a) for a, b in pairs])
        return rounds

    pairs = swaps(n_col)
    col_second = lax.ppermute(to_second, "col", pairs[1])
    col_first = lax.ppermute(to_first, "col", pairs[0])
    shards = [library, col_first]
    to_above, to_below = pl.pallas_call(
        mid_kernel,
        out_shape=(shape((STRIP + 16, WIDE), BF16),) * 2,
        in_specs=[VMEM] * 4,
        out_specs=(VMEM,) * 2,
        compiler_params=PARAMS,
        name="mid",
    )(edges, col_first, col_second, to_first)
    for d in range(2, n_col):
        if d == 2:
            block, col_second = lax.optimization_barrier((library, col_second))
        if d == 3:
            block, to_above, to_below = lax.optimization_barrier((library, to_above, to_below))
        shards.append(lax.ppermute(block, "col", [(i, i ^ d) for i in range(n_col)]))
    row_first, row_second = (
        lax.ppermute(x, "row", pairs) for x, pairs in zip((to_above, to_below), swaps(n_row))
    )

    windows, ahead, back, g_row, g_col = pl.pallas_call(
        own_kernel,
        out_shape=(
            shape((NB, rows, 256), F32),
            shape((kernels, 8, 128), F32),
            shape((kernels, 8, 128), F32),
            shape((256, 256), BF16),
            shape((256, 256), BF16),
        ),
        in_specs=[VMEM] * 2,
        out_specs=(VMEM,) * 5,
        compiler_params=PARAMS,
        cost_estimate=pl.CostEstimate(flops=10**6, bytes_accessed=10**6, transcendentals=0),
        name="own",
    )(mask_pixels, taps)

    acc, images = pl.pallas_call(
        functools.partial(socs_kernel, entries, per),
        out_shape=(shape((NB + 1, CB, 256), F32), shape((SLOTS, 128), jnp.int32)),
        in_specs=[HBM] + [VMEM] * 8,
        out_specs=(VMEM,) * 2,
        scratch_shapes=[
            pltpu.VMEM((NB + 1, 256, 256), BF16),
            pltpu.SMEM(kernel_weights.shape, F32),
            pltpu.SemaphoreType.DMA,
        ]
        + [pltpu.VMEM((2 * GROUP, CB, 256), BF16)] * 2
        + [pltpu.VMEM((2 * GROUP, 256, 256), BF16)] * 2
        + [pltpu.VMEM((2 * GROUP, NB + 1, CB, 256), BF16)] * 2,
        compiler_params=PARAMS,
        cost_estimate=pl.CostEstimate(flops=10**6, bytes_accessed=10**5, transcendentals=0),
        name="socs",
    )(in_hbm(kernel_weights), windows, row_first, row_second, col_first, col_second, to_first, ahead, back)

    return pl.pallas_call(
        functools.partial(final_kernel, n_row, n_col),
        out_shape=shape((rows, cols), F32),
        in_specs=[VMEM] * (4 + n_col),
        out_specs=VMEM,
        scratch_shapes=[
            pltpu.VMEM((n_col * per, 64, 128), BF16),
            pltpu.SMEM((SLOTS, 128), jnp.int32),
            pltpu.VMEM((384, cols + 256), F32),
            pltpu.VMEM((WIDE, 384), BF16),
            pltpu.VMEM((2, rows, WIDE), BF16),
            pltpu.SemaphoreType.DMA,
        ],
        compiler_params=PARAMS,
        name="final",
    )(acc, images, g_row, g_col, *shards)


def solution(mesh):
    placed = (
        P(("frames", "row"), "col"),
        P(),
        P(),
        P(),
        P("col", None, None),
        P(("frames", "row"), "col", None),
        P(("frames", "row"), "col", None),
        P(("frames", "row"), "col"),
    )
    return jax.shard_map(
        on_device,
        mesh=mesh,
        in_specs=placed,
        out_specs=P(("frames", "row"), "col"),
        check_vma=False,
    )
```

```python
import functools
import math

import jax
import jax.numpy as jnp
from jax import lax
from jax.experimental import pallas as pl
from jax.experimental.pallas import tpu as pltpu
from jax.sharding import PartitionSpec as P

BLUR_HALF = 8
BLUR_SIGMA = 4.0
HALF = 16
RIM = HALF + BLUR_HALF
STRIP = 32
CB = 176
NB = 3
MAIN = 224
EDGE_IN = 80
EDGE_OUT = 48
RIGHT_AT = 56
HALF_STRIP = STRIP + 16
GROUP = 4
WIDE = 640
SLOTS = 16
F32 = jnp.float32
BF16 = jnp.bfloat16
VMEM = pl.BlockSpec(memory_space=pltpu.VMEM)
SMEM = pl.BlockSpec(memory_space=pltpu.SMEM)
HBM = pl.BlockSpec(memory_space=pltpu.HBM)
PARAMS = pltpu.CompilerParams(vmem_limit_bytes=16 * 1024 * 1024)


def dot_nt(a, b):
    return lax.dot_general(a, b, (((1,), (1,)), ((), ())), preferred_element_type=F32)


def dot_nn(a, b):
    return lax.dot_general(a, b, (((1,), (0,)), ((), ())), preferred_element_type=F32)


def join(strip):
    halves = [strip[0:HALF_STRIP, :], strip[HALF_STRIP : 2 * HALF_STRIP, :]]
    return jnp.concatenate(halves, axis=1).astype(F32)


def eye(rows, cols, shift):
    at = lax.broadcasted_iota(jnp.int32, (rows, cols), 1) - lax.broadcasted_iota(jnp.int32, (rows, cols), 0)
    return jnp.where(at == shift, 1.0, 0.0).astype(BF16)


def sides(axis, first_swap, second_swap):
    index, count = lax.axis_index(axis), lax.axis_size(axis)
    even = lax.rem(index, 2) == 0
    lower = jnp.where(even, second_swap, first_swap)
    upper = jnp.where(even, first_swap, second_swap)
    return jnp.where(index > 0, lower, 0.0), jnp.where(index < count - 1, upper, 0.0)


def prep_kernel(
    mask, ids, slots, count, across, down, library, to_first, to_second, edges, taps, ends, a_ids, a_slots, sems
):
    rows, cols = mask.shape
    copies = [
        pltpu.make_async_copy(mask.at[:, 0:128], ends.at[0], sems.at[0]),
        pltpu.make_async_copy(mask.at[:, cols - 128 : cols], ends.at[1], sems.at[1]),
        pltpu.make_async_copy(ids, a_ids, sems.at[2]),
        pltpu.make_async_copy(slots, a_slots, sems.at[3]),
        pltpu.make_async_copy(mask.at[0:STRIP], edges.at[0], sems.at[4]),
        pltpu.make_async_copy(mask.at[rows - STRIP : rows], edges.at[1], sems.at[5]),
        pltpu.make_async_copy(across, taps.at[0], sems.at[6]),
        pltpu.make_async_copy(down, taps.at[1], sems.at[7]),
        pltpu.make_async_copy(library, to_first.at[2 * HALF_STRIP :], sems.at[8]),
    ]
    for copy in copies:
        copy.start()
    for copy in copies[2:4]:
        copy.wait()
    line = lax.broadcasted_iota(jnp.int32, (16, 128), 0)
    lane = lax.broadcasted_iota(jnp.int32, (16, 128), 1)

    def spread(x):
        x = x.astype(F32)
        x = jnp.concatenate([x, jnp.zeros((1, 128 - x.shape[1]), F32)], axis=1)
        return jnp.broadcast_to(x, (16, 128))

    table = jnp.where(line == 1, spread(a_slots[0]), count[0, 0].astype(F32))
    table = jnp.where(line == 0, spread(a_ids[0]), table)
    width = jnp.where(line == 2, 1, ids.shape[2])
    table = jnp.where((lane < width) & (line < 3), table, 0.0).astype(BF16)
    for strip in (to_first, to_second):
        strip[STRIP:HALF_STRIP, :] = table
        strip[HALF_STRIP + STRIP : 2 * HALF_STRIP, :] = jnp.zeros((16, 128), BF16)
    even = lax.rem(lax.axis_index("col"), 2) == 0
    copies[0].wait()
    first = dot_nt(eye(STRIP, 128, 0), ends[0].astype(F32).astype(BF16))
    copies[1].wait()
    last = dot_nt(eye(STRIP, 128, 128 - STRIP), ends[1].astype(F32).astype(BF16))
    for strip, part in ((to_first, jnp.where(even, last, first)), (to_second, jnp.where(even, first, last))):
        strip[0:STRIP, :] = part[:, 0:128].astype(BF16)
        strip[HALF_STRIP : HALF_STRIP + STRIP, :] = part[:, 128:256].astype(BF16)
    for copy in copies[4:]:
        copy.wait()


def mid_kernel(edges, from_first, from_second, own, to_first, to_second):
    cols = edges.shape[2]
    rows = 256
    left, right = sides("col", join(from_first), join(from_second))
    tables = jnp.concatenate(
        [left[STRIP:, 0:128], own[STRIP:HALF_STRIP, :].astype(F32), right[STRIP:, 0:128], jnp.zeros((16, 256), F32)],
        axis=1,
    ).astype(BF16)
    fill = jnp.zeros((128 - STRIP, 128), F32)
    strips = []
    for i in range(2):
        at = 0 if i == 0 else rows - 128
        pick = eye(STRIP, 128, 0 if i == 0 else 128 - STRIP)

        def turned(strip):
            return dot_nt(pick, jnp.concatenate([strip[0:STRIP, at : at + 128], fill], axis=0).astype(BF16))

        parts = [turned(left)[:, STRIP - RIM : STRIP], edges[i].astype(F32), turned(right)[:, 0 : WIDE - RIM - cols]]
        strips.append(jnp.concatenate(parts, axis=1))
    even = lax.rem(lax.axis_index("row"), 2) == 0
    to_first[0:STRIP, :] = jnp.where(even, strips[1], strips[0]).astype(BF16)
    to_second[0:STRIP, :] = jnp.where(even, strips[0], strips[1]).astype(BF16)
    to_first[STRIP:, :] = tables
    to_second[STRIP:, :] = tables


def blur_matrix(shape, axis):
    lag = lax.broadcasted_iota(jnp.int32, shape, axis) - lax.broadcasted_iota(jnp.int32, shape, 1 - axis)
    total = sum(math.exp(-(t * t) / (2 * BLUR_SIGMA**2)) for t in range(-BLUR_HALF, BLUR_HALF + 1))
    off = (lag - BLUR_HALF).astype(F32)
    g = jnp.exp(-off * off / (2.0 * BLUR_SIGMA * BLUR_SIGMA)) * (1.0 / total)
    g = jnp.where((lag >= 0) & (lag <= 2 * BLUR_HALF), g, 0.0)
    high = g.astype(BF16)
    return high, (g - high.astype(F32)).astype(BF16)


def own_kernel(mask, taps, windows, ahead, back, g_row, g_col):
    rows, cols = mask.shape
    full = jnp.concatenate(
        [jnp.zeros((rows, RIM), F32), mask[...].astype(F32), jnp.zeros((rows, WIDE - RIM - cols), F32)], axis=1
    )
    for b in range(NB):
        windows[b] = full[:, CB * b : CB * b + 256]
    kernels, _, count = taps.shape[1:]
    flip = lax.broadcasted_iota(jnp.int32, (128, 128), 0) + lax.broadcasted_iota(jnp.int32, (128, 128), 1)
    flip = jnp.where(flip % 128 == 0, 1.0, 0.0).astype(BF16)
    ahead[...] = jnp.zeros(ahead.shape, F32)
    back[...] = jnp.zeros(back.shape, F32)
    for k in range(kernels):
        ahead[k, 0:2, 0:count] = taps[0, k].astype(F32)
        back[k, 0:2, 0:count] = taps[1, k].astype(F32)
    back[...] = dot_nn(back[...].reshape(kernels * 8, 128).astype(BF16), flip).reshape(kernels, 8, 128)
    g_row[0:128], g_row[128:256] = blur_matrix((128, 256), 1)
    g_col[:, 0:128], g_col[:, 128:256] = blur_matrix((256, 128), 0)


def socs_kernel(
    entries,
    per,
    weights,
    windows,
    row_first,
    row_second,
    col_first,
    col_second,
    own,
    ahead,
    back,
    acc,
    images,
    x_win,
    scale,
    sem,
    *scratch,
):
    across = scratch[0:2]
    down = scratch[2:4]
    first = scratch[4:6]
    groups = ahead.shape[0] // GROUP
    fetch = pltpu.make_async_copy(weights, scale, sem)
    fetch.start()
    above, below = sides("row", row_first[...].astype(F32), row_second[...].astype(F32))
    left, right = sides("col", join(col_first), join(col_second))
    rows = windows.shape[1]
    turned = jnp.concatenate(
        [
            left[STRIP - RIM : STRIP],
            jnp.zeros((128 - RIM + RIGHT_AT, rows), F32),
            right[0:RIM],
            jnp.zeros((128 - RIM - RIGHT_AT, rows), F32),
        ],
        axis=0,
    )
    turned = dot_nt(eye(rows, rows, 0), turned.astype(BF16))
    left, right = left[STRIP:, 0:128], right[STRIP:, 0:128]
    upper_rows = above[STRIP - RIM : STRIP]
    lower_rows = below[0:RIM]
    edge_rows = []
    for b in range(NB):
        lanes = slice(CB * b, CB * b + 256)
        part = windows[b]
        if b == 0:
            part = jnp.concatenate([part[:, 0:128] + turned[:, 0:128], part[:, 128:256]], axis=1)
        if b == NB - 1:
            part = jnp.concatenate([part[:, 0:128], part[:, 128:256] + turned[:, 128:256]], axis=1)
        x_win[b] = jnp.concatenate([upper_rows[:, lanes], part[0 : 256 - RIM]], axis=0).astype(BF16)
        edge_rows += [part[MAIN - RIM :], lower_rows[:, lanes]]
    edge_rows.append(jnp.zeros((256 - NB * EDGE_IN, 256), F32))
    x_win[NB] = jnp.concatenate(edge_rows, axis=0).astype(BF16)
    acc[...] = jnp.zeros(acc.shape, F32)
    for ref in across + down:
        ref[...] = jnp.zeros(ref.shape, BF16)

    slot = lax.broadcasted_iota(jnp.int32, (SLOTS, 128), 0).astype(F32)
    lane = lax.broadcasted_iota(jnp.int32, (SLOTS, 128), 1)
    found = jnp.zeros((SLOTS, 128), F32)
    col = lax.axis_index("col")
    tables = [above[STRIP:, 128 * t : 128 * t + 128] for t in range(3)]
    tables += [left, own[STRIP:HALF_STRIP, :].astype(F32), right]
    tables += [below[STRIP:, 128 * t : 128 * t + 128] for t in range(3)]
    for t, table in enumerate(tables):
        live = lane.astype(F32) < table[2:3, 0:1]
        hit = live & (table[1:2] == slot) & (lane < entries)
        image = jnp.sum(jnp.where(hit, table[0:1] + 1.0, 0.0), axis=1, keepdims=True)
        found = jnp.where(lane == t, image, found)
    cell = found.astype(jnp.int32) - 1
    images[...] = jnp.where(cell >= 0, ((cell // per) ^ col) * per + cell % per + 1, 0)

    row = lax.broadcasted_iota(jnp.int32, (32, 128), 0)
    lane = lax.broadcasted_iota(jnp.int32, (32, 128), 1)
    low = lane >= row + 96

    def cycled(x):
        return pltpu.roll(jnp.broadcast_to(x, (128, 128)), 0, 1, stride=1, stride_axis=0)

    def build_across(m, s):
        for q in range(2 * GROUP):
            cyc = cycled(ahead[GROUP * m + q // 2, q % 2 : q % 2 + 1, :])
            head = cyc[0:96].astype(BF16)
            tail = cyc[96:128]
            over = jnp.where(low, 0.0, tail)
            across[s][q, 0:96, 0:128] = head
            across[s][q, 128:CB, 128:256] = head[0 : CB - 128]
            across[s][q, 96:128, 0:128] = jnp.where(low, tail, 0.0).astype(BF16)
            across[s][q, 96:128, 128:256] = over.astype(BF16)

    def build_down(m, s):
        for q in range(2 * GROUP):
            cyc = cycled(back[GROUP * m + q // 2, q % 2 : q % 2 + 1, :])
            head = cyc[0:32]
            over = jnp.where(low, head, 0.0).astype(BF16)
            head = jnp.where(low, 0.0, head)
            same = jnp.concatenate([head, cyc[32:128]], axis=0).astype(BF16)
            down[s][q, 0:128, 0:128] = same
            down[s][q, 128:256, 128:256] = same
            down[s][q, 128:160, 0:128] = over

    def pass_one(s):
        taps = across[s][...].reshape(2 * GROUP * CB, 256)
        for j in range(NB + 1):
            part = dot_nt(taps, x_win[j]).astype(BF16)
            for q in range(2 * GROUP):
                first[s][q, j] = part[q * CB : (q + 1) * CB]

    def pass_two(m, s):
        for q in range(2 * GROUP):
            second = dot_nn(first[s][q].reshape((NB + 1) * CB, 256), down[s][q])
            acc[...] += (scale[GROUP * m + q // 2] * (second * second)).reshape(acc.shape)

    def stage(m, s):
        pass_one(s)
        build_down(m, s)
        if m + 1 < groups:
            build_across(m + 1, 1 - s)
        pass_two(m - 1, 1 - s)

    build_across(0, 0)
    pass_one(0)
    build_down(0, 0)
    build_across(1, 1)
    fetch.wait()

    for m in range(1, groups):
        stage(m, m % 2)
    pass_two(groups - 1, (groups - 1) % 2)


def final_kernel(n_row, n_col, acc, images, g_row, g_col, *rest):
    shards = rest[:-7]
    out, cells, table, placed, flat, blurred, sem = rest[-7:]
    g_high = g_col[:, 0:128]
    per = cells.shape[0] // len(shards)
    rows, cols = out.shape
    row, col = lax.axis_index("row"), lax.axis_index("col")
    fetch = pltpu.make_async_copy(images, table, sem)
    fetch.start()
    for i, shard in enumerate(shards):
        rows_of = shard.shape[0] - per * 64
        cells[pl.ds(i * per, per)] = shard[rows_of:, :].reshape(per, 64, 128)

    at_row = lax.broadcasted_iota(jnp.int32, (8, 384), 1) - BLUR_HALF
    row_ok = ((row > 0) | (at_row >= 0)) & ((row < n_row - 1) | (at_row < rows))
    row_ok = jnp.where(row_ok, 1.0, 0.0)
    for b in range(NB):
        edge = acc[NB, :, EDGE_IN * b : EDGE_IN * b + EDGE_OUT]
        part = jnp.concatenate(
            [acc[b, :, 0:MAIN], edge, jnp.zeros((CB, 384 - MAIN - EDGE_OUT), F32)], axis=1
        )
        part = part * row_ok[0:1]
        if b == 0:
            part = jnp.concatenate([jnp.where(col > 0, part[0:8], 0.0), part[8:]], axis=0)
        if b == NB - 1:
            part = jnp.concatenate([part[0 : CB - 8], jnp.where(col < n_col - 1, part[CB - 8 :], 0.0)], axis=0)
        flat[b * CB : (b + 1) * CB, :] = part.astype(BF16)
    flat[NB * CB :, :] = jnp.zeros((flat.shape[0] - NB * CB, 384), BF16)

    halves = []
    for i in range(rows // 128):
        part = dot_nt(g_row[...], flat[:, 128 * i : 128 * i + 256])
        halves.append(part[0:128] + part[128:])

    fetch.wait()
    slot_rows, slot_cols = rows // 64, cols // 128
    for i in range(-1, slot_rows + 1):
        for j in range(-1, slot_cols + 1):
            ti = 0 if i < 0 else (2 if i == slot_rows else 1)
            tj = 0 if j < 0 else (2 if j == slot_cols else 1)
            found = table[(i % slot_rows) * slot_cols + j % slot_cols, 3 * ti + tj]
            image = jnp.maximum(found - 1, 0)
            lanes = slice(128 + 128 * j, 256 + 128 * j)
            show = lambda x: jnp.where(found > 0, x.astype(F32), 0.0)
            if i < 0:
                placed[0:8, lanes] = show(cells[image, 48:64, :])[8:16]
            elif i == slot_rows:
                placed[8 + rows : 16 + rows, lanes] = show(cells[image, 0:16, :])[0:8]
            else:
                placed[8 + 64 * i : 72 + 64 * i, lanes] = show(cells[image])
    placed[16 + rows :, :] = jnp.zeros((placed.shape[0] - 16 - rows, placed.shape[1]), F32)

    for i, part in enumerate(halves):
        cell = dot_nn(g_row[...], placed[128 * i : 128 * i + 256, :].astype(BF16))
        cell = cell[0:128] + cell[128:]
        part += cell[:, 128 - BLUR_HALF : 128 - BLUR_HALF + part.shape[1]]
        high = part.astype(BF16)
        blurred[0, 128 * i : 128 * i + 128, :] = high
        blurred[1, 128 * i : 128 * i + 128, :] = (part - high.astype(F32)).astype(BF16)
    for j in range(cols // 128):
        lanes = slice(128 * j, 128 * j + 256)
        part = dot_nn(blurred[0, :, lanes], g_col[...])
        out[:, 128 * j : 128 * j + 128] = (
            part[:, 0:128] + part[:, 128:] + dot_nn(blurred[1, :, lanes], g_high)
        )


def shape(dims, dtype):
    return jax.ShapeDtypeStruct(dims, dtype)


def on_device(
    mask_pixels, across_taps, down_taps, kernel_weights, library, cell_ids, cell_slots, cell_count
):
    rows, cols = mask_pixels.shape
    kernels = across_taps.shape[0]
    entries = cell_ids.shape[-1]
    per = library.shape[0]
    n_row, n_col = lax.axis_size("row"), lax.axis_size("col")
    library = library.reshape(per * 64, 128)
    in_hbm = lambda x: pltpu.with_memory_space_constraint(x, pltpu.HBM)
    mask_hbm = in_hbm(mask_pixels)

    to_first, to_second, edges, taps = pl.pallas_call(
        prep_kernel,
        out_shape=(
            shape((2 * HALF_STRIP + per * 64, 128), BF16),
            shape((2 * HALF_STRIP, 128), BF16),
            shape((2, STRIP, cols), jnp.int32),
            shape((2,) + across_taps.shape, BF16),
        ),
        in_specs=[HBM] * 3 + [SMEM] + [HBM] * 3,
        out_specs=(VMEM,) * 4,
        scratch_shapes=[
            pltpu.VMEM((2, rows, 128), jnp.int32),
            pltpu.VMEM(cell_ids.shape, jnp.int32),
            pltpu.VMEM(cell_slots.shape, jnp.int32),
            pltpu.SemaphoreType.DMA((9,)),
        ],
        compiler_params=PARAMS,
        name="prep",
    )(mask_hbm, in_hbm(cell_ids), in_hbm(cell_slots), cell_count, in_hbm(across_taps), in_hbm(down_taps), in_hbm(library))

    def swaps(n):
        rounds = []
        for start in (0, 1):
            pairs = [(i, (i + 1) % n) for i in range(start, n, 2)]
            rounds.append(pairs + [(b, a) for a, b in pairs])
        return rounds

    pairs = swaps(n_col)
    col_second = lax.ppermute(to_second, "col", pairs[1])
    col_first = lax.ppermute(to_first, "col", pairs[0])
    shards = [library, col_first]
    to_above, to_below = pl.pallas_call(
        mid_kernel,
        out_shape=(shape((STRIP + 16, WIDE), BF16),) * 2,
        in_specs=[VMEM] * 4,
        out_specs=(VMEM,) * 2,
        compiler_params=PARAMS,
        name="mid",
    )(edges, col_first, col_second, to_first)
    library, to_first, to_second = lax.optimization_barrier((library, to_first, to_second))
    for d in range(2, n_col):
        shards.append(lax.ppermute(library, "col", [(i, i ^ d) for i in range(n_col)]))
    row_first, row_second = (
        lax.ppermute(x, "row", pairs) for x, pairs in zip((to_above, to_below), swaps(n_row))
    )

    windows, ahead, back, g_row, g_col = pl.pallas_call(
        own_kernel,
        out_shape=(
            shape((NB, rows, 256), F32),
            shape((kernels, 8, 128), F32),
            shape((kernels, 8, 128), F32),
            shape((256, 256), BF16),
            shape((256, 256), BF16),
        ),
        in_specs=[VMEM] * 2,
        out_specs=(VMEM,) * 5,
        compiler_params=PARAMS,
        cost_estimate=pl.CostEstimate(flops=10**6, bytes_accessed=10**6, transcendentals=0),
        name="own",
    )(mask_pixels, taps)

    acc, images = pl.pallas_call(
        functools.partial(socs_kernel, entries, per),
        out_shape=(shape((NB + 1, CB, 256), F32), shape((SLOTS, 128), jnp.int32)),
        in_specs=[HBM] + [VMEM] * 8,
        out_specs=(VMEM,) * 2,
        scratch_shapes=[
            pltpu.VMEM((NB + 1, 256, 256), BF16),
            pltpu.SMEM(kernel_weights.shape, F32),
            pltpu.SemaphoreType.DMA,
        ]
        + [pltpu.VMEM((2 * GROUP, CB, 256), BF16)] * 2
        + [pltpu.VMEM((2 * GROUP, 256, 256), BF16)] * 2
        + [pltpu.VMEM((2 * GROUP, NB + 1, CB, 256), BF16)] * 2,
        compiler_params=PARAMS,
        cost_estimate=pl.CostEstimate(flops=6 * 10**8, bytes_accessed=10**5, transcendentals=0),
        name="socs",
    )(in_hbm(kernel_weights), windows, row_first, row_second, col_first, col_second, to_first, ahead, back)

    return pl.pallas_call(
        functools.partial(final_kernel, n_row, n_col),
        out_shape=shape((rows, cols), F32),
        in_specs=[VMEM] * (4 + n_col),
        out_specs=VMEM,
        scratch_shapes=[
            pltpu.VMEM((n_col * per, 64, 128), BF16),
            pltpu.SMEM((SLOTS, 128), jnp.int32),
            pltpu.VMEM((384, cols + 256), F32),
            pltpu.VMEM((WIDE, 384), BF16),
            pltpu.VMEM((2, rows, WIDE), BF16),
            pltpu.SemaphoreType.DMA,
        ],
        compiler_params=PARAMS,
        name="final",
    )(acc, images, g_row, g_col, *shards)


def solution(mesh):
    placed = (
        P(("frames", "row"), "col"),
        P(),
        P(),
        P(),
        P("col", None, None),
        P(("frames", "row"), "col", None),
        P(("frames", "row"), "col", None),
        P(("frames", "row"), "col"),
    )
    return jax.shard_map(
        on_device,
        mesh=mesh,
        in_specs=placed,
        out_specs=P(("frames", "row"), "col"),
        check_vma=False,
    )
```

```python
import functools
import math

import jax
import jax.numpy as jnp
from jax import lax
from jax.experimental import pallas as pl
from jax.experimental.pallas import tpu as pltpu
from jax.sharding import PartitionSpec as P

BLUR_HALF = 8
BLUR_SIGMA = 4.0
HALF = 16
RIM = HALF + BLUR_HALF
STRIP = 32
CB = 176
NB = 3
MAIN = 224
EDGE_IN = 80
EDGE_OUT = 48
RIGHT_AT = 56
HALF_STRIP = STRIP + 16
GROUP = 4
WIDE = 640
SLOTS = 16
F32 = jnp.float32
BF16 = jnp.bfloat16
VMEM = pl.BlockSpec(memory_space=pltpu.VMEM)
SMEM = pl.BlockSpec(memory_space=pltpu.SMEM)
HBM = pl.BlockSpec(memory_space=pltpu.HBM)
PARAMS = pltpu.CompilerParams(vmem_limit_bytes=16 * 1024 * 1024)


def dot_nt(a, b):
    return lax.dot_general(a, b, (((1,), (1,)), ((), ())), preferred_element_type=F32)


def dot_nn(a, b):
    return lax.dot_general(a, b, (((1,), (0,)), ((), ())), preferred_element_type=F32)


def join(strip):
    halves = [strip[0:HALF_STRIP, :], strip[HALF_STRIP : 2 * HALF_STRIP, :]]
    return jnp.concatenate(halves, axis=1).astype(F32)


def eye(rows, cols, shift):
    at = lax.broadcasted_iota(jnp.int32, (rows, cols), 1) - lax.broadcasted_iota(jnp.int32, (rows, cols), 0)
    return jnp.where(at == shift, 1.0, 0.0).astype(BF16)


def sides(axis, first_swap, second_swap):
    index, count = lax.axis_index(axis), lax.axis_size(axis)
    even = lax.rem(index, 2) == 0
    lower = jnp.where(even, second_swap, first_swap)
    upper = jnp.where(even, first_swap, second_swap)
    return jnp.where(index > 0, lower, 0.0), jnp.where(index < count - 1, upper, 0.0)


def prep_kernel(
    mask, ids, slots, count, across, down, library, to_first, to_second, taps, ends, a_ids, a_slots, sems
):
    rows, cols = mask.shape
    copies = [
        pltpu.make_async_copy(mask.at[:, 0:128], ends.at[0], sems.at[0]),
        pltpu.make_async_copy(mask.at[:, cols - 128 : cols], ends.at[1], sems.at[1]),
        pltpu.make_async_copy(ids, a_ids, sems.at[2]),
        pltpu.make_async_copy(slots, a_slots, sems.at[3]),
        pltpu.make_async_copy(across, taps.at[0], sems.at[4]),
        pltpu.make_async_copy(down, taps.at[1], sems.at[5]),
        pltpu.make_async_copy(library, to_first.at[2 * HALF_STRIP :], sems.at[6]),
    ]
    for copy in copies:
        copy.start()
    for copy in copies[2:4]:
        copy.wait()
    line = lax.broadcasted_iota(jnp.int32, (16, 128), 0)
    lane = lax.broadcasted_iota(jnp.int32, (16, 128), 1)

    def spread(x):
        x = x.astype(F32)
        x = jnp.concatenate([x, jnp.zeros((1, 128 - x.shape[1]), F32)], axis=1)
        return jnp.broadcast_to(x, (16, 128))

    table = jnp.where(line == 1, spread(a_slots[0]), jnp.broadcast_to(count[...].astype(F32), (16, 128)))
    table = jnp.where(line == 0, spread(a_ids[0]), table)
    width = jnp.where(line == 2, 1, ids.shape[2])
    table = jnp.where((lane < width) & (line < 3), table, 0.0).astype(BF16)
    for strip in (to_first, to_second):
        strip[STRIP:HALF_STRIP, :] = table
        strip[HALF_STRIP + STRIP : 2 * HALF_STRIP, :] = jnp.zeros((16, 128), BF16)
    even = lax.rem(lax.axis_index("col"), 2) == 0
    copies[0].wait()
    first = dot_nt(eye(STRIP, 128, 0), ends[0].astype(F32).astype(BF16))
    copies[1].wait()
    last = dot_nt(eye(STRIP, 128, 128 - STRIP), ends[1].astype(F32).astype(BF16))
    for strip, part in ((to_first, jnp.where(even, last, first)), (to_second, jnp.where(even, first, last))):
        strip[0:STRIP, :] = part[:, 0:128].astype(BF16)
        strip[HALF_STRIP : HALF_STRIP + STRIP, :] = part[:, 128:256].astype(BF16)
    for copy in copies[4:]:
        copy.wait()


def mid_kernel(mask, from_first, from_second, own, to_first, to_second):
    rows, cols = mask.shape
    left, right = sides("col", join(from_first), join(from_second))
    tables = jnp.concatenate(
        [left[STRIP:, 0:128], own[STRIP:HALF_STRIP, :].astype(F32), right[STRIP:, 0:128], jnp.zeros((16, 256), F32)],
        axis=1,
    ).astype(BF16)
    fill = jnp.zeros((128 - STRIP, 128), F32)
    strips = []
    for i in range(2):
        at = 0 if i == 0 else rows - 128
        pick = eye(STRIP, 128, 0 if i == 0 else 128 - STRIP)

        def turned(strip):
            return dot_nt(pick, jnp.concatenate([strip[0:STRIP, at : at + 128], fill], axis=0).astype(BF16))

        parts = [turned(left)[:, STRIP - RIM : STRIP], mask[(rows - STRIP) * i : (rows - STRIP) * i + STRIP, :].astype(F32), turned(right)[:, 0 : WIDE - RIM - cols]]
        strips.append(jnp.concatenate(parts, axis=1))
    even = lax.rem(lax.axis_index("row"), 2) == 0
    to_first[0:STRIP, :] = jnp.where(even, strips[1], strips[0]).astype(BF16)
    to_second[0:STRIP, :] = jnp.where(even, strips[0], strips[1]).astype(BF16)
    to_first[STRIP:, :] = tables
    to_second[STRIP:, :] = tables


def blur_matrix(shape, axis):
    lag = lax.broadcasted_iota(jnp.int32, shape, axis) - lax.broadcasted_iota(jnp.int32, shape, 1 - axis)
    total = sum(math.exp(-(t * t) / (2 * BLUR_SIGMA**2)) for t in range(-BLUR_HALF, BLUR_HALF + 1))
    off = (lag - BLUR_HALF).astype(F32)
    g = jnp.exp(-off * off / (2.0 * BLUR_SIGMA * BLUR_SIGMA)) * (1.0 / total)
    g = jnp.where((lag >= 0) & (lag <= 2 * BLUR_HALF), g, 0.0)
    high = g.astype(BF16)
    return high, (g - high.astype(F32)).astype(BF16)


def own_kernel(mask, taps, windows, ahead, back, g_row, g_col):
    rows, cols = mask.shape
    full = jnp.concatenate(
        [jnp.zeros((rows, RIM), F32), mask[...].astype(F32), jnp.zeros((rows, WIDE - RIM - cols), F32)], axis=1
    )
    for b in range(NB):
        windows[b] = full[:, CB * b : CB * b + 256]
    kernels, _, count = taps.shape[1:]
    flip = lax.broadcasted_iota(jnp.int32, (128, 128), 0) + lax.broadcasted_iota(jnp.int32, (128, 128), 1)
    flip = jnp.where(flip % 128 == 0, 1.0, 0.0).astype(BF16)
    ahead[...] = jnp.zeros(ahead.shape, F32)
    back[...] = jnp.zeros(back.shape, F32)
    for k in range(kernels):
        ahead[k, 0:2, 0:count] = taps[0, k].astype(F32)
        back[k, 0:2, 0:count] = taps[1, k].astype(F32)
    back[...] = dot_nn(back[...].reshape(kernels * 8, 128).astype(BF16), flip).reshape(kernels, 8, 128)
    g_row[0:128], g_row[128:256] = blur_matrix((128, 256), 1)
    g_col[:, 0:128], g_col[:, 128:256] = blur_matrix((256, 128), 0)


def socs_kernel(
    entries,
    per,
    weights,
    windows,
    row_first,
    row_second,
    col_first,
    col_second,
    own,
    ahead,
    back,
    acc,
    images,
    x_win,
    scale,
    sem,
    *scratch,
):
    across = scratch[0:2]
    down = scratch[2:4]
    first = scratch[4:6]
    groups = ahead.shape[0] // GROUP
    fetch = pltpu.make_async_copy(weights, scale, sem)
    fetch.start()
    above, below = sides("row", row_first[...].astype(F32), row_second[...].astype(F32))
    left, right = sides("col", join(col_first), join(col_second))
    rows = windows.shape[1]
    turned = jnp.concatenate(
        [
            left[STRIP - RIM : STRIP],
            jnp.zeros((128 - RIM + RIGHT_AT, rows), F32),
            right[0:RIM],
            jnp.zeros((128 - RIM - RIGHT_AT, rows), F32),
        ],
        axis=0,
    )
    turned = dot_nt(eye(rows, rows, 0), turned.astype(BF16))
    left, right = left[STRIP:, 0:128], right[STRIP:, 0:128]
    upper_rows = above[STRIP - RIM : STRIP]
    lower_rows = below[0:RIM]
    edge_rows = []
    for b in range(NB):
        lanes = slice(CB * b, CB * b + 256)
        part = windows[b]
        if b == 0:
            part = jnp.concatenate([part[:, 0:128] + turned[:, 0:128], part[:, 128:256]], axis=1)
        if b == NB - 1:
            part = jnp.concatenate([part[:, 0:128], part[:, 128:256] + turned[:, 128:256]], axis=1)
        x_win[b] = jnp.concatenate([upper_rows[:, lanes], part[0 : 256 - RIM]], axis=0).astype(BF16)
        edge_rows += [part[MAIN - RIM :], lower_rows[:, lanes]]
    edge_rows.append(jnp.zeros((256 - NB * EDGE_IN, 256), F32))
    x_win[NB] = jnp.concatenate(edge_rows, axis=0).astype(BF16)
    acc[...] = jnp.zeros(acc.shape, F32)
    for ref in across + down:
        ref[...] = jnp.zeros(ref.shape, BF16)

    slot = lax.broadcasted_iota(jnp.int32, (SLOTS, 128), 0).astype(F32)
    lane = lax.broadcasted_iota(jnp.int32, (SLOTS, 128), 1)
    found = jnp.zeros((SLOTS, 128), F32)
    col = lax.axis_index("col")
    tables = [above[STRIP:, 128 * t : 128 * t + 128] for t in range(3)]
    tables += [left, own[STRIP:HALF_STRIP, :].astype(F32), right]
    tables += [below[STRIP:, 128 * t : 128 * t + 128] for t in range(3)]
    for t, table in enumerate(tables):
        live = lane.astype(F32) < table[2:3, 0:1]
        hit = live & (table[1:2] == slot) & (lane < entries)
        image = jnp.sum(jnp.where(hit, table[0:1] + 1.0, 0.0), axis=1, keepdims=True)
        found = jnp.where(lane == t, image, found)
    cell = found.astype(jnp.int32) - 1
    images[...] = jnp.where(cell >= 0, ((cell // per) ^ col) * per + cell % per + 1, 0)

    row = lax.broadcasted_iota(jnp.int32, (32, 128), 0)
    lane = lax.broadcasted_iota(jnp.int32, (32, 128), 1)
    low = lane >= row + 96

    def cycled(x):
        return pltpu.roll(jnp.broadcast_to(x, (128, 128)), 0, 1, stride=1, stride_axis=0)

    def build_across(m, s):
        for q in range(2 * GROUP):
            cyc = cycled(ahead[GROUP * m + q // 2, q % 2 : q % 2 + 1, :])
            head = cyc[0:96].astype(BF16)
            tail = cyc[96:128]
            over = jnp.where(low, 0.0, tail)
            across[s][q, 0:96, 0:128] = head
            across[s][q, 128:CB, 128:256] = head[0 : CB - 128]
            across[s][q, 96:128, 0:128] = jnp.where(low, tail, 0.0).astype(BF16)
            across[s][q, 96:128, 128:256] = over.astype(BF16)

    def build_down(m, s):
        for q in range(2 * GROUP):
            cyc = cycled(back[GROUP * m + q // 2, q % 2 : q % 2 + 1, :])
            head = cyc[0:32]
            over = jnp.where(low, head, 0.0).astype(BF16)
            head = jnp.where(low, 0.0, head)
            same = jnp.concatenate([head, cyc[32:128]], axis=0).astype(BF16)
            down[s][q, 0:128, 0:128] = same
            down[s][q, 128:256, 128:256] = same
            down[s][q, 128:160, 0:128] = over

    def pass_one(s):
        taps = across[s][...].reshape(2 * GROUP * CB, 256)
        for j in range(NB + 1):
            part = dot_nt(taps, x_win[j]).astype(BF16)
            for q in range(2 * GROUP):
                first[s][q, j] = part[q * CB : (q + 1) * CB]

    def pass_two(m, s):
        for q in range(2 * GROUP):
            second = dot_nn(first[s][q].reshape((NB + 1) * CB, 256), down[s][q])
            acc[...] += (scale[GROUP * m + q // 2] * (second * second)).reshape(acc.shape)

    def stage(m, s):
        pass_one(s)
        build_down(m, s)
        if m + 1 < groups:
            build_across(m + 1, 1 - s)
        pass_two(m - 1, 1 - s)

    build_across(0, 0)
    pass_one(0)
    build_down(0, 0)
    build_across(1, 1)
    fetch.wait()

    for m in range(1, groups):
        stage(m, m % 2)
    pass_two(groups - 1, (groups - 1) % 2)


def final_kernel(n_row, n_col, acc, images, g_row, g_col, *rest):
    shards = rest[:-7]
    out, cells, table, placed, flat, blurred, sem = rest[-7:]
    g_high = g_col[:, 0:128]
    per = cells.shape[0] // len(shards)
    rows, cols = out.shape
    row, col = lax.axis_index("row"), lax.axis_index("col")
    fetch = pltpu.make_async_copy(images, table, sem)
    fetch.start()
    for i, shard in enumerate(shards):
        rows_of = shard.shape[0] - per * 64
        cells[pl.ds(i * per, per)] = shard[rows_of:, :].reshape(per, 64, 128)

    at_row = lax.broadcasted_iota(jnp.int32, (8, 384), 1) - BLUR_HALF
    row_ok = ((row > 0) | (at_row >= 0)) & ((row < n_row - 1) | (at_row < rows))
    row_ok = jnp.where(row_ok, 1.0, 0.0)
    for b in range(NB):
        edge = acc[NB, :, EDGE_IN * b : EDGE_IN * b + EDGE_OUT]
        part = jnp.concatenate(
            [acc[b, :, 0:MAIN], edge, jnp.zeros((CB, 384 - MAIN - EDGE_OUT), F32)], axis=1
        )
        part = part * row_ok[0:1]
        if b == 0:
            part = jnp.concatenate([jnp.where(col > 0, part[0:8], 0.0), part[8:]], axis=0)
        if b == NB - 1:
            part = jnp.concatenate([part[0 : CB - 8], jnp.where(col < n_col - 1, part[CB - 8 :], 0.0)], axis=0)
        flat[b * CB : (b + 1) * CB, :] = part.astype(BF16)
    flat[NB * CB :, :] = jnp.zeros((flat.shape[0] - NB * CB, 384), BF16)

    halves = []
    for i in range(rows // 128):
        part = dot_nt(g_row[...], flat[:, 128 * i : 128 * i + 256])
        halves.append(part[0:128] + part[128:])

    fetch.wait()
    slot_rows, slot_cols = rows // 64, cols // 128
    for i in range(-1, slot_rows + 1):
        for j in range(-1, slot_cols + 1):
            ti = 0 if i < 0 else (2 if i == slot_rows else 1)
            tj = 0 if j < 0 else (2 if j == slot_cols else 1)
            found = table[(i % slot_rows) * slot_cols + j % slot_cols, 3 * ti + tj]
            image = jnp.maximum(found - 1, 0)
            lanes = slice(128 + 128 * j, 256 + 128 * j)
            show = lambda x: jnp.where(found > 0, x.astype(F32), 0.0)
            if i < 0:
                placed[0:8, lanes] = show(cells[image, 48:64, :])[8:16]
            elif i == slot_rows:
                placed[8 + rows : 16 + rows, lanes] = show(cells[image, 0:16, :])[0:8]
            else:
                placed[8 + 64 * i : 72 + 64 * i, lanes] = show(cells[image])
    placed[16 + rows :, :] = jnp.zeros((placed.shape[0] - 16 - rows, placed.shape[1]), F32)

    for i, part in enumerate(halves):
        cell = dot_nn(g_row[...], placed[128 * i : 128 * i + 256, :].astype(BF16))
        cell = cell[0:128] + cell[128:]
        part += cell[:, 128 - BLUR_HALF : 128 - BLUR_HALF + part.shape[1]]
        high = part.astype(BF16)
        blurred[0, 128 * i : 128 * i + 128, :] = high
        blurred[1, 128 * i : 128 * i + 128, :] = (part - high.astype(F32)).astype(BF16)
    for j in range(cols // 128):
        lanes = slice(128 * j, 128 * j + 256)
        part = dot_nn(blurred[0, :, lanes], g_col[...])
        out[:, 128 * j : 128 * j + 128] = (
            part[:, 0:128] + part[:, 128:] + dot_nn(blurred[1, :, lanes], g_high)
        )


def shape(dims, dtype):
    return jax.ShapeDtypeStruct(dims, dtype)


def on_device(
    mask_pixels, across_taps, down_taps, kernel_weights, library, cell_ids, cell_slots, cell_count
):
    rows, cols = mask_pixels.shape
    kernels = across_taps.shape[0]
    entries = cell_ids.shape[-1]
    per = library.shape[0]
    n_row, n_col = lax.axis_size("row"), lax.axis_size("col")
    library = library.reshape(per * 64, 128)
    in_hbm = lambda x: pltpu.with_memory_space_constraint(x, pltpu.HBM)
    mask_hbm = in_hbm(mask_pixels)

    to_first, to_second, taps = pl.pallas_call(
        prep_kernel,
        out_shape=(
            shape((2 * HALF_STRIP + per * 64, 128), BF16),
            shape((2 * HALF_STRIP, 128), BF16),
            shape((2,) + across_taps.shape, BF16),
        ),
        in_specs=[HBM] * 3 + [VMEM] + [HBM] * 3,
        out_specs=(VMEM,) * 3,
        scratch_shapes=[
            pltpu.VMEM((2, rows, 128), jnp.int32),
            pltpu.VMEM(cell_ids.shape, jnp.int32),
            pltpu.VMEM(cell_slots.shape, jnp.int32),
            pltpu.SemaphoreType.DMA((7,)),
        ],
        compiler_params=PARAMS,
        name="prep",
    )(mask_hbm, in_hbm(cell_ids), in_hbm(cell_slots), cell_count, in_hbm(across_taps), in_hbm(down_taps), in_hbm(library))

    def swaps(n):
        rounds = []
        for start in (0, 1):
            pairs = [(i, i + 1) for i in range(start, n - 1, 2)]
            pairs += [(b, a) for a, b in pairs]
            rest = set(range(n)) - {a for a, b in pairs}
            rounds.append(pairs + [(i, i) for i in sorted(rest)])
        return rounds

    pairs = swaps(n_col)
    col_second = lax.ppermute(to_second, "col", pairs[1])
    col_first = lax.ppermute(to_first, "col", pairs[0])
    shards = [library, col_first]
    to_above, to_below = pl.pallas_call(
        mid_kernel,
        out_shape=(shape((STRIP + 16, WIDE), BF16),) * 2,
        in_specs=[VMEM] * 4,
        out_specs=(VMEM,) * 2,
        compiler_params=PARAMS,
        name="mid",
    )(mask_pixels, col_first, col_second, to_first)
    late, to_above, to_below = lax.optimization_barrier((library, to_above, to_below))
    for d in range(2, n_col):
        block = to_first if d < n_col - 1 else late
        shards.append(lax.ppermute(block, "col", [(i, i ^ d) for i in range(n_col)]))
    row_first, row_second = (
        lax.ppermute(x, "row", pairs) for x, pairs in zip((to_above, to_below), swaps(n_row))
    )

    windows, ahead, back, g_row, g_col = pl.pallas_call(
        own_kernel,
        out_shape=(
            shape((NB, rows, 256), F32),
            shape((kernels, 8, 128), F32),
            shape((kernels, 8, 128), F32),
            shape((256, 256), BF16),
            shape((256, 256), BF16),
        ),
        in_specs=[VMEM] * 2,
        out_specs=(VMEM,) * 5,
        compiler_params=PARAMS,
        cost_estimate=pl.CostEstimate(flops=10**6, bytes_accessed=10**6, transcendentals=0),
        name="own",
    )(mask_pixels, taps)

    acc, images = pl.pallas_call(
        functools.partial(socs_kernel, entries, per),
        out_shape=(shape((NB + 1, CB, 256), F32), shape((SLOTS, 128), jnp.int32)),
        in_specs=[HBM] + [VMEM] * 8,
        out_specs=(VMEM,) * 2,
        scratch_shapes=[
            pltpu.VMEM((NB + 1, 256, 256), BF16),
            pltpu.SMEM(kernel_weights.shape, F32),
            pltpu.SemaphoreType.DMA,
        ]
        + [pltpu.VMEM((2 * GROUP, CB, 256), BF16)] * 2
        + [pltpu.VMEM((2 * GROUP, 256, 256), BF16)] * 2
        + [pltpu.VMEM((2 * GROUP, NB + 1, CB, 256), BF16)] * 2,
        compiler_params=PARAMS,
        cost_estimate=pl.CostEstimate(flops=8 * 10**8, bytes_accessed=10**5, transcendentals=0),
        name="socs",
    )(in_hbm(kernel_weights), windows, row_first, row_second, col_first, col_second, to_first, ahead, back)

    return pl.pallas_call(
        functools.partial(final_kernel, n_row, n_col),
        out_shape=shape((rows, cols), F32),
        in_specs=[VMEM] * (4 + n_col),
        out_specs=VMEM,
        scratch_shapes=[
            pltpu.VMEM((n_col * per, 64, 128), BF16),
            pltpu.SMEM((SLOTS, 128), jnp.int32),
            pltpu.VMEM((384, cols + 256), F32),
            pltpu.VMEM((WIDE, 384), BF16),
            pltpu.VMEM((2, rows, WIDE), BF16),
            pltpu.SemaphoreType.DMA,
        ],
        compiler_params=PARAMS,
        name="final",
    )(acc, images, g_row, g_col, *shards)


def solution(mesh):
    placed = (
        P(("frames", "row"), "col"),
        P(),
        P(),
        P(),
        P("col", None, None),
        P(("frames", "row"), "col", None),
        P(("frames", "row"), "col", None),
        P(("frames", "row"), "col"),
    )
    return jax.shard_map(
        on_device,
        mesh=mesh,
        in_specs=placed,
        out_specs=P(("frames", "row"), "col"),
        check_vma=False,
    )
```

```python
import functools
import math

import jax
import jax.numpy as jnp
from jax import lax
from jax.experimental import pallas as pl
from jax.experimental.pallas import tpu as pltpu
from jax.sharding import PartitionSpec as P

BLUR_HALF = 8
BLUR_SIGMA = 4.0
HALF = 16
RIM = HALF + BLUR_HALF
STRIP = 32
CB = 176
NB = 3
MAIN = 224
EDGE_IN = 80
EDGE_OUT = 48
RIGHT_AT = 56
HALF_STRIP = STRIP + 16
GROUP = 4
WIDE = 640
SLOTS = 16
F32 = jnp.float32
BF16 = jnp.bfloat16
VMEM = pl.BlockSpec(memory_space=pltpu.VMEM)
SMEM = pl.BlockSpec(memory_space=pltpu.SMEM)
HBM = pl.BlockSpec(memory_space=pltpu.HBM)
PARAMS = pltpu.CompilerParams(vmem_limit_bytes=16 * 1024 * 1024)


def dot_nt(a, b):
    return lax.dot_general(a, b, (((1,), (1,)), ((), ())), preferred_element_type=F32)


def dot_nn(a, b):
    return lax.dot_general(a, b, (((1,), (0,)), ((), ())), preferred_element_type=F32)


def join(strip):
    halves = [strip[0:HALF_STRIP, :], strip[HALF_STRIP : 2 * HALF_STRIP, :]]
    return jnp.concatenate(halves, axis=1).astype(F32)


def eye(rows, cols, shift):
    at = lax.broadcasted_iota(jnp.int32, (rows, cols), 1) - lax.broadcasted_iota(jnp.int32, (rows, cols), 0)
    return jnp.where(at == shift, 1.0, 0.0).astype(BF16)


def sides(axis, first_swap, second_swap):
    index, count = lax.axis_index(axis), lax.axis_size(axis)
    even = lax.rem(index, 2) == 0
    lower = jnp.where(even, second_swap, first_swap)
    upper = jnp.where(even, first_swap, second_swap)
    return jnp.where(index > 0, lower, 0.0), jnp.where(index < count - 1, upper, 0.0)


def prep_kernel(
    mask, ids, slots, count, across, down, library, to_first, to_second, taps, ends, a_ids, a_slots, sems
):
    rows, cols = mask.shape
    copies = [
        pltpu.make_async_copy(mask.at[:, 0:128], ends.at[0], sems.at[0]),
        pltpu.make_async_copy(mask.at[:, cols - 128 : cols], ends.at[1], sems.at[1]),
        pltpu.make_async_copy(ids, a_ids, sems.at[2]),
        pltpu.make_async_copy(slots, a_slots, sems.at[3]),
        pltpu.make_async_copy(across, taps.at[0], sems.at[4]),
        pltpu.make_async_copy(down, taps.at[1], sems.at[5]),
        pltpu.make_async_copy(library, to_first.at[2 * HALF_STRIP :], sems.at[6]),
    ]
    for copy in copies:
        copy.start()
    for copy in copies[2:4]:
        copy.wait()
    line = lax.broadcasted_iota(jnp.int32, (16, 128), 0)
    lane = lax.broadcasted_iota(jnp.int32, (16, 128), 1)

    def spread(x):
        x = x.astype(F32)
        x = jnp.concatenate([x, jnp.zeros((1, 128 - x.shape[1]), F32)], axis=1)
        return jnp.broadcast_to(x, (16, 128))

    table = jnp.where(line == 1, spread(a_slots[0]), jnp.broadcast_to(count[...].astype(F32), (16, 128)))
    table = jnp.where(line == 0, spread(a_ids[0]), table)
    width = jnp.where(line == 2, 1, ids.shape[2])
    table = jnp.where((lane < width) & (line < 3), table, 0.0).astype(BF16)
    for strip in (to_first, to_second):
        strip[STRIP:HALF_STRIP, :] = table
        strip[HALF_STRIP + STRIP : 2 * HALF_STRIP, :] = jnp.zeros((16, 128), BF16)
    even = lax.rem(lax.axis_index("col"), 2) == 0
    copies[0].wait()
    first = dot_nt(eye(STRIP, 128, 0), ends[0].astype(F32).astype(BF16))
    copies[1].wait()
    last = dot_nt(eye(STRIP, 128, 128 - STRIP), ends[1].astype(F32).astype(BF16))
    for strip, part in ((to_first, jnp.where(even, last, first)), (to_second, jnp.where(even, first, last))):
        strip[0:STRIP, :] = part[:, 0:128].astype(BF16)
        strip[HALF_STRIP : HALF_STRIP + STRIP, :] = part[:, 128:256].astype(BF16)
    for copy in copies[4:]:
        copy.wait()


def mid_kernel(mask, from_first, from_second, own, to_first, to_second):
    rows, cols = mask.shape
    left, right = sides("col", join(from_first), join(from_second))
    tables = jnp.concatenate(
        [left[STRIP:, 0:128], own[STRIP:HALF_STRIP, :].astype(F32), right[STRIP:, 0:128], jnp.zeros((16, 256), F32)],
        axis=1,
    ).astype(BF16)
    fill = jnp.zeros((128 - STRIP, 128), F32)
    strips = []
    for i in range(2):
        at = 0 if i == 0 else rows - 128
        pick = eye(STRIP, 128, 0 if i == 0 else 128 - STRIP)

        def turned(strip):
            return dot_nt(pick, jnp.concatenate([strip[0:STRIP, at : at + 128], fill], axis=0).astype(BF16))

        parts = [turned(left)[:, STRIP - RIM : STRIP], mask[(rows - STRIP) * i : (rows - STRIP) * i + STRIP, :].astype(F32), turned(right)[:, 0 : WIDE - RIM - cols]]
        strips.append(jnp.concatenate(parts, axis=1))
    even = lax.rem(lax.axis_index("row"), 2) == 0
    to_first[0:STRIP, :] = jnp.where(even, strips[1], strips[0]).astype(BF16)
    to_second[0:STRIP, :] = jnp.where(even, strips[0], strips[1]).astype(BF16)
    to_first[STRIP:, :] = tables
    to_second[STRIP:, :] = tables


def blur_matrix(shape, axis):
    lag = lax.broadcasted_iota(jnp.int32, shape, axis) - lax.broadcasted_iota(jnp.int32, shape, 1 - axis)
    total = sum(math.exp(-(t * t) / (2 * BLUR_SIGMA**2)) for t in range(-BLUR_HALF, BLUR_HALF + 1))
    off = (lag - BLUR_HALF).astype(F32)
    g = jnp.exp(-off * off / (2.0 * BLUR_SIGMA * BLUR_SIGMA)) * (1.0 / total)
    g = jnp.where((lag >= 0) & (lag <= 2 * BLUR_HALF), g, 0.0)
    high = g.astype(BF16)
    return high, (g - high.astype(F32)).astype(BF16)


def own_kernel(mask, taps, windows, ahead, back, g_row, g_col):
    rows, cols = mask.shape
    full = jnp.concatenate(
        [jnp.zeros((rows, RIM), F32), mask[...].astype(F32), jnp.zeros((rows, WIDE - RIM - cols), F32)], axis=1
    )
    for b in range(NB):
        windows[b] = full[:, CB * b : CB * b + 256]
    kernels, _, count = taps.shape[1:]
    flip = lax.broadcasted_iota(jnp.int32, (128, 128), 0) + lax.broadcasted_iota(jnp.int32, (128, 128), 1)
    flip = jnp.where(flip % 128 == 0, 1.0, 0.0).astype(BF16)
    ahead[...] = jnp.zeros(ahead.shape, F32)
    back[...] = jnp.zeros(back.shape, F32)
    for k in range(kernels):
        ahead[k, 0:2, 0:count] = taps[0, k].astype(F32)
        back[k, 0:2, 0:count] = taps[1, k].astype(F32)
    back[...] = dot_nn(back[...].reshape(kernels * 8, 128).astype(BF16), flip).reshape(kernels, 8, 128)
    g_row[0:128], g_row[128:256] = blur_matrix((128, 256), 1)
    g_col[:, 0:128], g_col[:, 128:256] = blur_matrix((256, 128), 0)


def socs_kernel(
    entries,
    per,
    weights,
    windows,
    row_first,
    row_second,
    col_first,
    col_second,
    own,
    ahead,
    back,
    acc,
    images,
    x_win,
    scale,
    sem,
    *scratch,
):
    across = scratch[0:2]
    down = scratch[2:4]
    first = scratch[4:6]
    groups = ahead.shape[0] // GROUP
    fetch = pltpu.make_async_copy(weights, scale, sem)
    fetch.start()
    above, below = sides("row", row_first[...].astype(F32), row_second[...].astype(F32))
    left, right = sides("col", join(col_first), join(col_second))
    rows = windows.shape[1]
    turned = jnp.concatenate(
        [
            left[STRIP - RIM : STRIP],
            jnp.zeros((128 - RIM + RIGHT_AT, rows), F32),
            right[0:RIM],
            jnp.zeros((128 - RIM - RIGHT_AT, rows), F32),
        ],
        axis=0,
    )
    turned = dot_nt(eye(rows, rows, 0), turned.astype(BF16))
    left, right = left[STRIP:, 0:128], right[STRIP:, 0:128]
    upper_rows = above[STRIP - RIM : STRIP]
    lower_rows = below[0:RIM]
    edge_rows = []
    for b in range(NB):
        lanes = slice(CB * b, CB * b + 256)
        part = windows[b]
        if b == 0:
            part = jnp.concatenate([part[:, 0:128] + turned[:, 0:128], part[:, 128:256]], axis=1)
        if b == NB - 1:
            part = jnp.concatenate([part[:, 0:128], part[:, 128:256] + turned[:, 128:256]], axis=1)
        x_win[b] = jnp.concatenate([upper_rows[:, lanes], part[0 : 256 - RIM]], axis=0).astype(BF16)
        edge_rows += [part[MAIN - RIM :], lower_rows[:, lanes]]
    edge_rows.append(jnp.zeros((256 - NB * EDGE_IN, 256), F32))
    x_win[NB] = jnp.concatenate(edge_rows, axis=0).astype(BF16)
    acc[...] = jnp.zeros(acc.shape, F32)
    for ref in across + down:
        ref[...] = jnp.zeros(ref.shape, BF16)

    slot = lax.broadcasted_iota(jnp.int32, (SLOTS, 128), 0).astype(F32)
    lane = lax.broadcasted_iota(jnp.int32, (SLOTS, 128), 1)
    found = jnp.zeros((SLOTS, 128), F32)
    col = lax.axis_index("col")
    tables = [above[STRIP:, 128 * t : 128 * t + 128] for t in range(3)]
    tables += [left, own[STRIP:HALF_STRIP, :].astype(F32), right]
    tables += [below[STRIP:, 128 * t : 128 * t + 128] for t in range(3)]
    for t, table in enumerate(tables):
        live = lane.astype(F32) < table[2:3, 0:1]
        hit = live & (table[1:2] == slot) & (lane < entries)
        image = jnp.sum(jnp.where(hit, table[0:1] + 1.0, 0.0), axis=1, keepdims=True)
        found = jnp.where(lane == t, image, found)
    cell = found.astype(jnp.int32) - 1
    images[...] = jnp.where(cell >= 0, ((cell // per) ^ col) * per + cell % per + 1, 0)

    row = lax.broadcasted_iota(jnp.int32, (32, 128), 0)
    lane = lax.broadcasted_iota(jnp.int32, (32, 128), 1)
    low = lane >= row + 96

    def cycled(x):
        return pltpu.roll(jnp.broadcast_to(x, (128, 128)), 0, 1, stride=1, stride_axis=0)

    def build_across(m, s):
        for q in range(2 * GROUP):
            cyc = cycled(ahead[GROUP * m + q // 2, q % 2 : q % 2 + 1, :])
            head = cyc[0:96].astype(BF16)
            tail = cyc[96:128]
            over = jnp.where(low, 0.0, tail)
            across[s][q, 0:96, 0:128] = head
            across[s][q, 128:CB, 128:256] = head[0 : CB - 128]
            across[s][q, 96:128, 0:128] = jnp.where(low, tail, 0.0).astype(BF16)
            across[s][q, 96:128, 128:256] = over.astype(BF16)

    def build_down(m, s):
        for q in range(2 * GROUP):
            cyc = cycled(back[GROUP * m + q // 2, q % 2 : q % 2 + 1, :])
            head = cyc[0:32]
            over = jnp.where(low, head, 0.0).astype(BF16)
            head = jnp.where(low, 0.0, head)
            same = jnp.concatenate([head, cyc[32:128]], axis=0).astype(BF16)
            down[s][q, 0:128, 0:128] = same
            down[s][q, 128:256, 128:256] = same
            down[s][q, 128:160, 0:128] = over

    def pass_one(s):
        taps = across[s][...].reshape(2 * GROUP * CB, 256)
        for j in range(NB + 1):
            part = dot_nt(taps, x_win[j]).astype(BF16)
            for q in range(2 * GROUP):
                first[s][q, j] = part[q * CB : (q + 1) * CB]

    def pass_two(m, s):
        for q in range(2 * GROUP):
            second = dot_nn(first[s][q].reshape((NB + 1) * CB, 256), down[s][q])
            acc[...] += (scale[GROUP * m + q // 2] * (second * second)).reshape(acc.shape)

    def stage(m, s):
        pass_one(s)
        build_down(m, s)
        if m + 1 < groups:
            build_across(m + 1, 1 - s)
        pass_two(m - 1, 1 - s)

    build_across(0, 0)
    pass_one(0)
    build_down(0, 0)
    build_across(1, 1)
    fetch.wait()

    for m in range(1, groups):
        stage(m, m % 2)
    pass_two(groups - 1, (groups - 1) % 2)


def final_kernel(n_row, n_col, acc, images, g_row, g_col, *rest):
    shards = rest[:-7]
    out, cells, table, placed, flat, blurred, sem = rest[-7:]
    g_high = g_col[:, 0:128]
    per = cells.shape[0] // len(shards)
    rows, cols = out.shape
    row, col = lax.axis_index("row"), lax.axis_index("col")
    fetch = pltpu.make_async_copy(images, table, sem)
    fetch.start()
    for i, shard in enumerate(shards):
        rows_of = shard.shape[0] - per * 64
        cells[pl.ds(i * per, per)] = shard[rows_of:, :].reshape(per, 64, 128)

    at_row = lax.broadcasted_iota(jnp.int32, (8, 384), 1) - BLUR_HALF
    row_ok = ((row > 0) | (at_row >= 0)) & ((row < n_row - 1) | (at_row < rows))
    row_ok = jnp.where(row_ok, 1.0, 0.0)
    for b in range(NB):
        edge = acc[NB, :, EDGE_IN * b : EDGE_IN * b + EDGE_OUT]
        part = jnp.concatenate(
            [acc[b, :, 0:MAIN], edge, jnp.zeros((CB, 384 - MAIN - EDGE_OUT), F32)], axis=1
        )
        part = part * row_ok[0:1]
        if b == 0:
            part = jnp.concatenate([jnp.where(col > 0, part[0:8], 0.0), part[8:]], axis=0)
        if b == NB - 1:
            part = jnp.concatenate([part[0 : CB - 8], jnp.where(col < n_col - 1, part[CB - 8 :], 0.0)], axis=0)
        flat[b * CB : (b + 1) * CB, :] = part.astype(BF16)
    flat[NB * CB :, :] = jnp.zeros((flat.shape[0] - NB * CB, 384), BF16)

    halves = []
    for i in range(rows // 128):
        part = dot_nt(g_row[...], flat[:, 128 * i : 128 * i + 256])
        halves.append(part[0:128] + part[128:])

    fetch.wait()
    slot_rows, slot_cols = rows // 64, cols // 128
    for i in range(-1, slot_rows + 1):
        for j in range(-1, slot_cols + 1):
            ti = 0 if i < 0 else (2 if i == slot_rows else 1)
            tj = 0 if j < 0 else (2 if j == slot_cols else 1)
            found = table[(i % slot_rows) * slot_cols + j % slot_cols, 3 * ti + tj]
            image = jnp.maximum(found - 1, 0)
            lanes = slice(128 + 128 * j, 256 + 128 * j)
            show = lambda x: jnp.where(found > 0, x.astype(F32), 0.0)
            if i < 0:
                placed[0:8, lanes] = show(cells[image, 48:64, :])[8:16]
            elif i == slot_rows:
                placed[8 + rows : 16 + rows, lanes] = show(cells[image, 0:16, :])[0:8]
            else:
                placed[8 + 64 * i : 72 + 64 * i, lanes] = show(cells[image])
    placed[16 + rows :, :] = jnp.zeros((placed.shape[0] - 16 - rows, placed.shape[1]), F32)

    for i, part in enumerate(halves):
        cell = dot_nn(g_row[...], placed[128 * i : 128 * i + 256, :].astype(BF16))
        cell = cell[0:128] + cell[128:]
        part += cell[:, 128 - BLUR_HALF : 128 - BLUR_HALF + part.shape[1]]
        high = part.astype(BF16)
        blurred[0, 128 * i : 128 * i + 128, :] = high
        blurred[1, 128 * i : 128 * i + 128, :] = (part - high.astype(F32)).astype(BF16)
    for j in range(cols // 128):
        lanes = slice(128 * j, 128 * j + 256)
        part = dot_nn(blurred[0, :, lanes], g_col[...])
        out[:, 128 * j : 128 * j + 128] = (
            part[:, 0:128] + part[:, 128:] + dot_nn(blurred[1, :, lanes], g_high)
        )


def shape(dims, dtype):
    return jax.ShapeDtypeStruct(dims, dtype)


def on_device(
    mask_pixels, across_taps, down_taps, kernel_weights, library, cell_ids, cell_slots, cell_count
):
    rows, cols = mask_pixels.shape
    kernels = across_taps.shape[0]
    entries = cell_ids.shape[-1]
    per = library.shape[0]
    n_row, n_col = lax.axis_size("row"), lax.axis_size("col")
    library = library.reshape(per * 64, 128)
    in_hbm = lambda x: pltpu.with_memory_space_constraint(x, pltpu.HBM)
    mask_hbm = in_hbm(mask_pixels)

    to_first, to_second, taps = pl.pallas_call(
        prep_kernel,
        out_shape=(
            shape((2 * HALF_STRIP + per * 64, 128), BF16),
            shape((2 * HALF_STRIP, 128), BF16),
            shape((2,) + across_taps.shape, BF16),
        ),
        in_specs=[HBM] * 3 + [VMEM] + [HBM] * 3,
        out_specs=(VMEM,) * 3,
        scratch_shapes=[
            pltpu.VMEM((2, rows, 128), jnp.int32),
            pltpu.VMEM(cell_ids.shape, jnp.int32),
            pltpu.VMEM(cell_slots.shape, jnp.int32),
            pltpu.SemaphoreType.DMA((7,)),
        ],
        compiler_params=PARAMS,
        name="prep",
    )(mask_hbm, in_hbm(cell_ids), in_hbm(cell_slots), cell_count, in_hbm(across_taps), in_hbm(down_taps), in_hbm(library))

    def swaps(n):
        rounds = []
        for start in (0, 1):
            pairs = [(i, (i + 1) % n) for i in range(start, n, 2)]
            rounds.append(pairs + [(b, a) for a, b in pairs])
        return rounds

    second = []
    for r in range(n_row):
        second += [(r * n_col + a, r * n_col + b) for a, b in swaps(n_col)[1] if abs(a - b) == 1]
        second += [(r * n_col + a, (r ^ 1) * n_col + a) for a in (0, n_col - 1)]

    col_second = lax.ppermute(to_second, ("row", "col"), second)
    col_first = lax.ppermute(to_first, "col", swaps(n_col)[0])
    shards = [library, col_first]
    to_above, to_below = pl.pallas_call(
        mid_kernel,
        out_shape=(shape((STRIP + 16, WIDE), BF16),) * 2,
        in_specs=[VMEM] * 4,
        out_specs=(VMEM,) * 2,
        compiler_params=PARAMS,
        name="mid",
    )(mask_pixels, col_first, col_second, to_first)
    late, to_above, to_below = lax.optimization_barrier((library, to_above, to_below))
    for d in range(2, n_col):
        block = to_first if d < n_col - 1 else late
        shards.append(lax.ppermute(block, "col", [(i, i ^ d) for i in range(n_col)]))
    row_first, row_second = (
        lax.ppermute(x, "row", pairs) for x, pairs in zip((to_above, to_below), swaps(n_row))
    )

    windows, ahead, back, g_row, g_col = pl.pallas_call(
        own_kernel,
        out_shape=(
            shape((NB, rows, 256), F32),
            shape((kernels, 8, 128), F32),
            shape((kernels, 8, 128), F32),
            shape((256, 256), BF16),
            shape((256, 256), BF16),
        ),
        in_specs=[VMEM] * 2,
        out_specs=(VMEM,) * 5,
        compiler_params=PARAMS,
        cost_estimate=pl.CostEstimate(flops=10**6, bytes_accessed=10**6, transcendentals=0),
        name="own",
    )(mask_pixels, taps)

    acc, images = pl.pallas_call(
        functools.partial(socs_kernel, entries, per),
        out_shape=(shape((NB + 1, CB, 256), F32), shape((SLOTS, 128), jnp.int32)),
        in_specs=[HBM] + [VMEM] * 8,
        out_specs=(VMEM,) * 2,
        scratch_shapes=[
            pltpu.VMEM((NB + 1, 256, 256), BF16),
            pltpu.SMEM(kernel_weights.shape, F32),
            pltpu.SemaphoreType.DMA,
        ]
        + [pltpu.VMEM((2 * GROUP, CB, 256), BF16)] * 2
        + [pltpu.VMEM((2 * GROUP, 256, 256), BF16)] * 2
        + [pltpu.VMEM((2 * GROUP, NB + 1, CB, 256), BF16)] * 2,
        compiler_params=PARAMS,
        cost_estimate=pl.CostEstimate(flops=8 * 10**8, bytes_accessed=10**5, transcendentals=0),
        name="socs",
    )(in_hbm(kernel_weights), windows, row_first, row_second, col_first, col_second, to_first, ahead, back)

    return pl.pallas_call(
        functools.partial(final_kernel, n_row, n_col),
        out_shape=shape((rows, cols), F32),
        in_specs=[VMEM] * (4 + n_col),
        out_specs=VMEM,
        scratch_shapes=[
            pltpu.VMEM((n_col * per, 64, 128), BF16),
            pltpu.SMEM((SLOTS, 128), jnp.int32),
            pltpu.VMEM((384, cols + 256), F32),
            pltpu.VMEM((WIDE, 384), BF16),
            pltpu.VMEM((2, rows, WIDE), BF16),
            pltpu.SemaphoreType.DMA,
        ],
        compiler_params=PARAMS,
        name="final",
    )(acc, images, g_row, g_col, *shards)


def solution(mesh):
    placed = (
        P(("frames", "row"), "col"),
        P(),
        P(),
        P(),
        P("col", None, None),
        P(("frames", "row"), "col", None),
        P(("frames", "row"), "col", None),
        P(("frames", "row"), "col"),
    )
    return jax.shard_map(
        on_device,
        mesh=mesh,
        in_specs=placed,
        out_specs=P(("frames", "row"), "col"),
        check_vma=False,
    )
```

```python
import functools
import math

import jax
import jax.numpy as jnp
from jax import lax
from jax.experimental import pallas as pl
from jax.experimental.pallas import tpu as pltpu
from jax.sharding import PartitionSpec as P

BLUR_HALF = 8
BLUR_SIGMA = 4.0
HALF = 16
RIM = HALF + BLUR_HALF
STRIP = 32
CB = 176
NB = 3
MAIN = 224
EDGE_IN = 80
EDGE_OUT = 48
RIGHT_AT = 56
HALF_STRIP = STRIP + 16
GROUP = 2
WIDE = 640
SLOTS = 16
F32 = jnp.float32
BF16 = jnp.bfloat16
VMEM = pl.BlockSpec(memory_space=pltpu.VMEM)
SMEM = pl.BlockSpec(memory_space=pltpu.SMEM)
HBM = pl.BlockSpec(memory_space=pltpu.HBM)
PARAMS = pltpu.CompilerParams(vmem_limit_bytes=16 * 1024 * 1024)


def dot_nt(a, b):
    return lax.dot_general(a, b, (((1,), (1,)), ((), ())), preferred_element_type=F32)


def dot_nn(a, b):
    return lax.dot_general(a, b, (((1,), (0,)), ((), ())), preferred_element_type=F32)


def join(strip):
    halves = [strip[0:HALF_STRIP, :], strip[HALF_STRIP : 2 * HALF_STRIP, :]]
    return jnp.concatenate(halves, axis=1).astype(F32)


def eye(rows, cols, shift):
    at = lax.broadcasted_iota(jnp.int32, (rows, cols), 1) - lax.broadcasted_iota(jnp.int32, (rows, cols), 0)
    return jnp.where(at == shift, 1.0, 0.0).astype(BF16)


def sides(axis, first_swap, second_swap):
    index, count = lax.axis_index(axis), lax.axis_size(axis)
    even = lax.rem(index, 2) == 0
    lower = jnp.where(even, second_swap, first_swap)
    upper = jnp.where(even, first_swap, second_swap)
    return jnp.where(index > 0, lower, 0.0), jnp.where(index < count - 1, upper, 0.0)


def prep_kernel(
    mask, ids, slots, count, across, down, library, to_first, to_second, block, taps, ends, a_ids, a_slots, sems
):
    rows, cols = mask.shape
    copies = [
        pltpu.make_async_copy(mask.at[:, 0:128], ends.at[0], sems.at[0]),
        pltpu.make_async_copy(mask.at[:, cols - 128 : cols], ends.at[1], sems.at[1]),
        pltpu.make_async_copy(ids, a_ids, sems.at[2]),
        pltpu.make_async_copy(slots, a_slots, sems.at[3]),
        pltpu.make_async_copy(across, taps.at[0], sems.at[4]),
        pltpu.make_async_copy(down, taps.at[1], sems.at[5]),
        pltpu.make_async_copy(library, block.at[2 * HALF_STRIP :], sems.at[6]),
    ]
    for copy in copies:
        copy.start()
    for copy in copies[2:4]:
        copy.wait()
    line = lax.broadcasted_iota(jnp.int32, (16, 128), 0)
    lane = lax.broadcasted_iota(jnp.int32, (16, 128), 1)

    def spread(x):
        x = x.astype(F32)
        x = jnp.concatenate([x, jnp.zeros((1, 128 - x.shape[1]), F32)], axis=1)
        return jnp.broadcast_to(x, (16, 128))

    table = jnp.where(line == 1, spread(a_slots[0]), jnp.broadcast_to(count[...].astype(F32), (16, 128)))
    table = jnp.where(line == 0, spread(a_ids[0]), table)
    width = jnp.where(line == 2, 1, ids.shape[2])
    table = jnp.where((lane < width) & (line < 3), table, 0.0).astype(BF16)
    for strip in (to_first, to_second):
        strip[STRIP:HALF_STRIP, :] = table
        strip[HALF_STRIP + STRIP : 2 * HALF_STRIP, :] = jnp.zeros((16, 128), BF16)
    block[0 : 2 * HALF_STRIP, :] = jnp.zeros((2 * HALF_STRIP, 128), BF16)
    even = lax.rem(lax.axis_index("col"), 2) == 0
    copies[0].wait()
    first = dot_nt(eye(STRIP, 128, 0), ends[0].astype(F32).astype(BF16))
    copies[1].wait()
    last = dot_nt(eye(STRIP, 128, 128 - STRIP), ends[1].astype(F32).astype(BF16))
    for strip, part in ((to_first, jnp.where(even, last, first)), (to_second, jnp.where(even, first, last))):
        strip[0:STRIP, :] = part[:, 0:128].astype(BF16)
        strip[HALF_STRIP : HALF_STRIP + STRIP, :] = part[:, 128:256].astype(BF16)
    for copy in copies[4:]:
        copy.wait()


def mid_kernel(mask, from_first, from_second, own, to_first, to_second):
    rows, cols = mask.shape
    left, right = sides("col", join(from_first), join(from_second))
    tables = jnp.concatenate(
        [left[STRIP:, 0:128], own[STRIP:HALF_STRIP, :].astype(F32), right[STRIP:, 0:128], jnp.zeros((16, 256), F32)],
        axis=1,
    ).astype(BF16)
    fill = jnp.zeros((128 - STRIP, 128), F32)
    strips = []
    for i in range(2):
        at = 0 if i == 0 else rows - 128
        pick = eye(STRIP, 128, 0 if i == 0 else 128 - STRIP)

        def turned(strip):
            return dot_nt(pick, jnp.concatenate([strip[0:STRIP, at : at + 128], fill], axis=0).astype(BF16))

        parts = [turned(left)[:, STRIP - RIM : STRIP], mask[(rows - STRIP) * i : (rows - STRIP) * i + STRIP, :].astype(F32), turned(right)[:, 0 : WIDE - RIM - cols]]
        strips.append(jnp.concatenate(parts, axis=1))
    even = lax.rem(lax.axis_index("row"), 2) == 0
    to_first[0:STRIP, :] = jnp.where(even, strips[1], strips[0]).astype(BF16)
    to_second[0:STRIP, :] = jnp.where(even, strips[0], strips[1]).astype(BF16)
    to_first[STRIP:, :] = tables
    to_second[STRIP:, :] = tables


def blur_matrix(shape, axis, start=0):
    lag = lax.broadcasted_iota(jnp.int32, shape, axis) - lax.broadcasted_iota(jnp.int32, shape, 1 - axis) - start
    total = sum(math.exp(-(t * t) / (2 * BLUR_SIGMA**2)) for t in range(-BLUR_HALF, BLUR_HALF + 1))
    off = (lag - BLUR_HALF).astype(F32)
    g = jnp.exp(-off * off / (2.0 * BLUR_SIGMA * BLUR_SIGMA)) * (1.0 / total)
    g = jnp.where((lag >= 0) & (lag <= 2 * BLUR_HALF), g, 0.0)
    high = g.astype(BF16)
    return high, (g - high.astype(F32)).astype(BF16)


def own_kernel(mask, taps, windows, ahead, back, g_row, g_far, g_col):
    rows, cols = mask.shape
    full = jnp.concatenate(
        [jnp.zeros((rows, RIM), F32), mask[...].astype(F32), jnp.zeros((rows, WIDE - RIM - cols), F32)], axis=1
    )
    for b in range(NB):
        windows[b] = full[:, CB * b : CB * b + 256]
    kernels, _, count = taps.shape[1:]
    flip = lax.broadcasted_iota(jnp.int32, (128, 128), 0) + lax.broadcasted_iota(jnp.int32, (128, 128), 1)
    flip = jnp.where(flip % 128 == 0, 1.0, 0.0).astype(BF16)
    ahead[...] = jnp.zeros(ahead.shape, F32)
    back[...] = jnp.zeros(back.shape, F32)
    for k in range(kernels):
        ahead[k, 0:2, 0:count] = taps[0, k].astype(F32)
        back[k, 0:2, 0:count] = taps[1, k].astype(F32)
    back[...] = dot_nn(back[...].reshape(kernels * 8, 128).astype(BF16), flip).reshape(kernels, 8, 128)
    g_row[0:128], g_row[128:256] = blur_matrix((128, 256), 1)
    g_far[0:128], g_far[128:256] = blur_matrix((128, 256), 1, 16 - BLUR_HALF)
    g_col[:, 0:128], g_col[:, 128:256] = blur_matrix((256, 128), 0)


def socs_kernel(
    entries,
    per,
    empty,
    weights,
    windows,
    row_first,
    row_second,
    col_first,
    col_second,
    own,
    ahead,
    back,
    acc,
    images,
    x_win,
    scale,
    sem,
    *scratch,
):
    across = scratch[0:2]
    down = scratch[2:4]
    first = scratch[4:6]
    groups = ahead.shape[0] // GROUP
    fetch = pltpu.make_async_copy(weights, scale, sem)
    fetch.start()
    above, below = sides("row", row_first[...].astype(F32), row_second[...].astype(F32))
    left, right = sides("col", join(col_first), join(col_second))
    rows = windows.shape[1]
    turned = jnp.concatenate(
        [
            left[STRIP - RIM : STRIP],
            jnp.zeros((128 - RIM + RIGHT_AT, rows), F32),
            right[0:RIM],
            jnp.zeros((128 - RIM - RIGHT_AT, rows), F32),
        ],
        axis=0,
    )
    turned = dot_nt(eye(rows, rows, 0), turned.astype(BF16))
    left, right = left[STRIP:, 0:128], right[STRIP:, 0:128]
    upper_rows = above[STRIP - RIM : STRIP]
    lower_rows = below[0:RIM]
    edge_rows = []
    for b in range(NB):
        lanes = slice(CB * b, CB * b + 256)
        part = windows[b]
        if b == 0:
            part = jnp.concatenate([part[:, 0:128] + turned[:, 0:128], part[:, 128:256]], axis=1)
        if b == NB - 1:
            part = jnp.concatenate([part[:, 0:128], part[:, 128:256] + turned[:, 128:256]], axis=1)
        x_win[b] = jnp.concatenate([upper_rows[:, lanes], part[0 : 256 - RIM]], axis=0).astype(BF16)
        edge_rows += [part[MAIN - RIM :], lower_rows[:, lanes]]
    edge_rows.append(jnp.zeros((256 - NB * EDGE_IN, 256), F32))
    x_win[NB] = jnp.concatenate(edge_rows, axis=0).astype(BF16)
    acc[...] = jnp.zeros(acc.shape, F32)
    for ref in across + down:
        ref[...] = jnp.zeros(ref.shape, BF16)

    slot = lax.broadcasted_iota(jnp.int32, (SLOTS, 128), 0).astype(F32)
    lane = lax.broadcasted_iota(jnp.int32, (SLOTS, 128), 1)
    found = jnp.zeros((SLOTS, 128), F32)
    col = lax.axis_index("col")
    tables = [above[STRIP:, 128 * t : 128 * t + 128] for t in range(3)]
    tables += [left, own[STRIP:HALF_STRIP, :].astype(F32), right]
    tables += [below[STRIP:, 128 * t : 128 * t + 128] for t in range(3)]
    for t, table in enumerate(tables):
        live = lane.astype(F32) < table[2:3, 0:1]
        hit = live & (table[1:2] == slot) & (lane < entries)
        image = jnp.sum(jnp.where(hit, table[0:1] + 1.0, 0.0), axis=1, keepdims=True)
        found = jnp.where(lane == t, image, found)
    cell = found.astype(jnp.int32) - 1
    images[...] = jnp.where(cell >= 0, ((cell // per) ^ col) * per + cell % per, empty)

    row = lax.broadcasted_iota(jnp.int32, (32, 128), 0)
    lane = lax.broadcasted_iota(jnp.int32, (32, 128), 1)
    low = lane >= row + 96

    def cycled(x):
        return pltpu.roll(jnp.broadcast_to(x, (128, 128)), 0, 1, stride=1, stride_axis=0)

    def build_across(m, s):
        for q in range(2 * GROUP):
            cyc = cycled(ahead[GROUP * m + q // 2, q % 2 : q % 2 + 1, :])
            head = cyc[0:96].astype(BF16)
            tail = cyc[96:128]
            over = jnp.where(low, 0.0, tail)
            across[s][q, 0:96, 0:128] = head
            across[s][q, 128:CB, 128:256] = head[0 : CB - 128]
            across[s][q, 96:128, 0:128] = jnp.where(low, tail, 0.0).astype(BF16)
            across[s][q, 96:128, 128:256] = over.astype(BF16)

    def build_down(m, s):
        for q in range(2 * GROUP):
            cyc = cycled(back[GROUP * m + q // 2, q % 2 : q % 2 + 1, :])
            head = cyc[0:32]
            over = jnp.where(low, head, 0.0).astype(BF16)
            head = jnp.where(low, 0.0, head)
            same = jnp.concatenate([head, cyc[32:128]], axis=0).astype(BF16)
            down[s][q, 0:128, 0:128] = same
            down[s][q, 128:256, 128:256] = same
            down[s][q, 128:160, 0:128] = over

    def pass_one(s):
        taps = across[s][...].reshape(2 * GROUP * CB, 256)
        for j in range(NB + 1):
            part = dot_nt(taps, x_win[j]).astype(BF16)
            for q in range(2 * GROUP):
                first[s][q, j] = part[q * CB : (q + 1) * CB]

    def pass_two(m, s):
        for q in range(2 * GROUP):
            second = dot_nn(first[s][q].reshape((NB + 1) * CB, 256), down[s][q])
            acc[...] += (scale[GROUP * m + q // 2] * (second * second)).reshape(acc.shape)

    def stage(m, s):
        pass_one(s)
        build_down(m, s)
        if m + 1 < groups:
            build_across(m + 1, 1 - s)
        pass_two(m - 1, 1 - s)

    build_across(0, 0)
    pass_one(0)
    build_down(0, 0)
    build_across(1, 1)
    fetch.wait()

    for m in range(1, groups):
        stage(m, m % 2)
    pass_two(groups - 1, (groups - 1) % 2)


def final_kernel(n_row, n_col, acc, images, g_row, g_far, g_col, *rest):
    shards = rest[:-7]
    out, cells, table, placed, flat, blurred, sem = rest[-7:]
    per = (cells.shape[0] - 1) // len(shards)
    rows, cols = out.shape
    row, col = lax.axis_index("row"), lax.axis_index("col")
    fetch = pltpu.make_async_copy(images, table, sem)
    fetch.start()
    for i, shard in enumerate(shards):
        rows_of = shard.shape[0] - per * 64
        cells[i * per : (i + 1) * per] = shard[rows_of:, :].reshape(per, 64, 128)
    cells[len(shards) * per] = jnp.zeros((64, 128), BF16)

    at_row = lax.broadcasted_iota(jnp.int32, (8, 384), 1) - BLUR_HALF
    row_ok = ((row > 0) | (at_row >= 0)) & ((row < n_row - 1) | (at_row < rows))
    row_ok = jnp.where(row_ok, 1.0, 0.0)
    for b in range(NB):
        edge = acc[NB, :, EDGE_IN * b : EDGE_IN * b + EDGE_OUT]
        part = jnp.concatenate(
            [acc[b, :, 0:MAIN], edge, jnp.zeros((CB, 384 - MAIN - EDGE_OUT), F32)], axis=1
        )
        part = part * row_ok[0:1]
        if b == 0:
            part = jnp.concatenate([jnp.where(col > 0, part[0:8], 0.0), part[8:]], axis=0)
        if b == NB - 1:
            part = jnp.concatenate([part[0 : CB - 8], jnp.where(col < n_col - 1, part[CB - 8 :], 0.0)], axis=0)
        flat[b * CB : (b + 1) * CB, :] = part.astype(BF16)
    flat[NB * CB :, :] = jnp.zeros((flat.shape[0] - NB * CB, 384), BF16)

    halves = []
    for i in range(rows // 128):
        part = dot_nt(g_row[...], flat[:, 128 * i : 128 * i + 256])
        halves.append(part[0:128] + part[128:])

    fetch.wait()
    slot_rows, slot_cols = rows // 64, cols // 128
    for i in range(-1, slot_rows + 1):
        for j in range(-1, slot_cols + 1):
            ti = 0 if i < 0 else (2 if i == slot_rows else 1)
            tj = 0 if j < 0 else (2 if j == slot_cols else 1)
            image = table[(i % slot_rows) * slot_cols + j % slot_cols, 3 * ti + tj]
            lanes = slice(128 + 128 * j, 256 + 128 * j)
            if i < 0:
                placed[0:16, lanes] = cells[image, 48:64, :]
            elif i == slot_rows:
                placed[16 + rows : 32 + rows, lanes] = cells[image, 0:16, :]
            else:
                placed[16 + 64 * i : 80 + 64 * i, lanes] = cells[image]
    placed[32 + rows :, :] = jnp.zeros((placed.shape[0] - 32 - rows, placed.shape[1]), BF16)

    for i, part in enumerate(halves):
        cell = dot_nn(g_far[...], placed[128 * i : 128 * i + 256, :])
        cell = cell[0:128] + cell[128:]
        part += cell[:, 128 - BLUR_HALF : 128 - BLUR_HALF + part.shape[1]]
        high = part.astype(BF16)
        blurred[0, 128 * i : 128 * i + 128, :] = high
        blurred[1, 128 * i : 128 * i + 128, :] = (part - high.astype(F32)).astype(BF16)
    count = cols // 128
    stacked = [
        jnp.concatenate([blurred[p, :, 128 * j : 128 * j + 256] for j in range(count)], axis=0) for p in range(2)
    ]
    part = dot_nn(stacked[0], g_col[...])
    part = part[:, 0:128] + part[:, 128:] + dot_nn(stacked[1], g_col[:, 0:128])
    for j in range(count):
        out[:, 128 * j : 128 * j + 128] = part[rows * j : rows * j + rows]


def shape(dims, dtype):
    return jax.ShapeDtypeStruct(dims, dtype)


def on_device(
    mask_pixels, across_taps, down_taps, kernel_weights, library, cell_ids, cell_slots, cell_count
):
    rows, cols = mask_pixels.shape
    kernels = across_taps.shape[0]
    entries = cell_ids.shape[-1]
    per = library.shape[0]
    n_row, n_col = lax.axis_size("row"), lax.axis_size("col")
    library = library.reshape(per * 64, 128)
    in_hbm = lambda x: pltpu.with_memory_space_constraint(x, pltpu.HBM)
    mask_hbm = in_hbm(mask_pixels)

    to_first, to_second, block, taps = pl.pallas_call(
        prep_kernel,
        out_shape=(
            shape((2 * HALF_STRIP, 128), BF16),
            shape((2 * HALF_STRIP, 128), BF16),
            shape((2 * HALF_STRIP + per * 64, 128), BF16),
            shape((2,) + across_taps.shape, BF16),
        ),
        in_specs=[HBM] * 3 + [VMEM] + [HBM] * 3,
        out_specs=(VMEM,) * 4,
        scratch_shapes=[
            pltpu.VMEM((2, rows, 128), jnp.int32),
            pltpu.VMEM(cell_ids.shape, jnp.int32),
            pltpu.VMEM(cell_slots.shape, jnp.int32),
            pltpu.SemaphoreType.DMA((7,)),
        ],
        compiler_params=PARAMS,
        name="prep",
    )(mask_hbm, in_hbm(cell_ids), in_hbm(cell_slots), cell_count, in_hbm(across_taps), in_hbm(down_taps), in_hbm(library))

    def swaps(n):
        rounds = []
        for start in (0, 1):
            pairs = [(i, (i + 1) % n) for i in range(start, n, 2)]
            rounds.append(pairs + [(b, a) for a, b in pairs])
        return rounds

    second = []
    for r in range(n_row):
        second += [(r * n_col + a, r * n_col + b) for a, b in swaps(n_col)[1] if abs(a - b) == 1]
        second += [(r * n_col + a, (r ^ 1) * n_col + a) for a in (0, n_col - 1)]

    col_second = lax.ppermute(to_second, ("row", "col"), second)
    col_first = lax.ppermute(to_first, "col", swaps(n_col)[0])

    to_above, to_below = pl.pallas_call(
        mid_kernel,
        out_shape=(shape((STRIP + 16, WIDE), BF16),) * 2,
        in_specs=[VMEM] * 4,
        out_specs=(VMEM,) * 2,
        compiler_params=PARAMS,
        name="mid",
    )(mask_pixels, col_first, col_second, to_first)
    late, to_above, to_below = lax.optimization_barrier((library, to_above, to_below))
    shards = [library]
    for d in range(1, n_col):
        part = late if d in (1, n_col - 1) else block
        shards.append(lax.ppermute(part, "col", [(i, i ^ d) for i in range(n_col)]))
    row_first, row_second = (
        lax.ppermute(x, "row", pairs) for x, pairs in zip((to_above, to_below), swaps(n_row))
    )

    windows, ahead, back, g_row, g_far, g_col = pl.pallas_call(
        own_kernel,
        out_shape=(
            shape((NB, rows, 256), F32),
            shape((kernels, 8, 128), F32),
            shape((kernels, 8, 128), F32),
            shape((256, 256), BF16),
            shape((256, 256), BF16),
            shape((256, 256), BF16),
        ),
        in_specs=[VMEM] * 2,
        out_specs=(VMEM,) * 6,
        compiler_params=PARAMS,
        cost_estimate=pl.CostEstimate(flops=10**6, bytes_accessed=10**6, transcendentals=0),
        name="own",
    )(mask_pixels, taps)

    acc, images = pl.pallas_call(
        functools.partial(socs_kernel, entries, per, n_col * per),
        out_shape=(shape((NB + 1, CB, 256), F32), shape((SLOTS, 128), jnp.int32)),
        in_specs=[HBM] + [VMEM] * 8,
        out_specs=(VMEM,) * 2,
        scratch_shapes=[
            pltpu.VMEM((NB + 1, 256, 256), BF16),
            pltpu.SMEM(kernel_weights.shape, F32),
            pltpu.SemaphoreType.DMA,
        ]
        + [pltpu.VMEM((2 * GROUP, CB, 256), BF16)] * 2
        + [pltpu.VMEM((2 * GROUP, 256, 256), BF16)] * 2
        + [pltpu.VMEM((2 * GROUP, NB + 1, CB, 256), BF16)] * 2,
        compiler_params=PARAMS,
        cost_estimate=pl.CostEstimate(flops=8 * 10**8, bytes_accessed=10**5, transcendentals=0),
        name="socs",
    )(in_hbm(kernel_weights), windows, row_first, row_second, col_first, col_second, to_first, ahead, back)

    return pl.pallas_call(
        functools.partial(final_kernel, n_row, n_col),
        out_shape=shape((rows, cols), F32),
        in_specs=[VMEM] * (5 + n_col),
        out_specs=VMEM,
        scratch_shapes=[
            pltpu.VMEM((n_col * per + 1, 64, 128), BF16),
            pltpu.SMEM((SLOTS, 128), jnp.int32),
            pltpu.VMEM((384, cols + 256), BF16),
            pltpu.VMEM((WIDE, 384), BF16),
            pltpu.VMEM((2, rows, WIDE), BF16),
            pltpu.SemaphoreType.DMA,
        ],
        compiler_params=PARAMS,
        name="final",
    )(acc, images, g_row, g_far, g_col, *shards)


def solution(mesh):
    placed = (
        P(("frames", "row"), "col"),
        P(),
        P(),
        P(),
        P("col", None, None),
        P(("frames", "row"), "col", None),
        P(("frames", "row"), "col", None),
        P(("frames", "row"), "col"),
    )
    return jax.shard_map(
        on_device,
        mesh=mesh,
        in_specs=placed,
        out_specs=P(("frames", "row"), "col"),
        check_vma=False,
    )
```

```python
import functools
import math

import jax
import jax.numpy as jnp
from jax import lax
from jax.experimental import pallas as pl
from jax.experimental.pallas import tpu as pltpu
from jax.sharding import PartitionSpec as P

BLUR_HALF = 8
BLUR_SIGMA = 4.0
HALF = 16
RIM = HALF + BLUR_HALF
STRIP = 32
CB = 176
NB = 3
MAIN = 224
EDGE_IN = 80
EDGE_OUT = 48
RIGHT_AT = 56
HALF_STRIP = STRIP + 16
GROUP = 2
WIDE = 640
SLOTS = 16
F32 = jnp.float32
BF16 = jnp.bfloat16
VMEM = pl.BlockSpec(memory_space=pltpu.VMEM)
SMEM = pl.BlockSpec(memory_space=pltpu.SMEM)
HBM = pl.BlockSpec(memory_space=pltpu.HBM)
PARAMS = pltpu.CompilerParams(vmem_limit_bytes=16 * 1024 * 1024)


def dot_nt(a, b):
    return lax.dot_general(a, b, (((1,), (1,)), ((), ())), preferred_element_type=F32)


def dot_nn(a, b):
    return lax.dot_general(a, b, (((1,), (0,)), ((), ())), preferred_element_type=F32)


def join(strip):
    halves = [strip[0:HALF_STRIP, :], strip[HALF_STRIP : 2 * HALF_STRIP, :]]
    return jnp.concatenate(halves, axis=1).astype(F32)


def eye(rows, cols, shift):
    at = lax.broadcasted_iota(jnp.int32, (rows, cols), 1) - lax.broadcasted_iota(jnp.int32, (rows, cols), 0)
    return jnp.where(at == shift, 1.0, 0.0).astype(BF16)


def sides(axis, first_swap, second_swap):
    index, count = lax.axis_index(axis), lax.axis_size(axis)
    even = lax.rem(index, 2) == 0
    lower = jnp.where(even, second_swap, first_swap)
    upper = jnp.where(even, first_swap, second_swap)
    return jnp.where(index > 0, lower, 0.0), jnp.where(index < count - 1, upper, 0.0)


def prep_kernel(
    mask, ids, slots, count, across, down, library, to_first, to_second, block, taps, ends, a_ids, a_slots, sems
):
    rows, cols = mask.shape
    copies = [
        pltpu.make_async_copy(mask.at[:, 0:128], ends.at[0], sems.at[0]),
        pltpu.make_async_copy(mask.at[:, cols - 128 : cols], ends.at[1], sems.at[1]),
        pltpu.make_async_copy(ids, a_ids, sems.at[2]),
        pltpu.make_async_copy(slots, a_slots, sems.at[3]),
        pltpu.make_async_copy(across, taps.at[0], sems.at[4]),
        pltpu.make_async_copy(down, taps.at[1], sems.at[5]),
        pltpu.make_async_copy(library, block.at[2 * HALF_STRIP :], sems.at[6]),
    ]
    for copy in copies:
        copy.start()
    for copy in copies[2:4]:
        copy.wait()
    line = lax.broadcasted_iota(jnp.int32, (16, 128), 0)
    lane = lax.broadcasted_iota(jnp.int32, (16, 128), 1)

    def spread(x):
        x = x.astype(F32)
        x = jnp.concatenate([x, jnp.zeros((1, 128 - x.shape[1]), F32)], axis=1)
        return jnp.broadcast_to(x, (16, 128))

    table = jnp.where(line == 1, spread(a_slots[0]), jnp.broadcast_to(count[...].astype(F32), (16, 128)))
    table = jnp.where(line == 0, spread(a_ids[0]), table)
    width = jnp.where(line == 2, 1, ids.shape[2])
    table = jnp.where((lane < width) & (line < 3), table, 0.0).astype(BF16)
    for strip in (to_first, to_second):
        strip[STRIP:HALF_STRIP, :] = table
        strip[HALF_STRIP + STRIP : 2 * HALF_STRIP, :] = jnp.zeros((16, 128), BF16)
    block[0 : 2 * HALF_STRIP, :] = jnp.zeros((2 * HALF_STRIP, 128), BF16)
    to_second[2 * HALF_STRIP :, :] = jnp.zeros((128 - 2 * HALF_STRIP, 128), BF16)
    even = lax.rem(lax.axis_index("col"), 2) == 0
    copies[0].wait()
    first = dot_nt(eye(STRIP, 128, 0), ends[0].astype(F32).astype(BF16))
    copies[1].wait()
    last = dot_nt(eye(STRIP, 128, 128 - STRIP), ends[1].astype(F32).astype(BF16))
    for strip, part in ((to_first, jnp.where(even, last, first)), (to_second, jnp.where(even, first, last))):
        strip[0:STRIP, :] = part[:, 0:128].astype(BF16)
        strip[HALF_STRIP : HALF_STRIP + STRIP, :] = part[:, 128:256].astype(BF16)
    for copy in copies[4:]:
        copy.wait()


def mid_kernel(mask, from_first, from_second, own, to_first, to_second):
    rows, cols = mask.shape
    left, right = sides("col", join(from_first), join(from_second))
    tables = jnp.concatenate(
        [left[STRIP:, 0:128], own[STRIP:HALF_STRIP, :].astype(F32), right[STRIP:, 0:128], jnp.zeros((16, 256), F32)],
        axis=1,
    ).astype(BF16)
    fill = jnp.zeros((128 - STRIP, 128), F32)
    strips = []
    for i in range(2):
        at = 0 if i == 0 else rows - 128
        pick = eye(STRIP, 128, 0 if i == 0 else 128 - STRIP)

        def turned(strip):
            return dot_nt(pick, jnp.concatenate([strip[0:STRIP, at : at + 128], fill], axis=0).astype(BF16))

        parts = [turned(left)[:, STRIP - RIM : STRIP], mask[(rows - STRIP) * i : (rows - STRIP) * i + STRIP, :].astype(F32), turned(right)[:, 0 : WIDE - RIM - cols]]
        strips.append(jnp.concatenate(parts, axis=1))
    even = lax.rem(lax.axis_index("row"), 2) == 0
    to_first[0:STRIP, :] = jnp.where(even, strips[1], strips[0]).astype(BF16)
    to_second[0:STRIP, :] = jnp.where(even, strips[0], strips[1]).astype(BF16)
    to_first[STRIP:, :] = tables
    to_second[STRIP:, :] = tables


def blur_matrix(shape, axis, start=0):
    lag = lax.broadcasted_iota(jnp.int32, shape, axis) - lax.broadcasted_iota(jnp.int32, shape, 1 - axis) - start
    total = sum(math.exp(-(t * t) / (2 * BLUR_SIGMA**2)) for t in range(-BLUR_HALF, BLUR_HALF + 1))
    off = (lag - BLUR_HALF).astype(F32)
    g = jnp.exp(-off * off / (2.0 * BLUR_SIGMA * BLUR_SIGMA)) * (1.0 / total)
    g = jnp.where((lag >= 0) & (lag <= 2 * BLUR_HALF), g, 0.0)
    high = g.astype(BF16)
    return high, (g - high.astype(F32)).astype(BF16)


def own_kernel(mask, taps, windows, ahead, back, g_row, g_far, g_col):
    rows, cols = mask.shape
    full = jnp.concatenate(
        [jnp.zeros((rows, RIM), F32), mask[...].astype(F32), jnp.zeros((rows, WIDE - RIM - cols), F32)], axis=1
    )
    for b in range(NB):
        windows[b] = full[:, CB * b : CB * b + 256]
    kernels, _, count = taps.shape[1:]
    flip = lax.broadcasted_iota(jnp.int32, (128, 128), 0) + lax.broadcasted_iota(jnp.int32, (128, 128), 1)
    flip = jnp.where(flip % 128 == 0, 1.0, 0.0).astype(BF16)
    ahead[...] = jnp.zeros(ahead.shape, F32)
    back[...] = jnp.zeros(back.shape, F32)
    for k in range(kernels):
        ahead[k, 0:2, 0:count] = taps[0, k].astype(F32)
        back[k, 0:2, 0:count] = taps[1, k].astype(F32)
    back[...] = dot_nn(back[...].reshape(kernels * 8, 128).astype(BF16), flip).reshape(kernels, 8, 128)
    g_row[0:128], g_row[128:256] = blur_matrix((128, 256), 1)
    g_far[0:128], g_far[128:256] = blur_matrix((128, 256), 1, 16 - BLUR_HALF)
    g_col[:, 0:128], g_col[:, 128:256] = blur_matrix((256, 128), 0)


def socs_kernel(
    entries,
    per,
    empty,
    weights,
    windows,
    row_first,
    row_second,
    col_first,
    col_second,
    own,
    ahead,
    back,
    acc,
    images,
    x_win,
    scale,
    sem,
    *scratch,
):
    across = scratch[0:2]
    down = scratch[2:4]
    first = scratch[4:6]
    groups = ahead.shape[0] // GROUP
    fetch = pltpu.make_async_copy(weights, scale, sem)
    fetch.start()
    above, below = sides("row", row_first[...].astype(F32), row_second[...].astype(F32))
    left, right = sides("col", join(col_first), join(col_second))
    rows = windows.shape[1]
    turned = jnp.concatenate(
        [
            left[STRIP - RIM : STRIP],
            jnp.zeros((128 - RIM + RIGHT_AT, rows), F32),
            right[0:RIM],
            jnp.zeros((128 - RIM - RIGHT_AT, rows), F32),
        ],
        axis=0,
    )
    turned = dot_nt(eye(rows, rows, 0), turned.astype(BF16))
    left, right = left[STRIP:, 0:128], right[STRIP:, 0:128]
    upper_rows = above[STRIP - RIM : STRIP]
    lower_rows = below[0:RIM]
    edge_rows = []
    for b in range(NB):
        lanes = slice(CB * b, CB * b + 256)
        part = windows[b]
        if b == 0:
            part = jnp.concatenate([part[:, 0:128] + turned[:, 0:128], part[:, 128:256]], axis=1)
        if b == NB - 1:
            part = jnp.concatenate([part[:, 0:128], part[:, 128:256] + turned[:, 128:256]], axis=1)
        x_win[b] = jnp.concatenate([upper_rows[:, lanes], part[0 : 256 - RIM]], axis=0).astype(BF16)
        edge_rows += [part[MAIN - RIM :], lower_rows[:, lanes]]
    edge_rows.append(jnp.zeros((256 - NB * EDGE_IN, 256), F32))
    x_win[NB] = jnp.concatenate(edge_rows, axis=0).astype(BF16)
    acc[...] = jnp.zeros(acc.shape, F32)
    for ref in across + down:
        ref[...] = jnp.zeros(ref.shape, BF16)

    slot = lax.broadcasted_iota(jnp.int32, (SLOTS, 128), 0).astype(F32)
    lane = lax.broadcasted_iota(jnp.int32, (SLOTS, 128), 1)
    found = jnp.zeros((SLOTS, 128), F32)
    col = lax.axis_index("col")
    tables = [above[STRIP:, 128 * t : 128 * t + 128] for t in range(3)]
    tables += [left, own[STRIP:HALF_STRIP, :].astype(F32), right]
    tables += [below[STRIP:, 128 * t : 128 * t + 128] for t in range(3)]
    for t, table in enumerate(tables):
        live = lane.astype(F32) < table[2:3, 0:1]
        hit = live & (table[1:2] == slot) & (lane < entries)
        image = jnp.sum(jnp.where(hit, table[0:1] + 1.0, 0.0), axis=1, keepdims=True)
        found = jnp.where(lane == t, image, found)
    cell = found.astype(jnp.int32) - 1
    images[...] = jnp.where(cell >= 0, ((cell // per) ^ col) * per + cell % per, empty)

    row = lax.broadcasted_iota(jnp.int32, (32, 128), 0)
    lane = lax.broadcasted_iota(jnp.int32, (32, 128), 1)
    low = lane >= row + 96

    def cycled(x):
        return pltpu.roll(jnp.broadcast_to(x, (128, 128)), 0, 1, stride=1, stride_axis=0)

    def build_across(m, s):
        for q in range(2 * GROUP):
            cyc = cycled(ahead[GROUP * m + q // 2, q % 2 : q % 2 + 1, :])
            head = cyc[0:96].astype(BF16)
            tail = cyc[96:128]
            over = jnp.where(low, 0.0, tail)
            across[s][q, 0:96, 0:128] = head
            across[s][q, 128:CB, 128:256] = head[0 : CB - 128]
            across[s][q, 96:128, 0:128] = jnp.where(low, tail, 0.0).astype(BF16)
            across[s][q, 96:128, 128:256] = over.astype(BF16)

    def build_down(m, s):
        for q in range(2 * GROUP):
            cyc = cycled(back[GROUP * m + q // 2, q % 2 : q % 2 + 1, :])
            head = cyc[0:32]
            over = jnp.where(low, head, 0.0).astype(BF16)
            head = jnp.where(low, 0.0, head)
            same = jnp.concatenate([head, cyc[32:128]], axis=0).astype(BF16)
            down[s][q, 0:128, 0:128] = same
            down[s][q, 128:256, 128:256] = same
            down[s][q, 128:160, 0:128] = over

    def pass_one(s):
        taps = across[s][...].reshape(2 * GROUP * CB, 256)
        for j in range(NB + 1):
            part = dot_nt(taps, x_win[j]).astype(BF16)
            for q in range(2 * GROUP):
                first[s][q, j] = part[q * CB : (q + 1) * CB]

    def pass_two(m, s):
        for q in range(2 * GROUP):
            second = dot_nn(first[s][q].reshape((NB + 1) * CB, 256), down[s][q])
            acc[...] += (scale[GROUP * m + q // 2] * (second * second)).reshape(acc.shape)

    def stage(m, s):
        pass_one(s)
        build_down(m, s)
        if m + 1 < groups:
            build_across(m + 1, 1 - s)
        pass_two(m - 1, 1 - s)

    build_across(0, 0)
    pass_one(0)
    build_down(0, 0)
    build_across(1, 1)
    fetch.wait()

    for m in range(1, groups):
        stage(m, m % 2)
    pass_two(groups - 1, (groups - 1) % 2)


def final_kernel(n_row, n_col, acc, images, g_row, g_far, g_col, *rest):
    shards = rest[:-7]
    out, cells, table, placed, flat, blurred, sem = rest[-7:]
    per = (cells.shape[0] - 1) // len(shards)
    rows, cols = out.shape
    row, col = lax.axis_index("row"), lax.axis_index("col")
    fetch = pltpu.make_async_copy(images, table, sem)
    fetch.start()
    for i, shard in enumerate(shards):
        rows_of = shard.shape[0] - per * 64
        cells[i * per : (i + 1) * per] = shard[rows_of:, :].reshape(per, 64, 128)
    cells[len(shards) * per] = jnp.zeros((64, 128), BF16)

    at_row = lax.broadcasted_iota(jnp.int32, (8, 384), 1) - BLUR_HALF
    row_ok = ((row > 0) | (at_row >= 0)) & ((row < n_row - 1) | (at_row < rows))
    row_ok = jnp.where(row_ok, 1.0, 0.0)
    for b in range(NB):
        edge = acc[NB, :, EDGE_IN * b : EDGE_IN * b + EDGE_OUT]
        part = jnp.concatenate(
            [acc[b, :, 0:MAIN], edge, jnp.zeros((CB, 384 - MAIN - EDGE_OUT), F32)], axis=1
        )
        part = part * row_ok[0:1]
        if b == 0:
            part = jnp.concatenate([jnp.where(col > 0, part[0:8], 0.0), part[8:]], axis=0)
        if b == NB - 1:
            part = jnp.concatenate([part[0 : CB - 8], jnp.where(col < n_col - 1, part[CB - 8 :], 0.0)], axis=0)
        flat[b * CB : (b + 1) * CB, :] = part.astype(BF16)
    flat[NB * CB :, :] = jnp.zeros((flat.shape[0] - NB * CB, 384), BF16)

    halves = []
    for i in range(rows // 128):
        part = dot_nt(g_row[...], flat[:, 128 * i : 128 * i + 256])
        halves.append(part[0:128] + part[128:])

    fetch.wait()
    slot_rows, slot_cols = rows // 64, cols // 128
    for i in range(-1, slot_rows + 1):
        for j in range(-1, slot_cols + 1):
            ti = 0 if i < 0 else (2 if i == slot_rows else 1)
            tj = 0 if j < 0 else (2 if j == slot_cols else 1)
            image = table[(i % slot_rows) * slot_cols + j % slot_cols, 3 * ti + tj]
            lanes = slice(128 + 128 * j, 256 + 128 * j)
            if i < 0:
                placed[0:16, lanes] = cells[image, 48:64, :]
            elif i == slot_rows:
                placed[16 + rows : 32 + rows, lanes] = cells[image, 0:16, :]
            else:
                placed[16 + 64 * i : 80 + 64 * i, lanes] = cells[image]
    placed[32 + rows :, :] = jnp.zeros((placed.shape[0] - 32 - rows, placed.shape[1]), BF16)

    for i, part in enumerate(halves):
        cell = dot_nn(g_far[...], placed[128 * i : 128 * i + 256, :])
        cell = cell[0:128] + cell[128:]
        part += cell[:, 128 - BLUR_HALF : 128 - BLUR_HALF + part.shape[1]]
        high = part.astype(BF16)
        blurred[0, 128 * i : 128 * i + 128, :] = high
        blurred[1, 128 * i : 128 * i + 128, :] = (part - high.astype(F32)).astype(BF16)
    count = cols // 128
    stacked = [
        jnp.concatenate([blurred[p, :, 128 * j : 128 * j + 256] for j in range(count)], axis=0) for p in range(2)
    ]
    part = dot_nn(stacked[0], g_col[...])
    part = part[:, 0:128] + part[:, 128:] + dot_nn(stacked[1], g_col[:, 0:128])
    for j in range(count):
        out[:, 128 * j : 128 * j + 128] = part[rows * j : rows * j + rows]


def shape(dims, dtype):
    return jax.ShapeDtypeStruct(dims, dtype)


def on_device(
    mask_pixels, across_taps, down_taps, kernel_weights, library, cell_ids, cell_slots, cell_count
):
    rows, cols = mask_pixels.shape
    kernels = across_taps.shape[0]
    entries = cell_ids.shape[-1]
    per = library.shape[0]
    n_row, n_col = lax.axis_size("row"), lax.axis_size("col")
    library = library.reshape(per * 64, 128)
    in_hbm = lambda x: pltpu.with_memory_space_constraint(x, pltpu.HBM)
    mask_hbm = in_hbm(mask_pixels)

    to_first, to_second, block, taps = pl.pallas_call(
        prep_kernel,
        out_shape=(
            shape((2 * HALF_STRIP, 128), BF16),
            shape((128, 128), BF16),
            shape((2 * HALF_STRIP + per * 64, 128), BF16),
            shape((2,) + across_taps.shape, BF16),
        ),
        in_specs=[HBM] * 3 + [VMEM] + [HBM] * 3,
        out_specs=(VMEM,) * 4,
        scratch_shapes=[
            pltpu.VMEM((2, rows, 128), jnp.int32),
            pltpu.VMEM(cell_ids.shape, jnp.int32),
            pltpu.VMEM(cell_slots.shape, jnp.int32),
            pltpu.SemaphoreType.DMA((7,)),
        ],
        compiler_params=PARAMS,
        name="prep",
    )(mask_hbm, in_hbm(cell_ids), in_hbm(cell_slots), cell_count, in_hbm(across_taps), in_hbm(down_taps), in_hbm(library))

    def swaps(n):
        rounds = []
        for start in (0, 1):
            pairs = [(i, (i + 1) % n) for i in range(start, n, 2)]
            rounds.append(pairs + [(b, a) for a, b in pairs])
        return rounds

    second = []
    for r in range(n_row):
        second += [(r * n_col + a, r * n_col + b) for a, b in swaps(n_col)[1] if abs(a - b) == 1]
        second += [(r * n_col + a, (r ^ 1) * n_col + a) for a in (0, n_col - 1)]

    col_second = lax.ppermute(to_second, ("row", "col"), second)
    col_first = lax.ppermute(to_first, "col", swaps(n_col)[0])

    to_above, to_below = pl.pallas_call(
        mid_kernel,
        out_shape=(shape((STRIP + 16, WIDE), BF16),) * 2,
        in_specs=[VMEM] * 4,
        out_specs=(VMEM,) * 2,
        compiler_params=PARAMS,
        name="mid",
    )(mask_pixels, col_first, col_second, to_first)
    late, to_above, to_below = lax.optimization_barrier((library, to_above, to_below))
    shards = [library]
    for d in range(1, n_col):
        part = late if d in (1, n_col - 1) else block
        shards.append(lax.ppermute(part, "col", [(i, i ^ d) for i in range(n_col)]))
    row_first, row_second = (
        lax.ppermute(x, "row", pairs) for x, pairs in zip((to_above, to_below), swaps(n_row))
    )

    windows, ahead, back, g_row, g_far, g_col = pl.pallas_call(
        own_kernel,
        out_shape=(
            shape((NB, rows, 256), F32),
            shape((kernels, 8, 128), F32),
            shape((kernels, 8, 128), F32),
            shape((256, 256), BF16),
            shape((256, 256), BF16),
            shape((256, 256), BF16),
        ),
        in_specs=[VMEM] * 2,
        out_specs=(VMEM,) * 6,
        compiler_params=PARAMS,
        cost_estimate=pl.CostEstimate(flops=10**6, bytes_accessed=10**6, transcendentals=0),
        name="own",
    )(mask_pixels, taps)

    acc, images = pl.pallas_call(
        functools.partial(socs_kernel, entries, per, n_col * per),
        out_shape=(shape((NB + 1, CB, 256), F32), shape((SLOTS, 128), jnp.int32)),
        in_specs=[HBM] + [VMEM] * 8,
        out_specs=(VMEM,) * 2,
        scratch_shapes=[
            pltpu.VMEM((NB + 1, 256, 256), BF16),
            pltpu.SMEM(kernel_weights.shape, F32),
            pltpu.SemaphoreType.DMA,
        ]
        + [pltpu.VMEM((2 * GROUP, CB, 256), BF16)] * 2
        + [pltpu.VMEM((2 * GROUP, 256, 256), BF16)] * 2
        + [pltpu.VMEM((2 * GROUP, NB + 1, CB, 256), BF16)] * 2,
        compiler_params=PARAMS,
        cost_estimate=pl.CostEstimate(flops=8 * 10**8, bytes_accessed=10**5, transcendentals=0),
        name="socs",
    )(in_hbm(kernel_weights), windows, row_first, row_second, col_first, col_second, to_first, ahead, back)

    return pl.pallas_call(
        functools.partial(final_kernel, n_row, n_col),
        out_shape=shape((rows, cols), F32),
        in_specs=[VMEM] * (5 + n_col),
        out_specs=VMEM,
        scratch_shapes=[
            pltpu.VMEM((n_col * per + 1, 64, 128), BF16),
            pltpu.SMEM((SLOTS, 128), jnp.int32),
            pltpu.VMEM((384, cols + 256), BF16),
            pltpu.VMEM((WIDE, 384), BF16),
            pltpu.VMEM((2, rows, WIDE), BF16),
            pltpu.SemaphoreType.DMA,
        ],
        compiler_params=PARAMS,
        name="final",
    )(acc, images, g_row, g_far, g_col, *shards)


def solution(mesh):
    placed = (
        P(("frames", "row"), "col"),
        P(),
        P(),
        P(),
        P("col", None, None),
        P(("frames", "row"), "col", None),
        P(("frames", "row"), "col", None),
        P(("frames", "row"), "col"),
    )
    return jax.shard_map(
        on_device,
        mesh=mesh,
        in_specs=placed,
        out_specs=P(("frames", "row"), "col"),
        check_vma=False,
    )
```

```python
import functools
import math

import jax
import jax.numpy as jnp
from jax import lax
from jax.experimental import pallas as pl
from jax.experimental.pallas import tpu as pltpu
from jax.sharding import PartitionSpec as P

BLUR_HALF = 8
BLUR_SIGMA = 4.0
HALF = 16
RIM = HALF + BLUR_HALF
STRIP = 32
CB = 176
NB = 3
MAIN = 224
EDGE_IN = 80
EDGE_OUT = 48
RIGHT_AT = 56
HALF_STRIP = STRIP + 16
SPARE = 16
GROUP = 2
WIDE = 640
SLOTS = 16
F32 = jnp.float32
BF16 = jnp.bfloat16
VMEM = pl.BlockSpec(memory_space=pltpu.VMEM)
SMEM = pl.BlockSpec(memory_space=pltpu.SMEM)
HBM = pl.BlockSpec(memory_space=pltpu.HBM)
PARAMS = pltpu.CompilerParams(vmem_limit_bytes=16 * 1024 * 1024)


def dot_nt(a, b):
    return lax.dot_general(a, b, (((1,), (1,)), ((), ())), preferred_element_type=F32)


def dot_nn(a, b):
    return lax.dot_general(a, b, (((1,), (0,)), ((), ())), preferred_element_type=F32)


def join(strip):
    halves = [strip[0:HALF_STRIP, :], strip[HALF_STRIP : 2 * HALF_STRIP, :]]
    return jnp.concatenate(halves, axis=1).astype(F32)


def eye(rows, cols, shift):
    at = lax.broadcasted_iota(jnp.int32, (rows, cols), 1) - lax.broadcasted_iota(jnp.int32, (rows, cols), 0)
    return jnp.where(at == shift, 1.0, 0.0).astype(BF16)


def sides(axis, first_swap, second_swap):
    index, count = lax.axis_index(axis), lax.axis_size(axis)
    even = lax.rem(index, 2) == 0
    lower = jnp.where(even, second_swap, first_swap)
    upper = jnp.where(even, first_swap, second_swap)
    return jnp.where(index > 0, lower, 0.0), jnp.where(index < count - 1, upper, 0.0)


def prep_kernel(
    mask, ids, slots, count, across, down, library, to_first, to_second, block, taps, ends, a_ids, a_slots, sems
):
    rows, cols = mask.shape
    copies = [
        pltpu.make_async_copy(mask.at[:, 0:128], ends.at[0], sems.at[0]),
        pltpu.make_async_copy(mask.at[:, cols - 128 : cols], ends.at[1], sems.at[1]),
        pltpu.make_async_copy(ids, a_ids, sems.at[2]),
        pltpu.make_async_copy(slots, a_slots, sems.at[3]),
        pltpu.make_async_copy(across, taps.at[0], sems.at[4]),
        pltpu.make_async_copy(down, taps.at[1], sems.at[5]),
        pltpu.make_async_copy(library, block.at[SPARE:], sems.at[6]),
    ]
    for copy in copies:
        copy.start()
    for copy in copies[2:4]:
        copy.wait()
    line = lax.broadcasted_iota(jnp.int32, (16, 128), 0)
    lane = lax.broadcasted_iota(jnp.int32, (16, 128), 1)

    def spread(x):
        x = x.astype(F32)
        x = jnp.concatenate([x, jnp.zeros((1, 128 - x.shape[1]), F32)], axis=1)
        return jnp.broadcast_to(x, (16, 128))

    table = jnp.where(line == 1, spread(a_slots[0]), jnp.broadcast_to(count[...].astype(F32), (16, 128)))
    table = jnp.where(line == 0, spread(a_ids[0]), table)
    width = jnp.where(line == 2, 1, ids.shape[2])
    table = jnp.where((lane < width) & (line < 3), table, 0.0).astype(BF16)
    for strip in (to_first, to_second):
        strip[STRIP:HALF_STRIP, :] = table
        strip[HALF_STRIP + STRIP : 2 * HALF_STRIP, :] = jnp.zeros((16, 128), BF16)
    block[0:SPARE, :] = jnp.zeros((SPARE, 128), BF16)
    to_second[2 * HALF_STRIP :, :] = jnp.zeros((128 - 2 * HALF_STRIP, 128), BF16)
    even = lax.rem(lax.axis_index("col"), 2) == 0
    copies[0].wait()
    first = dot_nt(eye(STRIP, 128, 0), ends[0].astype(F32).astype(BF16))
    copies[1].wait()
    last = dot_nt(eye(STRIP, 128, 128 - STRIP), ends[1].astype(F32).astype(BF16))
    for strip, part in ((to_first, jnp.where(even, last, first)), (to_second, jnp.where(even, first, last))):
        strip[0:STRIP, :] = part[:, 0:128].astype(BF16)
        strip[HALF_STRIP : HALF_STRIP + STRIP, :] = part[:, 128:256].astype(BF16)
    for copy in copies[4:]:
        copy.wait()


def mid_kernel(mask, from_first, from_second, own, to_first, to_second):
    rows, cols = mask.shape
    left, right = sides("col", join(from_first), join(from_second))
    tables = jnp.concatenate(
        [left[STRIP:, 0:128], own[STRIP:HALF_STRIP, :].astype(F32), right[STRIP:, 0:128], jnp.zeros((16, 256), F32)],
        axis=1,
    ).astype(BF16)
    fill = jnp.zeros((128 - STRIP, 128), F32)
    strips = []
    for i in range(2):
        at = 0 if i == 0 else rows - 128
        pick = eye(STRIP, 128, 0 if i == 0 else 128 - STRIP)

        def turned(strip):
            return dot_nt(pick, jnp.concatenate([strip[0:STRIP, at : at + 128], fill], axis=0).astype(BF16))

        parts = [turned(left)[:, STRIP - RIM : STRIP], mask[(rows - STRIP) * i : (rows - STRIP) * i + STRIP, :].astype(F32), turned(right)[:, 0 : WIDE - RIM - cols]]
        strips.append(jnp.concatenate(parts, axis=1))
    even = lax.rem(lax.axis_index("row"), 2) == 0
    to_first[0:STRIP, :] = jnp.where(even, strips[1], strips[0]).astype(BF16)
    to_second[0:STRIP, :] = jnp.where(even, strips[0], strips[1]).astype(BF16)
    to_first[STRIP:, :] = tables
    to_second[STRIP:, :] = tables


def blur_matrix(shape, axis, start=0):
    lag = lax.broadcasted_iota(jnp.int32, shape, axis) - lax.broadcasted_iota(jnp.int32, shape, 1 - axis) - start
    total = sum(math.exp(-(t * t) / (2 * BLUR_SIGMA**2)) for t in range(-BLUR_HALF, BLUR_HALF + 1))
    off = (lag - BLUR_HALF).astype(F32)
    g = jnp.exp(-off * off / (2.0 * BLUR_SIGMA * BLUR_SIGMA)) * (1.0 / total)
    g = jnp.where((lag >= 0) & (lag <= 2 * BLUR_HALF), g, 0.0)
    high = g.astype(BF16)
    return high, (g - high.astype(F32)).astype(BF16)


def own_kernel(mask, taps, windows, ahead, back, g_row, g_far, g_col):
    rows, cols = mask.shape
    full = jnp.concatenate(
        [jnp.zeros((rows, RIM), F32), mask[...].astype(F32), jnp.zeros((rows, WIDE - RIM - cols), F32)], axis=1
    )
    for b in range(NB):
        windows[b] = full[:, CB * b : CB * b + 256]
    kernels, _, count = taps.shape[1:]
    flip = lax.broadcasted_iota(jnp.int32, (128, 128), 0) + lax.broadcasted_iota(jnp.int32, (128, 128), 1)
    flip = jnp.where(flip % 128 == 0, 1.0, 0.0).astype(BF16)
    ahead[...] = jnp.zeros(ahead.shape, F32)
    back[...] = jnp.zeros(back.shape, F32)
    for k in range(kernels):
        ahead[k, 0:2, 0:count] = taps[0, k].astype(F32)
        back[k, 0:2, 0:count] = taps[1, k].astype(F32)
    back[...] = dot_nn(back[...].reshape(kernels * 8, 128).astype(BF16), flip).reshape(kernels, 8, 128)
    g_row[0:128], g_row[128:256] = blur_matrix((128, 256), 1)
    g_far[0:128], g_far[128:256] = blur_matrix((128, 256), 1, 16 - BLUR_HALF)
    g_col[:, 0:128], g_col[:, 128:256] = blur_matrix((256, 128), 0)


def socs_kernel(
    entries,
    per,
    empty,
    weights,
    windows,
    row_first,
    row_second,
    col_first,
    col_second,
    own,
    ahead,
    back,
    acc,
    images,
    x_win,
    scale,
    sem,
    *scratch,
):
    across = scratch[0:2]
    down = scratch[2:4]
    first = scratch[4:6]
    groups = ahead.shape[0] // GROUP
    fetch = pltpu.make_async_copy(weights, scale, sem)
    fetch.start()
    above, below = sides("row", row_first[...].astype(F32), row_second[...].astype(F32))
    left, right = sides("col", join(col_first), join(col_second))
    rows = windows.shape[1]
    turned = jnp.concatenate(
        [
            left[STRIP - RIM : STRIP],
            jnp.zeros((128 - RIM + RIGHT_AT, rows), F32),
            right[0:RIM],
            jnp.zeros((128 - RIM - RIGHT_AT, rows), F32),
        ],
        axis=0,
    )
    turned = dot_nt(eye(rows, rows, 0), turned.astype(BF16))
    left, right = left[STRIP:, 0:128], right[STRIP:, 0:128]
    upper_rows = above[STRIP - RIM : STRIP]
    lower_rows = below[0:RIM]
    edge_rows = []
    for b in range(NB):
        lanes = slice(CB * b, CB * b + 256)
        part = windows[b]
        if b == 0:
            part = jnp.concatenate([part[:, 0:128] + turned[:, 0:128], part[:, 128:256]], axis=1)
        if b == NB - 1:
            part = jnp.concatenate([part[:, 0:128], part[:, 128:256] + turned[:, 128:256]], axis=1)
        x_win[b] = jnp.concatenate([upper_rows[:, lanes], part[0 : 256 - RIM]], axis=0).astype(BF16)
        edge_rows += [part[MAIN - RIM :], lower_rows[:, lanes]]
    edge_rows.append(jnp.zeros((256 - NB * EDGE_IN, 256), F32))
    x_win[NB] = jnp.concatenate(edge_rows, axis=0).astype(BF16)
    acc[...] = jnp.zeros(acc.shape, F32)
    for ref in across + down:
        ref[...] = jnp.zeros(ref.shape, BF16)

    slot = lax.broadcasted_iota(jnp.int32, (SLOTS, 128), 0).astype(F32)
    lane = lax.broadcasted_iota(jnp.int32, (SLOTS, 128), 1)
    found = jnp.zeros((SLOTS, 128), F32)
    col = lax.axis_index("col")
    tables = [above[STRIP:, 128 * t : 128 * t + 128] for t in range(3)]
    tables += [left, own[STRIP:HALF_STRIP, :].astype(F32), right]
    tables += [below[STRIP:, 128 * t : 128 * t + 128] for t in range(3)]
    for t, table in enumerate(tables):
        live = lane.astype(F32) < table[2:3, 0:1]
        hit = live & (table[1:2] == slot) & (lane < entries)
        image = jnp.sum(jnp.where(hit, table[0:1] + 1.0, 0.0), axis=1, keepdims=True)
        found = jnp.where(lane == t, image, found)
    cell = found.astype(jnp.int32) - 1
    images[...] = jnp.where(cell >= 0, ((cell // per) ^ col) * per + cell % per, empty)

    row = lax.broadcasted_iota(jnp.int32, (32, 128), 0)
    lane = lax.broadcasted_iota(jnp.int32, (32, 128), 1)
    low = lane >= row + 96

    def cycled(x):
        return pltpu.roll(jnp.broadcast_to(x, (128, 128)), 0, 1, stride=1, stride_axis=0)

    def build_across(m, s):
        for q in range(2 * GROUP):
            cyc = cycled(ahead[GROUP * m + q // 2, q % 2 : q % 2 + 1, :])
            head = cyc[0:96].astype(BF16)
            tail = cyc[96:128]
            over = jnp.where(low, 0.0, tail)
            across[s][q, 0:96, 0:128] = head
            across[s][q, 128:CB, 128:256] = head[0 : CB - 128]
            across[s][q, 96:128, 0:128] = jnp.where(low, tail, 0.0).astype(BF16)
            across[s][q, 96:128, 128:256] = over.astype(BF16)

    def build_down(m, s):
        for q in range(2 * GROUP):
            cyc = cycled(back[GROUP * m + q // 2, q % 2 : q % 2 + 1, :])
            head = cyc[0:32]
            over = jnp.where(low, head, 0.0).astype(BF16)
            head = jnp.where(low, 0.0, head)
            same = jnp.concatenate([head, cyc[32:128]], axis=0).astype(BF16)
            down[s][q, 0:128, 0:128] = same
            down[s][q, 128:256, 128:256] = same
            down[s][q, 128:160, 0:128] = over

    def pass_one(s):
        taps = across[s][...].reshape(2 * GROUP * CB, 256)
        for j in range(NB + 1):
            part = dot_nt(taps, x_win[j]).astype(BF16)
            for q in range(2 * GROUP):
                first[s][q, j] = part[q * CB : (q + 1) * CB]

    def pass_two(m, s):
        for q in range(2 * GROUP):
            second = dot_nn(first[s][q].reshape((NB + 1) * CB, 256), down[s][q])
            acc[...] += (scale[GROUP * m + q // 2] * (second * second)).reshape(acc.shape)

    def stage(m, s):
        pass_one(s)
        build_down(m, s)
        if m + 1 < groups:
            build_across(m + 1, 1 - s)
        pass_two(m - 1, 1 - s)

    build_across(0, 0)
    pass_one(0)
    build_down(0, 0)
    build_across(1, 1)
    fetch.wait()

    for m in range(1, groups):
        stage(m, m % 2)
    pass_two(groups - 1, (groups - 1) % 2)


def rows_kernel(n_row, n_col, acc, g_row, out, flat):
    rows = out.shape[0]
    cols = CB * NB - 2 * BLUR_HALF
    row, col = lax.axis_index("row"), lax.axis_index("col")
    at_row = lax.broadcasted_iota(jnp.int32, (8, 384), 1) - BLUR_HALF
    row_ok = ((row > 0) | (at_row >= 0)) & ((row < n_row - 1) | (at_row < rows))
    row_ok = jnp.where(row_ok, 1.0, 0.0)
    for b in range(NB):
        edge = acc[NB, :, EDGE_IN * b : EDGE_IN * b + EDGE_OUT]
        part = jnp.concatenate(
            [acc[b, :, 0:MAIN], edge, jnp.zeros((CB, 384 - MAIN - EDGE_OUT), F32)], axis=1
        )
        part = part * row_ok[0:1]
        if b == 0:
            part = jnp.concatenate([jnp.where(col > 0, part[0:8], 0.0), part[8:]], axis=0)
        if b == NB - 1:
            part = jnp.concatenate([part[0 : CB - 8], jnp.where(col < n_col - 1, part[CB - 8 :], 0.0)], axis=0)
        flat[b * CB : (b + 1) * CB, :] = part.astype(BF16)
    flat[NB * CB :, :] = jnp.zeros((flat.shape[0] - NB * CB, 384), BF16)

    for i in range(rows // 128):
        part = dot_nt(g_row[...], flat[:, 128 * i : 128 * i + 256])
        out[128 * i : 128 * i + 128, :] = part[0:128] + part[128:]


def final_kernel(images, blurred_rows, g_far, g_col, *rest):
    shards = rest[:-6]
    out, cells, table, placed, blurred, sem = rest[-6:]
    per = (cells.shape[0] - 1) // len(shards)
    rows, cols = out.shape
    fetch = pltpu.make_async_copy(images, table, sem)
    fetch.start()
    for i, shard in enumerate(shards):
        rows_of = shard.shape[0] - per * 64
        cells[i * per : (i + 1) * per] = shard[rows_of:, :].reshape(per, 64, 128)
    cells[len(shards) * per] = jnp.zeros((64, 128), BF16)

    fetch.wait()
    slot_rows, slot_cols = rows // 64, cols // 128
    for i in range(-1, slot_rows + 1):
        for j in range(-1, slot_cols + 1):
            ti = 0 if i < 0 else (2 if i == slot_rows else 1)
            tj = 0 if j < 0 else (2 if j == slot_cols else 1)
            image = table[(i % slot_rows) * slot_cols + j % slot_cols, 3 * ti + tj]
            lanes = slice(128 + 128 * j, 256 + 128 * j)
            if i < 0:
                placed[0:16, lanes] = cells[image, 48:64, :]
            elif i == slot_rows:
                placed[16 + rows : 32 + rows, lanes] = cells[image, 0:16, :]
            else:
                placed[16 + 64 * i : 80 + 64 * i, lanes] = cells[image]
    placed[32 + rows :, :] = jnp.zeros((placed.shape[0] - 32 - rows, placed.shape[1]), BF16)

    for i in range(rows // 128):
        part = blurred_rows[128 * i : 128 * i + 128, :]
        cell = dot_nn(g_far[...], placed[128 * i : 128 * i + 256, :])
        cell = cell[0:128] + cell[128:]
        part += cell[:, 128 - BLUR_HALF : 128 - BLUR_HALF + part.shape[1]]
        high = part.astype(BF16)
        blurred[0, 128 * i : 128 * i + 128, :] = high
        blurred[1, 128 * i : 128 * i + 128, :] = (part - high.astype(F32)).astype(BF16)
    count = cols // 128
    stacked = [
        jnp.concatenate([blurred[p, :, 128 * j : 128 * j + 256] for j in range(count)], axis=0) for p in range(2)
    ]
    part = dot_nn(stacked[0], g_col[...])
    part = part[:, 0:128] + part[:, 128:] + dot_nn(stacked[1], g_col[:, 0:128])
    for j in range(count):
        out[:, 128 * j : 128 * j + 128] = part[rows * j : rows * j + rows]


def shape(dims, dtype):
    return jax.ShapeDtypeStruct(dims, dtype)


def on_device(
    mask_pixels, across_taps, down_taps, kernel_weights, library, cell_ids, cell_slots, cell_count
):
    rows, cols = mask_pixels.shape
    kernels = across_taps.shape[0]
    entries = cell_ids.shape[-1]
    per = library.shape[0]
    n_row, n_col = lax.axis_size("row"), lax.axis_size("col")
    library = library.reshape(per * 64, 128)
    in_hbm = lambda x: pltpu.with_memory_space_constraint(x, pltpu.HBM)
    mask_hbm = in_hbm(mask_pixels)

    to_first, to_second, block, taps = pl.pallas_call(
        prep_kernel,
        out_shape=(
            shape((2 * HALF_STRIP, 128), BF16),
            shape((128, 128), BF16),
            shape((SPARE + per * 64, 128), BF16),
            shape((2,) + across_taps.shape, BF16),
        ),
        in_specs=[HBM] * 3 + [VMEM] + [HBM] * 3,
        out_specs=(VMEM,) * 4,
        scratch_shapes=[
            pltpu.VMEM((2, rows, 128), jnp.int32),
            pltpu.VMEM(cell_ids.shape, jnp.int32),
            pltpu.VMEM(cell_slots.shape, jnp.int32),
            pltpu.SemaphoreType.DMA((7,)),
        ],
        compiler_params=PARAMS,
        name="prep",
    )(mask_hbm, in_hbm(cell_ids), in_hbm(cell_slots), cell_count, in_hbm(across_taps), in_hbm(down_taps), in_hbm(library))

    def swaps(n):
        rounds = []
        for start in (0, 1):
            pairs = [(i, (i + 1) % n) for i in range(start, n, 2)]
            rounds.append(pairs + [(b, a) for a, b in pairs])
        return rounds

    second = []
    for r in range(n_row):
        second += [(r * n_col + a, r * n_col + b) for a, b in swaps(n_col)[1] if abs(a - b) == 1]
        second += [(r * n_col + a, (r ^ 1) * n_col + a) for a in (0, n_col - 1)]

    col_second = lax.ppermute(to_second, ("row", "col"), second)
    col_first = lax.ppermute(to_first, "col", swaps(n_col)[0])

    to_above, to_below = pl.pallas_call(
        mid_kernel,
        out_shape=(shape((STRIP + 16, WIDE), BF16),) * 2,
        in_specs=[VMEM] * 4,
        out_specs=(VMEM,) * 2,
        compiler_params=PARAMS,
        name="mid",
    )(mask_pixels, col_first, col_second, to_first)
    late, to_above, to_below = lax.optimization_barrier((library, to_above, to_below))
    blocks = {0: library}
    for d in sorted(range(1, n_col), key=lambda d: (d == n_col - 1, -(d & -d))):
        part = late if d == n_col - 1 else block
        blocks[d] = lax.ppermute(part, "col", [(i, i ^ d) for i in range(n_col)])
    shards = [blocks[d] for d in range(n_col)]
    row_first, row_second = (
        lax.ppermute(x, "row", pairs) for x, pairs in zip((to_above, to_below), swaps(n_row))
    )

    windows, ahead, back, g_row, g_far, g_col = pl.pallas_call(
        own_kernel,
        out_shape=(
            shape((NB, rows, 256), F32),
            shape((kernels, 8, 128), F32),
            shape((kernels, 8, 128), F32),
            shape((256, 256), BF16),
            shape((256, 256), BF16),
            shape((256, 256), BF16),
        ),
        in_specs=[VMEM] * 2,
        out_specs=(VMEM,) * 6,
        compiler_params=PARAMS,
        cost_estimate=pl.CostEstimate(flops=10**6, bytes_accessed=10**6, transcendentals=0),
        name="own",
    )(mask_pixels, taps)

    acc, images = pl.pallas_call(
        functools.partial(socs_kernel, entries, per, n_col * per),
        out_shape=(shape((NB + 1, CB, 256), F32), shape((SLOTS, 128), jnp.int32)),
        in_specs=[HBM] + [VMEM] * 8,
        out_specs=(VMEM,) * 2,
        scratch_shapes=[
            pltpu.VMEM((NB + 1, 256, 256), BF16),
            pltpu.SMEM(kernel_weights.shape, F32),
            pltpu.SemaphoreType.DMA,
        ]
        + [pltpu.VMEM((2 * GROUP, CB, 256), BF16)] * 2
        + [pltpu.VMEM((2 * GROUP, 256, 256), BF16)] * 2
        + [pltpu.VMEM((2 * GROUP, NB + 1, CB, 256), BF16)] * 2,
        compiler_params=PARAMS,
        cost_estimate=pl.CostEstimate(flops=75 * 10**7, bytes_accessed=10**5, transcendentals=0),
        name="socs",
    )(in_hbm(kernel_weights), windows, row_first, row_second, col_first, col_second, to_first, ahead, back)

    blurred_rows = pl.pallas_call(
        functools.partial(rows_kernel, n_row, n_col),
        out_shape=shape((rows, WIDE), F32),
        in_specs=[VMEM] * 2,
        out_specs=VMEM,
        scratch_shapes=[pltpu.VMEM((WIDE, 384), BF16)],
        compiler_params=PARAMS,
        cost_estimate=pl.CostEstimate(flops=10**6, bytes_accessed=10**5, transcendentals=0),
        name="rows",
    )(acc, g_row)

    return pl.pallas_call(
        final_kernel,
        out_shape=shape((rows, cols), F32),
        in_specs=[VMEM] * (4 + n_col),
        out_specs=VMEM,
        scratch_shapes=[
            pltpu.VMEM((n_col * per + 1, 64, 128), BF16),
            pltpu.SMEM((SLOTS, 128), jnp.int32),
            pltpu.VMEM((384, cols + 256), BF16),
            pltpu.VMEM((2, rows, WIDE), BF16),
            pltpu.SemaphoreType.DMA,
        ],
        compiler_params=PARAMS,
        name="final",
    )(images, blurred_rows, g_far, g_col, *shards)


def solution(mesh):
    placed = (
        P(("frames", "row"), "col"),
        P(),
        P(),
        P(),
        P("col", None, None),
        P(("frames", "row"), "col", None),
        P(("frames", "row"), "col", None),
        P(("frames", "row"), "col"),
    )
    return jax.shard_map(
        on_device,
        mesh=mesh,
        in_specs=placed,
        out_specs=P(("frames", "row"), "col"),
        check_vma=False,
    )
```

```python
import functools
import math

import jax
import jax.numpy as jnp
from jax import lax
from jax.experimental import pallas as pl
from jax.experimental.pallas import tpu as pltpu
from jax.sharding import PartitionSpec as P

BLUR_HALF = 8
BLUR_SIGMA = 4.0
HALF = 16
RIM = HALF + BLUR_HALF
STRIP = 32
CB = 176
NB = 3
MAIN = 224
EDGE_IN = 80
EDGE_OUT = 48
RIGHT_AT = 56
HALF_STRIP = STRIP + 16
SPARE = 16
GROUP = 2
WIDE = 640
SLOTS = 16
F32 = jnp.float32
BF16 = jnp.bfloat16
VMEM = pl.BlockSpec(memory_space=pltpu.VMEM)
SMEM = pl.BlockSpec(memory_space=pltpu.SMEM)
HBM = pl.BlockSpec(memory_space=pltpu.HBM)
PARAMS = pltpu.CompilerParams(vmem_limit_bytes=16 * 1024 * 1024)


def dot_nt(a, b):
    return lax.dot_general(a, b, (((1,), (1,)), ((), ())), preferred_element_type=F32)


def dot_nn(a, b):
    return lax.dot_general(a, b, (((1,), (0,)), ((), ())), preferred_element_type=F32)


def join(strip):
    halves = [strip[0:HALF_STRIP, :], strip[HALF_STRIP : 2 * HALF_STRIP, :]]
    return jnp.concatenate(halves, axis=1).astype(F32)


def eye(rows, cols, shift):
    at = lax.broadcasted_iota(jnp.int32, (rows, cols), 1) - lax.broadcasted_iota(jnp.int32, (rows, cols), 0)
    return jnp.where(at == shift, 1.0, 0.0).astype(BF16)


def sides(axis, first_swap, second_swap):
    index, count = lax.axis_index(axis), lax.axis_size(axis)
    even = lax.rem(index, 2) == 0
    lower = jnp.where(even, second_swap, first_swap)
    upper = jnp.where(even, first_swap, second_swap)
    return jnp.where(index > 0, lower, 0.0), jnp.where(index < count - 1, upper, 0.0)


def prep_kernel(
    mask, ids, slots, count, across, down, library, to_first, to_second, block, taps, ends, a_ids, a_slots, sems
):
    rows, cols = mask.shape
    copies = [
        pltpu.make_async_copy(mask.at[:, 0:128], ends.at[0], sems.at[0]),
        pltpu.make_async_copy(mask.at[:, cols - 128 : cols], ends.at[1], sems.at[1]),
        pltpu.make_async_copy(ids, a_ids, sems.at[2]),
        pltpu.make_async_copy(slots, a_slots, sems.at[3]),
        pltpu.make_async_copy(across, taps.at[0], sems.at[4]),
        pltpu.make_async_copy(down, taps.at[1], sems.at[5]),
        pltpu.make_async_copy(library, block.at[SPARE:], sems.at[6]),
    ]
    for copy in copies:
        copy.start()
    for copy in copies[2:4]:
        copy.wait()
    line = lax.broadcasted_iota(jnp.int32, (16, 128), 0)
    lane = lax.broadcasted_iota(jnp.int32, (16, 128), 1)

    def spread(x):
        x = x.astype(F32)
        x = jnp.concatenate([x, jnp.zeros((1, 128 - x.shape[1]), F32)], axis=1)
        return jnp.broadcast_to(x, (16, 128))

    table = jnp.where(line == 1, spread(a_slots[0]), jnp.broadcast_to(count[...].astype(F32), (16, 128)))
    table = jnp.where(line == 0, spread(a_ids[0]), table)
    width = jnp.where(line == 2, 1, ids.shape[2])
    table = jnp.where((lane < width) & (line < 3), table, 0.0).astype(BF16)
    for strip in (to_first, to_second):
        strip[STRIP:HALF_STRIP, :] = table
        strip[HALF_STRIP + STRIP : 2 * HALF_STRIP, :] = jnp.zeros((16, 128), BF16)
    block[0:SPARE, :] = jnp.zeros((SPARE, 128), BF16)
    to_second[2 * HALF_STRIP :, :] = jnp.zeros((128 - 2 * HALF_STRIP, 128), BF16)
    even = lax.rem(lax.axis_index("col"), 2) == 0
    copies[0].wait()
    first = dot_nt(eye(STRIP, 128, 0), ends[0].astype(F32).astype(BF16))
    copies[1].wait()
    last = dot_nt(eye(STRIP, 128, 128 - STRIP), ends[1].astype(F32).astype(BF16))
    for strip, part in ((to_first, jnp.where(even, last, first)), (to_second, jnp.where(even, first, last))):
        strip[0:STRIP, :] = part[:, 0:128].astype(BF16)
        strip[HALF_STRIP : HALF_STRIP + STRIP, :] = part[:, 128:256].astype(BF16)
    for copy in copies[4:]:
        copy.wait()


def mid_kernel(mask, from_first, from_second, own, to_first, to_second):
    rows, cols = mask.shape
    left, right = sides("col", join(from_first), join(from_second))
    tables = jnp.concatenate(
        [left[STRIP:, 0:128], own[STRIP:HALF_STRIP, :].astype(F32), right[STRIP:, 0:128], jnp.zeros((16, 256), F32)],
        axis=1,
    ).astype(BF16)
    fill = jnp.zeros((128 - STRIP, 128), F32)
    strips = []
    for i in range(2):
        at = 0 if i == 0 else rows - 128
        pick = eye(STRIP, 128, 0 if i == 0 else 128 - STRIP)

        def turned(strip):
            return dot_nt(pick, jnp.concatenate([strip[0:STRIP, at : at + 128], fill], axis=0).astype(BF16))

        parts = [turned(left)[:, STRIP - RIM : STRIP], mask[(rows - STRIP) * i : (rows - STRIP) * i + STRIP, :].astype(F32), turned(right)[:, 0 : WIDE - RIM - cols]]
        strips.append(jnp.concatenate(parts, axis=1))
    even = lax.rem(lax.axis_index("row"), 2) == 0
    to_first[0:STRIP, :] = jnp.where(even, strips[1], strips[0]).astype(BF16)
    to_second[0:STRIP, :] = jnp.where(even, strips[0], strips[1]).astype(BF16)
    to_first[STRIP:, :] = tables
    to_second[STRIP:, :] = tables


def blur_matrix(shape, axis, start=0):
    lag = lax.broadcasted_iota(jnp.int32, shape, axis) - lax.broadcasted_iota(jnp.int32, shape, 1 - axis) - start
    total = sum(math.exp(-(t * t) / (2 * BLUR_SIGMA**2)) for t in range(-BLUR_HALF, BLUR_HALF + 1))
    off = (lag - BLUR_HALF).astype(F32)
    g = jnp.exp(-off * off / (2.0 * BLUR_SIGMA * BLUR_SIGMA)) * (1.0 / total)
    g = jnp.where((lag >= 0) & (lag <= 2 * BLUR_HALF), g, 0.0)
    high = g.astype(BF16)
    return high, (g - high.astype(F32)).astype(BF16)


def own_kernel(mask, taps, windows, ahead, back, g_row, g_far, g_col):
    rows, cols = mask.shape
    full = jnp.concatenate(
        [jnp.zeros((rows, RIM), F32), mask[...].astype(F32), jnp.zeros((rows, WIDE - RIM - cols), F32)], axis=1
    )
    for b in range(NB):
        windows[b] = full[:, CB * b : CB * b + 256]
    kernels, _, count = taps.shape[1:]
    flip = lax.broadcasted_iota(jnp.int32, (128, 128), 0) + lax.broadcasted_iota(jnp.int32, (128, 128), 1)
    flip = jnp.where(flip % 128 == 0, 1.0, 0.0).astype(BF16)
    ahead[...] = jnp.zeros(ahead.shape, F32)
    back[...] = jnp.zeros(back.shape, F32)
    for k in range(kernels):
        ahead[k, 0:2, 0:count] = taps[0, k].astype(F32)
        back[k, 0:2, 0:count] = taps[1, k].astype(F32)
    back[...] = dot_nn(back[...].reshape(kernels * 8, 128).astype(BF16), flip).reshape(kernels, 8, 128)
    g_row[0:128], g_row[128:256] = blur_matrix((128, 256), 1)
    g_far[0:128], g_far[128:256] = blur_matrix((128, 256), 1, 16 - BLUR_HALF)
    g_col[:, 0:128], g_col[:, 128:256] = blur_matrix((256, 128), 0)


def socs_kernel(
    entries,
    per,
    empty,
    weights,
    windows,
    row_first,
    row_second,
    col_first,
    col_second,
    own,
    ahead,
    back,
    acc,
    images,
    x_win,
    scale,
    sem,
    *scratch,
):
    across = scratch[0:2]
    down = scratch[2:4]
    first = scratch[4:6]
    groups = ahead.shape[0] // GROUP
    fetch = pltpu.make_async_copy(weights, scale, sem)
    fetch.start()
    above, below = sides("row", row_first[...].astype(F32), row_second[...].astype(F32))
    left, right = sides("col", join(col_first), join(col_second))
    rows = windows.shape[1]
    turned = jnp.concatenate(
        [
            left[STRIP - RIM : STRIP],
            jnp.zeros((128 - RIM + RIGHT_AT, rows), F32),
            right[0:RIM],
            jnp.zeros((128 - RIM - RIGHT_AT, rows), F32),
        ],
        axis=0,
    )
    turned = dot_nt(eye(rows, rows, 0), turned.astype(BF16))
    left, right = left[STRIP:, 0:128], right[STRIP:, 0:128]
    upper_rows = above[STRIP - RIM : STRIP]
    lower_rows = below[0:RIM]
    edge_rows = []
    for b in range(NB):
        lanes = slice(CB * b, CB * b + 256)
        part = windows[b]
        if b == 0:
            part = jnp.concatenate([part[:, 0:128] + turned[:, 0:128], part[:, 128:256]], axis=1)
        if b == NB - 1:
            part = jnp.concatenate([part[:, 0:128], part[:, 128:256] + turned[:, 128:256]], axis=1)
        x_win[b] = jnp.concatenate([upper_rows[:, lanes], part[0 : 256 - RIM]], axis=0).astype(BF16)
        edge_rows += [part[MAIN - RIM :], lower_rows[:, lanes]]
    edge_rows.append(jnp.zeros((256 - NB * EDGE_IN, 256), F32))
    x_win[NB] = jnp.concatenate(edge_rows, axis=0).astype(BF16)
    acc[...] = jnp.zeros(acc.shape, F32)
    for ref in across + down:
        ref[...] = jnp.zeros(ref.shape, BF16)

    slot = lax.broadcasted_iota(jnp.int32, (SLOTS, 128), 0).astype(F32)
    lane = lax.broadcasted_iota(jnp.int32, (SLOTS, 128), 1)
    found = jnp.zeros((SLOTS, 128), F32)
    col = lax.axis_index("col")
    tables = [above[STRIP:, 128 * t : 128 * t + 128] for t in range(3)]
    tables += [left, own[STRIP:HALF_STRIP, :].astype(F32), right]
    tables += [below[STRIP:, 128 * t : 128 * t + 128] for t in range(3)]
    for t, table in enumerate(tables):
        live = lane.astype(F32) < table[2:3, 0:1]
        hit = live & (table[1:2] == slot) & (lane < entries)
        image = jnp.sum(jnp.where(hit, table[0:1] + 1.0, 0.0), axis=1, keepdims=True)
        found = jnp.where(lane == t, image, found)
    cell = found.astype(jnp.int32) - 1
    images[...] = jnp.where(cell >= 0, ((cell // per) ^ col) * per + cell % per, empty)

    row = lax.broadcasted_iota(jnp.int32, (32, 128), 0)
    lane = lax.broadcasted_iota(jnp.int32, (32, 128), 1)
    low = lane >= row + 96

    def cycled(x):
        return pltpu.roll(jnp.broadcast_to(x, (128, 128)), 0, 1, stride=1, stride_axis=0)

    def build_across(m, s):
        for q in range(2 * GROUP):
            cyc = cycled(ahead[GROUP * m + q // 2, q % 2 : q % 2 + 1, :])
            head = cyc[0:96].astype(BF16)
            tail = cyc[96:128]
            over = jnp.where(low, 0.0, tail)
            across[s][q, 0:96, 0:128] = head
            across[s][q, 128:CB, 128:256] = head[0 : CB - 128]
            across[s][q, 96:128, 0:128] = jnp.where(low, tail, 0.0).astype(BF16)
            across[s][q, 96:128, 128:256] = over.astype(BF16)

    def build_down(m, s):
        for q in range(2 * GROUP):
            cyc = cycled(back[GROUP * m + q // 2, q % 2 : q % 2 + 1, :])
            head = cyc[0:32]
            over = jnp.where(low, head, 0.0).astype(BF16)
            head = jnp.where(low, 0.0, head)
            same = jnp.concatenate([head, cyc[32:128]], axis=0).astype(BF16)
            down[s][q, 0:128, 0:128] = same
            down[s][q, 128:256, 128:256] = same
            down[s][q, 128:160, 0:128] = over

    def pass_one(s):
        taps = across[s][...].reshape(2 * GROUP * CB, 256)
        for j in range(NB + 1):
            part = dot_nt(taps, x_win[j]).astype(BF16)
            for q in range(2 * GROUP):
                first[s][q, j] = part[q * CB : (q + 1) * CB]

    def pass_two(m, s):
        for q in range(2 * GROUP):
            second = dot_nn(first[s][q].reshape((NB + 1) * CB, 256), down[s][q])
            acc[...] += (scale[GROUP * m + q // 2] * (second * second)).reshape(acc.shape)

    def stage(m, s):
        pass_one(s)
        build_down(m, s)
        if m + 1 < groups:
            build_across(m + 1, 1 - s)
        pass_two(m - 1, 1 - s)

    build_across(0, 0)
    pass_one(0)
    build_down(0, 0)
    build_across(1, 1)
    fetch.wait()

    for m in range(1, groups):
        stage(m, m % 2)
    pass_two(groups - 1, (groups - 1) % 2)


def rows_kernel(n_row, n_col, acc, g_row, out, flat):
    rows = out.shape[0]
    cols = CB * NB - 2 * BLUR_HALF
    row, col = lax.axis_index("row"), lax.axis_index("col")
    at_row = lax.broadcasted_iota(jnp.int32, (8, 384), 1) - BLUR_HALF
    row_ok = ((row > 0) | (at_row >= 0)) & ((row < n_row - 1) | (at_row < rows))
    row_ok = jnp.where(row_ok, 1.0, 0.0)
    for b in range(NB):
        edge = acc[NB, :, EDGE_IN * b : EDGE_IN * b + EDGE_OUT]
        part = jnp.concatenate(
            [acc[b, :, 0:MAIN], edge, jnp.zeros((CB, 384 - MAIN - EDGE_OUT), F32)], axis=1
        )
        part = part * row_ok[0:1]
        if b == 0:
            part = jnp.concatenate([jnp.where(col > 0, part[0:8], 0.0), part[8:]], axis=0)
        if b == NB - 1:
            part = jnp.concatenate([part[0 : CB - 8], jnp.where(col < n_col - 1, part[CB - 8 :], 0.0)], axis=0)
        flat[b * CB : (b + 1) * CB, :] = part.astype(BF16)
    flat[NB * CB :, :] = jnp.zeros((flat.shape[0] - NB * CB, 384), BF16)

    for i in range(rows // 128):
        part = dot_nt(g_row[...], flat[:, 128 * i : 128 * i + 256])
        out[128 * i : 128 * i + 128, :] = part[0:128] + part[128:]


def final_kernel(images, blurred_rows, g_far, g_col, *rest):
    shards = rest[:-4]
    out, cells, placed, blurred = rest[-4:]
    per = (cells.shape[0] - 1) // len(shards)
    rows, cols = out.shape
    table = images[...]
    for i, shard in enumerate(shards):
        rows_of = shard.shape[0] - per * 64
        cells[i * per : (i + 1) * per] = shard[rows_of:, :].reshape(per, 64, 128)
    cells[len(shards) * per] = jnp.zeros((64, 128), BF16)

    slot_rows, slot_cols = rows // 64, cols // 128
    for i in range(-1, slot_rows + 1):
        for j in range(-1, slot_cols + 1):
            ti = 0 if i < 0 else (2 if i == slot_rows else 1)
            tj = 0 if j < 0 else (2 if j == slot_cols else 1)
            image = table[(i % slot_rows) * slot_cols + j % slot_cols, 3 * ti + tj]
            lanes = slice(128 + 128 * j, 256 + 128 * j)
            if i < 0:
                placed[0:16, lanes] = cells[image, 48:64, :]
            elif i == slot_rows:
                placed[16 + rows : 32 + rows, lanes] = cells[image, 0:16, :]
            else:
                placed[16 + 64 * i : 80 + 64 * i, lanes] = cells[image]
    placed[32 + rows :, :] = jnp.zeros((placed.shape[0] - 32 - rows, placed.shape[1]), BF16)

    for i in range(rows // 128):
        part = blurred_rows[128 * i : 128 * i + 128, :]
        cell = dot_nn(g_far[...], placed[128 * i : 128 * i + 256, :])
        cell = cell[0:128] + cell[128:]
        part += cell[:, 128 - BLUR_HALF : 128 - BLUR_HALF + part.shape[1]]
        high = part.astype(BF16)
        blurred[0, 128 * i : 128 * i + 128, :] = high
        blurred[1, 128 * i : 128 * i + 128, :] = (part - high.astype(F32)).astype(BF16)
    count = cols // 128
    stacked = [
        jnp.concatenate([blurred[p, :, 128 * j : 128 * j + 256] for j in range(count)], axis=0) for p in range(2)
    ]
    part = dot_nn(stacked[0], g_col[...])
    part = part[:, 0:128] + part[:, 128:] + dot_nn(stacked[1], g_col[:, 0:128])
    for j in range(count):
        out[:, 128 * j : 128 * j + 128] = part[rows * j : rows * j + rows]


def shape(dims, dtype):
    return jax.ShapeDtypeStruct(dims, dtype)


def on_device(
    mask_pixels, across_taps, down_taps, kernel_weights, library, cell_ids, cell_slots, cell_count
):
    rows, cols = mask_pixels.shape
    kernels = across_taps.shape[0]
    entries = cell_ids.shape[-1]
    per = library.shape[0]
    n_row, n_col = lax.axis_size("row"), lax.axis_size("col")
    library = library.reshape(per * 64, 128)
    in_hbm = lambda x: pltpu.with_memory_space_constraint(x, pltpu.HBM)
    mask_hbm = in_hbm(mask_pixels)

    to_first, to_second, block, taps = pl.pallas_call(
        prep_kernel,
        out_shape=(
            shape((2 * HALF_STRIP, 128), BF16),
            shape((128, 128), BF16),
            shape((SPARE + per * 64, 128), BF16),
            shape((2,) + across_taps.shape, BF16),
        ),
        in_specs=[HBM] * 3 + [VMEM] + [HBM] * 3,
        out_specs=(VMEM,) * 4,
        scratch_shapes=[
            pltpu.VMEM((2, rows, 128), jnp.int32),
            pltpu.VMEM(cell_ids.shape, jnp.int32),
            pltpu.VMEM(cell_slots.shape, jnp.int32),
            pltpu.SemaphoreType.DMA((7,)),
        ],
        compiler_params=PARAMS,
        name="prep",
    )(mask_hbm, in_hbm(cell_ids), in_hbm(cell_slots), cell_count, in_hbm(across_taps), in_hbm(down_taps), in_hbm(library))

    def swaps(n):
        rounds = []
        for start in (0, 1):
            pairs = [(i, (i + 1) % n) for i in range(start, n, 2)]
            rounds.append(pairs + [(b, a) for a, b in pairs])
        return rounds

    second = []
    for r in range(n_row):
        second += [(r * n_col + a, r * n_col + b) for a, b in swaps(n_col)[1] if abs(a - b) == 1]
        second += [(r * n_col + a, (r ^ 1) * n_col + a) for a in (0, n_col - 1)]

    col_second = lax.ppermute(to_second, ("row", "col"), second)
    col_first = lax.ppermute(to_first, "col", swaps(n_col)[0])

    to_above, to_below = pl.pallas_call(
        mid_kernel,
        out_shape=(shape((STRIP + 16, WIDE), BF16),) * 2,
        in_specs=[VMEM] * 4,
        out_specs=(VMEM,) * 2,
        compiler_params=PARAMS,
        name="mid",
    )(mask_pixels, col_first, col_second, to_first)
    late, to_above, to_below = lax.optimization_barrier((library, to_above, to_below))
    blocks = {0: library}
    for d in sorted(range(1, n_col), key=lambda d: (d == n_col - 1, -(d & -d))):
        part = late if d == n_col - 1 else block
        blocks[d] = lax.ppermute(part, "col", [(i, i ^ d) for i in range(n_col)])
    shards = [blocks[d] for d in range(n_col)]
    row_first, row_second = (
        lax.ppermute(x, "row", pairs) for x, pairs in zip((to_above, to_below), swaps(n_row))
    )

    windows, ahead, back, g_row, g_far, g_col = pl.pallas_call(
        own_kernel,
        out_shape=(
            shape((NB, rows, 256), F32),
            shape((kernels, 8, 128), F32),
            shape((kernels, 8, 128), F32),
            shape((256, 256), BF16),
            shape((256, 256), BF16),
            shape((256, 256), BF16),
        ),
        in_specs=[VMEM] * 2,
        out_specs=(VMEM,) * 6,
        compiler_params=PARAMS,
        cost_estimate=pl.CostEstimate(flops=10**6, bytes_accessed=10**6, transcendentals=0),
        name="own",
    )(mask_pixels, taps)

    acc, images = pl.pallas_call(
        functools.partial(socs_kernel, entries, per, n_col * per),
        out_shape=(shape((NB + 1, CB, 256), F32), shape((SLOTS, 128), jnp.int32)),
        in_specs=[HBM] + [VMEM] * 8,
        out_specs=(VMEM,) * 2,
        scratch_shapes=[
            pltpu.VMEM((NB + 1, 256, 256), BF16),
            pltpu.SMEM(kernel_weights.shape, F32),
            pltpu.SemaphoreType.DMA,
        ]
        + [pltpu.VMEM((2 * GROUP, CB, 256), BF16)] * 2
        + [pltpu.VMEM((2 * GROUP, 256, 256), BF16)] * 2
        + [pltpu.VMEM((2 * GROUP, NB + 1, CB, 256), BF16)] * 2,
        compiler_params=PARAMS,
        cost_estimate=pl.CostEstimate(flops=75 * 10**7, bytes_accessed=10**5, transcendentals=0),
        name="socs",
    )(in_hbm(kernel_weights), windows, row_first, row_second, col_first, col_second, to_first, ahead, back)

    blurred_rows = pl.pallas_call(
        functools.partial(rows_kernel, n_row, n_col),
        out_shape=shape((rows, WIDE), F32),
        in_specs=[VMEM] * 2,
        out_specs=VMEM,
        scratch_shapes=[pltpu.VMEM((WIDE, 384), BF16)],
        compiler_params=PARAMS,
        cost_estimate=pl.CostEstimate(flops=10**6, bytes_accessed=10**5, transcendentals=0),
        name="rows",
    )(acc, g_row)

    return pl.pallas_call(
        final_kernel,
        out_shape=shape((rows, cols), F32),
        in_specs=[VMEM] * (4 + n_col),
        out_specs=VMEM,
        scratch_shapes=[
            pltpu.VMEM((n_col * per + 1, 64, 128), BF16),
            pltpu.VMEM((384, cols + 256), BF16),
            pltpu.VMEM((2, rows, WIDE), BF16),
        ],
        compiler_params=PARAMS,
        name="final",
    )(images, blurred_rows, g_far, g_col, *shards)


def solution(mesh):
    placed = (
        P(("frames", "row"), "col"),
        P(),
        P(),
        P(),
        P("col", None, None),
        P(("frames", "row"), "col", None),
        P(("frames", "row"), "col", None),
        P(("frames", "row"), "col"),
    )
    return jax.shard_map(
        on_device,
        mesh=mesh,
        in_specs=placed,
        out_specs=P(("frames", "row"), "col"),
        check_vma=False,
    )
```

```python
import functools
import math

import jax
import jax.numpy as jnp
from jax import lax
from jax.experimental import pallas as pl
from jax.experimental.pallas import tpu as pltpu
from jax.sharding import PartitionSpec as P

BLUR_HALF = 8
BLUR_SIGMA = 4.0
HALF = 16
RIM = HALF + BLUR_HALF
STRIP = 32
CB = 176
NB = 3
MAIN = 224
EDGE_IN = 80
EDGE_OUT = 48
RIGHT_AT = 56
HALF_STRIP = STRIP + 16
SPARE = 16
GROUP = 1
WIDE = 640
SLOTS = 16
F32 = jnp.float32
BF16 = jnp.bfloat16
VMEM = pl.BlockSpec(memory_space=pltpu.VMEM)
SMEM = pl.BlockSpec(memory_space=pltpu.SMEM)
HBM = pl.BlockSpec(memory_space=pltpu.HBM)
PARAMS = pltpu.CompilerParams(vmem_limit_bytes=16 * 1024 * 1024)


def dot_nt(a, b):
    return lax.dot_general(a, b, (((1,), (1,)), ((), ())), preferred_element_type=F32)


def dot_nn(a, b):
    return lax.dot_general(a, b, (((1,), (0,)), ((), ())), preferred_element_type=F32)


def join(strip):
    halves = [strip[0:HALF_STRIP, :], strip[HALF_STRIP : 2 * HALF_STRIP, :]]
    return jnp.concatenate(halves, axis=1).astype(F32)


def eye(rows, cols, shift):
    at = lax.broadcasted_iota(jnp.int32, (rows, cols), 1) - lax.broadcasted_iota(jnp.int32, (rows, cols), 0)
    return jnp.where(at == shift, 1.0, 0.0).astype(BF16)


def sides(axis, first_swap, second_swap):
    index, count = lax.axis_index(axis), lax.axis_size(axis)
    even = lax.rem(index, 2) == 0
    lower = jnp.where(even, second_swap, first_swap)
    upper = jnp.where(even, first_swap, second_swap)
    return jnp.where(index > 0, lower, 0.0), jnp.where(index < count - 1, upper, 0.0)


def prep_kernel(
    mask, ids, slots, count, across, down, library, to_first, to_second, block, taps, ends, a_ids, a_slots, sems
):
    rows, cols = mask.shape
    copies = [
        pltpu.make_async_copy(mask.at[:, 0:128], ends.at[0], sems.at[0]),
        pltpu.make_async_copy(mask.at[:, cols - 128 : cols], ends.at[1], sems.at[1]),
        pltpu.make_async_copy(ids, a_ids, sems.at[2]),
        pltpu.make_async_copy(slots, a_slots, sems.at[3]),
        pltpu.make_async_copy(across, taps.at[0], sems.at[4]),
        pltpu.make_async_copy(down, taps.at[1], sems.at[5]),
        pltpu.make_async_copy(library, block.at[SPARE:], sems.at[6]),
    ]
    for copy in copies:
        copy.start()
    for copy in copies[2:4]:
        copy.wait()
    line = lax.broadcasted_iota(jnp.int32, (16, 128), 0)
    lane = lax.broadcasted_iota(jnp.int32, (16, 128), 1)

    def spread(x):
        x = x.astype(F32)
        x = jnp.concatenate([x, jnp.zeros((1, 128 - x.shape[1]), F32)], axis=1)
        return jnp.broadcast_to(x, (16, 128))

    table = jnp.where(line == 1, spread(a_slots[0]), jnp.broadcast_to(count[...].astype(F32), (16, 128)))
    table = jnp.where(line == 0, spread(a_ids[0]), table)
    width = jnp.where(line == 2, 1, ids.shape[2])
    table = jnp.where((lane < width) & (line < 3), table, 0.0).astype(BF16)
    for strip in (to_first, to_second):
        strip[STRIP:HALF_STRIP, :] = table
        strip[HALF_STRIP + STRIP : 2 * HALF_STRIP, :] = jnp.zeros((16, 128), BF16)
    block[0:SPARE, :] = jnp.zeros((SPARE, 128), BF16)
    to_second[2 * HALF_STRIP :, :] = jnp.zeros((128 - 2 * HALF_STRIP, 128), BF16)
    even = lax.rem(lax.axis_index("col"), 2) == 0
    copies[0].wait()
    first = dot_nt(eye(STRIP, 128, 0), ends[0].astype(F32).astype(BF16))
    copies[1].wait()
    last = dot_nt(eye(STRIP, 128, 128 - STRIP), ends[1].astype(F32).astype(BF16))
    for strip, part in ((to_first, jnp.where(even, last, first)), (to_second, jnp.where(even, first, last))):
        strip[0:STRIP, :] = part[:, 0:128].astype(BF16)
        strip[HALF_STRIP : HALF_STRIP + STRIP, :] = part[:, 128:256].astype(BF16)
    for copy in copies[4:]:
        copy.wait()


def mid_kernel(mask, from_first, from_second, own, to_first, to_second):
    rows, cols = mask.shape
    left, right = sides("col", join(from_first), join(from_second))
    tables = jnp.concatenate(
        [left[STRIP:, 0:128], own[STRIP:HALF_STRIP, :].astype(F32), right[STRIP:, 0:128], jnp.zeros((16, 256), F32)],
        axis=1,
    ).astype(BF16)
    fill = jnp.zeros((128 - STRIP, 128), F32)
    strips = []
    for i in range(2):
        at = 0 if i == 0 else rows - 128
        pick = eye(STRIP, 128, 0 if i == 0 else 128 - STRIP)

        def turned(strip):
            return dot_nt(pick, jnp.concatenate([strip[0:STRIP, at : at + 128], fill], axis=0).astype(BF16))

        parts = [turned(left)[:, STRIP - RIM : STRIP], mask[(rows - STRIP) * i : (rows - STRIP) * i + STRIP, :].astype(F32), turned(right)[:, 0 : WIDE - RIM - cols]]
        strips.append(jnp.concatenate(parts, axis=1))
    even = lax.rem(lax.axis_index("row"), 2) == 0
    to_first[0:STRIP, :] = jnp.where(even, strips[1], strips[0]).astype(BF16)
    to_second[0:STRIP, :] = jnp.where(even, strips[0], strips[1]).astype(BF16)
    to_first[STRIP:, :] = tables
    to_second[STRIP:, :] = tables


def blur_matrix(shape, axis, start=0):
    lag = lax.broadcasted_iota(jnp.int32, shape, axis) - lax.broadcasted_iota(jnp.int32, shape, 1 - axis) - start
    total = sum(math.exp(-(t * t) / (2 * BLUR_SIGMA**2)) for t in range(-BLUR_HALF, BLUR_HALF + 1))
    off = (lag - BLUR_HALF).astype(F32)
    g = jnp.exp(-off * off / (2.0 * BLUR_SIGMA * BLUR_SIGMA)) * (1.0 / total)
    g = jnp.where((lag >= 0) & (lag <= 2 * BLUR_HALF), g, 0.0)
    high = g.astype(BF16)
    return high, (g - high.astype(F32)).astype(BF16)


def own_kernel(mask, taps, windows, ahead, back, g_row, g_far, g_col):
    rows, cols = mask.shape
    full = jnp.concatenate(
        [jnp.zeros((rows, RIM), F32), mask[...].astype(F32), jnp.zeros((rows, WIDE - RIM - cols), F32)], axis=1
    )
    for b in range(NB):
        windows[b] = full[:, CB * b : CB * b + 256]
    kernels, _, count = taps.shape[1:]
    flip = lax.broadcasted_iota(jnp.int32, (128, 128), 0) + lax.broadcasted_iota(jnp.int32, (128, 128), 1)
    flip = jnp.where(flip % 128 == 0, 1.0, 0.0).astype(BF16)
    ahead[...] = jnp.zeros(ahead.shape, F32)
    back[...] = jnp.zeros(back.shape, F32)
    for k in range(kernels):
        ahead[k, 0:2, 0:count] = taps[0, k].astype(F32)
        back[k, 0:2, 0:count] = taps[1, k].astype(F32)
    back[...] = dot_nn(back[...].reshape(kernels * 8, 128).astype(BF16), flip).reshape(kernels, 8, 128)
    g_row[0:128], g_row[128:256] = blur_matrix((128, 256), 1)
    g_far[0:128], g_far[128:256] = blur_matrix((128, 256), 1, 16 - BLUR_HALF)
    g_col[:, 0:128], g_col[:, 128:256] = blur_matrix((256, 128), 0)


def socs_kernel(
    entries,
    per,
    empty,
    weights,
    windows,
    row_first,
    row_second,
    col_first,
    col_second,
    own,
    ahead,
    back,
    acc,
    images,
    x_win,
    scale,
    sem,
    *scratch,
):
    across = scratch[0:2]
    down = scratch[2:4]
    first = scratch[4:6]
    groups = ahead.shape[0] // GROUP
    fetch = pltpu.make_async_copy(weights, scale, sem)
    fetch.start()
    above, below = sides("row", row_first[...].astype(F32), row_second[...].astype(F32))
    left, right = sides("col", join(col_first), join(col_second))
    rows = windows.shape[1]
    turned = jnp.concatenate(
        [
            left[STRIP - RIM : STRIP],
            jnp.zeros((128 - RIM + RIGHT_AT, rows), F32),
            right[0:RIM],
            jnp.zeros((128 - RIM - RIGHT_AT, rows), F32),
        ],
        axis=0,
    )
    turned = dot_nt(eye(rows, rows, 0), turned.astype(BF16))
    left, right = left[STRIP:, 0:128], right[STRIP:, 0:128]
    upper_rows = above[STRIP - RIM : STRIP]
    lower_rows = below[0:RIM]
    edge_rows = []
    for b in range(NB):
        lanes = slice(CB * b, CB * b + 256)
        part = windows[b]
        if b == 0:
            part = jnp.concatenate([part[:, 0:128] + turned[:, 0:128], part[:, 128:256]], axis=1)
        if b == NB - 1:
            part = jnp.concatenate([part[:, 0:128], part[:, 128:256] + turned[:, 128:256]], axis=1)
        x_win[b] = jnp.concatenate([upper_rows[:, lanes], part[0 : 256 - RIM]], axis=0).astype(BF16)
        edge_rows += [part[MAIN - RIM :], lower_rows[:, lanes]]
    edge_rows.append(jnp.zeros((256 - NB * EDGE_IN, 256), F32))
    x_win[NB] = jnp.concatenate(edge_rows, axis=0).astype(BF16)
    for s in range(2):
        for q in range(2 * GROUP):
            across[s][q, 0:96, 128:256] = jnp.zeros((96, 128), BF16)
            across[s][q, 128:CB, 0:128] = jnp.zeros((CB - 128, 128), BF16)
            down[s][q, 0:128, 128:256] = jnp.zeros((128, 128), BF16)
            down[s][q, 160:256, 0:128] = jnp.zeros((96, 128), BF16)

    slot = lax.broadcasted_iota(jnp.int32, (SLOTS, 128), 0).astype(F32)
    lane = lax.broadcasted_iota(jnp.int32, (SLOTS, 128), 1)
    found = jnp.zeros((SLOTS, 128), F32)
    col = lax.axis_index("col")
    tables = [above[STRIP:, 128 * t : 128 * t + 128] for t in range(3)]
    tables += [left, own[STRIP:HALF_STRIP, :].astype(F32), right]
    tables += [below[STRIP:, 128 * t : 128 * t + 128] for t in range(3)]
    for t, table in enumerate(tables):
        live = lane.astype(F32) < table[2:3, 0:1]
        hit = live & (table[1:2] == slot) & (lane < entries)
        image = jnp.sum(jnp.where(hit, table[0:1] + 1.0, 0.0), axis=1, keepdims=True)
        found = jnp.where(lane == t, image, found)
    cell = found.astype(jnp.int32) - 1
    images[...] = jnp.where(cell >= 0, ((cell // per) ^ col) * per + cell % per, empty)

    row = lax.broadcasted_iota(jnp.int32, (32, 128), 0)
    lane = lax.broadcasted_iota(jnp.int32, (32, 128), 1)
    low = lane >= row + 96

    def cycled(x):
        return pltpu.roll(jnp.broadcast_to(x, (128, 128)), 0, 1, stride=1, stride_axis=0)

    def build_across(m, s):
        for q in range(2 * GROUP):
            cyc = cycled(ahead[GROUP * m + q // 2, q % 2 : q % 2 + 1, :])
            head = cyc[0:96].astype(BF16)
            tail = cyc[96:128]
            over = jnp.where(low, 0.0, tail)
            across[s][q, 0:96, 0:128] = head
            across[s][q, 128:CB, 128:256] = head[0 : CB - 128]
            across[s][q, 96:128, 0:128] = jnp.where(low, tail, 0.0).astype(BF16)
            across[s][q, 96:128, 128:256] = over.astype(BF16)

    def build_down(m, s):
        for q in range(2 * GROUP):
            cyc = cycled(back[GROUP * m + q // 2, q % 2 : q % 2 + 1, :])
            head = cyc[0:32]
            over = jnp.where(low, head, 0.0).astype(BF16)
            head = jnp.where(low, 0.0, head)
            same = jnp.concatenate([head, cyc[32:128]], axis=0).astype(BF16)
            down[s][q, 0:128, 0:128] = same
            down[s][q, 128:256, 128:256] = same
            down[s][q, 128:160, 0:128] = over

    def pass_one(s):
        taps = across[s][...].reshape(2 * GROUP * CB, 256)
        for j in range(NB + 1):
            part = dot_nt(taps, x_win[j]).astype(BF16)
            for q in range(2 * GROUP):
                first[s][q, j] = part[q * CB : (q + 1) * CB]

    def pass_two(m, s):
        for q in range(2 * GROUP):
            second = dot_nn(first[s][q].reshape((NB + 1) * CB, 256), down[s][q])
            part = (scale[GROUP * m + q // 2] * (second * second)).reshape(acc.shape)
            acc[...] = part if m == 0 and q == 0 else acc[...] + part

    def stage(m, s):
        pass_one(s)
        build_down(m, s)
        if m + 1 < groups:
            build_across(m + 1, 1 - s)
        pass_two(m - 1, 1 - s)

    build_across(0, 0)
    pass_one(0)
    build_down(0, 0)
    build_across(1, 1)
    fetch.wait()

    for m in range(1, groups):
        stage(m, m % 2)
    pass_two(groups - 1, (groups - 1) % 2)


def rows_kernel(n_row, n_col, acc, g_row, out, flat):
    rows = out.shape[0]
    cols = CB * NB - 2 * BLUR_HALF
    row, col = lax.axis_index("row"), lax.axis_index("col")
    at_row = lax.broadcasted_iota(jnp.int32, (8, 384), 1) - BLUR_HALF
    row_ok = ((row > 0) | (at_row >= 0)) & ((row < n_row - 1) | (at_row < rows))
    row_ok = jnp.where(row_ok, 1.0, 0.0)
    for b in range(NB):
        edge = acc[NB, :, EDGE_IN * b : EDGE_IN * b + EDGE_OUT]
        part = jnp.concatenate(
            [acc[b, :, 0:MAIN], edge, jnp.zeros((CB, 384 - MAIN - EDGE_OUT), F32)], axis=1
        )
        part = part * row_ok[0:1]
        if b == 0:
            part = jnp.concatenate([jnp.where(col > 0, part[0:8], 0.0), part[8:]], axis=0)
        if b == NB - 1:
            part = jnp.concatenate([part[0 : CB - 8], jnp.where(col < n_col - 1, part[CB - 8 :], 0.0)], axis=0)
        flat[b * CB : (b + 1) * CB, :] = part.astype(BF16)
    flat[NB * CB :, :] = jnp.zeros((flat.shape[0] - NB * CB, 384), BF16)

    for i in range(rows // 128):
        part = dot_nt(g_row[...], flat[:, 128 * i : 128 * i + 256])
        out[128 * i : 128 * i + 128, :] = part[0:128] + part[128:]


def final_kernel(images, blurred_rows, g_far, g_col, *rest):
    shards = rest[:-4]
    out, cells, placed, blurred = rest[-4:]
    per = (cells.shape[0] - 1) // len(shards)
    rows, cols = out.shape
    table = images[...]
    for i, shard in enumerate(shards):
        rows_of = shard.shape[0] - per * 64
        cells[i * per : (i + 1) * per] = shard[rows_of:, :].reshape(per, 64, 128)
    cells[len(shards) * per] = jnp.zeros((64, 128), BF16)

    slot_rows, slot_cols = rows // 64, cols // 128
    for i in range(-1, slot_rows + 1):
        for j in range(-1, slot_cols + 1):
            ti = 0 if i < 0 else (2 if i == slot_rows else 1)
            tj = 0 if j < 0 else (2 if j == slot_cols else 1)
            image = table[(i % slot_rows) * slot_cols + j % slot_cols, 3 * ti + tj]
            lanes = slice(128 + 128 * j, 256 + 128 * j)
            if i < 0:
                placed[0:16, lanes] = cells[image, 48:64, :]
            elif i == slot_rows:
                placed[16 + rows : 32 + rows, lanes] = cells[image, 0:16, :]
            else:
                placed[16 + 64 * i : 80 + 64 * i, lanes] = cells[image]
    placed[32 + rows :, :] = jnp.zeros((placed.shape[0] - 32 - rows, placed.shape[1]), BF16)

    for i in range(rows // 128):
        part = blurred_rows[128 * i : 128 * i + 128, :]
        cell = dot_nn(g_far[...], placed[128 * i : 128 * i + 256, :])
        cell = cell[0:128] + cell[128:]
        part += cell[:, 128 - BLUR_HALF : 128 - BLUR_HALF + part.shape[1]]
        high = part.astype(BF16)
        blurred[0, 128 * i : 128 * i + 128, :] = high
        blurred[1, 128 * i : 128 * i + 128, :] = (part - high.astype(F32)).astype(BF16)
    count = cols // 128
    stacked = [
        jnp.concatenate([blurred[p, :, 128 * j : 128 * j + 256] for j in range(count)], axis=0) for p in range(2)
    ]
    part = dot_nn(stacked[0], g_col[...])
    part = part[:, 0:128] + part[:, 128:] + dot_nn(stacked[1], g_col[:, 0:128])
    for j in range(count):
        out[:, 128 * j : 128 * j + 128] = part[rows * j : rows * j + rows]


def shape(dims, dtype):
    return jax.ShapeDtypeStruct(dims, dtype)


def on_device(
    mask_pixels, across_taps, down_taps, kernel_weights, library, cell_ids, cell_slots, cell_count
):
    rows, cols = mask_pixels.shape
    kernels = across_taps.shape[0]
    entries = cell_ids.shape[-1]
    per = library.shape[0]
    n_row, n_col = lax.axis_size("row"), lax.axis_size("col")
    library = library.reshape(per * 64, 128)
    in_hbm = lambda x: pltpu.with_memory_space_constraint(x, pltpu.HBM)
    mask_hbm = in_hbm(mask_pixels)

    to_first, to_second, block, taps = pl.pallas_call(
        prep_kernel,
        out_shape=(
            shape((2 * HALF_STRIP, 128), BF16),
            shape((128, 128), BF16),
            shape((SPARE + per * 64, 128), BF16),
            shape((2,) + across_taps.shape, BF16),
        ),
        in_specs=[HBM] * 3 + [VMEM] + [HBM] * 3,
        out_specs=(VMEM,) * 4,
        scratch_shapes=[
            pltpu.VMEM((2, rows, 128), jnp.int32),
            pltpu.VMEM(cell_ids.shape, jnp.int32),
            pltpu.VMEM(cell_slots.shape, jnp.int32),
            pltpu.SemaphoreType.DMA((7,)),
        ],
        compiler_params=PARAMS,
        name="prep",
    )(mask_hbm, in_hbm(cell_ids), in_hbm(cell_slots), cell_count, in_hbm(across_taps), in_hbm(down_taps), in_hbm(library))

    def swaps(n):
        rounds = []
        for start in (0, 1):
            pairs = [(i, (i + 1) % n) for i in range(start, n, 2)]
            rounds.append(pairs + [(b, a) for a, b in pairs])
        return rounds

    second = []
    for r in range(n_row):
        second += [(r * n_col + a, r * n_col + b) for a, b in swaps(n_col)[1] if abs(a - b) == 1]
        second += [(r * n_col + a, (r ^ 1) * n_col + a) for a in (0, n_col - 1)]

    col_second = lax.ppermute(to_second, ("row", "col"), second)
    col_first = lax.ppermute(to_first, "col", swaps(n_col)[0])

    to_above, to_below = pl.pallas_call(
        mid_kernel,
        out_shape=(shape((STRIP + 16, WIDE), BF16),) * 2,
        in_specs=[VMEM] * 4,
        out_specs=(VMEM,) * 2,
        compiler_params=PARAMS,
        name="mid",
    )(mask_pixels, col_first, col_second, to_first)
    late, to_above, to_below = lax.optimization_barrier((library, to_above, to_below))
    blocks = {0: library}
    for d in sorted(range(1, n_col), key=lambda d: (d == n_col - 1, -(d & -d))):
        part = late if d == n_col - 1 else block
        blocks[d] = lax.ppermute(part, "col", [(i, i ^ d) for i in range(n_col)])
    shards = [blocks[d] for d in range(n_col)]
    row_first, row_second = (
        lax.ppermute(x, "row", pairs) for x, pairs in zip((to_above, to_below), swaps(n_row))
    )

    windows, ahead, back, g_row, g_far, g_col = pl.pallas_call(
        own_kernel,
        out_shape=(
            shape((NB, rows, 256), F32),
            shape((kernels, 8, 128), F32),
            shape((kernels, 8, 128), F32),
            shape((256, 256), BF16),
            shape((256, 256), BF16),
            shape((256, 256), BF16),
        ),
        in_specs=[VMEM] * 2,
        out_specs=(VMEM,) * 6,
        compiler_params=PARAMS,
        cost_estimate=pl.CostEstimate(flops=10**6, bytes_accessed=10**6, transcendentals=0),
        name="own",
    )(mask_pixels, taps)

    acc, images = pl.pallas_call(
        functools.partial(socs_kernel, entries, per, n_col * per),
        out_shape=(shape((NB + 1, CB, 256), F32), shape((SLOTS, 128), jnp.int32)),
        in_specs=[HBM] + [VMEM] * 8,
        out_specs=(VMEM,) * 2,
        scratch_shapes=[
            pltpu.VMEM((NB + 1, 256, 256), BF16),
            pltpu.SMEM(kernel_weights.shape, F32),
            pltpu.SemaphoreType.DMA,
        ]
        + [pltpu.VMEM((2 * GROUP, CB, 256), BF16)] * 2
        + [pltpu.VMEM((2 * GROUP, 256, 256), BF16)] * 2
        + [pltpu.VMEM((2 * GROUP, NB + 1, CB, 256), BF16)] * 2,
        compiler_params=PARAMS,
        cost_estimate=pl.CostEstimate(flops=75 * 10**7, bytes_accessed=10**5, transcendentals=0),
        name="socs",
    )(in_hbm(kernel_weights), windows, row_first, row_second, col_first, col_second, to_first, ahead, back)

    blurred_rows = pl.pallas_call(
        functools.partial(rows_kernel, n_row, n_col),
        out_shape=shape((rows, WIDE), F32),
        in_specs=[VMEM] * 2,
        out_specs=VMEM,
        scratch_shapes=[pltpu.VMEM((WIDE, 384), BF16)],
        compiler_params=PARAMS,
        cost_estimate=pl.CostEstimate(flops=10**6, bytes_accessed=10**5, transcendentals=0),
        name="rows",
    )(acc, g_row)

    return pl.pallas_call(
        final_kernel,
        out_shape=shape((rows, cols), F32),
        in_specs=[VMEM] * (4 + n_col),
        out_specs=VMEM,
        scratch_shapes=[
            pltpu.VMEM((n_col * per + 1, 64, 128), BF16),
            pltpu.VMEM((384, cols + 256), BF16),
            pltpu.VMEM((2, rows, WIDE), BF16),
        ],
        compiler_params=PARAMS,
        name="final",
    )(images, blurred_rows, g_far, g_col, *shards)


def solution(mesh):
    placed = (
        P(("frames", "row"), "col"),
        P(),
        P(),
        P(),
        P("col", None, None),
        P(("frames", "row"), "col", None),
        P(("frames", "row"), "col", None),
        P(("frames", "row"), "col"),
    )
    return jax.shard_map(
        on_device,
        mesh=mesh,
        in_specs=placed,
        out_specs=P(("frames", "row"), "col"),
        check_vma=False,
    )
```

```python
import functools
import math

import jax
import jax.numpy as jnp
from jax import lax
from jax.experimental import pallas as pl
from jax.experimental.pallas import tpu as pltpu
from jax.sharding import PartitionSpec as P

BLUR_HALF = 8
BLUR_SIGMA = 4.0
HALF = 16
RIM = HALF + BLUR_HALF
STRIP = 32
CB = 176
NB = 3
MAIN = 224
EDGE_IN = 80
EDGE_OUT = 48
RIGHT_AT = 56
HALF_STRIP = STRIP + 16
SPARE = 16
GROUP = 2
WIDE = 640
SLOTS = 16
F32 = jnp.float32
BF16 = jnp.bfloat16
VMEM = pl.BlockSpec(memory_space=pltpu.VMEM)
SMEM = pl.BlockSpec(memory_space=pltpu.SMEM)
HBM = pl.BlockSpec(memory_space=pltpu.HBM)
PARAMS = pltpu.CompilerParams(vmem_limit_bytes=16 * 1024 * 1024)


def dot_nt(a, b):
    return lax.dot_general(a, b, (((1,), (1,)), ((), ())), preferred_element_type=F32)


def dot_nn(a, b):
    return lax.dot_general(a, b, (((1,), (0,)), ((), ())), preferred_element_type=F32)


def join(strip):
    halves = [strip[0:HALF_STRIP, :], strip[HALF_STRIP : 2 * HALF_STRIP, :]]
    return jnp.concatenate(halves, axis=1).astype(F32)


def eye(rows, cols, shift):
    at = lax.broadcasted_iota(jnp.int32, (rows, cols), 1) - lax.broadcasted_iota(jnp.int32, (rows, cols), 0)
    return jnp.where(at == shift, 1.0, 0.0).astype(BF16)


def sides(axis, first_swap, second_swap):
    index, count = lax.axis_index(axis), lax.axis_size(axis)
    even = lax.rem(index, 2) == 0
    lower = jnp.where(even, second_swap, first_swap)
    upper = jnp.where(even, first_swap, second_swap)
    return jnp.where(index > 0, lower, 0.0), jnp.where(index < count - 1, upper, 0.0)


def prep_kernel(
    mask, ids, slots, count, across, down, library, to_first, to_second, block, taps, ends, a_ids, a_slots, sems
):
    rows, cols = mask.shape
    copies = [
        pltpu.make_async_copy(mask.at[:, 0:128], ends.at[0], sems.at[0]),
        pltpu.make_async_copy(mask.at[:, cols - 128 : cols], ends.at[1], sems.at[1]),
        pltpu.make_async_copy(ids, a_ids, sems.at[2]),
        pltpu.make_async_copy(slots, a_slots, sems.at[3]),
        pltpu.make_async_copy(across, taps.at[0], sems.at[4]),
        pltpu.make_async_copy(down, taps.at[1], sems.at[5]),
        pltpu.make_async_copy(library, block.at[SPARE:], sems.at[6]),
    ]
    for copy in copies:
        copy.start()
    for copy in copies[2:4]:
        copy.wait()
    line = lax.broadcasted_iota(jnp.int32, (16, 128), 0)
    lane = lax.broadcasted_iota(jnp.int32, (16, 128), 1)

    def spread(x):
        x = x.astype(F32)
        x = jnp.concatenate([x, jnp.zeros((1, 128 - x.shape[1]), F32)], axis=1)
        return jnp.broadcast_to(x, (16, 128))

    table = jnp.where(line == 1, spread(a_slots[0]), jnp.broadcast_to(count[...].astype(F32), (16, 128)))
    table = jnp.where(line == 0, spread(a_ids[0]), table)
    width = jnp.where(line == 2, 1, ids.shape[2])
    table = jnp.where((lane < width) & (line < 3), table, 0.0).astype(BF16)
    for strip in (to_first, to_second):
        strip[STRIP:HALF_STRIP, :] = table
        strip[HALF_STRIP + STRIP : 2 * HALF_STRIP, :] = jnp.zeros((16, 128), BF16)
    block[0:SPARE, :] = jnp.zeros((SPARE, 128), BF16)
    to_second[2 * HALF_STRIP :, :] = jnp.zeros((128 - 2 * HALF_STRIP, 128), BF16)
    even = lax.rem(lax.axis_index("col"), 2) == 0
    copies[0].wait()
    first = dot_nt(eye(STRIP, 128, 0), ends[0].astype(F32).astype(BF16))
    copies[1].wait()
    last = dot_nt(eye(STRIP, 128, 128 - STRIP), ends[1].astype(F32).astype(BF16))
    for strip, part in ((to_first, jnp.where(even, last, first)), (to_second, jnp.where(even, first, last))):
        strip[0:STRIP, :] = part[:, 0:128].astype(BF16)
        strip[HALF_STRIP : HALF_STRIP + STRIP, :] = part[:, 128:256].astype(BF16)
    for copy in copies[4:]:
        copy.wait()


def mid_kernel(mask, from_first, from_second, own, to_first, to_second):
    rows, cols = mask.shape
    left, right = sides("col", join(from_first), join(from_second))
    tables = jnp.concatenate(
        [left[STRIP:, 0:128], own[STRIP:HALF_STRIP, :].astype(F32), right[STRIP:, 0:128], jnp.zeros((16, 256), F32)],
        axis=1,
    ).astype(BF16)
    fill = jnp.zeros((128 - STRIP, 128), F32)
    strips = []
    for i in range(2):
        at = 0 if i == 0 else rows - 128
        pick = eye(STRIP, 128, 0 if i == 0 else 128 - STRIP)

        def turned(strip):
            return dot_nt(pick, jnp.concatenate([strip[0:STRIP, at : at + 128], fill], axis=0).astype(BF16))

        parts = [turned(left)[:, STRIP - RIM : STRIP], mask[(rows - STRIP) * i : (rows - STRIP) * i + STRIP, :].astype(F32), turned(right)[:, 0 : WIDE - RIM - cols]]
        strips.append(jnp.concatenate(parts, axis=1))
    even = lax.rem(lax.axis_index("row"), 2) == 0
    to_first[0:STRIP, :] = jnp.where(even, strips[1], strips[0]).astype(BF16)
    to_second[0:STRIP, :] = jnp.where(even, strips[0], strips[1]).astype(BF16)
    to_first[STRIP:, :] = tables
    to_second[STRIP:, :] = tables


def blur_matrix(shape, axis, start=0):
    lag = lax.broadcasted_iota(jnp.int32, shape, axis) - lax.broadcasted_iota(jnp.int32, shape, 1 - axis) - start
    total = sum(math.exp(-(t * t) / (2 * BLUR_SIGMA**2)) for t in range(-BLUR_HALF, BLUR_HALF + 1))
    off = (lag - BLUR_HALF).astype(F32)
    g = jnp.exp(-off * off / (2.0 * BLUR_SIGMA * BLUR_SIGMA)) * (1.0 / total)
    g = jnp.where((lag >= 0) & (lag <= 2 * BLUR_HALF), g, 0.0)
    high = g.astype(BF16)
    return high, (g - high.astype(F32)).astype(BF16)


def own_kernel(mask, taps, windows, ahead, back, g_row, g_far, g_col):
    rows, cols = mask.shape
    full = jnp.concatenate(
        [jnp.zeros((rows, RIM), F32), mask[...].astype(F32), jnp.zeros((rows, WIDE - RIM - cols), F32)], axis=1
    )
    for b in range(NB):
        windows[b] = full[:, CB * b : CB * b + 256]
    kernels, _, count = taps.shape[1:]
    flip = lax.broadcasted_iota(jnp.int32, (128, 128), 0) + lax.broadcasted_iota(jnp.int32, (128, 128), 1)
    flip = jnp.where(flip % 128 == 0, 1.0, 0.0).astype(BF16)
    ahead[...] = jnp.zeros(ahead.shape, F32)
    back[...] = jnp.zeros(back.shape, F32)
    for k in range(kernels):
        ahead[k, 0:2, 0:count] = taps[0, k].astype(F32)
        back[k, 0:2, 0:count] = taps[1, k].astype(F32)
    back[...] = dot_nn(back[...].reshape(kernels * 8, 128).astype(BF16), flip).reshape(kernels, 8, 128)
    g_row[0:128], g_row[128:256] = blur_matrix((128, 256), 1)
    g_far[0:128], g_far[128:256] = blur_matrix((128, 256), 1, 16 - BLUR_HALF)
    g_col[:, 0:128], g_col[:, 128:256] = blur_matrix((256, 128), 0)


def socs_kernel(
    entries,
    per,
    empty,
    weights,
    windows,
    row_first,
    row_second,
    col_first,
    col_second,
    own,
    ahead,
    back,
    acc,
    images,
    x_win,
    scale,
    sem,
    *scratch,
):
    across = scratch[0:2]
    down = scratch[2:4]
    first = scratch[4:6]
    groups = ahead.shape[0] // GROUP
    fetch = pltpu.make_async_copy(weights, scale, sem)
    fetch.start()
    above, below = sides("row", row_first[...].astype(F32), row_second[...].astype(F32))
    left, right = sides("col", join(col_first), join(col_second))
    rows = windows.shape[1]
    turned = jnp.concatenate(
        [
            left[STRIP - RIM : STRIP],
            jnp.zeros((128 - RIM + RIGHT_AT, rows), F32),
            right[0:RIM],
            jnp.zeros((128 - RIM - RIGHT_AT, rows), F32),
        ],
        axis=0,
    )
    turned = dot_nt(eye(rows, rows, 0), turned.astype(BF16))
    left, right = left[STRIP:, 0:128], right[STRIP:, 0:128]
    upper_rows = above[STRIP - RIM : STRIP]
    lower_rows = below[0:RIM]
    edge_rows = []
    for b in range(NB):
        lanes = slice(CB * b, CB * b + 256)
        part = windows[b]
        if b == 0:
            part = jnp.concatenate([part[:, 0:128] + turned[:, 0:128], part[:, 128:256]], axis=1)
        if b == NB - 1:
            part = jnp.concatenate([part[:, 0:128], part[:, 128:256] + turned[:, 128:256]], axis=1)
        x_win[b] = jnp.concatenate([upper_rows[:, lanes], part[0 : 256 - RIM]], axis=0).astype(BF16)
        edge_rows += [part[MAIN - RIM :], lower_rows[:, lanes]]
    edge_rows.append(jnp.zeros((256 - NB * EDGE_IN, 256), F32))
    x_win[NB] = jnp.concatenate(edge_rows, axis=0).astype(BF16)
    for s in range(2):
        for q in range(2 * GROUP):
            across[s][q, 0:96, 128:256] = jnp.zeros((96, 128), BF16)
            across[s][q, 128:CB, 0:128] = jnp.zeros((CB - 128, 128), BF16)
            down[s][q, 0:128, 128:256] = jnp.zeros((128, 128), BF16)
            down[s][q, 160:256, 0:128] = jnp.zeros((96, 128), BF16)

    slot = lax.broadcasted_iota(jnp.int32, (SLOTS, 128), 0).astype(F32)
    lane = lax.broadcasted_iota(jnp.int32, (SLOTS, 128), 1)
    found = jnp.zeros((SLOTS, 128), F32)
    col = lax.axis_index("col")
    tables = [above[STRIP:, 128 * t : 128 * t + 128] for t in range(3)]
    tables += [left, own[STRIP:HALF_STRIP, :].astype(F32), right]
    tables += [below[STRIP:, 128 * t : 128 * t + 128] for t in range(3)]
    for t, table in enumerate(tables):
        live = lane.astype(F32) < table[2:3, 0:1]
        hit = live & (table[1:2] == slot) & (lane < entries)
        image = jnp.sum(jnp.where(hit, table[0:1] + 1.0, 0.0), axis=1, keepdims=True)
        found = jnp.where(lane == t, image, found)
    cell = found.astype(jnp.int32) - 1
    images[...] = jnp.where(cell >= 0, ((cell // per) ^ col) * per + cell % per, empty)

    row = lax.broadcasted_iota(jnp.int32, (32, 128), 0)
    lane = lax.broadcasted_iota(jnp.int32, (32, 128), 1)
    low = lane >= row + 96

    def cycled(x):
        return pltpu.roll(jnp.broadcast_to(x, (128, 128)), 0, 1, stride=1, stride_axis=0)

    def build_across(m, s):
        for q in range(2 * GROUP):
            cyc = cycled(ahead[GROUP * m + q // 2, q % 2 : q % 2 + 1, :])
            head = cyc[0:96].astype(BF16)
            tail = cyc[96:128]
            over = jnp.where(low, 0.0, tail)
            across[s][q, 0:96, 0:128] = head
            across[s][q, 128:CB, 128:256] = head[0 : CB - 128]
            across[s][q, 96:128, 0:128] = jnp.where(low, tail, 0.0).astype(BF16)
            across[s][q, 96:128, 128:256] = over.astype(BF16)

    def build_down(m, s):
        for q in range(2 * GROUP):
            cyc = cycled(back[GROUP * m + q // 2, q % 2 : q % 2 + 1, :])
            head = cyc[0:32]
            over = jnp.where(low, head, 0.0).astype(BF16)
            head = jnp.where(low, 0.0, head)
            same = jnp.concatenate([head, cyc[32:128]], axis=0).astype(BF16)
            down[s][q, 0:128, 0:128] = same
            down[s][q, 128:256, 128:256] = same
            down[s][q, 128:160, 0:128] = over

    def pass_one(s):
        taps = across[s][...].reshape(2 * GROUP * CB, 256)
        for j in range(NB + 1):
            part = dot_nt(taps, x_win[j]).astype(BF16)
            for q in range(2 * GROUP):
                first[s][q, j] = part[q * CB : (q + 1) * CB]

    def pass_two(m, s):
        for q in range(2 * GROUP):
            second = dot_nn(first[s][q].reshape((NB + 1) * CB, 256), down[s][q])
            part = (scale[GROUP * m + q // 2] * (second * second)).reshape(acc.shape)
            acc[...] = part if m == 0 and q == 0 else acc[...] + part

    def stage(m, s):
        pass_one(s)
        build_down(m, s)
        if m + 1 < groups:
            build_across(m + 1, 1 - s)
        pass_two(m - 1, 1 - s)

    build_across(0, 0)
    pass_one(0)
    build_down(0, 0)
    build_across(1, 1)
    fetch.wait()

    for m in range(1, groups):
        stage(m, m % 2)
    pass_two(groups - 1, (groups - 1) % 2)


def rows_kernel(n_row, n_col, acc, g_row, out, flat):
    rows = out.shape[0]
    cols = CB * NB - 2 * BLUR_HALF
    row, col = lax.axis_index("row"), lax.axis_index("col")
    at_row = lax.broadcasted_iota(jnp.int32, (8, 384), 1) - BLUR_HALF
    row_ok = ((row > 0) | (at_row >= 0)) & ((row < n_row - 1) | (at_row < rows))
    row_ok = jnp.where(row_ok, 1.0, 0.0)
    for b in range(NB):
        edge = acc[NB, :, EDGE_IN * b : EDGE_IN * b + EDGE_OUT]
        part = jnp.concatenate(
            [acc[b, :, 0:MAIN], edge, jnp.zeros((CB, 384 - MAIN - EDGE_OUT), F32)], axis=1
        )
        part = part * row_ok[0:1]
        if b == 0:
            part = jnp.concatenate([jnp.where(col > 0, part[0:8], 0.0), part[8:]], axis=0)
        if b == NB - 1:
            part = jnp.concatenate([part[0 : CB - 8], jnp.where(col < n_col - 1, part[CB - 8 :], 0.0)], axis=0)
        flat[b * CB : (b + 1) * CB, :] = part.astype(BF16)
    flat[NB * CB :, :] = jnp.zeros((flat.shape[0] - NB * CB, 384), BF16)

    for i in range(rows // 128):
        part = dot_nt(g_row[...], flat[:, 128 * i : 128 * i + 256])
        out[128 * i : 128 * i + 128, :] = part[0:128] + part[128:]


def final_kernel(images, blurred_rows, g_far, g_col, *rest):
    shards = rest[:-4]
    out, cells, placed, blurred = rest[-4:]
    per = (cells.shape[0] - 1) // len(shards)
    rows, cols = out.shape
    table = images[...]
    for i, shard in enumerate(shards):
        rows_of = shard.shape[0] - per * 64
        cells[i * per : (i + 1) * per] = shard[rows_of:, :].reshape(per, 64, 128)
    cells[len(shards) * per] = jnp.zeros((64, 128), BF16)

    slot_rows, slot_cols = rows // 64, cols // 128
    for i in range(-1, slot_rows + 1):
        for j in range(-1, slot_cols + 1):
            ti = 0 if i < 0 else (2 if i == slot_rows else 1)
            tj = 0 if j < 0 else (2 if j == slot_cols else 1)
            image = table[(i % slot_rows) * slot_cols + j % slot_cols, 3 * ti + tj]
            lanes = slice(128 + 128 * j, 256 + 128 * j)
            if i < 0:
                placed[0:16, lanes] = cells[image, 48:64, :]
            elif i == slot_rows:
                placed[16 + rows : 32 + rows, lanes] = cells[image, 0:16, :]
            else:
                placed[16 + 64 * i : 80 + 64 * i, lanes] = cells[image]
    placed[32 + rows :, :] = jnp.zeros((placed.shape[0] - 32 - rows, placed.shape[1]), BF16)

    for i in range(rows // 128):
        part = blurred_rows[128 * i : 128 * i + 128, :]
        cell = dot_nn(g_far[...], placed[128 * i : 128 * i + 256, :])
        cell = cell[0:128] + cell[128:]
        part += cell[:, 128 - BLUR_HALF : 128 - BLUR_HALF + part.shape[1]]
        high = part.astype(BF16)
        blurred[0, 128 * i : 128 * i + 128, :] = high
        blurred[1, 128 * i : 128 * i + 128, :] = (part - high.astype(F32)).astype(BF16)
    count = cols // 128
    stacked = [
        jnp.concatenate([blurred[p, :, 128 * j : 128 * j + 256] for j in range(count)], axis=0) for p in range(2)
    ]
    part = dot_nn(stacked[0], g_col[...])
    part = part[:, 0:128] + part[:, 128:] + dot_nn(stacked[1], g_col[:, 0:128])
    for j in range(count):
        out[:, 128 * j : 128 * j + 128] = part[rows * j : rows * j + rows]


def shape(dims, dtype):
    return jax.ShapeDtypeStruct(dims, dtype)


def on_device(
    mask_pixels, across_taps, down_taps, kernel_weights, library, cell_ids, cell_slots, cell_count
):
    rows, cols = mask_pixels.shape
    kernels = across_taps.shape[0]
    entries = cell_ids.shape[-1]
    per = library.shape[0]
    n_row, n_col = lax.axis_size("row"), lax.axis_size("col")
    library = library.reshape(per * 64, 128)
    in_hbm = lambda x: pltpu.with_memory_space_constraint(x, pltpu.HBM)
    mask_hbm = in_hbm(mask_pixels)

    to_first, to_second, block, taps = pl.pallas_call(
        prep_kernel,
        out_shape=(
            shape((2 * HALF_STRIP, 128), BF16),
            shape((128, 128), BF16),
            shape((SPARE + per * 64, 128), BF16),
            shape((2,) + across_taps.shape, BF16),
        ),
        in_specs=[HBM] * 3 + [VMEM] + [HBM] * 3,
        out_specs=(VMEM,) * 4,
        scratch_shapes=[
            pltpu.VMEM((2, rows, 128), jnp.int32),
            pltpu.VMEM(cell_ids.shape, jnp.int32),
            pltpu.VMEM(cell_slots.shape, jnp.int32),
            pltpu.SemaphoreType.DMA((7,)),
        ],
        compiler_params=PARAMS,
        name="prep",
    )(mask_hbm, in_hbm(cell_ids), in_hbm(cell_slots), cell_count, in_hbm(across_taps), in_hbm(down_taps), in_hbm(library))

    def swaps(n):
        rounds = []
        for start in (0, 1):
            pairs = [(i, (i + 1) % n) for i in range(start, n, 2)]
            rounds.append(pairs + [(b, a) for a, b in pairs])
        return rounds

    second = []
    for r in range(n_row):
        second += [(r * n_col + a, r * n_col + b) for a, b in swaps(n_col)[1] if abs(a - b) == 1]
        second += [(r * n_col + a, (r ^ 1) * n_col + a) for a in (0, n_col - 1)]

    col_second = lax.ppermute(to_second, ("row", "col"), second)
    col_first = lax.ppermute(to_first, "col", swaps(n_col)[0])

    to_above, to_below = pl.pallas_call(
        mid_kernel,
        out_shape=(shape((STRIP + 16, WIDE), BF16),) * 2,
        in_specs=[VMEM] * 4,
        out_specs=(VMEM,) * 2,
        compiler_params=PARAMS,
        name="mid",
    )(mask_pixels, col_first, col_second, to_first)
    late, to_above, to_below = lax.optimization_barrier((library, to_above, to_below))
    met = lax.ppermute(kernel_weights, "row", [(i, i ^ 1) for i in range(n_row)])
    block, met = lax.optimization_barrier((block, met))
    blocks = {0: library}
    for d in sorted(range(1, n_col), key=lambda d: (d == n_col - 1, -(d & -d))):
        part = late if d == n_col - 1 else block
        blocks[d] = lax.ppermute(part, "col", [(i, i ^ d) for i in range(n_col)])
    shards = [blocks[d] for d in range(n_col)]
    row_first, row_second = (
        lax.ppermute(x, "row", pairs) for x, pairs in zip((to_above, to_below), swaps(n_row))
    )

    windows, ahead, back, g_row, g_far, g_col = pl.pallas_call(
        own_kernel,
        out_shape=(
            shape((NB, rows, 256), F32),
            shape((kernels, 8, 128), F32),
            shape((kernels, 8, 128), F32),
            shape((256, 256), BF16),
            shape((256, 256), BF16),
            shape((256, 256), BF16),
        ),
        in_specs=[VMEM] * 2,
        out_specs=(VMEM,) * 6,
        compiler_params=PARAMS,
        cost_estimate=pl.CostEstimate(flops=10**6, bytes_accessed=10**6, transcendentals=0),
        name="own",
    )(mask_pixels, taps)

    acc, images = pl.pallas_call(
        functools.partial(socs_kernel, entries, per, n_col * per),
        out_shape=(shape((NB + 1, CB, 256), F32), shape((SLOTS, 128), jnp.int32)),
        in_specs=[pl.BlockSpec(memory_space=pl.ANY)] + [VMEM] * 8,
        out_specs=(VMEM,) * 2,
        scratch_shapes=[
            pltpu.VMEM((NB + 1, 256, 256), BF16),
            pltpu.SMEM(kernel_weights.shape, F32),
            pltpu.SemaphoreType.DMA,
        ]
        + [pltpu.VMEM((2 * GROUP, CB, 256), BF16)] * 2
        + [pltpu.VMEM((2 * GROUP, 256, 256), BF16)] * 2
        + [pltpu.VMEM((2 * GROUP, NB + 1, CB, 256), BF16)] * 2,
        compiler_params=PARAMS,
        cost_estimate=pl.CostEstimate(flops=75 * 10**7, bytes_accessed=10**5, transcendentals=0),
        name="socs",
    )(met, windows, row_first, row_second, col_first, col_second, to_first, ahead, back)

    blurred_rows = pl.pallas_call(
        functools.partial(rows_kernel, n_row, n_col),
        out_shape=shape((rows, WIDE), F32),
        in_specs=[VMEM] * 2,
        out_specs=VMEM,
        scratch_shapes=[pltpu.VMEM((WIDE, 384), BF16)],
        compiler_params=PARAMS,
        cost_estimate=pl.CostEstimate(flops=10**6, bytes_accessed=10**5, transcendentals=0),
        name="rows",
    )(acc, g_row)

    return pl.pallas_call(
        final_kernel,
        out_shape=shape((rows, cols), F32),
        in_specs=[VMEM] * (4 + n_col),
        out_specs=VMEM,
        scratch_shapes=[
            pltpu.VMEM((n_col * per + 1, 64, 128), BF16),
            pltpu.VMEM((384, cols + 256), BF16),
            pltpu.VMEM((2, rows, WIDE), BF16),
        ],
        compiler_params=PARAMS,
        name="final",
    )(images, blurred_rows, g_far, g_col, *shards)


def solution(mesh):
    placed = (
        P(("frames", "row"), "col"),
        P(),
        P(),
        P(),
        P("col", None, None),
        P(("frames", "row"), "col", None),
        P(("frames", "row"), "col", None),
        P(("frames", "row"), "col"),
    )
    return jax.shard_map(
        on_device,
        mesh=mesh,
        in_specs=placed,
        out_specs=P(("frames", "row"), "col"),
        check_vma=False,
    )
```

```python
import functools
import math

import jax
import jax.numpy as jnp
from jax import lax
from jax.experimental import pallas as pl
from jax.experimental.pallas import tpu as pltpu
from jax.sharding import PartitionSpec as P

BLUR_HALF = 8
BLUR_SIGMA = 4.0
HALF = 16
RIM = HALF + BLUR_HALF
STRIP = 32
CB = 176
NB = 3
MAIN = 224
EDGE_IN = 80
EDGE_OUT = 48
RIGHT_AT = 56
HALF_STRIP = STRIP + 16
SPARE = 16
GROUP = 2
WIDE = 640
SLOTS = 16
F32 = jnp.float32
BF16 = jnp.bfloat16
VMEM = pl.BlockSpec(memory_space=pltpu.VMEM)
SMEM = pl.BlockSpec(memory_space=pltpu.SMEM)
HBM = pl.BlockSpec(memory_space=pltpu.HBM)
PARAMS = pltpu.CompilerParams(vmem_limit_bytes=16 * 1024 * 1024)


def dot_nt(a, b):
    return lax.dot_general(a, b, (((1,), (1,)), ((), ())), preferred_element_type=F32)


def dot_nn(a, b):
    return lax.dot_general(a, b, (((1,), (0,)), ((), ())), preferred_element_type=F32)


def join(strip):
    halves = [strip[0:HALF_STRIP, :], strip[HALF_STRIP : 2 * HALF_STRIP, :]]
    return jnp.concatenate(halves, axis=1).astype(F32)


def eye(rows, cols, shift):
    at = lax.broadcasted_iota(jnp.int32, (rows, cols), 1) - lax.broadcasted_iota(jnp.int32, (rows, cols), 0)
    return jnp.where(at == shift, 1.0, 0.0).astype(BF16)


def sides(axis, first_swap, second_swap):
    index, count = lax.axis_index(axis), lax.axis_size(axis)
    even = lax.rem(index, 2) == 0
    lower = jnp.where(even, second_swap, first_swap)
    upper = jnp.where(even, first_swap, second_swap)
    return jnp.where(index > 0, lower, 0.0), jnp.where(index < count - 1, upper, 0.0)


def prep_kernel(
    mask, ids, slots, count, across, down, library, to_first, to_second, block, taps, ends, a_ids, a_slots, sems
):
    rows, cols = mask.shape
    copies = [
        pltpu.make_async_copy(mask.at[:, 0:128], ends.at[0], sems.at[0]),
        pltpu.make_async_copy(mask.at[:, cols - 128 : cols], ends.at[1], sems.at[1]),
        pltpu.make_async_copy(ids, a_ids, sems.at[2]),
        pltpu.make_async_copy(slots, a_slots, sems.at[3]),
        pltpu.make_async_copy(across, taps.at[0], sems.at[4]),
        pltpu.make_async_copy(down, taps.at[1], sems.at[5]),
        pltpu.make_async_copy(library, block.at[SPARE:], sems.at[6]),
    ]
    for copy in copies:
        copy.start()
    for copy in copies[2:4]:
        copy.wait()
    line = lax.broadcasted_iota(jnp.int32, (16, 128), 0)
    lane = lax.broadcasted_iota(jnp.int32, (16, 128), 1)

    def spread(x):
        x = x.astype(F32)
        x = jnp.concatenate([x, jnp.zeros((1, 128 - x.shape[1]), F32)], axis=1)
        return jnp.broadcast_to(x, (16, 128))

    table = jnp.where(line == 1, spread(a_slots[0]), jnp.broadcast_to(count[...].astype(F32), (16, 128)))
    table = jnp.where(line == 0, spread(a_ids[0]), table)
    width = jnp.where(line == 2, 1, ids.shape[2])
    table = jnp.where((lane < width) & (line < 3), table, 0.0).astype(BF16)
    for strip in (to_first, to_second):
        strip[STRIP:HALF_STRIP, :] = table
        strip[HALF_STRIP + STRIP : 2 * HALF_STRIP, :] = jnp.zeros((16, 128), BF16)
    block[0:SPARE, :] = jnp.zeros((SPARE, 128), BF16)
    to_second[2 * HALF_STRIP :, :] = jnp.zeros((128 - 2 * HALF_STRIP, 128), BF16)
    even = lax.rem(lax.axis_index("col"), 2) == 0
    copies[0].wait()
    first = dot_nt(eye(STRIP, 128, 0), ends[0].astype(F32).astype(BF16))
    copies[1].wait()
    last = dot_nt(eye(STRIP, 128, 128 - STRIP), ends[1].astype(F32).astype(BF16))
    for strip, part in ((to_first, jnp.where(even, last, first)), (to_second, jnp.where(even, first, last))):
        strip[0:STRIP, :] = part[:, 0:128].astype(BF16)
        strip[HALF_STRIP : HALF_STRIP + STRIP, :] = part[:, 128:256].astype(BF16)
    for copy in copies[4:]:
        copy.wait()


def mid_kernel(mask, from_first, from_second, own, to_first, to_second):
    rows, cols = mask.shape
    left, right = sides("col", join(from_first), join(from_second))
    tables = jnp.concatenate(
        [left[STRIP:, 0:128], own[STRIP:HALF_STRIP, :].astype(F32), right[STRIP:, 0:128], jnp.zeros((16, 256), F32)],
        axis=1,
    ).astype(BF16)
    fill = jnp.zeros((128 - STRIP, 128), F32)
    strips = []
    for i in range(2):
        at = 0 if i == 0 else rows - 128
        pick = eye(STRIP, 128, 0 if i == 0 else 128 - STRIP)

        def turned(strip):
            return dot_nt(pick, jnp.concatenate([strip[0:STRIP, at : at + 128], fill], axis=0).astype(BF16))

        parts = [turned(left)[:, STRIP - RIM : STRIP], mask[(rows - STRIP) * i : (rows - STRIP) * i + STRIP, :].astype(F32), turned(right)[:, 0 : WIDE - RIM - cols]]
        strips.append(jnp.concatenate(parts, axis=1))
    even = lax.rem(lax.axis_index("row"), 2) == 0
    to_first[0:STRIP, :] = jnp.where(even, strips[1], strips[0]).astype(BF16)
    to_second[0:STRIP, :] = jnp.where(even, strips[0], strips[1]).astype(BF16)
    to_first[STRIP:, :] = tables
    to_second[STRIP:, :] = tables


def blur_matrix(shape, axis, start=0):
    lag = lax.broadcasted_iota(jnp.int32, shape, axis) - lax.broadcasted_iota(jnp.int32, shape, 1 - axis) - start
    total = sum(math.exp(-(t * t) / (2 * BLUR_SIGMA**2)) for t in range(-BLUR_HALF, BLUR_HALF + 1))
    off = (lag - BLUR_HALF).astype(F32)
    g = jnp.exp(-off * off / (2.0 * BLUR_SIGMA * BLUR_SIGMA)) * (1.0 / total)
    g = jnp.where((lag >= 0) & (lag <= 2 * BLUR_HALF), g, 0.0)
    high = g.astype(BF16)
    return high, (g - high.astype(F32)).astype(BF16)


def own_kernel(mask, taps, windows, ahead, back, g_row, g_far, g_col):
    rows, cols = mask.shape
    full = jnp.concatenate(
        [jnp.zeros((rows, RIM), F32), mask[...].astype(F32), jnp.zeros((rows, WIDE - RIM - cols), F32)], axis=1
    )
    for b in range(NB):
        windows[b] = full[:, CB * b : CB * b + 256]
    kernels, _, count = taps.shape[1:]
    flip = lax.broadcasted_iota(jnp.int32, (128, 128), 0) + lax.broadcasted_iota(jnp.int32, (128, 128), 1)
    flip = jnp.where(flip % 128 == 0, 1.0, 0.0).astype(BF16)
    ahead[...] = jnp.zeros(ahead.shape, F32)
    back[...] = jnp.zeros(back.shape, F32)
    for k in range(kernels):
        ahead[k, 0:2, 0:count] = taps[0, k].astype(F32)
        back[k, 0:2, 0:count] = taps[1, k].astype(F32)
    back[...] = dot_nn(back[...].reshape(kernels * 8, 128).astype(BF16), flip).reshape(kernels, 8, 128)
    g_row[0:128], g_row[128:256] = blur_matrix((128, 256), 1)
    g_far[0:128], g_far[128:256] = blur_matrix((128, 256), 1, 16 - BLUR_HALF)
    g_col[:, 0:128], g_col[:, 128:256] = blur_matrix((256, 128), 0)


def socs_kernel(
    entries,
    per,
    empty,
    weights,
    windows,
    row_first,
    row_second,
    col_first,
    col_second,
    own,
    ahead,
    back,
    acc,
    images,
    x_win,
    scale,
    sem,
    *scratch,
):
    across = scratch[0:2]
    down = scratch[2:4]
    first = scratch[4:6]
    groups = ahead.shape[0] // GROUP
    fetch = pltpu.make_async_copy(weights, scale, sem)
    fetch.start()
    above, below = sides("row", row_first[...].astype(F32), row_second[...].astype(F32))
    left, right = sides("col", join(col_first), join(col_second))
    rows = windows.shape[1]
    turned = jnp.concatenate(
        [
            left[STRIP - RIM : STRIP],
            jnp.zeros((128 - RIM + RIGHT_AT, rows), F32),
            right[0:RIM],
            jnp.zeros((128 - RIM - RIGHT_AT, rows), F32),
        ],
        axis=0,
    )
    turned = dot_nt(eye(rows, rows, 0), turned.astype(BF16))
    left, right = left[STRIP:, 0:128], right[STRIP:, 0:128]
    upper_rows = above[STRIP - RIM : STRIP]
    lower_rows = below[0:RIM]
    edge_rows = []
    for b in range(NB):
        lanes = slice(CB * b, CB * b + 256)
        part = windows[b]
        if b == 0:
            part = jnp.concatenate([part[:, 0:128] + turned[:, 0:128], part[:, 128:256]], axis=1)
        if b == NB - 1:
            part = jnp.concatenate([part[:, 0:128], part[:, 128:256] + turned[:, 128:256]], axis=1)
        x_win[b] = jnp.concatenate([upper_rows[:, lanes], part[0 : 256 - RIM]], axis=0).astype(BF16)
        edge_rows += [part[MAIN - RIM :], lower_rows[:, lanes]]
    edge_rows.append(jnp.zeros((256 - NB * EDGE_IN, 256), F32))
    x_win[NB] = jnp.concatenate(edge_rows, axis=0).astype(BF16)
    for s in range(2):
        for q in range(2 * GROUP):
            across[s][q, 0:96, 128:256] = jnp.zeros((96, 128), BF16)
            across[s][q, 128:CB, 0:128] = jnp.zeros((CB - 128, 128), BF16)
            down[s][q, 0:128, 128:256] = jnp.zeros((128, 128), BF16)
            down[s][q, 160:256, 0:128] = jnp.zeros((96, 128), BF16)

    slot = lax.broadcasted_iota(jnp.int32, (SLOTS, 128), 0).astype(F32)
    lane = lax.broadcasted_iota(jnp.int32, (SLOTS, 128), 1)
    found = jnp.zeros((SLOTS, 128), F32)
    col = lax.axis_index("col")
    tables = [above[STRIP:, 128 * t : 128 * t + 128] for t in range(3)]
    tables += [left, own[STRIP:HALF_STRIP, :].astype(F32), right]
    tables += [below[STRIP:, 128 * t : 128 * t + 128] for t in range(3)]
    for t, table in enumerate(tables):
        live = lane.astype(F32) < table[2:3, 0:1]
        hit = live & (table[1:2] == slot) & (lane < entries)
        image = jnp.sum(jnp.where(hit, table[0:1] + 1.0, 0.0), axis=1, keepdims=True)
        found = jnp.where(lane == t, image, found)
    cell = found.astype(jnp.int32) - 1
    images[...] = jnp.where(cell >= 0, ((cell // per) ^ col) * per + cell % per, empty)

    row = lax.broadcasted_iota(jnp.int32, (32, 128), 0)
    lane = lax.broadcasted_iota(jnp.int32, (32, 128), 1)
    low = lane >= row + 96

    def cycled(x):
        return pltpu.roll(jnp.broadcast_to(x, (128, 128)), 0, 1, stride=1, stride_axis=0)

    def build_across(m, s):
        for q in range(2 * GROUP):
            cyc = cycled(ahead[GROUP * m + q // 2, q % 2 : q % 2 + 1, :])
            head = cyc[0:96].astype(BF16)
            tail = cyc[96:128]
            over = jnp.where(low, 0.0, tail)
            across[s][q, 0:96, 0:128] = head
            across[s][q, 128:CB, 128:256] = head[0 : CB - 128]
            across[s][q, 96:128, 0:128] = jnp.where(low, tail, 0.0).astype(BF16)
            across[s][q, 96:128, 128:256] = over.astype(BF16)

    def build_down(m, s):
        for q in range(2 * GROUP):
            cyc = cycled(back[GROUP * m + q // 2, q % 2 : q % 2 + 1, :])
            head = cyc[0:32]
            over = jnp.where(low, head, 0.0).astype(BF16)
            head = jnp.where(low, 0.0, head)
            same = jnp.concatenate([head, cyc[32:128]], axis=0).astype(BF16)
            down[s][q, 0:128, 0:128] = same
            down[s][q, 128:256, 128:256] = same
            down[s][q, 128:160, 0:128] = over

    def pass_one(s):
        taps = across[s][...].reshape(2 * GROUP * CB, 256)
        for j in range(NB + 1):
            part = dot_nt(taps, x_win[j]).astype(BF16)
            for q in range(2 * GROUP):
                first[s][q, j] = part[q * CB : (q + 1) * CB]

    def pass_two(m, s):
        for q in range(2 * GROUP):
            second = dot_nn(first[s][q].reshape((NB + 1) * CB, 256), down[s][q])
            part = (scale[GROUP * m + q // 2] * (second * second)).reshape(acc.shape)
            acc[...] = part if m == 0 and q == 0 else acc[...] + part

    def stage(m, s):
        pass_one(s)
        build_down(m, s)
        if m + 1 < groups:
            build_across(m + 1, 1 - s)
        pass_two(m - 1, 1 - s)

    build_across(0, 0)
    pass_one(0)
    build_down(0, 0)
    build_across(1, 1)
    fetch.wait()

    for m in range(1, groups):
        stage(m, m % 2)
    pass_two(groups - 1, (groups - 1) % 2)


def rows_kernel(n_row, n_col, acc, g_row, out, flat):
    rows = out.shape[0]
    cols = CB * NB - 2 * BLUR_HALF
    row, col = lax.axis_index("row"), lax.axis_index("col")
    at_row = lax.broadcasted_iota(jnp.int32, (8, 384), 1) - BLUR_HALF
    row_ok = ((row > 0) | (at_row >= 0)) & ((row < n_row - 1) | (at_row < rows))
    row_ok = jnp.where(row_ok, 1.0, 0.0)
    for b in range(NB):
        edge = acc[NB, :, EDGE_IN * b : EDGE_IN * b + EDGE_OUT]
        part = jnp.concatenate(
            [acc[b, :, 0:MAIN], edge, jnp.zeros((CB, 384 - MAIN - EDGE_OUT), F32)], axis=1
        )
        part = part * row_ok[0:1]
        if b == 0:
            part = jnp.concatenate([jnp.where(col > 0, part[0:8], 0.0), part[8:]], axis=0)
        if b == NB - 1:
            part = jnp.concatenate([part[0 : CB - 8], jnp.where(col < n_col - 1, part[CB - 8 :], 0.0)], axis=0)
        flat[b * CB : (b + 1) * CB, :] = part.astype(BF16)
    flat[NB * CB :, :] = jnp.zeros((flat.shape[0] - NB * CB, 384), BF16)

    for i in range(rows // 128):
        part = dot_nt(g_row[...], flat[:, 128 * i : 128 * i + 256])
        out[128 * i : 128 * i + 128, :] = part[0:128] + part[128:]


def final_kernel(images, blurred_rows, g_far, g_col, *rest):
    shards = rest[:-4]
    out, cells, placed, blurred = rest[-4:]
    per = (cells.shape[0] - 1) // len(shards)
    rows, cols = out.shape
    table = images[...]
    for i, shard in enumerate(shards):
        rows_of = shard.shape[0] - per * 64
        cells[i * per : (i + 1) * per] = shard[rows_of:, :].reshape(per, 64, 128)
    cells[len(shards) * per] = jnp.zeros((64, 128), BF16)

    slot_rows, slot_cols = rows // 64, cols // 128
    for i in range(-1, slot_rows + 1):
        for j in range(-1, slot_cols + 1):
            ti = 0 if i < 0 else (2 if i == slot_rows else 1)
            tj = 0 if j < 0 else (2 if j == slot_cols else 1)
            image = table[(i % slot_rows) * slot_cols + j % slot_cols, 3 * ti + tj]
            lanes = slice(128 + 128 * j, 256 + 128 * j)
            if i < 0:
                placed[0:16, lanes] = cells[image, 48:64, :]
            elif i == slot_rows:
                placed[16 + rows : 32 + rows, lanes] = cells[image, 0:16, :]
            else:
                placed[16 + 64 * i : 80 + 64 * i, lanes] = cells[image]
    placed[32 + rows :, :] = jnp.zeros((placed.shape[0] - 32 - rows, placed.shape[1]), BF16)

    for i in range(rows // 128):
        part = blurred_rows[128 * i : 128 * i + 128, :]
        cell = dot_nn(g_far[...], placed[128 * i : 128 * i + 256, :])
        cell = cell[0:128] + cell[128:]
        part += cell[:, 128 - BLUR_HALF : 128 - BLUR_HALF + part.shape[1]]
        high = part.astype(BF16)
        blurred[0, 128 * i : 128 * i + 128, :] = high
        blurred[1, 128 * i : 128 * i + 128, :] = (part - high.astype(F32)).astype(BF16)
    count = cols // 128
    stacked = [
        jnp.concatenate([blurred[p, :, 128 * j : 128 * j + 256] for j in range(count)], axis=0) for p in range(2)
    ]
    part = dot_nn(stacked[0], g_col[...])
    part = part[:, 0:128] + part[:, 128:] + dot_nn(stacked[1], g_col[:, 0:128])
    for j in range(count):
        out[:, 128 * j : 128 * j + 128] = part[rows * j : rows * j + rows]


def shape(dims, dtype):
    return jax.ShapeDtypeStruct(dims, dtype)


def on_device(
    mask_pixels, across_taps, down_taps, kernel_weights, library, cell_ids, cell_slots, cell_count
):
    rows, cols = mask_pixels.shape
    kernels = across_taps.shape[0]
    entries = cell_ids.shape[-1]
    per = library.shape[0]
    n_row, n_col = lax.axis_size("row"), lax.axis_size("col")
    library = library.reshape(per * 64, 128)
    in_hbm = lambda x: pltpu.with_memory_space_constraint(x, pltpu.HBM)
    mask_hbm = in_hbm(mask_pixels)

    to_first, to_second, block, taps = pl.pallas_call(
        prep_kernel,
        out_shape=(
            shape((2 * HALF_STRIP, 128), BF16),
            shape((128, 128), BF16),
            shape((SPARE + per * 64, 128), BF16),
            shape((2,) + across_taps.shape, BF16),
        ),
        in_specs=[HBM] * 3 + [VMEM] + [HBM] * 3,
        out_specs=(VMEM,) * 4,
        scratch_shapes=[
            pltpu.VMEM((2, rows, 128), jnp.int32),
            pltpu.VMEM(cell_ids.shape, jnp.int32),
            pltpu.VMEM(cell_slots.shape, jnp.int32),
            pltpu.SemaphoreType.DMA((7,)),
        ],
        compiler_params=PARAMS,
        name="prep",
    )(mask_hbm, in_hbm(cell_ids), in_hbm(cell_slots), cell_count, in_hbm(across_taps), in_hbm(down_taps), in_hbm(library))

    def swaps(n):
        rounds = []
        for start in (0, 1):
            pairs = [(i, (i + 1) % n) for i in range(start, n, 2)]
            rounds.append(pairs + [(b, a) for a, b in pairs])
        return rounds

    second = []
    for r in range(n_row):
        second += [(r * n_col + a, r * n_col + b) for a, b in swaps(n_col)[1] if abs(a - b) == 1]
        second += [(r * n_col + a, (r ^ 1) * n_col + a) for a in (0, n_col - 1)]

    col_second = lax.ppermute(to_second, ("row", "col"), second)
    col_first = lax.ppermute(to_first, "col", swaps(n_col)[0])

    to_above, to_below = pl.pallas_call(
        mid_kernel,
        out_shape=(shape((STRIP + 16, WIDE), BF16),) * 2,
        in_specs=[VMEM] * 4,
        out_specs=(VMEM,) * 2,
        compiler_params=PARAMS,
        name="mid",
    )(mask_pixels, col_first, col_second, to_first)
    late, to_above, to_below = lax.optimization_barrier((library, to_above, to_below))
    blocks = {0: library}
    for d in sorted(range(1, n_col), key=lambda d: d == 2):
        part = late if d == 2 else block
        blocks[d] = lax.ppermute(part, "col", [(i, i ^ d) for i in range(n_col)])
    shards = [blocks[d] for d in range(n_col)]
    row_first, row_second = (
        lax.ppermute(x, "row", pairs) for x, pairs in zip((to_above, to_below), swaps(n_row))
    )

    windows, ahead, back, g_row, g_far, g_col = pl.pallas_call(
        own_kernel,
        out_shape=(
            shape((NB, rows, 256), F32),
            shape((kernels, 8, 128), F32),
            shape((kernels, 8, 128), F32),
            shape((256, 256), BF16),
            shape((256, 256), BF16),
            shape((256, 256), BF16),
        ),
        in_specs=[VMEM] * 2,
        out_specs=(VMEM,) * 6,
        compiler_params=PARAMS,
        cost_estimate=pl.CostEstimate(flops=10**6, bytes_accessed=10**6, transcendentals=0),
        name="own",
    )(mask_pixels, taps)

    acc, images = pl.pallas_call(
        functools.partial(socs_kernel, entries, per, n_col * per),
        out_shape=(shape((NB + 1, CB, 256), F32), shape((SLOTS, 128), jnp.int32)),
        in_specs=[HBM] + [VMEM] * 8,
        out_specs=(VMEM,) * 2,
        scratch_shapes=[
            pltpu.VMEM((NB + 1, 256, 256), BF16),
            pltpu.SMEM(kernel_weights.shape, F32),
            pltpu.SemaphoreType.DMA,
        ]
        + [pltpu.VMEM((2 * GROUP, CB, 256), BF16)] * 2
        + [pltpu.VMEM((2 * GROUP, 256, 256), BF16)] * 2
        + [pltpu.VMEM((2 * GROUP, NB + 1, CB, 256), BF16)] * 2,
        compiler_params=PARAMS,
        cost_estimate=pl.CostEstimate(flops=75 * 10**7, bytes_accessed=10**5, transcendentals=0),
        name="socs",
    )(in_hbm(kernel_weights), windows, row_first, row_second, col_first, col_second, to_first, ahead, back)

    blurred_rows = pl.pallas_call(
        functools.partial(rows_kernel, n_row, n_col),
        out_shape=shape((rows, WIDE), F32),
        in_specs=[VMEM] * 2,
        out_specs=VMEM,
        scratch_shapes=[pltpu.VMEM((WIDE, 384), BF16)],
        compiler_params=PARAMS,
        cost_estimate=pl.CostEstimate(flops=10**6, bytes_accessed=10**5, transcendentals=0),
        name="rows",
    )(acc, g_row)

    return pl.pallas_call(
        final_kernel,
        out_shape=shape((rows, cols), F32),
        in_specs=[VMEM] * (4 + n_col),
        out_specs=VMEM,
        scratch_shapes=[
            pltpu.VMEM((n_col * per + 1, 64, 128), BF16),
            pltpu.VMEM((384, cols + 256), BF16),
            pltpu.VMEM((2, rows, WIDE), BF16),
        ],
        compiler_params=PARAMS,
        name="final",
    )(images, blurred_rows, g_far, g_col, *shards)


def solution(mesh):
    placed = (
        P(("frames", "row"), "col"),
        P(),
        P(),
        P(),
        P("col", None, None),
        P(("frames", "row"), "col", None),
        P(("frames", "row"), "col", None),
        P(("frames", "row"), "col"),
    )
    return jax.shard_map(
        on_device,
        mesh=mesh,
        in_specs=placed,
        out_specs=P(("frames", "row"), "col"),
        check_vma=False,
    )
```

```python
import functools
import math

import jax
import jax.numpy as jnp
from jax import lax
from jax.experimental import pallas as pl
from jax.experimental.pallas import tpu as pltpu
from jax.sharding import PartitionSpec as P

BLUR_HALF = 8
BLUR_SIGMA = 4.0
HALF = 16
RIM = HALF + BLUR_HALF
STRIP = 32
CB = 176
NB = 3
MAIN = 224
EDGE_IN = 80
EDGE_OUT = 48
RIGHT_AT = 56
HALF_STRIP = STRIP + 16
SPARE = 16
GROUP = 2
WIDE = 640
SLOTS = 16
F32 = jnp.float32
BF16 = jnp.bfloat16
VMEM = pl.BlockSpec(memory_space=pltpu.VMEM)
SMEM = pl.BlockSpec(memory_space=pltpu.SMEM)
HBM = pl.BlockSpec(memory_space=pltpu.HBM)
PARAMS = pltpu.CompilerParams(vmem_limit_bytes=16 * 1024 * 1024)


def dot_nt(a, b):
    return lax.dot_general(a, b, (((1,), (1,)), ((), ())), preferred_element_type=F32)


def dot_nn(a, b):
    return lax.dot_general(a, b, (((1,), (0,)), ((), ())), preferred_element_type=F32)


def join(strip):
    halves = [strip[0:HALF_STRIP, :], strip[HALF_STRIP : 2 * HALF_STRIP, :]]
    return jnp.concatenate(halves, axis=1).astype(F32)


def eye(rows, cols, shift):
    at = lax.broadcasted_iota(jnp.int32, (rows, cols), 1) - lax.broadcasted_iota(jnp.int32, (rows, cols), 0)
    return jnp.where(at == shift, 1.0, 0.0).astype(BF16)


def sides(axis, first_swap, second_swap):
    index, count = lax.axis_index(axis), lax.axis_size(axis)
    even = lax.rem(index, 2) == 0
    lower = jnp.where(even, second_swap, first_swap)
    upper = jnp.where(even, first_swap, second_swap)
    return jnp.where(index > 0, lower, 0.0), jnp.where(index < count - 1, upper, 0.0)


def prep_kernel(
    mask, ids, slots, count, across, down, library, weights, to_first, to_second, block, taps, line_weights, ends, a_ids, a_slots, sems
):
    rows, cols = mask.shape
    copies = [
        pltpu.make_async_copy(mask.at[:, 0:128], ends.at[0], sems.at[0]),
        pltpu.make_async_copy(mask.at[:, cols - 128 : cols], ends.at[1], sems.at[1]),
        pltpu.make_async_copy(ids, a_ids, sems.at[2]),
        pltpu.make_async_copy(slots, a_slots, sems.at[3]),
        pltpu.make_async_copy(across, taps.at[0], sems.at[4]),
        pltpu.make_async_copy(down, taps.at[1], sems.at[5]),
        pltpu.make_async_copy(library, block.at[SPARE:], sems.at[6]),
        pltpu.make_async_copy(weights, line_weights, sems.at[7]),
    ]
    for copy in copies:
        copy.start()
    for copy in copies[2:4]:
        copy.wait()
    line = lax.broadcasted_iota(jnp.int32, (16, 128), 0)
    lane = lax.broadcasted_iota(jnp.int32, (16, 128), 1)

    def spread(x):
        x = x.astype(F32)
        x = jnp.concatenate([x, jnp.zeros((1, 128 - x.shape[1]), F32)], axis=1)
        return jnp.broadcast_to(x, (16, 128))

    table = jnp.where(line == 1, spread(a_slots[0]), jnp.broadcast_to(count[...].astype(F32), (16, 128)))
    table = jnp.where(line == 0, spread(a_ids[0]), table)
    width = jnp.where(line == 2, 1, ids.shape[2])
    table = jnp.where((lane < width) & (line < 3), table, 0.0).astype(BF16)
    for strip in (to_first, to_second):
        strip[STRIP:HALF_STRIP, :] = table
        strip[HALF_STRIP + STRIP : 2 * HALF_STRIP, :] = jnp.zeros((16, 128), BF16)
    block[0:SPARE, :] = jnp.zeros((SPARE, 128), BF16)
    to_second[2 * HALF_STRIP :, :] = jnp.zeros((128 - 2 * HALF_STRIP, 128), BF16)
    even = lax.rem(lax.axis_index("col"), 2) == 0
    copies[0].wait()
    first = dot_nt(eye(STRIP, 128, 0), ends[0].astype(F32).astype(BF16))
    copies[1].wait()
    last = dot_nt(eye(STRIP, 128, 128 - STRIP), ends[1].astype(F32).astype(BF16))
    for strip, part in ((to_first, jnp.where(even, last, first)), (to_second, jnp.where(even, first, last))):
        strip[0:STRIP, :] = part[:, 0:128].astype(BF16)
        strip[HALF_STRIP : HALF_STRIP + STRIP, :] = part[:, 128:256].astype(BF16)
    for copy in copies[4:]:
        copy.wait()


def mid_kernel(mask, from_first, from_second, own, to_first, to_second):
    rows, cols = mask.shape
    left, right = sides("col", join(from_first), join(from_second))
    tables = jnp.concatenate(
        [left[STRIP:, 0:128], own[STRIP:HALF_STRIP, :].astype(F32), right[STRIP:, 0:128], jnp.zeros((16, 256), F32)],
        axis=1,
    ).astype(BF16)
    fill = jnp.zeros((128 - STRIP, 128), F32)
    strips = []
    for i in range(2):
        at = 0 if i == 0 else rows - 128
        pick = eye(STRIP, 128, 0 if i == 0 else 128 - STRIP)

        def turned(strip):
            return dot_nt(pick, jnp.concatenate([strip[0:STRIP, at : at + 128], fill], axis=0).astype(BF16))

        parts = [turned(left)[:, STRIP - RIM : STRIP], mask[(rows - STRIP) * i : (rows - STRIP) * i + STRIP, :].astype(F32), turned(right)[:, 0 : WIDE - RIM - cols]]
        strips.append(jnp.concatenate(parts, axis=1))
    even = lax.rem(lax.axis_index("row"), 2) == 0
    to_first[0:STRIP, :] = jnp.where(even, strips[1], strips[0]).astype(BF16)
    to_second[0:STRIP, :] = jnp.where(even, strips[0], strips[1]).astype(BF16)
    to_first[STRIP:, :] = tables
    to_second[STRIP:, :] = tables


def blur_matrix(shape, axis, start=0):
    lag = lax.broadcasted_iota(jnp.int32, shape, axis) - lax.broadcasted_iota(jnp.int32, shape, 1 - axis) - start
    total = sum(math.exp(-(t * t) / (2 * BLUR_SIGMA**2)) for t in range(-BLUR_HALF, BLUR_HALF + 1))
    off = (lag - BLUR_HALF).astype(F32)
    g = jnp.exp(-off * off / (2.0 * BLUR_SIGMA * BLUR_SIGMA)) * (1.0 / total)
    g = jnp.where((lag >= 0) & (lag <= 2 * BLUR_HALF), g, 0.0)
    high = g.astype(BF16)
    return high, (g - high.astype(F32)).astype(BF16)


def own_kernel(mask, taps, windows, ahead, back, g_row, g_far, g_col):
    rows, cols = mask.shape
    full = jnp.concatenate(
        [jnp.zeros((rows, RIM), F32), mask[...].astype(F32), jnp.zeros((rows, WIDE - RIM - cols), F32)], axis=1
    )
    for b in range(NB):
        windows[b] = full[:, CB * b : CB * b + 256]
    kernels, _, count = taps.shape[1:]
    flip = lax.broadcasted_iota(jnp.int32, (128, 128), 0) + lax.broadcasted_iota(jnp.int32, (128, 128), 1)
    flip = jnp.where(flip % 128 == 0, 1.0, 0.0).astype(BF16)
    ahead[...] = jnp.zeros(ahead.shape, F32)
    back[...] = jnp.zeros(back.shape, F32)
    for k in range(kernels):
        ahead[k, 0:2, 0:count] = taps[0, k].astype(F32)
        back[k, 0:2, 0:count] = taps[1, k].astype(F32)
    back[...] = dot_nn(back[...].reshape(kernels * 8, 128).astype(BF16), flip).reshape(kernels, 8, 128)
    g_row[0:128], g_row[128:256] = blur_matrix((128, 256), 1)
    g_far[0:128], g_far[128:256] = blur_matrix((128, 256), 1, 16 - BLUR_HALF)
    g_col[:, 0:128], g_col[:, 128:256] = blur_matrix((256, 128), 0)


def socs_kernel(
    entries,
    per,
    empty,
    weights,
    windows,
    row_first,
    row_second,
    col_first,
    col_second,
    own,
    ahead,
    back,
    acc,
    images,
    x_win,
    scale,
    sem,
    *scratch,
):
    across = scratch[0:2]
    down = scratch[2:4]
    first = scratch[4:6]
    groups = ahead.shape[0] // GROUP
    fetch = pltpu.make_async_copy(weights, scale, sem)
    fetch.start()
    above, below = sides("row", row_first[...].astype(F32), row_second[...].astype(F32))
    left, right = sides("col", join(col_first), join(col_second))
    rows = windows.shape[1]
    turned = jnp.concatenate(
        [
            left[STRIP - RIM : STRIP],
            jnp.zeros((128 - RIM + RIGHT_AT, rows), F32),
            right[0:RIM],
            jnp.zeros((128 - RIM - RIGHT_AT, rows), F32),
        ],
        axis=0,
    )
    turned = dot_nt(eye(rows, rows, 0), turned.astype(BF16))
    left, right = left[STRIP:, 0:128], right[STRIP:, 0:128]
    upper_rows = above[STRIP - RIM : STRIP]
    lower_rows = below[0:RIM]
    edge_rows = []
    for b in range(NB):
        lanes = slice(CB * b, CB * b + 256)
        part = windows[b]
        if b == 0:
            part = jnp.concatenate([part[:, 0:128] + turned[:, 0:128], part[:, 128:256]], axis=1)
        if b == NB - 1:
            part = jnp.concatenate([part[:, 0:128], part[:, 128:256] + turned[:, 128:256]], axis=1)
        x_win[b] = jnp.concatenate([upper_rows[:, lanes], part[0 : 256 - RIM]], axis=0).astype(BF16)
        edge_rows += [part[MAIN - RIM :], lower_rows[:, lanes]]
    edge_rows.append(jnp.zeros((256 - NB * EDGE_IN, 256), F32))
    x_win[NB] = jnp.concatenate(edge_rows, axis=0).astype(BF16)
    for s in range(2):
        for q in range(2 * GROUP):
            across[s][q, 0:96, 128:256] = jnp.zeros((96, 128), BF16)
            across[s][q, 128:CB, 0:128] = jnp.zeros((CB - 128, 128), BF16)
            down[s][q, 0:128, 128:256] = jnp.zeros((128, 128), BF16)
            down[s][q, 160:256, 0:128] = jnp.zeros((96, 128), BF16)

    slot = lax.broadcasted_iota(jnp.int32, (SLOTS, 128), 0).astype(F32)
    lane = lax.broadcasted_iota(jnp.int32, (SLOTS, 128), 1)
    found = jnp.zeros((SLOTS, 128), F32)
    col = lax.axis_index("col")
    tables = [above[STRIP:, 128 * t : 128 * t + 128] for t in range(3)]
    tables += [left, own[STRIP:HALF_STRIP, :].astype(F32), right]
    tables += [below[STRIP:, 128 * t : 128 * t + 128] for t in range(3)]
    for t, table in enumerate(tables):
        live = lane.astype(F32) < table[2:3, 0:1]
        hit = live & (table[1:2] == slot) & (lane < entries)
        image = jnp.sum(jnp.where(hit, table[0:1] + 1.0, 0.0), axis=1, keepdims=True)
        found = jnp.where(lane == t, image, found)
    cell = found.astype(jnp.int32) - 1
    images[...] = jnp.where(cell >= 0, ((cell // per) ^ col) * per + cell % per, empty)

    row = lax.broadcasted_iota(jnp.int32, (32, 128), 0)
    lane = lax.broadcasted_iota(jnp.int32, (32, 128), 1)
    low = lane >= row + 96

    def cycled(x):
        return pltpu.roll(jnp.broadcast_to(x, (128, 128)), 0, 1, stride=1, stride_axis=0)

    def build_across(m, s):
        for q in range(2 * GROUP):
            cyc = cycled(ahead[GROUP * m + q // 2, q % 2 : q % 2 + 1, :])
            head = cyc[0:96].astype(BF16)
            tail = cyc[96:128]
            over = jnp.where(low, 0.0, tail)
            across[s][q, 0:96, 0:128] = head
            across[s][q, 128:CB, 128:256] = head[0 : CB - 128]
            across[s][q, 96:128, 0:128] = jnp.where(low, tail, 0.0).astype(BF16)
            across[s][q, 96:128, 128:256] = over.astype(BF16)

    def build_down(m, s):
        for q in range(2 * GROUP):
            cyc = cycled(back[GROUP * m + q // 2, q % 2 : q % 2 + 1, :])
            head = cyc[0:32]
            over = jnp.where(low, head, 0.0).astype(BF16)
            head = jnp.where(low, 0.0, head)
            same = jnp.concatenate([head, cyc[32:128]], axis=0).astype(BF16)
            down[s][q, 0:128, 0:128] = same
            down[s][q, 128:256, 128:256] = same
            down[s][q, 128:160, 0:128] = over

    def pass_one(s):
        taps = across[s][...].reshape(2 * GROUP * CB, 256)
        for j in range(NB + 1):
            part = dot_nt(taps, x_win[j]).astype(BF16)
            for q in range(2 * GROUP):
                first[s][q, j] = part[q * CB : (q + 1) * CB]

    def pass_two(m, s):
        for q in range(2 * GROUP):
            second = dot_nn(first[s][q].reshape((NB + 1) * CB, 256), down[s][q])
            part = (scale[GROUP * m + q // 2] * (second * second)).reshape(acc.shape)
            acc[...] = part if m == 0 and q == 0 else acc[...] + part

    def stage(m, s):
        pass_one(s)
        build_down(m, s)
        if m + 1 < groups:
            build_across(m + 1, 1 - s)
        pass_two(m - 1, 1 - s)

    build_across(0, 0)
    pass_one(0)
    build_down(0, 0)
    build_across(1, 1)
    fetch.wait()

    for m in range(1, groups):
        stage(m, m % 2)
    pass_two(groups - 1, (groups - 1) % 2)


def rows_kernel(n_row, n_col, acc, g_row, out, flat):
    rows = out.shape[0]
    cols = CB * NB - 2 * BLUR_HALF
    row, col = lax.axis_index("row"), lax.axis_index("col")
    at_row = lax.broadcasted_iota(jnp.int32, (8, 384), 1) - BLUR_HALF
    row_ok = ((row > 0) | (at_row >= 0)) & ((row < n_row - 1) | (at_row < rows))
    row_ok = jnp.where(row_ok, 1.0, 0.0)
    for b in range(NB):
        edge = acc[NB, :, EDGE_IN * b : EDGE_IN * b + EDGE_OUT]
        part = jnp.concatenate(
            [acc[b, :, 0:MAIN], edge, jnp.zeros((CB, 384 - MAIN - EDGE_OUT), F32)], axis=1
        )
        part = part * row_ok[0:1]
        if b == 0:
            part = jnp.concatenate([jnp.where(col > 0, part[0:8], 0.0), part[8:]], axis=0)
        if b == NB - 1:
            part = jnp.concatenate([part[0 : CB - 8], jnp.where(col < n_col - 1, part[CB - 8 :], 0.0)], axis=0)
        flat[b * CB : (b + 1) * CB, :] = part.astype(BF16)
    flat[NB * CB :, :] = jnp.zeros((flat.shape[0] - NB * CB, 384), BF16)

    for i in range(rows // 128):
        part = dot_nt(g_row[...], flat[:, 128 * i : 128 * i + 256])
        out[128 * i : 128 * i + 128, :] = part[0:128] + part[128:]


def final_kernel(images, blurred_rows, g_far, g_col, *rest):
    shards = rest[:-4]
    out, cells, placed, blurred = rest[-4:]
    per = (cells.shape[0] - 1) // len(shards)
    rows, cols = out.shape
    table = images[...]
    for i, shard in enumerate(shards):
        rows_of = shard.shape[0] - per * 64
        cells[i * per : (i + 1) * per] = shard[rows_of:, :].reshape(per, 64, 128)
    cells[len(shards) * per] = jnp.zeros((64, 128), BF16)

    slot_rows, slot_cols = rows // 64, cols // 128
    for i in range(-1, slot_rows + 1):
        for j in range(-1, slot_cols + 1):
            ti = 0 if i < 0 else (2 if i == slot_rows else 1)
            tj = 0 if j < 0 else (2 if j == slot_cols else 1)
            image = table[(i % slot_rows) * slot_cols + j % slot_cols, 3 * ti + tj]
            lanes = slice(128 + 128 * j, 256 + 128 * j)
            if i < 0:
                placed[0:16, lanes] = cells[image, 48:64, :]
            elif i == slot_rows:
                placed[16 + rows : 32 + rows, lanes] = cells[image, 0:16, :]
            else:
                placed[16 + 64 * i : 80 + 64 * i, lanes] = cells[image]
    placed[32 + rows :, :] = jnp.zeros((placed.shape[0] - 32 - rows, placed.shape[1]), BF16)

    for i in range(rows // 128):
        part = blurred_rows[128 * i : 128 * i + 128, :]
        cell = dot_nn(g_far[...], placed[128 * i : 128 * i + 256, :])
        cell = cell[0:128] + cell[128:]
        part += cell[:, 128 - BLUR_HALF : 128 - BLUR_HALF + part.shape[1]]
        high = part.astype(BF16)
        blurred[0, 128 * i : 128 * i + 128, :] = high
        blurred[1, 128 * i : 128 * i + 128, :] = (part - high.astype(F32)).astype(BF16)
    count = cols // 128
    stacked = [
        jnp.concatenate([blurred[p, :, 128 * j : 128 * j + 256] for j in range(count)], axis=0) for p in range(2)
    ]
    part = dot_nn(stacked[0], g_col[...])
    part = part[:, 0:128] + part[:, 128:] + dot_nn(stacked[1], g_col[:, 0:128])
    for j in range(count):
        out[:, 128 * j : 128 * j + 128] = part[rows * j : rows * j + rows]


def shape(dims, dtype):
    return jax.ShapeDtypeStruct(dims, dtype)


def on_device(
    mask_pixels, across_taps, down_taps, kernel_weights, library, cell_ids, cell_slots, cell_count
):
    rows, cols = mask_pixels.shape
    kernels = across_taps.shape[0]
    entries = cell_ids.shape[-1]
    per = library.shape[0]
    n_row, n_col = lax.axis_size("row"), lax.axis_size("col")
    library = library.reshape(per * 64, 128)
    in_hbm = lambda x: pltpu.with_memory_space_constraint(x, pltpu.HBM)
    mask_hbm = in_hbm(mask_pixels)

    to_first, to_second, block, taps, line_weights = pl.pallas_call(
        prep_kernel,
        out_shape=(
            shape((2 * HALF_STRIP, 128), BF16),
            shape((128, 128), BF16),
            shape((SPARE + per * 64, 128), BF16),
            shape((2,) + across_taps.shape, BF16),
            shape(kernel_weights.shape, F32),
        ),
        in_specs=[HBM] * 3 + [VMEM] + [HBM] * 4,
        out_specs=(VMEM,) * 5,
        scratch_shapes=[
            pltpu.VMEM((2, rows, 128), jnp.int32),
            pltpu.VMEM(cell_ids.shape, jnp.int32),
            pltpu.VMEM(cell_slots.shape, jnp.int32),
            pltpu.SemaphoreType.DMA((8,)),
        ],
        compiler_params=PARAMS,
        name="prep",
    )(mask_hbm, in_hbm(cell_ids), in_hbm(cell_slots), cell_count, in_hbm(across_taps), in_hbm(down_taps), in_hbm(library), in_hbm(kernel_weights))

    def swaps(n):
        rounds = []
        for start in (0, 1):
            pairs = [(i, (i + 1) % n) for i in range(start, n, 2)]
            rounds.append(pairs + [(b, a) for a, b in pairs])
        return rounds

    second = []
    for r in range(n_row):
        second += [(r * n_col + a, r * n_col + b) for a, b in swaps(n_col)[1] if abs(a - b) == 1]
        second += [(r * n_col + a, (r ^ 1) * n_col + a) for a in (0, n_col - 1)]

    col_second = lax.ppermute(to_second, ("row", "col"), second)
    col_first = lax.ppermute(to_first, "col", swaps(n_col)[0])

    to_above, to_below = pl.pallas_call(
        mid_kernel,
        out_shape=(shape((STRIP + 16, WIDE), BF16),) * 2,
        in_specs=[VMEM] * 4,
        out_specs=(VMEM,) * 2,
        compiler_params=PARAMS,
        name="mid",
    )(mask_pixels, col_first, col_second, to_first)
    late, to_above, to_below = lax.optimization_barrier((library, to_above, to_below))
    blocks = {0: library}
    for d in sorted(range(1, n_col), key=lambda d: (d == n_col - 1, -(d & -d))):
        part = late if d == n_col - 1 else block
        blocks[d] = lax.ppermute(part, "col", [(i, i ^ d) for i in range(n_col)])
    shards = [blocks[d] for d in range(n_col)]
    ends = []
    for f in range(lax.axis_size("frames")):
        ends += [(f * n_row + a, f * n_row + b) for a, b in swaps(n_row)[1] if abs(a - b) == 1]
        ends += [(f * n_row + a, (f ^ 1) * n_row + a) for a in (0, n_row - 1)]
    row_first = lax.ppermute(to_above, "row", swaps(n_row)[0])
    row_second = lax.ppermute(to_below, ("frames", "row"), ends)

    windows, ahead, back, g_row, g_far, g_col = pl.pallas_call(
        own_kernel,
        out_shape=(
            shape((NB, rows, 256), F32),
            shape((kernels, 8, 128), F32),
            shape((kernels, 8, 128), F32),
            shape((256, 256), BF16),
            shape((256, 256), BF16),
            shape((256, 256), BF16),
        ),
        in_specs=[VMEM] * 2,
        out_specs=(VMEM,) * 6,
        compiler_params=PARAMS,
        cost_estimate=pl.CostEstimate(flops=10**6, bytes_accessed=10**6, transcendentals=0),
        name="own",
    )(mask_pixels, taps)

    acc, images = pl.pallas_call(
        functools.partial(socs_kernel, entries, per, n_col * per),
        out_shape=(shape((NB + 1, CB, 256), F32), shape((SLOTS, 128), jnp.int32)),
        in_specs=[VMEM] * 9,
        out_specs=(VMEM,) * 2,
        scratch_shapes=[
            pltpu.VMEM((NB + 1, 256, 256), BF16),
            pltpu.SMEM(kernel_weights.shape, F32),
            pltpu.SemaphoreType.DMA,
        ]
        + [pltpu.VMEM((2 * GROUP, CB, 256), BF16)] * 2
        + [pltpu.VMEM((2 * GROUP, 256, 256), BF16)] * 2
        + [pltpu.VMEM((2 * GROUP, NB + 1, CB, 256), BF16)] * 2,
        compiler_params=PARAMS,
        cost_estimate=pl.CostEstimate(flops=75 * 10**7, bytes_accessed=10**5, transcendentals=0),
        name="socs",
    )(line_weights, windows, row_first, row_second, col_first, col_second, to_first, ahead, back)

    blurred_rows = pl.pallas_call(
        functools.partial(rows_kernel, n_row, n_col),
        out_shape=shape((rows, WIDE), F32),
        in_specs=[VMEM] * 2,
        out_specs=VMEM,
        scratch_shapes=[pltpu.VMEM((WIDE, 384), BF16)],
        compiler_params=PARAMS,
        cost_estimate=pl.CostEstimate(flops=10**6, bytes_accessed=10**5, transcendentals=0),
        name="rows",
    )(acc, g_row)

    return pl.pallas_call(
        final_kernel,
        out_shape=shape((rows, cols), F32),
        in_specs=[VMEM] * (4 + n_col),
        out_specs=VMEM,
        scratch_shapes=[
            pltpu.VMEM((n_col * per + 1, 64, 128), BF16),
            pltpu.VMEM((384, cols + 256), BF16),
            pltpu.VMEM((2, rows, WIDE), BF16),
        ],
        compiler_params=PARAMS,
        name="final",
    )(images, blurred_rows, g_far, g_col, *shards)


def solution(mesh):
    placed = (
        P(("frames", "row"), "col"),
        P(),
        P(),
        P(),
        P("col", None, None),
        P(("frames", "row"), "col", None),
        P(("frames", "row"), "col", None),
        P(("frames", "row"), "col"),
    )
    return jax.shard_map(
        on_device,
        mesh=mesh,
        in_specs=placed,
        out_specs=P(("frames", "row"), "col"),
        check_vma=False,
    )
```

```python
import functools
import math

import jax
import jax.numpy as jnp
from jax import lax
from jax.experimental import pallas as pl
from jax.experimental.pallas import tpu as pltpu
from jax.sharding import PartitionSpec as P

BLUR_HALF = 8
BLUR_SIGMA = 4.0
HALF = 16
RIM = HALF + BLUR_HALF
STRIP = 32
CB = 176
NB = 3
MAIN = 224
EDGE_IN = 80
EDGE_OUT = 48
RIGHT_AT = 56
HALF_STRIP = STRIP + 16
SPARE = 16
GROUP = 2
WIDE = 640
SLOTS = 16
F32 = jnp.float32
BF16 = jnp.bfloat16
VMEM = pl.BlockSpec(memory_space=pltpu.VMEM)
SMEM = pl.BlockSpec(memory_space=pltpu.SMEM)
HBM = pl.BlockSpec(memory_space=pltpu.HBM)
PARAMS = pltpu.CompilerParams(vmem_limit_bytes=16 * 1024 * 1024)


def dot_nt(a, b):
    return lax.dot_general(a, b, (((1,), (1,)), ((), ())), preferred_element_type=F32)


def dot_nn(a, b):
    return lax.dot_general(a, b, (((1,), (0,)), ((), ())), preferred_element_type=F32)


def join(strip):
    halves = [strip[0:HALF_STRIP, :], strip[HALF_STRIP : 2 * HALF_STRIP, :]]
    return jnp.concatenate(halves, axis=1).astype(F32)


def eye(rows, cols, shift):
    at = lax.broadcasted_iota(jnp.int32, (rows, cols), 1) - lax.broadcasted_iota(jnp.int32, (rows, cols), 0)
    return jnp.where(at == shift, 1.0, 0.0).astype(BF16)


def sides(axis, first_swap, second_swap):
    index, count = lax.axis_index(axis), lax.axis_size(axis)
    even = lax.rem(index, 2) == 0
    lower = jnp.where(even, second_swap, first_swap)
    upper = jnp.where(even, first_swap, second_swap)
    return jnp.where(index > 0, lower, 0.0), jnp.where(index < count - 1, upper, 0.0)


def prep_kernel(
    mask, ids, slots, count, across, down, library, weights, to_first, to_second, block, taps, line_weights, ends, a_ids, a_slots, sems
):
    rows, cols = mask.shape
    copies = [
        pltpu.make_async_copy(mask.at[:, 0:128], ends.at[0], sems.at[0]),
        pltpu.make_async_copy(mask.at[:, cols - 128 : cols], ends.at[1], sems.at[1]),
        pltpu.make_async_copy(ids, a_ids, sems.at[2]),
        pltpu.make_async_copy(slots, a_slots, sems.at[3]),
        pltpu.make_async_copy(across, taps.at[0], sems.at[4]),
        pltpu.make_async_copy(down, taps.at[1], sems.at[5]),
        pltpu.make_async_copy(library, block.at[SPARE:], sems.at[6]),
        pltpu.make_async_copy(weights, line_weights, sems.at[7]),
    ]
    for copy in copies:
        copy.start()
    even = lax.rem(lax.axis_index("col"), 2) == 0
    copies[0].wait()
    first = dot_nt(eye(STRIP, 128, 0), ends[0].astype(F32).astype(BF16))
    copies[1].wait()
    last = dot_nt(eye(STRIP, 128, 128 - STRIP), ends[1].astype(F32).astype(BF16))
    for copy in copies[2:4]:
        copy.wait()
    line = lax.broadcasted_iota(jnp.int32, (16, 128), 0)
    lane = lax.broadcasted_iota(jnp.int32, (16, 128), 1)

    def spread(x):
        x = x.astype(F32)
        x = jnp.concatenate([x, jnp.zeros((1, 128 - x.shape[1]), F32)], axis=1)
        return jnp.broadcast_to(x, (16, 128))

    table = jnp.where(line == 1, spread(a_slots[0]), jnp.broadcast_to(count[...].astype(F32), (16, 128)))
    table = jnp.where(line == 0, spread(a_ids[0]), table)
    width = jnp.where(line == 2, 1, ids.shape[2])
    table = jnp.where((lane < width) & (line < 3), table, 0.0).astype(BF16)
    for strip in (to_first, to_second):
        strip[STRIP:HALF_STRIP, :] = table
        strip[HALF_STRIP + STRIP : 2 * HALF_STRIP, :] = jnp.zeros((16, 128), BF16)
    block[0:SPARE, :] = jnp.zeros((SPARE, 128), BF16)
    to_second[2 * HALF_STRIP :, :] = jnp.zeros((128 - 2 * HALF_STRIP, 128), BF16)
    for strip, part in ((to_first, jnp.where(even, last, first)), (to_second, jnp.where(even, first, last))):
        strip[0:STRIP, :] = part[:, 0:128].astype(BF16)
        strip[HALF_STRIP : HALF_STRIP + STRIP, :] = part[:, 128:256].astype(BF16)
    for copy in copies[4:]:
        copy.wait()


def mid_kernel(mask, from_first, from_second, own, to_first, to_second):
    rows, cols = mask.shape
    left, right = sides("col", join(from_first), join(from_second))
    tables = jnp.concatenate(
        [left[STRIP:, 0:128], own[STRIP:HALF_STRIP, :].astype(F32), right[STRIP:, 0:128], jnp.zeros((16, 256), F32)],
        axis=1,
    ).astype(BF16)
    fill = jnp.zeros((128 - STRIP, 128), F32)
    strips = []
    for i in range(2):
        at = 0 if i == 0 else rows - 128
        pick = eye(STRIP, 128, 0 if i == 0 else 128 - STRIP)

        def turned(strip):
            return dot_nt(pick, jnp.concatenate([strip[0:STRIP, at : at + 128], fill], axis=0).astype(BF16))

        parts = [turned(left)[:, STRIP - RIM : STRIP], mask[(rows - STRIP) * i : (rows - STRIP) * i + STRIP, :].astype(F32), turned(right)[:, 0 : WIDE - RIM - cols]]
        strips.append(jnp.concatenate(parts, axis=1))
    even = lax.rem(lax.axis_index("row"), 2) == 0
    to_first[0:STRIP, :] = jnp.where(even, strips[1], strips[0]).astype(BF16)
    to_second[0:STRIP, :] = jnp.where(even, strips[0], strips[1]).astype(BF16)
    to_first[STRIP:, :] = tables
    to_second[STRIP:, :] = tables


def blur_matrix(shape, axis, start=0):
    lag = lax.broadcasted_iota(jnp.int32, shape, axis) - lax.broadcasted_iota(jnp.int32, shape, 1 - axis) - start
    total = sum(math.exp(-(t * t) / (2 * BLUR_SIGMA**2)) for t in range(-BLUR_HALF, BLUR_HALF + 1))
    off = (lag - BLUR_HALF).astype(F32)
    g = jnp.exp(-off * off / (2.0 * BLUR_SIGMA * BLUR_SIGMA)) * (1.0 / total)
    g = jnp.where((lag >= 0) & (lag <= 2 * BLUR_HALF), g, 0.0)
    high = g.astype(BF16)
    return high, (g - high.astype(F32)).astype(BF16)


def own_kernel(mask, taps, windows, ahead, back, g_row, g_far, g_col):
    rows, cols = mask.shape
    full = jnp.concatenate(
        [jnp.zeros((rows, RIM), F32), mask[...].astype(F32), jnp.zeros((rows, WIDE - RIM - cols), F32)], axis=1
    )
    for b in range(NB):
        windows[b] = full[:, CB * b : CB * b + 256]
    kernels, _, count = taps.shape[1:]
    flip = lax.broadcasted_iota(jnp.int32, (128, 128), 0) + lax.broadcasted_iota(jnp.int32, (128, 128), 1)
    flip = jnp.where(flip % 128 == 0, 1.0, 0.0).astype(BF16)
    ahead[...] = jnp.zeros(ahead.shape, F32)
    back[...] = jnp.zeros(back.shape, F32)
    for k in range(kernels):
        ahead[k, 0:2, 0:count] = taps[0, k].astype(F32)
        back[k, 0:2, 0:count] = taps[1, k].astype(F32)
    back[...] = dot_nn(back[...].reshape(kernels * 8, 128).astype(BF16), flip).reshape(kernels, 8, 128)
    g_row[0:128], g_row[128:256] = blur_matrix((128, 256), 1)
    g_far[0:128], g_far[128:256] = blur_matrix((128, 256), 1, 16 - BLUR_HALF)
    g_col[:, 0:128], g_col[:, 128:256] = blur_matrix((256, 128), 0)


def blur_rows(n_row, n_col, acc, g_row, out, flat):
    rows = out.shape[0]
    cols = CB * NB - 2 * BLUR_HALF
    row, col = lax.axis_index("row"), lax.axis_index("col")
    at_row = lax.broadcasted_iota(jnp.int32, (8, 384), 1) - BLUR_HALF
    row_ok = ((row > 0) | (at_row >= 0)) & ((row < n_row - 1) | (at_row < rows))
    row_ok = jnp.where(row_ok, 1.0, 0.0)
    for b in range(NB):
        edge = acc[NB, :, EDGE_IN * b : EDGE_IN * b + EDGE_OUT]
        part = jnp.concatenate(
            [acc[b, :, 0:MAIN], edge, jnp.zeros((CB, 384 - MAIN - EDGE_OUT), F32)], axis=1
        )
        part = part * row_ok[0:1]
        if b == 0:
            part = jnp.concatenate([jnp.where(col > 0, part[0:8], 0.0), part[8:]], axis=0)
        if b == NB - 1:
            part = jnp.concatenate([part[0 : CB - 8], jnp.where(col < n_col - 1, part[CB - 8 :], 0.0)], axis=0)
        flat[b * CB : (b + 1) * CB, :] = part.astype(BF16)
    flat[NB * CB :, :] = jnp.zeros((flat.shape[0] - NB * CB, 384), BF16)

    for i in range(rows // 128):
        part = dot_nt(g_row[...], flat[:, 128 * i : 128 * i + 256])
        out[128 * i : 128 * i + 128, :] = part[0:128] + part[128:]


def socs_kernel(
    entries,
    per,
    empty,
    n_row,
    n_col,
    weights,
    windows,
    row_first,
    row_second,
    col_first,
    col_second,
    own,
    ahead,
    back,
    g_row,
    out,
    images,
    acc,
    flat,
    x_win,
    scale,
    sem,
    *scratch,
):
    across = scratch[0:2]
    down = scratch[2:4]
    first = scratch[4:6]
    groups = ahead.shape[0] // GROUP
    fetch = pltpu.make_async_copy(weights, scale, sem)
    fetch.start()
    above, below = sides("row", row_first[...].astype(F32), row_second[...].astype(F32))
    left, right = sides("col", join(col_first), join(col_second))
    rows = windows.shape[1]
    turned = jnp.concatenate(
        [
            left[STRIP - RIM : STRIP],
            jnp.zeros((128 - RIM + RIGHT_AT, rows), F32),
            right[0:RIM],
            jnp.zeros((128 - RIM - RIGHT_AT, rows), F32),
        ],
        axis=0,
    )
    turned = dot_nt(eye(rows, rows, 0), turned.astype(BF16))
    left, right = left[STRIP:, 0:128], right[STRIP:, 0:128]
    upper_rows = above[STRIP - RIM : STRIP]
    lower_rows = below[0:RIM]
    edge_rows = []
    for b in range(NB):
        lanes = slice(CB * b, CB * b + 256)
        part = windows[b]
        if b == 0:
            part = jnp.concatenate([part[:, 0:128] + turned[:, 0:128], part[:, 128:256]], axis=1)
        if b == NB - 1:
            part = jnp.concatenate([part[:, 0:128], part[:, 128:256] + turned[:, 128:256]], axis=1)
        x_win[b] = jnp.concatenate([upper_rows[:, lanes], part[0 : 256 - RIM]], axis=0).astype(BF16)
        edge_rows += [part[MAIN - RIM :], lower_rows[:, lanes]]
    edge_rows.append(jnp.zeros((256 - NB * EDGE_IN, 256), F32))
    x_win[NB] = jnp.concatenate(edge_rows, axis=0).astype(BF16)
    for s in range(2):
        for q in range(2 * GROUP):
            across[s][q, 0:96, 128:256] = jnp.zeros((96, 128), BF16)
            across[s][q, 128:CB, 0:128] = jnp.zeros((CB - 128, 128), BF16)
            down[s][q, 0:128, 128:256] = jnp.zeros((128, 128), BF16)
            down[s][q, 160:256, 0:128] = jnp.zeros((96, 128), BF16)

    slot = lax.broadcasted_iota(jnp.int32, (SLOTS, 128), 0).astype(F32)
    lane = lax.broadcasted_iota(jnp.int32, (SLOTS, 128), 1)
    found = jnp.zeros((SLOTS, 128), F32)
    col = lax.axis_index("col")
    tables = [above[STRIP:, 128 * t : 128 * t + 128] for t in range(3)]
    tables += [left, own[STRIP:HALF_STRIP, :].astype(F32), right]
    tables += [below[STRIP:, 128 * t : 128 * t + 128] for t in range(3)]
    for t, table in enumerate(tables):
        live = lane.astype(F32) < table[2:3, 0:1]
        hit = live & (table[1:2] == slot) & (lane < entries)
        image = jnp.sum(jnp.where(hit, table[0:1] + 1.0, 0.0), axis=1, keepdims=True)
        found = jnp.where(lane == t, image, found)
    cell = found.astype(jnp.int32) - 1
    images[...] = jnp.where(cell >= 0, ((cell // per) ^ col) * per + cell % per, empty)

    row = lax.broadcasted_iota(jnp.int32, (32, 128), 0)
    lane = lax.broadcasted_iota(jnp.int32, (32, 128), 1)
    low = lane >= row + 96

    def cycled(x):
        return pltpu.roll(jnp.broadcast_to(x, (128, 128)), 0, 1, stride=1, stride_axis=0)

    def build_across(m, s):
        for q in range(2 * GROUP):
            cyc = cycled(ahead[GROUP * m + q // 2, q % 2 : q % 2 + 1, :])
            head = cyc[0:96].astype(BF16)
            tail = cyc[96:128]
            over = jnp.where(low, 0.0, tail)
            across[s][q, 0:96, 0:128] = head
            across[s][q, 128:CB, 128:256] = head[0 : CB - 128]
            across[s][q, 96:128, 0:128] = jnp.where(low, tail, 0.0).astype(BF16)
            across[s][q, 96:128, 128:256] = over.astype(BF16)

    def build_down(m, s):
        for q in range(2 * GROUP):
            cyc = cycled(back[GROUP * m + q // 2, q % 2 : q % 2 + 1, :])
            head = cyc[0:32]
            over = jnp.where(low, head, 0.0).astype(BF16)
            head = jnp.where(low, 0.0, head)
            same = jnp.concatenate([head, cyc[32:128]], axis=0).astype(BF16)
            down[s][q, 0:128, 0:128] = same
            down[s][q, 128:256, 128:256] = same
            down[s][q, 128:160, 0:128] = over

    def pass_one(s):
        taps = across[s][...].reshape(2 * GROUP * CB, 256)
        for j in range(NB + 1):
            part = dot_nt(taps, x_win[j]).astype(BF16)
            for q in range(2 * GROUP):
                first[s][q, j] = part[q * CB : (q + 1) * CB]

    def pass_two(m, s):
        for q in range(2 * GROUP):
            second = dot_nn(first[s][q].reshape((NB + 1) * CB, 256), down[s][q])
            part = (scale[GROUP * m + q // 2] * (second * second)).reshape(acc.shape)
            acc[...] = part if m == 0 and q == 0 else acc[...] + part

    def stage(m, s):
        pass_one(s)
        build_down(m, s)
        if m + 1 < groups:
            build_across(m + 1, 1 - s)
        pass_two(m - 1, 1 - s)

    build_across(0, 0)
    pass_one(0)
    build_down(0, 0)
    build_across(1, 1)
    fetch.wait()

    for m in range(1, groups):
        stage(m, m % 2)
    pass_two(groups - 1, (groups - 1) % 2)
    blur_rows(n_row, n_col, acc, g_row, out, flat)


def final_kernel(images, blurred_rows, g_far, g_col, *rest):
    shards = rest[:-4]
    out, cells, placed, blurred = rest[-4:]
    per = (cells.shape[0] - 1) // len(shards)
    rows, cols = out.shape
    table = images[...]
    for i, shard in enumerate(shards):
        rows_of = shard.shape[0] - per * 64
        cells[i * per : (i + 1) * per] = shard[rows_of:, :].reshape(per, 64, 128)
    cells[len(shards) * per] = jnp.zeros((64, 128), BF16)

    slot_rows, slot_cols = rows // 64, cols // 128
    for i in range(-1, slot_rows + 1):
        for j in range(-1, slot_cols + 1):
            ti = 0 if i < 0 else (2 if i == slot_rows else 1)
            tj = 0 if j < 0 else (2 if j == slot_cols else 1)
            image = table[(i % slot_rows) * slot_cols + j % slot_cols, 3 * ti + tj]
            lanes = slice(128 + 128 * j, 256 + 128 * j)
            if i < 0:
                placed[0:16, lanes] = cells[image, 48:64, :]
            elif i == slot_rows:
                placed[16 + rows : 32 + rows, lanes] = cells[image, 0:16, :]
            else:
                placed[16 + 64 * i : 80 + 64 * i, lanes] = cells[image]
    placed[32 + rows :, :] = jnp.zeros((placed.shape[0] - 32 - rows, placed.shape[1]), BF16)

    for i in range(rows // 128):
        part = blurred_rows[128 * i : 128 * i + 128, :]
        cell = dot_nn(g_far[...], placed[128 * i : 128 * i + 256, :])
        cell = cell[0:128] + cell[128:]
        part += cell[:, 128 - BLUR_HALF : 128 - BLUR_HALF + part.shape[1]]
        high = part.astype(BF16)
        blurred[0, 128 * i : 128 * i + 128, :] = high
        blurred[1, 128 * i : 128 * i + 128, :] = (part - high.astype(F32)).astype(BF16)
    count = cols // 128
    stacked = [
        jnp.concatenate([blurred[p, :, 128 * j : 128 * j + 256] for j in range(count)], axis=0) for p in range(2)
    ]
    part = dot_nn(stacked[0], g_col[...])
    part = part[:, 0:128] + part[:, 128:] + dot_nn(stacked[1], g_col[:, 0:128])
    for j in range(count):
        out[:, 128 * j : 128 * j + 128] = part[rows * j : rows * j + rows]


def shape(dims, dtype):
    return jax.ShapeDtypeStruct(dims, dtype)


def on_device(
    mask_pixels, across_taps, down_taps, kernel_weights, library, cell_ids, cell_slots, cell_count
):
    rows, cols = mask_pixels.shape
    kernels = across_taps.shape[0]
    entries = cell_ids.shape[-1]
    per = library.shape[0]
    n_row, n_col = lax.axis_size("row"), lax.axis_size("col")
    library = library.reshape(per * 64, 128)
    in_hbm = lambda x: pltpu.with_memory_space_constraint(x, pltpu.HBM)
    mask_hbm = in_hbm(mask_pixels)

    to_first, to_second, block, taps, line_weights = pl.pallas_call(
        prep_kernel,
        out_shape=(
            shape((2 * HALF_STRIP, 128), BF16),
            shape((128, 128), BF16),
            shape((SPARE + per * 64, 128), BF16),
            shape((2,) + across_taps.shape, BF16),
            shape(kernel_weights.shape, F32),
        ),
        in_specs=[HBM] * 3 + [VMEM] + [HBM] * 4,
        out_specs=(VMEM,) * 5,
        scratch_shapes=[
            pltpu.VMEM((2, rows, 128), jnp.int32),
            pltpu.VMEM(cell_ids.shape, jnp.int32),
            pltpu.VMEM(cell_slots.shape, jnp.int32),
            pltpu.SemaphoreType.DMA((8,)),
        ],
        compiler_params=PARAMS,
        name="prep",
    )(mask_hbm, in_hbm(cell_ids), in_hbm(cell_slots), cell_count, in_hbm(across_taps), in_hbm(down_taps), in_hbm(library), in_hbm(kernel_weights))

    def swaps(n):
        rounds = []
        for start in (0, 1):
            pairs = [(i, (i + 1) % n) for i in range(start, n, 2)]
            rounds.append(pairs + [(b, a) for a, b in pairs])
        return rounds

    second = []
    for r in range(n_row):
        second += [(r * n_col + a, r * n_col + b) for a, b in swaps(n_col)[1] if abs(a - b) == 1]
        second += [(r * n_col + a, (r ^ 1) * n_col + a) for a in (0, n_col - 1)]

    col_second = lax.ppermute(to_second, ("row", "col"), second)
    col_first = lax.ppermute(to_first, "col", swaps(n_col)[0])

    to_above, to_below = pl.pallas_call(
        mid_kernel,
        out_shape=(shape((STRIP + 16, WIDE), BF16),) * 2,
        in_specs=[VMEM] * 4,
        out_specs=(VMEM,) * 2,
        compiler_params=PARAMS,
        name="mid",
    )(mask_pixels, col_first, col_second, to_first)
    late, to_above, to_below = lax.optimization_barrier((library, to_above, to_below))
    blocks = {0: library}
    for d in sorted(range(1, n_col), key=lambda d: (d == n_col - 1, -(d & -d))):
        part = late if d == n_col - 1 else block
        blocks[d] = lax.ppermute(part, "col", [(i, i ^ d) for i in range(n_col)])
    shards = [blocks[d] for d in range(n_col)]
    ends = []
    for f in range(lax.axis_size("frames")):
        ends += [(f * n_row + a, f * n_row + b) for a, b in swaps(n_row)[1] if abs(a - b) == 1]
        ends += [(f * n_row + a, (f ^ 1) * n_row + a) for a in (0, n_row - 1)]
    row_first = lax.ppermute(to_above, "row", swaps(n_row)[0])
    row_second = lax.ppermute(to_below, ("frames", "row"), ends)

    windows, ahead, back, g_row, g_far, g_col = pl.pallas_call(
        own_kernel,
        out_shape=(
            shape((NB, rows, 256), F32),
            shape((kernels, 8, 128), F32),
            shape((kernels, 8, 128), F32),
            shape((256, 256), BF16),
            shape((256, 256), BF16),
            shape((256, 256), BF16),
        ),
        in_specs=[VMEM] * 2,
        out_specs=(VMEM,) * 6,
        compiler_params=PARAMS,
        cost_estimate=pl.CostEstimate(flops=10**6, bytes_accessed=10**6, transcendentals=0),
        name="own",
    )(mask_pixels, taps)

    blurred_rows, images = pl.pallas_call(
        functools.partial(socs_kernel, entries, per, n_col * per, n_row, n_col),
        out_shape=(shape((rows, WIDE), F32), shape((SLOTS, 128), jnp.int32)),
        in_specs=[VMEM] * 10,
        out_specs=(VMEM,) * 2,
        scratch_shapes=[
            pltpu.VMEM((NB + 1, CB, 256), F32),
            pltpu.VMEM((WIDE, 384), BF16),
            pltpu.VMEM((NB + 1, 256, 256), BF16),
            pltpu.SMEM(kernel_weights.shape, F32),
            pltpu.SemaphoreType.DMA,
        ]
        + [pltpu.VMEM((2 * GROUP, CB, 256), BF16)] * 2
        + [pltpu.VMEM((2 * GROUP, 256, 256), BF16)] * 2
        + [pltpu.VMEM((2 * GROUP, NB + 1, CB, 256), BF16)] * 2,
        compiler_params=PARAMS,
        cost_estimate=pl.CostEstimate(flops=75 * 10**7, bytes_accessed=10**5, transcendentals=0),
        name="socs",
    )(line_weights, windows, row_first, row_second, col_first, col_second, to_first, ahead, back, g_row)

    return pl.pallas_call(
        final_kernel,
        out_shape=shape((rows, cols), F32),
        in_specs=[VMEM] * (4 + n_col),
        out_specs=VMEM,
        scratch_shapes=[
            pltpu.VMEM((n_col * per + 1, 64, 128), BF16),
            pltpu.VMEM((384, cols + 256), BF16),
            pltpu.VMEM((2, rows, WIDE), BF16),
        ],
        compiler_params=PARAMS,
        name="final",
    )(images, blurred_rows, g_far, g_col, *shards)


def solution(mesh):
    placed = (
        P(("frames", "row"), "col"),
        P(),
        P(),
        P(),
        P("col", None, None),
        P(("frames", "row"), "col", None),
        P(("frames", "row"), "col", None),
        P(("frames", "row"), "col"),
    )
    return jax.shard_map(
        on_device,
        mesh=mesh,
        in_specs=placed,
        out_specs=P(("frames", "row"), "col"),
        check_vma=False,
    )
```

```python
import functools
import math

import jax
import jax.numpy as jnp
from jax import lax
from jax.experimental import pallas as pl
from jax.experimental.pallas import tpu as pltpu
from jax.sharding import PartitionSpec as P

BLUR_HALF = 8
BLUR_SIGMA = 4.0
HALF = 16
RIM = HALF + BLUR_HALF
STRIP = 32
CB = 176
NB = 3
MAIN = 224
EDGE_IN = 80
EDGE_OUT = 48
RIGHT_AT = 56
HALF_STRIP = STRIP + 16
SPARE = 16
GROUP = 2
WIDE = 640
SLOTS = 16
F32 = jnp.float32
BF16 = jnp.bfloat16
VMEM = pl.BlockSpec(memory_space=pltpu.VMEM)
SMEM = pl.BlockSpec(memory_space=pltpu.SMEM)
HBM = pl.BlockSpec(memory_space=pltpu.HBM)
PARAMS = pltpu.CompilerParams(vmem_limit_bytes=16 * 1024 * 1024)


def dot_nt(a, b):
    return lax.dot_general(a, b, (((1,), (1,)), ((), ())), preferred_element_type=F32)


def dot_nn(a, b):
    return lax.dot_general(a, b, (((1,), (0,)), ((), ())), preferred_element_type=F32)


def join(strip):
    halves = [strip[0:HALF_STRIP, :], strip[HALF_STRIP : 2 * HALF_STRIP, :]]
    return jnp.concatenate(halves, axis=1).astype(F32)


def eye(rows, cols, shift):
    at = lax.broadcasted_iota(jnp.int32, (rows, cols), 1) - lax.broadcasted_iota(jnp.int32, (rows, cols), 0)
    return jnp.where(at == shift, 1.0, 0.0).astype(BF16)


def sides(axis, first_swap, second_swap):
    index, count = lax.axis_index(axis), lax.axis_size(axis)
    even = lax.rem(index, 2) == 0
    lower = jnp.where(even, second_swap, first_swap)
    upper = jnp.where(even, first_swap, second_swap)
    return jnp.where(index > 0, lower, 0.0), jnp.where(index < count - 1, upper, 0.0)


def prep_kernel(
    mask, ids, slots, count, across, down, library, weights, to_first, to_second, block, taps, line_weights, ends, a_ids, a_slots, sems
):
    rows, cols = mask.shape
    copies = [
        pltpu.make_async_copy(mask.at[:, 0:128], ends.at[0], sems.at[0]),
        pltpu.make_async_copy(mask.at[:, cols - 128 : cols], ends.at[1], sems.at[1]),
        pltpu.make_async_copy(ids, a_ids, sems.at[2]),
        pltpu.make_async_copy(slots, a_slots, sems.at[3]),
        pltpu.make_async_copy(across, taps.at[0], sems.at[4]),
        pltpu.make_async_copy(down, taps.at[1], sems.at[5]),
        pltpu.make_async_copy(library, block.at[SPARE:], sems.at[6]),
        pltpu.make_async_copy(weights, line_weights, sems.at[7]),
    ]
    for copy in copies:
        copy.start()
    for copy in copies[2:4]:
        copy.wait()
    line = lax.broadcasted_iota(jnp.int32, (16, 128), 0)
    lane = lax.broadcasted_iota(jnp.int32, (16, 128), 1)

    def spread(x):
        x = x.astype(F32)
        x = jnp.concatenate([x, jnp.zeros((1, 128 - x.shape[1]), F32)], axis=1)
        return jnp.broadcast_to(x, (16, 128))

    table = jnp.where(line == 1, spread(a_slots[0]), jnp.broadcast_to(count[...].astype(F32), (16, 128)))
    table = jnp.where(line == 0, spread(a_ids[0]), table)
    width = jnp.where(line == 2, 1, ids.shape[2])
    table = jnp.where((lane < width) & (line < 3), table, 0.0).astype(BF16)
    for strip in (to_first, to_second):
        strip[STRIP:HALF_STRIP, :] = table
        strip[HALF_STRIP + STRIP : 2 * HALF_STRIP, :] = jnp.zeros((16, 128), BF16)
    block[0:SPARE, :] = jnp.zeros((SPARE, 128), BF16)
    to_second[2 * HALF_STRIP :, :] = jnp.zeros((128 - 2 * HALF_STRIP, 128), BF16)
    even = lax.rem(lax.axis_index("col"), 2) == 0
    copies[0].wait()
    first = dot_nt(eye(STRIP, 128, 0), ends[0].astype(F32).astype(BF16))
    copies[1].wait()
    last = dot_nt(eye(STRIP, 128, 128 - STRIP), ends[1].astype(F32).astype(BF16))
    for strip, part in ((to_first, jnp.where(even, last, first)), (to_second, jnp.where(even, first, last))):
        strip[0:STRIP, :] = part[:, 0:128].astype(BF16)
        strip[HALF_STRIP : HALF_STRIP + STRIP, :] = part[:, 128:256].astype(BF16)
    for copy in copies[4:]:
        copy.wait()


def mid_kernel(mask, from_first, from_second, own, to_first, to_second):
    rows, cols = mask.shape
    left, right = sides("col", join(from_first), join(from_second))
    tables = jnp.concatenate(
        [left[STRIP:, 0:128], own[STRIP:HALF_STRIP, :].astype(F32), right[STRIP:, 0:128], jnp.zeros((16, 256), F32)],
        axis=1,
    ).astype(BF16)
    fill = jnp.zeros((128 - STRIP, 128), F32)
    strips = []
    for i in range(2):
        at = 0 if i == 0 else rows - 128
        pick = eye(STRIP, 128, 0 if i == 0 else 128 - STRIP)

        def turned(strip):
            return dot_nt(pick, jnp.concatenate([strip[0:STRIP, at : at + 128], fill], axis=0).astype(BF16))

        parts = [turned(left)[:, STRIP - RIM : STRIP], mask[(rows - STRIP) * i : (rows - STRIP) * i + STRIP, :].astype(F32), turned(right)[:, 0 : WIDE - RIM - cols]]
        strips.append(jnp.concatenate(parts, axis=1))
    even = lax.rem(lax.axis_index("row"), 2) == 0
    to_first[0:STRIP, :] = jnp.where(even, strips[1], strips[0]).astype(BF16)
    to_second[0:STRIP, :] = jnp.where(even, strips[0], strips[1]).astype(BF16)
    to_first[STRIP:, :] = tables
    to_second[STRIP:, :] = tables


def blur_matrix(shape, axis, start=0):
    lag = lax.broadcasted_iota(jnp.int32, shape, axis) - lax.broadcasted_iota(jnp.int32, shape, 1 - axis) - start
    total = sum(math.exp(-(t * t) / (2 * BLUR_SIGMA**2)) for t in range(-BLUR_HALF, BLUR_HALF + 1))
    off = (lag - BLUR_HALF).astype(F32)
    g = jnp.exp(-off * off / (2.0 * BLUR_SIGMA * BLUR_SIGMA)) * (1.0 / total)
    g = jnp.where((lag >= 0) & (lag <= 2 * BLUR_HALF), g, 0.0)
    high = g.astype(BF16)
    return high, (g - high.astype(F32)).astype(BF16)


def own_kernel(mask, taps, windows, ahead, back, g_row, g_far, g_col):
    rows, cols = mask.shape
    full = jnp.concatenate(
        [jnp.zeros((rows, RIM), F32), mask[...].astype(F32), jnp.zeros((rows, WIDE - RIM - cols), F32)], axis=1
    )
    for b in range(NB):
        windows[b] = full[:, CB * b : CB * b + 256]
    kernels, _, count = taps.shape[1:]
    flip = lax.broadcasted_iota(jnp.int32, (128, 128), 0) + lax.broadcasted_iota(jnp.int32, (128, 128), 1)
    flip = jnp.where(flip % 128 == 0, 1.0, 0.0).astype(BF16)
    ahead[...] = jnp.zeros(ahead.shape, F32)
    back[...] = jnp.zeros(back.shape, F32)
    for k in range(kernels):
        ahead[k, 0:2, 0:count] = taps[0, k].astype(F32)
        back[k, 0:2, 0:count] = taps[1, k].astype(F32)
    back[...] = dot_nn(back[...].reshape(kernels * 8, 128).astype(BF16), flip).reshape(kernels, 8, 128)
    g_row[0:128], g_row[128:256] = blur_matrix((128, 256), 1)
    g_far[0:128], g_far[128:256] = blur_matrix((128, 256), 1, 16 - BLUR_HALF)
    g_col[:, 0:128], g_col[:, 128:256] = blur_matrix((256, 128), 0)


def socs_kernel(
    entries,
    per,
    empty,
    weights,
    windows,
    row_first,
    row_second,
    col_first,
    col_second,
    own,
    ahead,
    back,
    acc,
    images,
    x_win,
    scale,
    sem,
    *scratch,
):
    across = scratch[0:2]
    down = scratch[2:4]
    first = scratch[4:6]
    groups = ahead.shape[0] // GROUP
    fetch = pltpu.make_async_copy(weights, scale, sem)
    fetch.start()
    above, below = sides("row", row_first[...].astype(F32), row_second[...].astype(F32))
    left, right = sides("col", join(col_first), join(col_second))
    rows = windows.shape[1]
    turned = jnp.concatenate(
        [
            left[STRIP - RIM : STRIP],
            jnp.zeros((128 - RIM + RIGHT_AT, rows), F32),
            right[0:RIM],
            jnp.zeros((128 - RIM - RIGHT_AT, rows), F32),
        ],
        axis=0,
    )
    turned = dot_nt(eye(rows, rows, 0), turned.astype(BF16))
    left, right = left[STRIP:, 0:128], right[STRIP:, 0:128]
    upper_rows = above[STRIP - RIM : STRIP]
    lower_rows = below[0:RIM]
    edge_rows = []
    for b in range(NB):
        lanes = slice(CB * b, CB * b + 256)
        part = windows[b]
        if b == 0:
            part = jnp.concatenate([part[:, 0:128] + turned[:, 0:128], part[:, 128:256]], axis=1)
        if b == NB - 1:
            part = jnp.concatenate([part[:, 0:128], part[:, 128:256] + turned[:, 128:256]], axis=1)
        x_win[b] = jnp.concatenate([upper_rows[:, lanes], part[0 : 256 - RIM]], axis=0).astype(BF16)
        edge_rows += [part[MAIN - RIM :], lower_rows[:, lanes]]
    edge_rows.append(jnp.zeros((256 - NB * EDGE_IN, 256), F32))
    x_win[NB] = jnp.concatenate(edge_rows, axis=0).astype(BF16)
    for s in range(2):
        for q in range(2 * GROUP):
            across[s][q, 0:96, 128:256] = jnp.zeros((96, 128), BF16)
            across[s][q, 128:CB, 0:128] = jnp.zeros((CB - 128, 128), BF16)
            down[s][q, 0:128, 128:256] = jnp.zeros((128, 128), BF16)
            down[s][q, 160:256, 0:128] = jnp.zeros((96, 128), BF16)

    slot = lax.broadcasted_iota(jnp.int32, (SLOTS, 128), 0).astype(F32)
    lane = lax.broadcasted_iota(jnp.int32, (SLOTS, 128), 1)
    found = jnp.zeros((SLOTS, 128), F32)
    col = lax.axis_index("col")
    tables = [above[STRIP:, 128 * t : 128 * t + 128] for t in range(3)]
    tables += [left, own[STRIP:HALF_STRIP, :].astype(F32), right]
    tables += [below[STRIP:, 128 * t : 128 * t + 128] for t in range(3)]
    for t, table in enumerate(tables):
        live = lane.astype(F32) < table[2:3, 0:1]
        hit = live & (table[1:2] == slot) & (lane < entries)
        image = jnp.sum(jnp.where(hit, table[0:1] + 1.0, 0.0), axis=1, keepdims=True)
        found = jnp.where(lane == t, image, found)
    cell = found.astype(jnp.int32) - 1
    images[...] = jnp.where(cell >= 0, ((cell // per) ^ col) * per + cell % per, empty)

    row = lax.broadcasted_iota(jnp.int32, (32, 128), 0)
    lane = lax.broadcasted_iota(jnp.int32, (32, 128), 1)
    low = lane >= row + 96

    def cycled(x):
        return pltpu.roll(jnp.broadcast_to(x, (128, 128)), 0, 1, stride=1, stride_axis=0)

    def build_across(m, s):
        for q in range(2 * GROUP):
            cyc = cycled(ahead[GROUP * m + q // 2, q % 2 : q % 2 + 1, :])
            head = cyc[0:96].astype(BF16)
            tail = cyc[96:128]
            over = jnp.where(low, 0.0, tail)
            across[s][q, 0:96, 0:128] = head
            across[s][q, 128:CB, 128:256] = head[0 : CB - 128]
            across[s][q, 96:128, 0:128] = jnp.where(low, tail, 0.0).astype(BF16)
            across[s][q, 96:128, 128:256] = over.astype(BF16)

    def build_down(m, s):
        for q in range(2 * GROUP):
            cyc = cycled(back[GROUP * m + q // 2, q % 2 : q % 2 + 1, :])
            head = cyc[0:32]
            over = jnp.where(low, head, 0.0).astype(BF16)
            head = jnp.where(low, 0.0, head)
            same = jnp.concatenate([head, cyc[32:128]], axis=0).astype(BF16)
            down[s][q, 0:128, 0:128] = same
            down[s][q, 128:256, 128:256] = same
            down[s][q, 128:160, 0:128] = over

    def pass_one(s):
        taps = across[s][...].reshape(2 * GROUP * CB, 256)
        for j in range(NB + 1):
            part = dot_nt(taps, x_win[j]).astype(BF16)
            for q in range(2 * GROUP):
                first[s][q, j] = part[q * CB : (q + 1) * CB]

    def pass_two(m, s):
        for g in range(GROUP):
            total = None
            for q in (2 * g, 2 * g + 1):
                second = dot_nn(first[s][q].reshape((NB + 1) * CB, 256), down[s][q])
                total = second * second if total is None else total + second * second
            part = (scale[GROUP * m + g] * total).reshape(acc.shape)
            acc[...] = part if m == 0 and g == 0 else acc[...] + part

    def stage(m, s):
        pass_one(s)
        build_down(m, s)
        if m + 1 < groups:
            build_across(m + 1, 1 - s)
        pass_two(m - 1, 1 - s)

    build_across(0, 0)
    pass_one(0)
    build_down(0, 0)
    build_across(1, 1)
    fetch.wait()

    for m in range(1, groups):
        stage(m, m % 2)
    pass_two(groups - 1, (groups - 1) % 2)


def rows_kernel(n_row, n_col, acc, g_row, out, flat):
    rows = out.shape[0]
    cols = CB * NB - 2 * BLUR_HALF
    row, col = lax.axis_index("row"), lax.axis_index("col")
    at_row = lax.broadcasted_iota(jnp.int32, (8, 384), 1) - BLUR_HALF
    row_ok = ((row > 0) | (at_row >= 0)) & ((row < n_row - 1) | (at_row < rows))
    row_ok = jnp.where(row_ok, 1.0, 0.0)
    for b in range(NB):
        edge = acc[NB, :, EDGE_IN * b : EDGE_IN * b + EDGE_OUT]
        part = jnp.concatenate(
            [acc[b, :, 0:MAIN], edge, jnp.zeros((CB, 384 - MAIN - EDGE_OUT), F32)], axis=1
        )
        part = part * row_ok[0:1]
        if b == 0:
            part = jnp.concatenate([jnp.where(col > 0, part[0:8], 0.0), part[8:]], axis=0)
        if b == NB - 1:
            part = jnp.concatenate([part[0 : CB - 8], jnp.where(col < n_col - 1, part[CB - 8 :], 0.0)], axis=0)
        flat[b * CB : (b + 1) * CB, :] = part.astype(BF16)
    flat[NB * CB :, :] = jnp.zeros((flat.shape[0] - NB * CB, 384), BF16)

    for i in range(rows // 128):
        part = dot_nt(g_row[...], flat[:, 128 * i : 128 * i + 256])
        out[128 * i : 128 * i + 128, :] = part[0:128] + part[128:]


def final_kernel(images, blurred_rows, g_far, g_col, *rest):
    shards = rest[:-4]
    out, cells, placed, blurred = rest[-4:]
    per = (cells.shape[0] - 1) // len(shards)
    rows, cols = out.shape
    table = images[...]
    for i, shard in enumerate(shards):
        rows_of = shard.shape[0] - per * 64
        cells[i * per : (i + 1) * per] = shard[rows_of:, :].reshape(per, 64, 128)
    cells[len(shards) * per] = jnp.zeros((64, 128), BF16)

    slot_rows, slot_cols = rows // 64, cols // 128
    for i in range(-1, slot_rows + 1):
        for j in range(-1, slot_cols + 1):
            ti = 0 if i < 0 else (2 if i == slot_rows else 1)
            tj = 0 if j < 0 else (2 if j == slot_cols else 1)
            image = table[(i % slot_rows) * slot_cols + j % slot_cols, 3 * ti + tj]
            lanes = slice(128 + 128 * j, 256 + 128 * j)
            if i < 0:
                placed[0:16, lanes] = cells[image, 48:64, :]
            elif i == slot_rows:
                placed[16 + rows : 32 + rows, lanes] = cells[image, 0:16, :]
            else:
                placed[16 + 64 * i : 80 + 64 * i, lanes] = cells[image]
    placed[32 + rows :, :] = jnp.zeros((placed.shape[0] - 32 - rows, placed.shape[1]), BF16)

    for i in range(rows // 128):
        part = blurred_rows[128 * i : 128 * i + 128, :]
        cell = dot_nn(g_far[...], placed[128 * i : 128 * i + 256, :])
        cell = cell[0:128] + cell[128:]
        part += cell[:, 128 - BLUR_HALF : 128 - BLUR_HALF + part.shape[1]]
        high = part.astype(BF16)
        blurred[0, 128 * i : 128 * i + 128, :] = high
        blurred[1, 128 * i : 128 * i + 128, :] = (part - high.astype(F32)).astype(BF16)
    count = cols // 128
    stacked = [
        jnp.concatenate([blurred[p, :, 128 * j : 128 * j + 256] for j in range(count)], axis=0) for p in range(2)
    ]
    part = dot_nn(stacked[0], g_col[...])
    part = part[:, 0:128] + part[:, 128:] + dot_nn(stacked[1], g_col[:, 0:128])
    for j in range(count):
        out[:, 128 * j : 128 * j + 128] = part[rows * j : rows * j + rows]


def shape(dims, dtype):
    return jax.ShapeDtypeStruct(dims, dtype)


def on_device(
    mask_pixels, across_taps, down_taps, kernel_weights, library, cell_ids, cell_slots, cell_count
):
    rows, cols = mask_pixels.shape
    kernels = across_taps.shape[0]
    entries = cell_ids.shape[-1]
    per = library.shape[0]
    n_row, n_col = lax.axis_size("row"), lax.axis_size("col")
    library = library.reshape(per * 64, 128)
    in_hbm = lambda x: pltpu.with_memory_space_constraint(x, pltpu.HBM)
    mask_hbm = in_hbm(mask_pixels)

    to_first, to_second, block, taps, line_weights = pl.pallas_call(
        prep_kernel,
        out_shape=(
            shape((2 * HALF_STRIP, 128), BF16),
            shape((128, 128), BF16),
            shape((SPARE + per * 64, 128), BF16),
            shape((2,) + across_taps.shape, BF16),
            shape(kernel_weights.shape, F32),
        ),
        in_specs=[HBM] * 3 + [VMEM] + [HBM] * 4,
        out_specs=(VMEM,) * 5,
        scratch_shapes=[
            pltpu.VMEM((2, rows, 128), jnp.int32),
            pltpu.VMEM(cell_ids.shape, jnp.int32),
            pltpu.VMEM(cell_slots.shape, jnp.int32),
            pltpu.SemaphoreType.DMA((8,)),
        ],
        compiler_params=PARAMS,
        name="prep",
    )(mask_hbm, in_hbm(cell_ids), in_hbm(cell_slots), cell_count, in_hbm(across_taps), in_hbm(down_taps), in_hbm(library), in_hbm(kernel_weights))

    def swaps(n):
        rounds = []
        for start in (0, 1):
            pairs = [(i, (i + 1) % n) for i in range(start, n, 2)]
            rounds.append(pairs + [(b, a) for a, b in pairs])
        return rounds

    second = []
    for r in range(n_row):
        second += [(r * n_col + a, r * n_col + b) for a, b in swaps(n_col)[1] if abs(a - b) == 1]
        second += [(r * n_col + a, (r ^ 1) * n_col + a) for a in (0, n_col - 1)]

    col_second = lax.ppermute(to_second, ("row", "col"), second)
    col_first = lax.ppermute(to_first, "col", swaps(n_col)[0])

    to_above, to_below = pl.pallas_call(
        mid_kernel,
        out_shape=(shape((STRIP + 16, WIDE), BF16),) * 2,
        in_specs=[VMEM] * 4,
        out_specs=(VMEM,) * 2,
        compiler_params=PARAMS,
        name="mid",
    )(mask_pixels, col_first, col_second, to_first)
    late, to_above, to_below = lax.optimization_barrier((library, to_above, to_below))
    blocks = {0: library}
    for d in sorted(range(1, n_col), key=lambda d: d == 1):
        part = late if d == 1 else block
        blocks[d] = lax.ppermute(part, "col", [(i, i ^ d) for i in range(n_col)])
    shards = [blocks[d] for d in range(n_col)]
    ends = []
    for f in range(lax.axis_size("frames")):
        ends += [(f * n_row + a, f * n_row + b) for a, b in swaps(n_row)[1] if abs(a - b) == 1]
        ends += [(f * n_row + a, (f ^ 1) * n_row + a) for a in (0, n_row - 1)]
    row_first = lax.ppermute(to_above, "row", swaps(n_row)[0])
    row_second = lax.ppermute(to_below, ("frames", "row"), ends)

    windows, ahead, back, g_row, g_far, g_col = pl.pallas_call(
        own_kernel,
        out_shape=(
            shape((NB, rows, 256), F32),
            shape((kernels, 8, 128), F32),
            shape((kernels, 8, 128), F32),
            shape((256, 256), BF16),
            shape((256, 256), BF16),
            shape((256, 256), BF16),
        ),
        in_specs=[VMEM] * 2,
        out_specs=(VMEM,) * 6,
        compiler_params=PARAMS,
        cost_estimate=pl.CostEstimate(flops=10**6, bytes_accessed=10**6, transcendentals=0),
        name="own",
    )(mask_pixels, taps)

    acc, images = pl.pallas_call(
        functools.partial(socs_kernel, entries, per, n_col * per),
        out_shape=(shape((NB + 1, CB, 256), F32), shape((SLOTS, 128), jnp.int32)),
        in_specs=[VMEM] * 9,
        out_specs=(VMEM,) * 2,
        scratch_shapes=[
            pltpu.VMEM((NB + 1, 256, 256), BF16),
            pltpu.SMEM(kernel_weights.shape, F32),
            pltpu.SemaphoreType.DMA,
        ]
        + [pltpu.VMEM((2 * GROUP, CB, 256), BF16)] * 2
        + [pltpu.VMEM((2 * GROUP, 256, 256), BF16)] * 2
        + [pltpu.VMEM((2 * GROUP, NB + 1, CB, 256), BF16)] * 2,
        compiler_params=PARAMS,
        cost_estimate=pl.CostEstimate(flops=75 * 10**7, bytes_accessed=10**5, transcendentals=0),
        name="socs",
    )(line_weights, windows, row_first, row_second, col_first, col_second, to_first, ahead, back)

    blurred_rows = pl.pallas_call(
        functools.partial(rows_kernel, n_row, n_col),
        out_shape=shape((rows, WIDE), F32),
        in_specs=[VMEM] * 2,
        out_specs=VMEM,
        scratch_shapes=[pltpu.VMEM((WIDE, 384), BF16)],
        compiler_params=PARAMS,
        cost_estimate=pl.CostEstimate(flops=10**6, bytes_accessed=10**5, transcendentals=0),
        name="rows",
    )(acc, g_row)

    return pl.pallas_call(
        final_kernel,
        out_shape=shape((rows, cols), F32),
        in_specs=[VMEM] * (4 + n_col),
        out_specs=VMEM,
        scratch_shapes=[
            pltpu.VMEM((n_col * per + 1, 64, 128), BF16),
            pltpu.VMEM((384, cols + 256), BF16),
            pltpu.VMEM((2, rows, WIDE), BF16),
        ],
        compiler_params=PARAMS,
        name="final",
    )(images, blurred_rows, g_far, g_col, *shards)


def solution(mesh):
    placed = (
        P(("frames", "row"), "col"),
        P(),
        P(),
        P(),
        P("col", None, None),
        P(("frames", "row"), "col", None),
        P(("frames", "row"), "col", None),
        P(("frames", "row"), "col"),
    )
    return jax.shard_map(
        on_device,
        mesh=mesh,
        in_specs=placed,
        out_specs=P(("frames", "row"), "col"),
        check_vma=False,
    )
```

```python
import functools
import math

import jax
import jax.numpy as jnp
from jax import lax
from jax.experimental import pallas as pl
from jax.experimental.pallas import tpu as pltpu
from jax.sharding import PartitionSpec as P

BLUR_HALF = 8
BLUR_SIGMA = 4.0
HALF = 16
RIM = HALF + BLUR_HALF
STRIP = 32
CB = 176
NB = 3
MAIN = 224
EDGE_IN = 80
EDGE_OUT = 48
RIGHT_AT = 56
HALF_STRIP = STRIP + 16
SPARE = 16
GROUP = 2
WIDE = 640
SLOTS = 16
F32 = jnp.float32
BF16 = jnp.bfloat16
VMEM = pl.BlockSpec(memory_space=pltpu.VMEM)
SMEM = pl.BlockSpec(memory_space=pltpu.SMEM)
HBM = pl.BlockSpec(memory_space=pltpu.HBM)
PARAMS = pltpu.CompilerParams(vmem_limit_bytes=16 * 1024 * 1024)


def dot_nt(a, b):
    return lax.dot_general(a, b, (((1,), (1,)), ((), ())), preferred_element_type=F32)


def dot_nn(a, b):
    return lax.dot_general(a, b, (((1,), (0,)), ((), ())), preferred_element_type=F32)


def join(strip):
    halves = [strip[0:HALF_STRIP, :], strip[HALF_STRIP : 2 * HALF_STRIP, :]]
    return jnp.concatenate(halves, axis=1).astype(F32)


def eye(rows, cols, shift):
    at = lax.broadcasted_iota(jnp.int32, (rows, cols), 1) - lax.broadcasted_iota(jnp.int32, (rows, cols), 0)
    return jnp.where(at == shift, 1.0, 0.0).astype(BF16)


def sides(axis, first_swap, second_swap):
    index, count = lax.axis_index(axis), lax.axis_size(axis)
    even = lax.rem(index, 2) == 0
    lower = jnp.where(even, second_swap, first_swap)
    upper = jnp.where(even, first_swap, second_swap)
    return jnp.where(index > 0, lower, 0.0), jnp.where(index < count - 1, upper, 0.0)


def prep_kernel(
    mask, ids, slots, count, across, down, library, weights, to_first, to_second, block, taps, line_weights, ends, a_ids, a_slots, sems
):
    rows, cols = mask.shape
    copies = [
        pltpu.make_async_copy(mask.at[:, 0:128], ends.at[0], sems.at[0]),
        pltpu.make_async_copy(mask.at[:, cols - 128 : cols], ends.at[1], sems.at[1]),
        pltpu.make_async_copy(ids, a_ids, sems.at[2]),
        pltpu.make_async_copy(slots, a_slots, sems.at[3]),
        pltpu.make_async_copy(across, taps.at[0], sems.at[4]),
        pltpu.make_async_copy(down, taps.at[1], sems.at[5]),
        pltpu.make_async_copy(library, block.at[SPARE:], sems.at[6]),
        pltpu.make_async_copy(weights, line_weights, sems.at[7]),
    ]
    for copy in copies:
        copy.start()
    for copy in copies[2:4]:
        copy.wait()
    line = lax.broadcasted_iota(jnp.int32, (16, 128), 0)
    lane = lax.broadcasted_iota(jnp.int32, (16, 128), 1)

    def spread(x):
        x = x.astype(F32)
        x = jnp.concatenate([x, jnp.zeros((1, 128 - x.shape[1]), F32)], axis=1)
        return jnp.broadcast_to(x, (16, 128))

    table = jnp.where(line == 1, spread(a_slots[0]), jnp.broadcast_to(count[...].astype(F32), (16, 128)))
    table = jnp.where(line == 0, spread(a_ids[0]), table)
    width = jnp.where(line == 2, 1, ids.shape[2])
    table = jnp.where((lane < width) & (line < 3), table, 0.0).astype(BF16)
    for strip in (to_first, to_second):
        strip[STRIP:HALF_STRIP, :] = table
        strip[HALF_STRIP + STRIP : 2 * HALF_STRIP, :] = jnp.zeros((16, 128), BF16)
    block[0:SPARE, :] = jnp.zeros((SPARE, 128), BF16)
    to_second[2 * HALF_STRIP :, :] = jnp.zeros((128 - 2 * HALF_STRIP, 128), BF16)
    even = lax.rem(lax.axis_index("col"), 2) == 0
    copies[0].wait()
    first = dot_nt(eye(STRIP, 128, 0), ends[0].astype(F32).astype(BF16))
    copies[1].wait()
    last = dot_nt(eye(STRIP, 128, 128 - STRIP), ends[1].astype(F32).astype(BF16))
    for strip, part in ((to_first, jnp.where(even, last, first)), (to_second, jnp.where(even, first, last))):
        strip[0:STRIP, :] = part[:, 0:128].astype(BF16)
        strip[HALF_STRIP : HALF_STRIP + STRIP, :] = part[:, 128:256].astype(BF16)
    for copy in copies[4:]:
        copy.wait()


def mid_kernel(mask, from_first, from_second, own, earlier, to_first, to_second):
    rows, cols = mask.shape
    left, right = sides("col", join(from_first), join(from_second))
    tables = jnp.concatenate(
        [left[STRIP:, 0:128], own[STRIP:HALF_STRIP, :].astype(F32), right[STRIP:, 0:128], jnp.zeros((16, 256), F32)],
        axis=1,
    ).astype(BF16)
    fill = jnp.zeros((128 - STRIP, 128), F32)
    strips = []
    for i in range(2):
        at = 0 if i == 0 else rows - 128
        pick = eye(STRIP, 128, 0 if i == 0 else 128 - STRIP)

        def turned(strip):
            return dot_nt(pick, jnp.concatenate([strip[0:STRIP, at : at + 128], fill], axis=0).astype(BF16))

        parts = [turned(left)[:, STRIP - RIM : STRIP], mask[(rows - STRIP) * i : (rows - STRIP) * i + STRIP, :].astype(F32), turned(right)[:, 0 : WIDE - RIM - cols]]
        strips.append(jnp.concatenate(parts, axis=1))
    even = lax.rem(lax.axis_index("row"), 2) == 0
    to_first[0:STRIP, :] = jnp.where(even, strips[1], strips[0]).astype(BF16)
    to_second[0:STRIP, :] = jnp.where(even, strips[0], strips[1]).astype(BF16)
    to_first[STRIP:, :] = tables
    to_second[STRIP:, :] = tables


def blur_matrix(shape, axis, start=0):
    lag = lax.broadcasted_iota(jnp.int32, shape, axis) - lax.broadcasted_iota(jnp.int32, shape, 1 - axis) - start
    total = sum(math.exp(-(t * t) / (2 * BLUR_SIGMA**2)) for t in range(-BLUR_HALF, BLUR_HALF + 1))
    off = (lag - BLUR_HALF).astype(F32)
    g = jnp.exp(-off * off / (2.0 * BLUR_SIGMA * BLUR_SIGMA)) * (1.0 / total)
    g = jnp.where((lag >= 0) & (lag <= 2 * BLUR_HALF), g, 0.0)
    high = g.astype(BF16)
    return high, (g - high.astype(F32)).astype(BF16)


def own_kernel(mask, taps, windows, ahead, back, g_row, g_far, g_col):
    rows, cols = mask.shape
    full = jnp.concatenate(
        [jnp.zeros((rows, RIM), F32), mask[...].astype(F32), jnp.zeros((rows, WIDE - RIM - cols), F32)], axis=1
    )
    for b in range(NB):
        windows[b] = full[:, CB * b : CB * b + 256]
    kernels, _, count = taps.shape[1:]
    flip = lax.broadcasted_iota(jnp.int32, (128, 128), 0) + lax.broadcasted_iota(jnp.int32, (128, 128), 1)
    flip = jnp.where(flip % 128 == 0, 1.0, 0.0).astype(BF16)
    ahead[...] = jnp.zeros(ahead.shape, F32)
    back[...] = jnp.zeros(back.shape, F32)
    for k in range(kernels):
        ahead[k, 0:2, 0:count] = taps[0, k].astype(F32)
        back[k, 0:2, 0:count] = taps[1, k].astype(F32)
    back[...] = dot_nn(back[...].reshape(kernels * 8, 128).astype(BF16), flip).reshape(kernels, 8, 128)
    g_row[0:128], g_row[128:256] = blur_matrix((128, 256), 1)
    g_far[0:128], g_far[128:256] = blur_matrix((128, 256), 1, 16 - BLUR_HALF)
    g_col[:, 0:128], g_col[:, 128:256] = blur_matrix((256, 128), 0)


def socs_kernel(
    entries,
    per,
    empty,
    weights,
    windows,
    row_first,
    row_second,
    col_first,
    col_second,
    own,
    ahead,
    back,
    acc,
    images,
    x_win,
    scale,
    sem,
    *scratch,
):
    across = scratch[0:2]
    down = scratch[2:4]
    first = scratch[4:6]
    groups = ahead.shape[0] // GROUP
    fetch = pltpu.make_async_copy(weights, scale, sem)
    fetch.start()
    above, below = sides("row", row_first[...].astype(F32), row_second[...].astype(F32))
    left, right = sides("col", join(col_first), join(col_second))
    rows = windows.shape[1]
    turned = jnp.concatenate(
        [
            left[STRIP - RIM : STRIP],
            jnp.zeros((128 - RIM + RIGHT_AT, rows), F32),
            right[0:RIM],
            jnp.zeros((128 - RIM - RIGHT_AT, rows), F32),
        ],
        axis=0,
    )
    turned = dot_nt(eye(rows, rows, 0), turned.astype(BF16))
    left, right = left[STRIP:, 0:128], right[STRIP:, 0:128]
    upper_rows = above[STRIP - RIM : STRIP]
    lower_rows = below[0:RIM]
    edge_rows = []
    for b in range(NB):
        lanes = slice(CB * b, CB * b + 256)
        part = windows[b]
        if b == 0:
            part = jnp.concatenate([part[:, 0:128] + turned[:, 0:128], part[:, 128:256]], axis=1)
        if b == NB - 1:
            part = jnp.concatenate([part[:, 0:128], part[:, 128:256] + turned[:, 128:256]], axis=1)
        x_win[b] = jnp.concatenate([upper_rows[:, lanes], part[0 : 256 - RIM]], axis=0).astype(BF16)
        edge_rows += [part[MAIN - RIM :], lower_rows[:, lanes]]
    edge_rows.append(jnp.zeros((256 - NB * EDGE_IN, 256), F32))
    x_win[NB] = jnp.concatenate(edge_rows, axis=0).astype(BF16)
    for s in range(2):
        for q in range(2 * GROUP):
            across[s][q, 0:96, 128:256] = jnp.zeros((96, 128), BF16)
            across[s][q, 128:CB, 0:128] = jnp.zeros((CB - 128, 128), BF16)
            down[s][q, 0:128, 128:256] = jnp.zeros((128, 128), BF16)
            down[s][q, 160:256, 0:128] = jnp.zeros((96, 128), BF16)

    slot = lax.broadcasted_iota(jnp.int32, (SLOTS, 128), 0).astype(F32)
    lane = lax.broadcasted_iota(jnp.int32, (SLOTS, 128), 1)
    found = jnp.zeros((SLOTS, 128), F32)
    col = lax.axis_index("col")
    tables = [above[STRIP:, 128 * t : 128 * t + 128] for t in range(3)]
    tables += [left, own[STRIP:HALF_STRIP, :].astype(F32), right]
    tables += [below[STRIP:, 128 * t : 128 * t + 128] for t in range(3)]
    for t, table in enumerate(tables):
        live = lane.astype(F32) < table[2:3, 0:1]
        hit = live & (table[1:2] == slot) & (lane < entries)
        image = jnp.sum(jnp.where(hit, table[0:1] + 1.0, 0.0), axis=1, keepdims=True)
        found = jnp.where(lane == t, image, found)
    cell = found.astype(jnp.int32) - 1
    images[...] = jnp.where(cell >= 0, ((cell // per) ^ col) * per + cell % per, empty)

    row = lax.broadcasted_iota(jnp.int32, (32, 128), 0)
    lane = lax.broadcasted_iota(jnp.int32, (32, 128), 1)
    low = lane >= row + 96

    def cycled(x):
        return pltpu.roll(jnp.broadcast_to(x, (128, 128)), 0, 1, stride=1, stride_axis=0)

    def build_across(m, s):
        for q in range(2 * GROUP):
            cyc = cycled(ahead[GROUP * m + q // 2, q % 2 : q % 2 + 1, :])
            head = cyc[0:96].astype(BF16)
            tail = cyc[96:128]
            over = jnp.where(low, 0.0, tail)
            across[s][q, 0:96, 0:128] = head
            across[s][q, 128:CB, 128:256] = head[0 : CB - 128]
            across[s][q, 96:128, 0:128] = jnp.where(low, tail, 0.0).astype(BF16)
            across[s][q, 96:128, 128:256] = over.astype(BF16)

    def build_down(m, s):
        for q in range(2 * GROUP):
            cyc = cycled(back[GROUP * m + q // 2, q % 2 : q % 2 + 1, :])
            head = cyc[0:32]
            over = jnp.where(low, head, 0.0).astype(BF16)
            head = jnp.where(low, 0.0, head)
            same = jnp.concatenate([head, cyc[32:128]], axis=0).astype(BF16)
            down[s][q, 0:128, 0:128] = same
            down[s][q, 128:256, 128:256] = same
            down[s][q, 128:160, 0:128] = over

    def pass_one(s):
        taps = across[s][...].reshape(2 * GROUP * CB, 256)
        for j in range(NB + 1):
            part = dot_nt(taps, x_win[j]).astype(BF16)
            for q in range(2 * GROUP):
                first[s][q, j] = part[q * CB : (q + 1) * CB]

    def pass_two(m, s):
        for g in range(GROUP):
            total = None
            for q in (2 * g, 2 * g + 1):
                second = dot_nn(first[s][q].reshape((NB + 1) * CB, 256), down[s][q])
                total = second * second if total is None else total + second * second
            part = (scale[GROUP * m + g] * total).reshape(acc.shape)
            acc[...] = part if m == 0 and g == 0 else acc[...] + part

    def stage(m, s):
        pass_one(s)
        build_down(m, s)
        if m + 1 < groups:
            build_across(m + 1, 1 - s)
        pass_two(m - 1, 1 - s)

    build_across(0, 0)
    pass_one(0)
    build_down(0, 0)
    build_across(1, 1)
    fetch.wait()

    for m in range(1, groups):
        stage(m, m % 2)
    pass_two(groups - 1, (groups - 1) % 2)


def rows_kernel(n_row, n_col, acc, g_row, out, flat):
    rows = out.shape[0]
    cols = CB * NB - 2 * BLUR_HALF
    row, col = lax.axis_index("row"), lax.axis_index("col")
    at_row = lax.broadcasted_iota(jnp.int32, (8, 384), 1) - BLUR_HALF
    row_ok = ((row > 0) | (at_row >= 0)) & ((row < n_row - 1) | (at_row < rows))
    row_ok = jnp.where(row_ok, 1.0, 0.0)
    for b in range(NB):
        edge = acc[NB, :, EDGE_IN * b : EDGE_IN * b + EDGE_OUT]
        part = jnp.concatenate(
            [acc[b, :, 0:MAIN], edge, jnp.zeros((CB, 384 - MAIN - EDGE_OUT), F32)], axis=1
        )
        part = part * row_ok[0:1]
        if b == 0:
            part = jnp.concatenate([jnp.where(col > 0, part[0:8], 0.0), part[8:]], axis=0)
        if b == NB - 1:
            part = jnp.concatenate([part[0 : CB - 8], jnp.where(col < n_col - 1, part[CB - 8 :], 0.0)], axis=0)
        flat[b * CB : (b + 1) * CB, :] = part.astype(BF16)
    flat[NB * CB :, :] = jnp.zeros((flat.shape[0] - NB * CB, 384), BF16)

    for i in range(rows // 128):
        part = dot_nt(g_row[...], flat[:, 128 * i : 128 * i + 256])
        out[128 * i : 128 * i + 128, :] = part[0:128] + part[128:]


def final_kernel(images, blurred_rows, g_far, g_col, *rest):
    shards = rest[:-4]
    out, cells, placed, blurred = rest[-4:]
    per = (cells.shape[0] - 1) // len(shards)
    rows, cols = out.shape
    table = images[...]
    for i, shard in enumerate(shards):
        rows_of = shard.shape[0] - per * 64
        cells[i * per : (i + 1) * per] = shard[rows_of:, :].reshape(per, 64, 128)
    cells[len(shards) * per] = jnp.zeros((64, 128), BF16)

    slot_rows, slot_cols = rows // 64, cols // 128
    for i in range(-1, slot_rows + 1):
        for j in range(-1, slot_cols + 1):
            ti = 0 if i < 0 else (2 if i == slot_rows else 1)
            tj = 0 if j < 0 else (2 if j == slot_cols else 1)
            image = table[(i % slot_rows) * slot_cols + j % slot_cols, 3 * ti + tj]
            lanes = slice(128 + 128 * j, 256 + 128 * j)
            if i < 0:
                placed[0:16, lanes] = cells[image, 48:64, :]
            elif i == slot_rows:
                placed[16 + rows : 32 + rows, lanes] = cells[image, 0:16, :]
            else:
                placed[16 + 64 * i : 80 + 64 * i, lanes] = cells[image]
    placed[32 + rows :, :] = jnp.zeros((placed.shape[0] - 32 - rows, placed.shape[1]), BF16)

    for i in range(rows // 128):
        part = blurred_rows[128 * i : 128 * i + 128, :]
        cell = dot_nn(g_far[...], placed[128 * i : 128 * i + 256, :])
        cell = cell[0:128] + cell[128:]
        part += cell[:, 128 - BLUR_HALF : 128 - BLUR_HALF + part.shape[1]]
        high = part.astype(BF16)
        blurred[0, 128 * i : 128 * i + 128, :] = high
        blurred[1, 128 * i : 128 * i + 128, :] = (part - high.astype(F32)).astype(BF16)
    count = cols // 128
    stacked = [
        jnp.concatenate([blurred[p, :, 128 * j : 128 * j + 256] for j in range(count)], axis=0) for p in range(2)
    ]
    part = dot_nn(stacked[0], g_col[...])
    part = part[:, 0:128] + part[:, 128:] + dot_nn(stacked[1], g_col[:, 0:128])
    for j in range(count):
        out[:, 128 * j : 128 * j + 128] = part[rows * j : rows * j + rows]


def shape(dims, dtype):
    return jax.ShapeDtypeStruct(dims, dtype)


def on_device(
    mask_pixels, across_taps, down_taps, kernel_weights, library, cell_ids, cell_slots, cell_count
):
    rows, cols = mask_pixels.shape
    kernels = across_taps.shape[0]
    entries = cell_ids.shape[-1]
    per = library.shape[0]
    n_row, n_col = lax.axis_size("row"), lax.axis_size("col")
    library = library.reshape(per * 64, 128)
    in_hbm = lambda x: pltpu.with_memory_space_constraint(x, pltpu.HBM)
    mask_hbm = in_hbm(mask_pixels)

    to_first, to_second, block, taps, line_weights = pl.pallas_call(
        prep_kernel,
        out_shape=(
            shape((2 * HALF_STRIP, 128), BF16),
            shape((128, 128), BF16),
            shape((SPARE + per * 64, 128), BF16),
            shape((2,) + across_taps.shape, BF16),
            shape(kernel_weights.shape, F32),
        ),
        in_specs=[HBM] * 3 + [VMEM] + [HBM] * 4,
        out_specs=(VMEM,) * 5,
        scratch_shapes=[
            pltpu.VMEM((2, rows, 128), jnp.int32),
            pltpu.VMEM(cell_ids.shape, jnp.int32),
            pltpu.VMEM(cell_slots.shape, jnp.int32),
            pltpu.SemaphoreType.DMA((8,)),
        ],
        compiler_params=PARAMS,
        name="prep",
    )(mask_hbm, in_hbm(cell_ids), in_hbm(cell_slots), cell_count, in_hbm(across_taps), in_hbm(down_taps), in_hbm(library), in_hbm(kernel_weights))

    def swaps(n):
        rounds = []
        for start in (0, 1):
            pairs = [(i, (i + 1) % n) for i in range(start, n, 2)]
            rounds.append(pairs + [(b, a) for a, b in pairs])
        return rounds

    second = []
    for r in range(n_row):
        second += [(r * n_col + a, r * n_col + b) for a, b in swaps(n_col)[1] if abs(a - b) == 1]
        second += [(r * n_col + a, (r ^ 1) * n_col + a) for a in (0, n_col - 1)]

    col_second = lax.ppermute(to_second, ("row", "col"), second)
    col_first = lax.ppermute(to_first, "col", swaps(n_col)[0])

    windows, ahead, back, g_row, g_far, g_col = pl.pallas_call(
        own_kernel,
        out_shape=(
            shape((NB, rows, 256), F32),
            shape((kernels, 8, 128), F32),
            shape((kernels, 8, 128), F32),
            shape((256, 256), BF16),
            shape((256, 256), BF16),
            shape((256, 256), BF16),
        ),
        in_specs=[VMEM] * 2,
        out_specs=(VMEM,) * 6,
        compiler_params=PARAMS,
        cost_estimate=pl.CostEstimate(flops=10**6, bytes_accessed=10**6, transcendentals=0),
        name="own",
    )(mask_pixels, taps)

    to_above, to_below = pl.pallas_call(
        mid_kernel,
        out_shape=(shape((STRIP + 16, WIDE), BF16),) * 2,
        in_specs=[VMEM] * 5,
        out_specs=(VMEM,) * 2,
        compiler_params=PARAMS,
        name="mid",
    )(mask_pixels, col_first, col_second, to_first, g_row)
    late, to_above, to_below = lax.optimization_barrier((library, to_above, to_below))
    blocks = {0: library}
    for d in sorted(range(1, n_col), key=lambda d: (d == n_col - 1, -(d & -d))):
        part = late if d == n_col - 1 else block
        blocks[d] = lax.ppermute(part, "col", [(i, i ^ d) for i in range(n_col)])
    shards = [blocks[d] for d in range(n_col)]
    ends = []
    for f in range(lax.axis_size("frames")):
        ends += [(f * n_row + a, f * n_row + b) for a, b in swaps(n_row)[1] if abs(a - b) == 1]
        ends += [(f * n_row + a, (f ^ 1) * n_row + a) for a in (0, n_row - 1)]
    row_first = lax.ppermute(to_above, "row", swaps(n_row)[0])
    row_second = lax.ppermute(to_below, ("frames", "row"), ends)

    acc, images = pl.pallas_call(
        functools.partial(socs_kernel, entries, per, n_col * per),
        out_shape=(shape((NB + 1, CB, 256), F32), shape((SLOTS, 128), jnp.int32)),
        in_specs=[VMEM] * 9,
        out_specs=(VMEM,) * 2,
        scratch_shapes=[
            pltpu.VMEM((NB + 1, 256, 256), BF16),
            pltpu.SMEM(kernel_weights.shape, F32),
            pltpu.SemaphoreType.DMA,
        ]
        + [pltpu.VMEM((2 * GROUP, CB, 256), BF16)] * 2
        + [pltpu.VMEM((2 * GROUP, 256, 256), BF16)] * 2
        + [pltpu.VMEM((2 * GROUP, NB + 1, CB, 256), BF16)] * 2,
        compiler_params=PARAMS,
        cost_estimate=pl.CostEstimate(flops=75 * 10**7, bytes_accessed=10**5, transcendentals=0),
        name="socs",
    )(line_weights, windows, row_first, row_second, col_first, col_second, to_first, ahead, back)

    blurred_rows = pl.pallas_call(
        functools.partial(rows_kernel, n_row, n_col),
        out_shape=shape((rows, WIDE), F32),
        in_specs=[VMEM] * 2,
        out_specs=VMEM,
        scratch_shapes=[pltpu.VMEM((WIDE, 384), BF16)],
        compiler_params=PARAMS,
        cost_estimate=pl.CostEstimate(flops=10**6, bytes_accessed=10**5, transcendentals=0),
        name="rows",
    )(acc, g_row)

    return pl.pallas_call(
        final_kernel,
        out_shape=shape((rows, cols), F32),
        in_specs=[VMEM] * (4 + n_col),
        out_specs=VMEM,
        scratch_shapes=[
            pltpu.VMEM((n_col * per + 1, 64, 128), BF16),
            pltpu.VMEM((384, cols + 256), BF16),
            pltpu.VMEM((2, rows, WIDE), BF16),
        ],
        compiler_params=PARAMS,
        name="final",
    )(images, blurred_rows, g_far, g_col, *shards)


def solution(mesh):
    placed = (
        P(("frames", "row"), "col"),
        P(),
        P(),
        P(),
        P("col", None, None),
        P(("frames", "row"), "col", None),
        P(("frames", "row"), "col", None),
        P(("frames", "row"), "col"),
    )
    return jax.shard_map(
        on_device,
        mesh=mesh,
        in_specs=placed,
        out_specs=P(("frames", "row"), "col"),
        check_vma=False,
    )
```

```python
import functools
import math

import jax
import jax.numpy as jnp
from jax import lax
from jax.experimental import pallas as pl
from jax.experimental.pallas import tpu as pltpu
from jax.sharding import PartitionSpec as P

BLUR_HALF = 8
BLUR_SIGMA = 4.0
HALF = 16
RIM = HALF + BLUR_HALF
STRIP = 32
CB = 176
NB = 3
MAIN = 224
EDGE_IN = 80
EDGE_OUT = 48
RIGHT_AT = 56
HALF_STRIP = STRIP + 16
SPARE = 16
GROUP = 2
WIDE = 640
SLOTS = 16
F32 = jnp.float32
BF16 = jnp.bfloat16
VMEM = pl.BlockSpec(memory_space=pltpu.VMEM)
SMEM = pl.BlockSpec(memory_space=pltpu.SMEM)
HBM = pl.BlockSpec(memory_space=pltpu.HBM)
PARAMS = pltpu.CompilerParams(vmem_limit_bytes=16 * 1024 * 1024)


def dot_nt(a, b):
    return lax.dot_general(a, b, (((1,), (1,)), ((), ())), preferred_element_type=F32)


def dot_nn(a, b):
    return lax.dot_general(a, b, (((1,), (0,)), ((), ())), preferred_element_type=F32)


def join(strip):
    halves = [strip[0:HALF_STRIP, :], strip[HALF_STRIP : 2 * HALF_STRIP, :]]
    return jnp.concatenate(halves, axis=1).astype(F32)


def eye(rows, cols, shift):
    at = lax.broadcasted_iota(jnp.int32, (rows, cols), 1) - lax.broadcasted_iota(jnp.int32, (rows, cols), 0)
    return jnp.where(at == shift, 1.0, 0.0).astype(BF16)


def sides(axis, first_swap, second_swap):
    index, count = lax.axis_index(axis), lax.axis_size(axis)
    even = lax.rem(index, 2) == 0
    lower = jnp.where(even, second_swap, first_swap)
    upper = jnp.where(even, first_swap, second_swap)
    return jnp.where(index > 0, lower, 0.0), jnp.where(index < count - 1, upper, 0.0)


def prep_kernel(
    mask, ids, slots, count, across, down, library, weights, to_first, to_second, block, taps, line_weights, ends, a_ids, a_slots, sems
):
    rows, cols = mask.shape
    copies = [
        pltpu.make_async_copy(mask.at[:, 0:128], ends.at[0], sems.at[0]),
        pltpu.make_async_copy(mask.at[:, cols - 128 : cols], ends.at[1], sems.at[1]),
        pltpu.make_async_copy(ids, a_ids, sems.at[2]),
        pltpu.make_async_copy(slots, a_slots, sems.at[3]),
        pltpu.make_async_copy(across, taps.at[0], sems.at[4]),
        pltpu.make_async_copy(down, taps.at[1], sems.at[5]),
        pltpu.make_async_copy(library, block.at[SPARE:], sems.at[6]),
        pltpu.make_async_copy(weights, line_weights, sems.at[7]),
    ]
    for copy in copies:
        copy.start()
    for copy in copies[2:4]:
        copy.wait()
    line = lax.broadcasted_iota(jnp.int32, (16, 128), 0)
    lane = lax.broadcasted_iota(jnp.int32, (16, 128), 1)

    def spread(x):
        x = x.astype(F32)
        x = jnp.concatenate([x, jnp.zeros((1, 128 - x.shape[1]), F32)], axis=1)
        return jnp.broadcast_to(x, (16, 128))

    table = jnp.where(line == 1, spread(a_slots[0]), jnp.broadcast_to(count[...].astype(F32), (16, 128)))
    table = jnp.where(line == 0, spread(a_ids[0]), table)
    width = jnp.where(line == 2, 1, ids.shape[2])
    table = jnp.where((lane < width) & (line < 3), table, 0.0).astype(BF16)
    for strip in (to_first, to_second):
        strip[STRIP:HALF_STRIP, :] = table
        strip[HALF_STRIP + STRIP : 2 * HALF_STRIP, :] = jnp.zeros((16, 128), BF16)
    block[0:SPARE, :] = jnp.zeros((SPARE, 128), BF16)
    to_second[2 * HALF_STRIP :, :] = jnp.zeros((128 - 2 * HALF_STRIP, 128), BF16)
    even = lax.rem(lax.axis_index("col"), 2) == 0
    copies[0].wait()
    first = dot_nt(eye(STRIP, 128, 0), ends[0].astype(F32).astype(BF16))
    copies[1].wait()
    last = dot_nt(eye(STRIP, 128, 128 - STRIP), ends[1].astype(F32).astype(BF16))
    for strip, part in ((to_first, jnp.where(even, last, first)), (to_second, jnp.where(even, first, last))):
        strip[0:STRIP, :] = part[:, 0:128].astype(BF16)
        strip[HALF_STRIP : HALF_STRIP + STRIP, :] = part[:, 128:256].astype(BF16)
    for copy in copies[4:]:
        copy.wait()


def mid_kernel(mask, from_first, from_second, own, to_first, to_second):
    rows, cols = mask.shape
    left, right = sides("col", join(from_first), join(from_second))
    tables = jnp.concatenate(
        [left[STRIP:, 0:128], own[STRIP:HALF_STRIP, :].astype(F32), right[STRIP:, 0:128], jnp.zeros((16, 256), F32)],
        axis=1,
    ).astype(BF16)
    fill = jnp.zeros((128 - STRIP, 128), F32)
    strips = []
    for i in range(2):
        at = 0 if i == 0 else rows - 128
        pick = eye(STRIP, 128, 0 if i == 0 else 128 - STRIP)

        def turned(strip):
            return dot_nt(pick, jnp.concatenate([strip[0:STRIP, at : at + 128], fill], axis=0).astype(BF16))

        parts = [turned(left)[:, STRIP - RIM : STRIP], mask[(rows - STRIP) * i : (rows - STRIP) * i + STRIP, :].astype(F32), turned(right)[:, 0 : WIDE - RIM - cols]]
        strips.append(jnp.concatenate(parts, axis=1))
    even = lax.rem(lax.axis_index("row"), 2) == 0
    to_first[0:STRIP, :] = jnp.where(even, strips[1], strips[0]).astype(BF16)
    to_second[0:STRIP, :] = jnp.where(even, strips[0], strips[1]).astype(BF16)
    to_first[STRIP:, :] = tables
    to_second[STRIP:, :] = tables


def blur_matrix(shape, axis, start=0):
    lag = lax.broadcasted_iota(jnp.int32, shape, axis) - lax.broadcasted_iota(jnp.int32, shape, 1 - axis) - start
    total = sum(math.exp(-(t * t) / (2 * BLUR_SIGMA**2)) for t in range(-BLUR_HALF, BLUR_HALF + 1))
    off = (lag - BLUR_HALF).astype(F32)
    g = jnp.exp(-off * off / (2.0 * BLUR_SIGMA * BLUR_SIGMA)) * (1.0 / total)
    g = jnp.where((lag >= 0) & (lag <= 2 * BLUR_HALF), g, 0.0)
    high = g.astype(BF16)
    return high, (g - high.astype(F32)).astype(BF16)


def own_kernel(mask, taps, windows, ahead, back, g_row, g_far, g_col):
    rows, cols = mask.shape
    full = jnp.concatenate(
        [jnp.zeros((rows, RIM), F32), mask[...].astype(F32), jnp.zeros((rows, WIDE - RIM - cols), F32)], axis=1
    )
    for b in range(NB):
        windows[b] = full[:, CB * b : CB * b + 256]
    kernels, _, count = taps.shape[1:]
    flip = lax.broadcasted_iota(jnp.int32, (128, 128), 0) + lax.broadcasted_iota(jnp.int32, (128, 128), 1)
    flip = jnp.where(flip % 128 == 0, 1.0, 0.0).astype(BF16)
    ahead[...] = jnp.zeros(ahead.shape, F32)
    back[...] = jnp.zeros(back.shape, F32)
    for k in range(kernels):
        ahead[k, 0:2, 0:count] = taps[0, k].astype(F32)
        back[k, 0:2, 0:count] = taps[1, k].astype(F32)
    back[...] = dot_nn(back[...].reshape(kernels * 8, 128).astype(BF16), flip).reshape(kernels, 8, 128)
    g_row[0:128], g_row[128:256] = blur_matrix((128, 256), 1)
    g_far[0:128], g_far[128:256] = blur_matrix((128, 256), 1, 16 - BLUR_HALF)
    g_col[:, 0:128], g_col[:, 128:256] = blur_matrix((256, 128), 0)


def socs_kernel(
    entries,
    per,
    empty,
    weights,
    windows,
    row_first,
    row_second,
    col_first,
    col_second,
    own,
    ahead,
    back,
    acc,
    images,
    x_win,
    scale,
    sem,
    *scratch,
):
    across = scratch[0:2]
    down = scratch[2:4]
    first = scratch[4:6]
    groups = ahead.shape[0] // GROUP
    fetch = pltpu.make_async_copy(weights, scale, sem)
    fetch.start()
    above, below = sides("row", row_first[...].astype(F32), row_second[...].astype(F32))
    left, right = sides("col", join(col_first), join(col_second))
    rows = windows.shape[1]
    turned = jnp.concatenate(
        [
            left[STRIP - RIM : STRIP],
            jnp.zeros((128 - RIM + RIGHT_AT, rows), F32),
            right[0:RIM],
            jnp.zeros((128 - RIM - RIGHT_AT, rows), F32),
        ],
        axis=0,
    )
    turned = dot_nt(eye(rows, rows, 0), turned.astype(BF16))
    left, right = left[STRIP:, 0:128], right[STRIP:, 0:128]
    upper_rows = above[STRIP - RIM : STRIP]
    lower_rows = below[0:RIM]
    edge_rows = []
    for b in range(NB):
        lanes = slice(CB * b, CB * b + 256)
        part = windows[b]
        if b == 0:
            part = jnp.concatenate([part[:, 0:128] + turned[:, 0:128], part[:, 128:256]], axis=1)
        if b == NB - 1:
            part = jnp.concatenate([part[:, 0:128], part[:, 128:256] + turned[:, 128:256]], axis=1)
        x_win[b] = jnp.concatenate([upper_rows[:, lanes], part[0 : 256 - RIM]], axis=0).astype(BF16)
        edge_rows += [part[MAIN - RIM :], lower_rows[:, lanes]]
    edge_rows.append(jnp.zeros((256 - NB * EDGE_IN, 256), F32))
    x_win[NB] = jnp.concatenate(edge_rows, axis=0).astype(BF16)
    for s in range(2):
        for q in range(2 * GROUP):
            across[s][q, 0:96, 128:256] = jnp.zeros((96, 128), BF16)
            across[s][q, 128:CB, 0:128] = jnp.zeros((CB - 128, 128), BF16)
            down[s][q, 0:128, 128:256] = jnp.zeros((128, 128), BF16)
            down[s][q, 160:256, 0:128] = jnp.zeros((96, 128), BF16)

    slot = lax.broadcasted_iota(jnp.int32, (SLOTS, 128), 0).astype(F32)
    lane = lax.broadcasted_iota(jnp.int32, (SLOTS, 128), 1)
    found = jnp.zeros((SLOTS, 128), F32)
    col = lax.axis_index("col")
    tables = [above[STRIP:, 128 * t : 128 * t + 128] for t in range(3)]
    tables += [left, own[STRIP:HALF_STRIP, :].astype(F32), right]
    tables += [below[STRIP:, 128 * t : 128 * t + 128] for t in range(3)]
    for t, table in enumerate(tables):
        live = lane.astype(F32) < table[2:3, 0:1]
        hit = live & (table[1:2] == slot) & (lane < entries)
        image = jnp.sum(jnp.where(hit, table[0:1] + 1.0, 0.0), axis=1, keepdims=True)
        found = jnp.where(lane == t, image, found)
    cell = found.astype(jnp.int32) - 1
    images[...] = jnp.where(cell >= 0, ((cell // per) ^ col) * per + cell % per, empty)

    row = lax.broadcasted_iota(jnp.int32, (32, 128), 0)
    lane = lax.broadcasted_iota(jnp.int32, (32, 128), 1)
    low = lane >= row + 96

    def cycled(x):
        return pltpu.roll(jnp.broadcast_to(x, (128, 128)), 0, 1, stride=1, stride_axis=0)

    def build_across(m, s):
        for q in range(2 * GROUP):
            cyc = cycled(ahead[GROUP * m + q // 2, q % 2 : q % 2 + 1, :])
            head = cyc[0:96].astype(BF16)
            tail = cyc[96:128]
            over = jnp.where(low, 0.0, tail)
            across[s][q, 0:96, 0:128] = head
            across[s][q, 128:CB, 128:256] = head[0 : CB - 128]
            across[s][q, 96:128, 0:128] = jnp.where(low, tail, 0.0).astype(BF16)
            across[s][q, 96:128, 128:256] = over.astype(BF16)

    def build_down(m, s):
        for q in range(2 * GROUP):
            cyc = cycled(back[GROUP * m + q // 2, q % 2 : q % 2 + 1, :])
            head = cyc[0:32]
            over = jnp.where(low, head, 0.0).astype(BF16)
            head = jnp.where(low, 0.0, head)
            same = jnp.concatenate([head, cyc[32:128]], axis=0).astype(BF16)
            down[s][q, 0:128, 0:128] = same
            down[s][q, 128:256, 128:256] = same
            down[s][q, 128:160, 0:128] = over

    def pass_one(s):
        taps = across[s][...].reshape(2 * GROUP * CB, 256)
        for j in range(NB + 1):
            part = dot_nt(taps, x_win[j]).astype(BF16)
            for q in range(2 * GROUP):
                first[s][q, j] = part[q * CB : (q + 1) * CB]

    def pass_two(m, s):
        for g in range(GROUP):
            total = None
            for q in (2 * g, 2 * g + 1):
                second = dot_nn(first[s][q].reshape((NB + 1) * CB, 256), down[s][q])
                total = second * second if total is None else total + second * second
            part = (scale[GROUP * m + g] * total).reshape(acc.shape)
            acc[...] = part if m == 0 and g == 0 else acc[...] + part

    def stage(m, s):
        pass_one(s)
        build_down(m, s)
        if m + 1 < groups:
            build_across(m + 1, 1 - s)
        pass_two(m - 1, 1 - s)

    build_across(0, 0)
    pass_one(0)
    build_down(0, 0)
    build_across(1, 1)
    fetch.wait()

    for m in range(1, groups):
        stage(m, m % 2)
    pass_two(groups - 1, (groups - 1) % 2)


def rows_kernel(n_row, n_col, acc, g_row, out, flat):
    rows = out.shape[0]
    cols = CB * NB - 2 * BLUR_HALF
    row, col = lax.axis_index("row"), lax.axis_index("col")
    at_row = lax.broadcasted_iota(jnp.int32, (8, 384), 1) - BLUR_HALF
    row_ok = ((row > 0) | (at_row >= 0)) & ((row < n_row - 1) | (at_row < rows))
    row_ok = jnp.where(row_ok, 1.0, 0.0)
    for b in range(NB):
        edge = acc[NB, :, EDGE_IN * b : EDGE_IN * b + EDGE_OUT]
        part = jnp.concatenate(
            [acc[b, :, 0:MAIN], edge, jnp.zeros((CB, 384 - MAIN - EDGE_OUT), F32)], axis=1
        )
        part = part * row_ok[0:1]
        if b == 0:
            part = jnp.concatenate([jnp.where(col > 0, part[0:8], 0.0), part[8:]], axis=0)
        if b == NB - 1:
            part = jnp.concatenate([part[0 : CB - 8], jnp.where(col < n_col - 1, part[CB - 8 :], 0.0)], axis=0)
        flat[b * CB : (b + 1) * CB, :] = part.astype(BF16)
    flat[NB * CB :, :] = jnp.zeros((flat.shape[0] - NB * CB, 384), BF16)

    for i in range(rows // 128):
        part = dot_nt(g_row[...], flat[:, 128 * i : 128 * i + 256])
        out[128 * i : 128 * i + 128, :] = part[0:128] + part[128:]


def final_kernel(images, blurred_rows, g_far, g_col, *rest):
    shards = rest[:-4]
    out, cells, placed, blurred = rest[-4:]
    per = (cells.shape[0] - 1) // len(shards)
    rows, cols = out.shape
    table = images[...]
    for i, shard in enumerate(shards):
        rows_of = shard.shape[0] - per * 64
        cells[i * per : (i + 1) * per] = shard[rows_of:, :].reshape(per, 64, 128)
    cells[len(shards) * per] = jnp.zeros((64, 128), BF16)

    slot_rows, slot_cols = rows // 64, cols // 128
    for i in range(-1, slot_rows + 1):
        for j in range(-1, slot_cols + 1):
            ti = 0 if i < 0 else (2 if i == slot_rows else 1)
            tj = 0 if j < 0 else (2 if j == slot_cols else 1)
            image = table[(i % slot_rows) * slot_cols + j % slot_cols, 3 * ti + tj]
            lanes = slice(128 + 128 * j, 256 + 128 * j)
            if i < 0:
                placed[0:16, lanes] = cells[image, 48:64, :]
            elif i == slot_rows:
                placed[16 + rows : 32 + rows, lanes] = cells[image, 0:16, :]
            else:
                placed[16 + 64 * i : 80 + 64 * i, lanes] = cells[image]
    placed[32 + rows :, :] = jnp.zeros((placed.shape[0] - 32 - rows, placed.shape[1]), BF16)

    for i in range(rows // 128):
        part = blurred_rows[128 * i : 128 * i + 128, :]
        cell = dot_nn(g_far[...], placed[128 * i : 128 * i + 256, :])
        cell = cell[0:128] + cell[128:]
        part += cell[:, 128 - BLUR_HALF : 128 - BLUR_HALF + part.shape[1]]
        high = part.astype(BF16)
        blurred[0, 128 * i : 128 * i + 128, :] = high
        blurred[1, 128 * i : 128 * i + 128, :] = (part - high.astype(F32)).astype(BF16)
    count = cols // 128
    stacked = [
        jnp.concatenate([blurred[p, :, 128 * j : 128 * j + 256] for j in range(count)], axis=0) for p in range(2)
    ]
    part = dot_nn(stacked[0], g_col[...])
    part = part[:, 0:128] + part[:, 128:] + dot_nn(stacked[1], g_col[:, 0:128])
    for j in range(count):
        out[:, 128 * j : 128 * j + 128] = part[rows * j : rows * j + rows]


def shape(dims, dtype):
    return jax.ShapeDtypeStruct(dims, dtype)


def on_device(
    mask_pixels, across_taps, down_taps, kernel_weights, library, cell_ids, cell_slots, cell_count
):
    rows, cols = mask_pixels.shape
    kernels = across_taps.shape[0]
    entries = cell_ids.shape[-1]
    per = library.shape[0]
    n_row, n_col = lax.axis_size("row"), lax.axis_size("col")
    library = library.reshape(per * 64, 128)
    in_hbm = lambda x: pltpu.with_memory_space_constraint(x, pltpu.HBM)
    mask_hbm = in_hbm(mask_pixels)

    to_first, to_second, block, taps, line_weights = pl.pallas_call(
        prep_kernel,
        out_shape=(
            shape((2 * HALF_STRIP, 128), BF16),
            shape((128, 128), BF16),
            shape((SPARE + per * 64, 128), BF16),
            shape((2,) + across_taps.shape, BF16),
            shape(kernel_weights.shape, F32),
        ),
        in_specs=[HBM] * 3 + [VMEM] + [HBM] * 4,
        out_specs=(VMEM,) * 5,
        scratch_shapes=[
            pltpu.VMEM((2, rows, 128), jnp.int32),
            pltpu.VMEM(cell_ids.shape, jnp.int32),
            pltpu.VMEM(cell_slots.shape, jnp.int32),
            pltpu.SemaphoreType.DMA((8,)),
        ],
        compiler_params=PARAMS,
        name="prep",
    )(mask_hbm, in_hbm(cell_ids), in_hbm(cell_slots), cell_count, in_hbm(across_taps), in_hbm(down_taps), in_hbm(library), in_hbm(kernel_weights))

    def swaps(n):
        rounds = []
        for start in (0, 1):
            pairs = [(i, (i + 1) % n) for i in range(start, n, 2)]
            rounds.append(pairs + [(b, a) for a, b in pairs])
        return rounds

    second = []
    for r in range(n_row):
        second += [(r * n_col + a, r * n_col + b) for a, b in swaps(n_col)[1] if abs(a - b) == 1]
        second += [(r * n_col + a, (r ^ 1) * n_col + a) for a in (0, n_col - 1)]

    col_second = lax.ppermute(to_second, ("row", "col"), second)
    col_first = lax.ppermute(to_first, "col", swaps(n_col)[0])

    to_above, to_below = pl.pallas_call(
        mid_kernel,
        out_shape=(shape((STRIP + 16, WIDE), BF16),) * 2,
        in_specs=[VMEM] * 4,
        out_specs=(VMEM,) * 2,
        compiler_params=PARAMS,
        name="mid",
    )(mask_pixels, col_first, col_second, to_first)
    late, to_above, to_below = lax.optimization_barrier((library, to_above, to_below))
    blocks = {0: library}
    for d in sorted(range(1, n_col), key=lambda d: (d == n_col - 1, -(d & -d))):
        part = late if d == n_col - 1 else block
        blocks[d] = lax.ppermute(part, "col", [(i, i ^ d) for i in range(n_col)])
    shards = [blocks[d] for d in range(n_col)]
    ends = []
    for f in range(lax.axis_size("frames")):
        ends += [(f * n_row + a, f * n_row + b) for a, b in swaps(n_row)[1] if abs(a - b) == 1]
        ends += [(f * n_row + a, (f ^ 1) * n_row + a) for a in (0, n_row - 1)]
    row_first = lax.ppermute(to_above, "row", swaps(n_row)[0])
    row_second = lax.ppermute(to_below, ("frames", "row"), ends)

    windows, ahead, back, g_row, g_far, g_col = pl.pallas_call(
        own_kernel,
        out_shape=(
            shape((NB, rows, 256), F32),
            shape((kernels, 8, 128), F32),
            shape((kernels, 8, 128), F32),
            shape((256, 256), BF16),
            shape((256, 256), BF16),
            shape((256, 256), BF16),
        ),
        in_specs=[VMEM] * 2,
        out_specs=(VMEM,) * 6,
        compiler_params=PARAMS,
        cost_estimate=pl.CostEstimate(flops=10**6, bytes_accessed=10**6, transcendentals=0),
        name="own",
    )(mask_pixels, taps)

    acc, images = pl.pallas_call(
        functools.partial(socs_kernel, entries, per, n_col * per),
        out_shape=(shape((NB + 1, CB, 256), F32), shape((SLOTS, 128), jnp.int32)),
        in_specs=[VMEM] * 9,
        out_specs=(VMEM,) * 2,
        scratch_shapes=[
            pltpu.VMEM((NB + 1, 256, 256), BF16),
            pltpu.SMEM(kernel_weights.shape, F32),
            pltpu.SemaphoreType.DMA,
        ]
        + [pltpu.VMEM((2 * GROUP, CB, 256), BF16)] * 2
        + [pltpu.VMEM((2 * GROUP, 256, 256), BF16)] * 2
        + [pltpu.VMEM((2 * GROUP, NB + 1, CB, 256), BF16)] * 2,
        compiler_params=PARAMS,
        cost_estimate=pl.CostEstimate(flops=75 * 10**7, bytes_accessed=10**5, transcendentals=0),
        name="socs",
    )(line_weights, windows, row_first, row_second, col_first, col_second, to_first, ahead, back)

    blurred_rows = pl.pallas_call(
        functools.partial(rows_kernel, n_row, n_col),
        out_shape=shape((rows, WIDE), F32),
        in_specs=[VMEM] * 2,
        out_specs=VMEM,
        scratch_shapes=[pltpu.VMEM((WIDE, 384), BF16)],
        compiler_params=PARAMS,
        cost_estimate=pl.CostEstimate(flops=10**6, bytes_accessed=10**5, transcendentals=0),
        name="rows",
    )(acc, g_row)

    return pl.pallas_call(
        final_kernel,
        out_shape=shape((rows, cols), F32),
        in_specs=[VMEM] * (4 + n_col),
        out_specs=VMEM,
        scratch_shapes=[
            pltpu.VMEM((n_col * per + 1, 64, 128), BF16),
            pltpu.VMEM((384, cols + 256), BF16),
            pltpu.VMEM((2, rows, WIDE), BF16),
        ],
        compiler_params=PARAMS,
        name="final",
    )(images, blurred_rows, g_far, g_col, *shards)


def solution(mesh):
    placed = (
        P(("frames", "row"), "col"),
        P(),
        P(),
        P(),
        P("col", None, None),
        P(("frames", "row"), "col", None),
        P(("frames", "row"), "col", None),
        P(("frames", "row"), "col"),
    )
    return jax.shard_map(
        on_device,
        mesh=mesh,
        in_specs=placed,
        out_specs=P(("frames", "row"), "col"),
        check_vma=False,
    )
```
